256 devices in a mesh: lat: 4 (over y_hi, core), lon: 32 (over z, x), tp: 2 (over y_lo).
Axes of the slice: x: 4, y: 4 (y_hi: 2, y_lo: 2; y = y_hi * 2 + y_lo), z: 8, core: 2. Of those that a mesh axis runs over, the one named last changes fastest.
Arguments:
- inputs: bfloat16 [8, 24, 384, 192], P(None, 'lat', 'lon'), may hold values from -6 to 6
- residual_mid: bfloat16 [8, 24, 384, 192], P(None, 'lat', 'lon'), may hold values from -6 to 6
- grad_out: bfloat16 [8, 24, 384, 192], P(None, 'lat', 'lon'), may hold values from -6 to 6
- mask_ids: int32 [8, 24, 384], P(None, 'lat', 'lon'), may hold values from 0 to 2
- key_valid: int32 [8, 24, 384], P(None, 'lat', 'lon'), may hold values 0 or 1
- bias_index: int32 [144, 144], replicated, may hold values from 0 to 3311
- pos_bias: float32 [4, 4, 6, 3312], P('lat', None, 'tp'), may hold values from -3 to 257
- norm1_gain: float32 [192], replicated, may hold values from 0.1 to 1.9
- qkv_weight: bfloat16 [3, 192, 192], P(None, None, 'tp'), may hold values from -0.4375 to 0.4375
- proj_weight: bfloat16 [192, 192], P('tp'), may hold values from -0.4375 to 0.4375
- norm2_gain: float32 [192], replicated, may hold values from 0.1 to 1.9
- fc1_weight: bfloat16 [192, 768], P(None, 'tp'), may hold values from -0.4375 to 0.4375
- fc2_weight: bfloat16 [768, 192], P('tp'), may hold values from -0.21875 to 0.21875
Outputs:
- grad_inputs: bfloat16 [8, 24, 384, 192], P(None, 'lat', 'lon')
- qkv_grad: float32 [3, 192, 192], P(None, None, 'tp')
- proj_grad: float32 [192, 192], P('tp')
- fc1_grad: float32 [192, 768], P(None, 'tp')
- fc2_grad: float32 [768, 192], P('tp')
- norm1_gain_grad: float32 [192], P('tp')
- norm2_gain_grad: float32 [192], P('tp')
- pos_bias_grad: float32 [4, 4, 6, 3312], P('lat', None, 'tp')
The draws below stay inside these ranges and needn't reach their ends.
All inputs are finite; a program needn't handle non-finite values. No bound on the sum of `key_valid` on one device may be relied on, other than what follows from the above.
Results may differ from the reference program's by a relative error of at most 0.024.
Values may be sent and summed in bfloat16 or wider, within the bound.
No kernel may reach another device: no remote copies, remote signals or barrier semaphores. Data moves between devices by JAX's collectives and lax.ppermute only.
A program may use at most 128 MiB of HBM per device.

```python
import jax
import jax.numpy as jnp
from jax import lax

C = 192
HEADS = 6
HD = 32
HID = 768
NZ = 8
WZ = 2
WLAT = 6
WLON = 12
WIN = 144
TABLE = 3312
NLAT = 24
NLON = 384
NZW = 4
NLATW = 4
N_TP = 2


def draw_pos_bias(key, part):
    key = jax.random.fold_in(key, 11)
    shape = (NLATW, NZW, HEADS, TABLE)
    base_key = jax.random.fold_in(key, 0)
    return jnp.clip(0.6 * jax.random.normal(base_key, shape, jnp.float32), -3.0, 3.0)


def touch_ends(array, stream_key, low, high):
    dims = array.shape
    place = [jax.random.randint(jax.random.fold_in(stream_key, axis), (), 0, dims[axis]) for axis in range(len(dims))]
    array = array.at[tuple(place)].set(low)
    longest = dims.index(max(dims))
    place[longest] = (place[longest] + 1) % dims[longest]
    return array.at[tuple(place)].set(high)


def levels(stream_key, extent, cuts, low, largest):
    def one(position, shards_of):
        heights = jax.random.uniform(jax.random.fold_in(jax.random.fold_in(stream_key, 6), position), (shards_of,), jnp.float32, low / len(cuts), largest / len(cuts))
        return jnp.repeat(jnp.exp(heights), extent[position] // shards_of).reshape((-1,) + (1,) * (len(extent) - position - 1))

    factor_of = one(*cuts[0])
    for cut in cuts[1:]:
        factor_of = factor_of * one(*cut)
    return factor_of


def gaussian(key, shape, spread, bound, shards=(), kind=jnp.bfloat16):
    values = spread * jax.random.normal(key, shape, jnp.float32)
    if shards:
        values = values * levels(key, shape, shards, -0.22, 0.18)
    return jnp.clip(values, -bound, bound).astype(kind)


def setup_inputs(seed: int = 0) -> dict:
    splits = jax.random.split(jax.random.key(seed), 14)
    return {
        "inputs": gaussian(splits[0], (NZ, NLAT, NLON, C), 1.0, 6.0, ((1, 4), (2, 32))),
        "residual_mid": gaussian(splits[1], (NZ, NLAT, NLON, C), 1.0, 6.0, ((1, 4), (2, 32))),
        "grad_out": gaussian(splits[2], (NZ, NLAT, NLON, C), 1.0, 6.0, ((1, 4), (2, 32))),
        "mask_ids": touch_ends(jax.random.randint(splits[3], (NZ, NLAT, NLON), 0, 3), jax.random.fold_in(splits[3], 1), 0, 2).astype(jnp.int32),
        "key_valid": touch_ends((jax.random.randint(splits[4], (NZ, NLAT, NLON), 0, 4) < 3).astype(jnp.int32), jax.random.fold_in(splits[4], 1), 0, 1),
        "bias_index": touch_ends(jax.random.randint(splits[5], (WIN, WIN), 0, TABLE), jax.random.fold_in(splits[5], 1), 0, TABLE - 1).astype(jnp.int32),
        "pos_bias": draw_pos_bias(jax.random.fold_in(splits[13], 71), 0),
        "norm1_gain": jnp.clip(1.0 + 0.18 * jax.random.normal(splits[7], (C,), jnp.float32), 0.1, 1.9),
        "qkv_weight": gaussian(splits[8], (3, C, C), C ** -0.5, 0.4375, ((2, 2),)),
        "proj_weight": gaussian(splits[9], (C, C), C ** -0.5, 0.4375, ((0, 2),)),
        "norm2_gain": jnp.clip(1.0 + 0.18 * jax.random.normal(splits[10], (C,), jnp.float32), 0.1, 1.9),
        "fc1_weight": gaussian(splits[11], (C, HID), C ** -0.5, 0.4375, ((1, 2),)),
        "fc2_weight": gaussian(splits[12], (HID, C), HID ** -0.5, 0.21875, ((0, 2),)),
    }


EPSILON = 1e-05
EXCLUDED = -1e+30

def layer_stats(field_rows):
    mean_value = lax.optimization_barrier(jnp.mean(field_rows, axis=-1, keepdims=True))
    centred = field_rows - mean_value
    inverse = lax.rsqrt(lax.optimization_barrier(jnp.mean(centred * centred, axis=-1, keepdims=True)) + EPSILON)
    return (centred * inverse, inverse)

def norm_backward(grad_normed, gain, normed, inverse):
    scaled = grad_normed * gain
    first = lax.optimization_barrier(jnp.mean(scaled, axis=-1, keepdims=True))
    second = lax.optimization_barrier(jnp.mean(scaled * normed, axis=-1, keepdims=True))
    return (scaled - first - normed * second) * inverse

def gelu_pair(pre_act):
    normal_cdf = 0.5 * (1.0 + lax.erf(pre_act * 0.7071067811865476))
    normal_pdf = 0.3989422804014327 * jnp.exp(-0.5 * pre_act * pre_act)
    return (pre_act * normal_cdf, normal_cdf + pre_act * normal_pdf)

def rounded(values):
    return lax.optimization_barrier(values.astype(jnp.bfloat16)).astype(jnp.float32)

def band_windows(band):
    depth = band.shape[-1]
    parts = band.reshape(NZ // WZ, WZ, WLAT, band.shape[2] // WLON, WLON, depth)
    return parts.transpose(0, 3, 1, 2, 4, 5).reshape(NZ // WZ, band.shape[2] // WLON, WIN, depth)

def windows_band(windows, lon_cells):
    depth = windows.shape[-1]
    parts = windows.reshape(NZ // WZ, lon_cells // WLON, WZ, WLAT, WLON, depth)
    return parts.transpose(0, 2, 3, 1, 4, 5).reshape(NZ, WLAT, lon_cells, depth)

def as_bands(field):
    return jnp.swapaxes(field.reshape((NZ, NLATW, WLAT) + field.shape[2:]), 0, 1)

def reference(inputs, residual_mid, grad_out, mask_ids, key_valid, bias_index, pos_bias, norm1_gain, qkv_weight, proj_weight, norm2_gain, fc1_weight, fc2_weight):
    hid_share = HID // N_TP
    head_share = C // N_TP
    weight_scale = (NZ * NLAT * NLON) ** (-0.5)
    table_scale = (NLON // WLON) ** (-0.5)
    attn_scale = HD ** (-0.5)

    def mlp_level(totals, level_pair):
        grad_up, grad_down, grad_gain = totals
        mid_rows = level_pair[0].reshape(-1, C).astype(jnp.float32)
        up_rows = level_pair[1].reshape(-1, C)
        normed, inverse = layer_stats(mid_rows)
        lowered = (normed * norm2_gain).astype(jnp.bfloat16)
        pre_act = jnp.dot(lowered, fc1_weight, preferred_element_type=jnp.float32)
        active, slopes = gelu_pair(pre_act)
        active = active.astype(jnp.bfloat16)
        grad_down = grad_down + jnp.dot(active.T, up_rows, preferred_element_type=jnp.float32)
        grad_pre = (jnp.dot(up_rows, fc2_weight.T, preferred_element_type=jnp.float32) * slopes).astype(jnp.bfloat16)
        grad_up = grad_up + jnp.dot(lowered.T, grad_pre, preferred_element_type=jnp.float32)
        grad_normed = jnp.zeros(mid_rows.shape, jnp.float32)
        for head_part in range(N_TP):
            lower = head_part * hid_share
            grad_normed = grad_normed + rounded(jnp.dot(grad_pre[:, lower:lower + hid_share], fc1_weight[:, lower:lower + hid_share].T, preferred_element_type=jnp.float32))
        grad_gain = grad_gain + lax.optimization_barrier(jnp.sum(grad_normed * normed, axis=0))
        grad_mid = (up_rows.astype(jnp.float32) + norm_backward(grad_normed, norm2_gain, normed, inverse)).astype(jnp.bfloat16)
        return ((grad_up, grad_down, grad_gain), grad_mid.reshape(NLAT, NLON, C))
    mlp_start = (jnp.zeros((C, HID), jnp.float32), jnp.zeros((HID, C), jnp.float32), jnp.zeros((C,), jnp.float32))
    (grad_up, grad_down, grad_gain2), grad_mid = lax.scan(mlp_level, mlp_start, (residual_mid, grad_out))

    def norm_level(level_in):
        normed, inverse = layer_stats(level_in.reshape(-1, C).astype(jnp.float32))
        return (normed * norm1_gain).astype(jnp.bfloat16).reshape(NLAT, NLON, C)
    lowered_one = lax.map(norm_level, inputs)
    forward_shift = (-(WZ // 2), -(WLAT // 2), -(WLON // 2))
    shifted_low = jnp.roll(lowered_one, forward_shift, axis=(0, 1, 2))
    shifted_grad = jnp.roll(grad_mid, forward_shift, axis=(0, 1, 2))
    lon_windows = NLON // WLON
    heads_shape = (NZ // WZ, lon_windows, WIN, HEADS, HD)

    def attend_band(totals, band):
        grad_qkv, grad_proj = totals
        band_low, band_grad, band_ids, band_valid, band_table = band
        win_low = band_windows(band_low).reshape(-1, C)
        win_grad = band_windows(band_grad).reshape(-1, C)
        ids_win = band_windows(band_ids[..., None])[..., 0]
        valid_win = band_windows(band_valid[..., None])[..., 0]
        query_f = rounded(jnp.dot(win_low, qkv_weight[0], preferred_element_type=jnp.float32)).reshape(heads_shape)
        key_f = rounded(jnp.dot(win_low, qkv_weight[1], preferred_element_type=jnp.float32)).reshape(heads_shape)
        value_f = rounded(jnp.dot(win_low, qkv_weight[2], preferred_element_type=jnp.float32)).reshape(heads_shape)
        scores = jnp.einsum('abqhd,abkhd->abhqk', query_f, key_f) * attn_scale
        table = jnp.take(band_table, bias_index, axis=2)
        scores = scores + table[:, None]
        allowed = (ids_win[..., :, None] == ids_win[..., None, :]) & (valid_win[..., None, :] > 0)
        allowed = allowed | jnp.eye(WIN, dtype=bool)
        scores = jnp.where(allowed[:, :, None], scores, EXCLUDED)
        top = lax.optimization_barrier(jnp.max(scores, axis=-1, keepdims=True))
        expo = jnp.exp(scores - top)
        prob = expo / lax.optimization_barrier(jnp.sum(expo, axis=-1, keepdims=True))
        prob_low = rounded(prob)
        attended = jnp.einsum('abhqk,abkhd->abqhd', prob_low, value_f).astype(jnp.bfloat16).reshape(-1, C)
        grad_proj = grad_proj + jnp.dot(attended.T, win_grad, preferred_element_type=jnp.float32)
        grad_att = rounded(jnp.dot(win_grad, proj_weight.T, preferred_element_type=jnp.float32)).reshape(heads_shape)
        grad_value = jnp.einsum('abhqk,abqhd->abkhd', prob_low, grad_att).astype(jnp.bfloat16).reshape(-1, C)
        grad_prob = jnp.einsum('abqhd,abkhd->abhqk', grad_att, value_f)
        grad_score = prob * (grad_prob - lax.optimization_barrier(jnp.sum(grad_prob * prob, axis=-1, keepdims=True)))
        table_terms = lax.optimization_barrier(jnp.sum(grad_score, axis=1)).reshape(-1, WIN * WIN)
        grad_table = jax.ops.segment_sum(table_terms.T, bias_index.reshape(-1), num_segments=TABLE).T.reshape(NZ // WZ, HEADS, TABLE)
        score_low = rounded(grad_score * attn_scale)
        grad_query = jnp.einsum('abhqk,abkhd->abqhd', score_low, key_f).astype(jnp.bfloat16).reshape(-1, C)
        grad_key = jnp.einsum('abhqk,abqhd->abkhd', score_low, query_f).astype(jnp.bfloat16).reshape(-1, C)
        grad_qkv = grad_qkv + jnp.stack([jnp.dot(win_low.T, grad_query, preferred_element_type=jnp.float32), jnp.dot(win_low.T, grad_key, preferred_element_type=jnp.float32), jnp.dot(win_low.T, grad_value, preferred_element_type=jnp.float32)])
        grad_low = jnp.zeros(win_low.shape, jnp.float32)
        for head_part in range(N_TP):
            lower = head_part * head_share
            upper = lower + head_share
            partial_value = jnp.dot(grad_query[:, lower:upper], qkv_weight[0][:, lower:upper].T, preferred_element_type=jnp.float32)
            partial_value = partial_value + jnp.dot(grad_key[:, lower:upper], qkv_weight[1][:, lower:upper].T, preferred_element_type=jnp.float32)
            partial_value = partial_value + jnp.dot(grad_value[:, lower:upper], qkv_weight[2][:, lower:upper].T, preferred_element_type=jnp.float32)
            grad_low = grad_low + rounded(partial_value)
        grad_band = windows_band(grad_low.reshape(NZ // WZ, lon_windows, WIN, C), NLON)
        return ((grad_qkv, grad_proj), (grad_table, grad_band))
    band_inputs = (as_bands(shifted_low), as_bands(shifted_grad), as_bands(mask_ids), as_bands(key_valid), pos_bias)
    attn_start = (jnp.zeros((3, C, C), jnp.float32), jnp.zeros((C, C), jnp.float32))
    (grad_qkv, grad_proj), (grad_table, grad_bands) = lax.scan(attend_band, attn_start, band_inputs)
    grad_shifted = jnp.swapaxes(grad_bands, 0, 1).reshape(NZ, NLAT, NLON, C)
    grad_lowered = jnp.roll(grad_shifted, (WZ // 2, WLAT // 2, WLON // 2), axis=(0, 1, 2))

    def input_level(totals, level_trio):
        level_in, level_mid, level_grad = level_trio
        normed, inverse = layer_stats(level_in.reshape(-1, C).astype(jnp.float32))
        grad_rows = level_grad.reshape(-1, C)
        totals = totals + lax.optimization_barrier(jnp.sum(grad_rows * normed, axis=0))
        result = (level_mid.reshape(-1, C).astype(jnp.float32) + norm_backward(grad_rows, norm1_gain, normed, inverse)).astype(jnp.bfloat16)
        return (totals, result.reshape(NLAT, NLON, C))
    grad_gain1, grad_inputs = lax.scan(input_level, jnp.zeros((C,), jnp.float32), (inputs, grad_mid, grad_lowered))
    return (grad_inputs, grad_qkv * weight_scale, grad_proj * weight_scale, grad_up * weight_scale, grad_down * weight_scale, grad_gain1 * weight_scale, grad_gain2 * weight_scale, grad_table * table_scale)
```

```python
import functools

import jax
import jax.numpy as jnp
import numpy as np
from jax import lax
from jax.experimental import pallas as pl
from jax.experimental.pallas import tpu as pltpu
from jax.sharding import PartitionSpec as P

HD = 32
EPSILON = 1e-05
EXCLUDED = -1e30
BF = jnp.bfloat16
F32 = jnp.float32
I32 = jnp.int32
VM = pltpu.CompilerParams(vmem_limit_bytes=48 * 1024 * 1024)


def shape(dims, kind):
    return jax.ShapeDtypeStruct(dims, kind)


def dot_nn(a, b):
    return lax.dot_general(a, b, (((1,), (0,)), ((), ())), preferred_element_type=F32)


def dot_nt(a, b):
    return lax.dot_general(a, b, (((1,), (1,)), ((), ())), preferred_element_type=F32)


def dot_tn(a, b):
    return lax.dot_general(a, b, (((0,), (0,)), ((), ())), preferred_element_type=F32)


def layer_stats(rows):
    mean = jnp.mean(rows, axis=-1, keepdims=True)
    centred = rows - mean
    inverse = lax.rsqrt(jnp.mean(centred * centred, axis=-1, keepdims=True) + EPSILON)
    return centred * inverse, inverse


def norm_backward(grad_normed, gain, normed, inverse):
    scaled = grad_normed * gain
    first = jnp.mean(scaled, axis=-1, keepdims=True)
    second = jnp.mean(scaled * normed, axis=-1, keepdims=True)
    return (scaled - first - normed * second) * inverse


def gelu_pair(pre):
    cdf = 0.5 * (1.0 + lax.erf(pre * 0.7071067811865476))
    pdf = 0.3989422804014327 * jnp.exp(-0.5 * pre * pre)
    return pre * cdf, cdf + pre * pdf


def to_quarters(field_ref, scratch):
    for level in range(8):
        for lat in range(6):
            rows = field_ref[((level + 1) % 8) * 6 + lat].astype(F32)
            quarter = (lat // 3) * 2
            start = quarter * 144 + level * 18 + (lat % 3) * 6
            scratch[start : start + 6, :] = rows[0:6]
            scratch[start + 144 : start + 150, :] = rows[6:12]


def to_windows(parts, scratch):
    for s in range(4):
        rows = parts[s][...].astype(F32)
        for w in range(4):
            scratch[w * 144 + s * 36 : w * 144 + s * 36 + 36, :] = rows[w * 36 : w * 36 + 36]


def split_kernel(field_ref, o0, o1, o2, o3, scratch):
    to_quarters(field_ref, scratch)
    for q, out in enumerate((o0, o1, o2, o3)):
        out[...] = scratch[q * 144 : q * 144 + 144, :].astype(BF)


def split(field):
    return pl.pallas_call(
        split_kernel,
        out_shape=tuple(shape((144, 192), BF) for _ in range(4)),
        scratch_shapes=[pltpu.VMEM((576, 192), F32)],
        compiler_params=VM,
        name="split",
    )(field)


def mlp_kernel(mid_ref, up_ref, gain_ref, fc1_ref, fc2_ref, part_ref, midq_ref, upq_ref, down_ref, upg_ref, mid_s, up_s):
    to_quarters(mid_ref, mid_s)
    to_quarters(up_ref, up_s)
    mid = mid_s[...]
    up = up_s[...].astype(BF)
    midq_ref[...] = mid.astype(BF)
    upq_ref[...] = up
    normed, _ = layer_stats(mid)
    lowered = (normed * gain_ref[...]).astype(BF)
    pre = dot_nn(lowered, fc1_ref[...])
    active, slopes = gelu_pair(pre)
    grad_pre = (dot_nt(up, fc2_ref[...]) * slopes).astype(BF)
    part_ref[...] = dot_nt(grad_pre, fc1_ref[...]).astype(BF)
    down_ref[...] = dot_tn(active.astype(BF), up).astype(BF)
    upg_ref[...] = dot_tn(lowered, grad_pre).astype(BF)


def mlp(mid, up, gain, fc1, fc2):
    return pl.pallas_call(
        mlp_kernel,
        out_shape=(
            shape((576, 192), BF),
            shape((576, 192), BF),
            shape((576, 192), BF),
            shape((384, 192), BF),
            shape((192, 384), BF),
        ),
        scratch_shapes=[pltpu.VMEM((576, 192), F32)] * 2,
        compiler_params=VM,
        name="mlp",
    )(mid, up, gain, fc1, fc2)


def middle_kernel(mid_ref, up_ref, own_ref, other_ref, gain_ref, o0, o1, o2, o3, gain_out):
    normed, inverse = layer_stats(mid_ref[...].astype(F32))
    grad = own_ref[...].astype(F32) + other_ref[...].astype(F32)
    gain_out[...] = jnp.sum(grad * normed, axis=0, keepdims=True)
    out = up_ref[...].astype(F32) + norm_backward(grad, gain_ref[...], normed, inverse)
    for q, o in enumerate((o0, o1, o2, o3)):
        o[...] = out[q * 144 : q * 144 + 144].astype(BF)


def middle(mid, up, own, other, gain):
    return pl.pallas_call(
        middle_kernel,
        out_shape=tuple(shape((144, 192), BF) for _ in range(4)) + (shape((1, 192), F32),),
        compiler_params=VM,
        name="middle",
    )(mid, up, own, other, gain)


def window_order():
    canon = np.arange(144).reshape(2, 2, 3, 2, 6).transpose(1, 3, 0, 2, 4).reshape(-1)
    order = np.zeros((144, 144), np.float32)
    order[np.arange(144), canon] = 1.0
    return order


def pack_tail(tail):
    spread = (lax.broadcasted_iota(I32, (16, 128), 1) & 15) == lax.broadcasted_iota(I32, (16, 128), 0)
    wide = dot_nn(tail, spread.astype(F32).astype(BF))
    here = (lax.broadcasted_iota(I32, (144, 128), 1) >> 4) == (lax.broadcasted_iota(I32, (144, 128), 0) & 7)
    wide = jnp.where(here, wide, 0.0).astype(BF)
    rows = (lax.broadcasted_iota(I32, (24, 144), 1) >> 3) == lax.broadcasted_iota(I32, (24, 144), 0)
    return dot_nn(rows.astype(F32).astype(BF), wide)


def gather_kernel(index_ref, order_ref, bias_ref, main_ref, tail_ref, lo_ref, hi_ref, table, tail_s):
    index = index_ref[...]
    order = order_ref[...]
    pieces = []
    for part in (index & 127, index >> 7):
        moved = dot_nt(dot_nn(order, part.astype(F32).astype(BF)).astype(BF), order)
        pieces.append((moved[:, 0:128].astype(I32), pack_tail(moved[:, 128:144].astype(BF)).astype(I32)))
    lo_ref[0:144, :] = pieces[0][0]
    lo_ref[144:168, :] = pieces[0][1]
    hi_ref[0:144, :] = pieces[1][0]
    hi_ref[144:168, :] = pieces[1][1]
    for r in range(12):
        for c in range(26):
            wide = min(128, 3312 - c * 128)
            table[r, c : c + 1, 0:wide] = bias_ref[r // 3, r % 3 : r % 3 + 1, c * 128 : c * 128 + wide]

    def look_up(r, rows, count):
        lo, hi = lo_ref[rows, :], hi_ref[rows, :]
        acc = jnp.zeros((count, 128), F32)
        for c in range(26):
            entry = jnp.broadcast_to(table[r, c : c + 1, :], (count, 128))
            got = jnp.take_along_axis(entry, lo, axis=1, mode="promise_in_bounds")
            acc = jnp.where(hi == c, got, acc)
        return acc

    def one(r, _):
        main_ref[r, 0:72, :] = look_up(r, slice(0, 72), 72)
        main_ref[r, 72:144, :] = look_up(r, slice(72, 144), 72)
        acc = look_up(r, slice(144, 168), 24)
        for s in range(8):
            moved = pltpu.roll(acc, 128 - 16 * s, 1) if s else acc
            tail_ref[r, pl.ds(s, 18, stride=8), :] = moved[0:18]
        return 0

    lax.fori_loop(0, 12, one, 0)


def gather(index, bias):
    return pl.pallas_call(
        gather_kernel,
        out_shape=(
            shape((12, 144, 128), F32),
            shape((12, 144, 128), F32),
            shape((168, 128), I32),
            shape((168, 128), I32),
        ),
        scratch_shapes=[pltpu.VMEM((12, 26, 128), F32), pltpu.VMEM((8, 128), F32)],
        compiler_params=VM,
        name="gather",
    )(index, jnp.asarray(window_order(), BF), bias)


def forward_kernel(x0, x1, x2, x3, gain_ref, qkv_ref, main_ref, tail_ref, code_ref,
                   low_ref, q_ref, k_ref, v_ref, prob_ref, att_ref, scratch):
    to_windows((x0, x1, x2, x3), scratch)
    normed, _ = layer_stats(scratch[...])
    low = (normed * gain_ref[...]).astype(BF)
    low_ref[...] = low
    for j, out in enumerate((q_ref, k_ref, v_ref)):
        out[...] = dot_nn(low, qkv_ref[j]).astype(BF)
    eye = lax.broadcasted_iota(I32, (144, 144), 0) == lax.broadcasted_iota(I32, (144, 144), 1)

    def window(w, _):
        rows = pl.ds(pl.multiple_of(w * 144, 16), 144)
        code = code_ref[w]
        label = code >> 1
        column = jnp.sum(jnp.where(eye, label, 0), axis=1, keepdims=True)
        allowed = eye | ((column == label) & ((code & 1) > 0))
        query, key, value = q_ref[rows, :], k_ref[rows, :], v_ref[rows, :]
        heads = []
        for h in range(3):
            cols = slice(h * HD, h * HD + HD)
            bias = jnp.concatenate([main_ref[w * 3 + h], tail_ref[w * 3 + h][:, 0:16]], axis=1)
            scores = dot_nt(query[:, cols], key[:, cols]) * (HD ** -0.5) + bias
            scores = jnp.where(allowed, scores, EXCLUDED)
            expo = jnp.exp(scores - jnp.max(scores, axis=-1, keepdims=True))
            prob = expo * (1.0 / jnp.sum(expo, axis=-1, keepdims=True))
            prob_ref[w * 3 + h] = prob
            heads.append(dot_nn(prob.astype(BF), value[:, cols]))
        att_ref[rows, :] = jnp.concatenate(heads, axis=1).astype(BF)
        return 0

    lax.fori_loop(0, 4, window, 0)


def forward(x, gain, qkv, main, tail, code):
    return pl.pallas_call(
        forward_kernel,
        out_shape=(
            shape((576, 192), BF),
            shape((576, 96), BF),
            shape((576, 96), BF),
            shape((576, 96), BF),
            shape((12, 144, 144), F32),
            shape((576, 96), BF),
        ),
        scratch_shapes=[pltpu.VMEM((576, 192), F32)],
        compiler_params=VM,
        name="forward",
    )(*x, gain, qkv, main, tail, code)


def backward_kernel(g0, g1, g2, g3, proj_ref, qkv_ref, low_ref, q_ref, k_ref, v_ref, prob_ref, att_ref,
                    part_ref, score_ref, gqkv_ref, gproj_ref, scratch, gatt, gcols):
    to_windows((g0, g1, g2, g3), scratch)
    grad = scratch[...].astype(BF)
    gproj_ref[...] = dot_tn(att_ref[...], grad).astype(BF)
    gatt[...] = dot_nt(grad, proj_ref[...]).astype(BF)

    def window(w, _):
        rows = pl.ds(pl.multiple_of(w * 144, 16), 144)
        query, key, value, above = q_ref[rows, :], k_ref[rows, :], v_ref[rows, :], gatt[rows, :]
        queries, keys, values = [], [], []
        for h in range(3):
            cols = slice(h * HD, h * HD + HD)
            prob = prob_ref[w * 3 + h]
            values.append(dot_tn(prob.astype(BF), above[:, cols]))
            grad_prob = dot_nt(above[:, cols], value[:, cols])
            score = prob * (grad_prob - jnp.sum(grad_prob * prob, axis=-1, keepdims=True))
            score_ref[w * 3 + h, 0:144, :] = score[:, 0:128]
            score_ref[w * 3 + h, 144:168, :] = pack_tail(score[:, 128:144].astype(BF))
            low_score = (score * (HD ** -0.5)).astype(BF)
            queries.append(dot_nn(low_score, key[:, cols]))
            keys.append(dot_tn(low_score, query[:, cols]))
        gcols[0, rows, :] = jnp.concatenate(queries, axis=1).astype(BF)
        gcols[1, rows, :] = jnp.concatenate(keys, axis=1).astype(BF)
        gcols[2, rows, :] = jnp.concatenate(values, axis=1).astype(BF)
        return 0

    lax.fori_loop(0, 4, window, 0)
    low = low_ref[...]
    total = None
    for j in range(3):
        cols = gcols[j]
        gqkv_ref[j] = dot_tn(low, cols).astype(BF)
        term = dot_nt(cols, qkv_ref[j])
        total = term if total is None else total + term
    scratch[...] = total
    for s in range(4):
        pieces = [scratch[w * 144 + s * 36 : w * 144 + s * 36 + 36, :] for w in range(4)]
        part_ref[s * 144 : s * 144 + 144, :] = jnp.concatenate(pieces, axis=0).astype(BF)


def backward(g, proj, qkv, low, q, k, v, prob, att):
    return pl.pallas_call(
        backward_kernel,
        out_shape=(
            shape((576, 192), BF),
            shape((12, 168, 128), F32),
            shape((3, 192, 96), BF),
            shape((96, 192), BF),
        ),
        scratch_shapes=[pltpu.VMEM((576, 192), F32), pltpu.VMEM((576, 96), BF), pltpu.VMEM((3, 576, 96), BF)],
        compiler_params=VM,
        name="backward",
    )(*g, proj, qkv, low, q, k, v, prob, att)


def scatter_kernel(score_ref, lo_ref, hi_ref, out_ref):
    out_ref[...] = jnp.zeros((192, 256), F32)
    place = lax.broadcasted_iota(I32, (16, 128), 0)
    entry = lax.broadcasted_iota(I32, (256, 128), 0)

    def step(i, _):
        left, right = [], []
        for j in range(18):
            row = pl.ds(i * 18 + j, 1)
            high, low = hi_ref[row, :], lo_ref[row, :]
            here = place == (high >> 1)
            right.append((entry == (low + (high & 1) * 128)).astype(F32).astype(BF))
            left.append(
                jnp.concatenate([jnp.where(here, score_ref[r, row, :], 0.0).astype(BF) for r in range(12)], axis=0)
            )
        out_ref[...] += dot_nt(jnp.concatenate(left, axis=1), jnp.concatenate(right, axis=1))
        return 0

    lax.fori_loop(0, 9, step, 0)


def scatter(score, lo, hi):
    return pl.pallas_call(
        scatter_kernel, out_shape=shape((192, 256), F32), compiler_params=VM, name="scatter"
    )(score, lo, hi)


def meet_kernel(own_ref, other_ref, x0, x1, x2, x3, o0, o1, o2, o3, gain_out):
    gain = jnp.zeros((1, 192), F32)
    for s, (x, o) in enumerate(zip((x0, x1, x2, x3), (o0, o1, o2, o3))):
        rows = slice(s * 144, s * 144 + 144)
        grad = own_ref[rows, :].astype(F32) + other_ref[rows, :].astype(F32)
        normed, _ = layer_stats(x[...].astype(F32))
        gain = gain + jnp.sum(grad * normed, axis=0, keepdims=True)
        o[...] = grad.astype(BF)
    gain_out[...] = gain


def meet(own, other, x):
    return pl.pallas_call(
        meet_kernel,
        out_shape=tuple(shape((144, 192), BF) for _ in range(4)) + (shape((1, 192), F32),),
        compiler_params=VM,
        name="meet",
    )(own, other, *x)


def finish_kernel(x0, x1, x2, x3, m0, m1, m2, m3, g0, g1, g2, g3, gain_ref, out_ref, scratch):
    for q, (x, m, g) in enumerate(zip((x0, x1, x2, x3), (m0, m1, m2, m3), (g0, g1, g2, g3))):
        normed, inverse = layer_stats(x[...].astype(F32))
        rows = m[...].astype(F32) + norm_backward(g[...].astype(F32), gain_ref[...], normed, inverse)
        for level in range(8):
            for lat in range(3):
                target = (((level + 1) % 8) * 6 + (q // 2) * 3 + lat) * 16 + (q % 2) * 6
                start = level * 18 + lat * 6
                scratch[target : target + 6, :] = rows[start : start + 6]
    for g in range(48):
        out_ref[g] = scratch[g * 16 : g * 16 + 12, :].astype(BF)


def finish(x, m, g, gain):
    return pl.pallas_call(
        finish_kernel,
        out_shape=shape((48, 12, 192), BF),
        scratch_shapes=[pltpu.VMEM((768, 192), F32)],
        compiler_params=VM,
        name="finish",
    )(*x, *m, *g, gain)


def pack_kernel(down_ref, upg_ref, gqkv_ref, gproj_ref, table_ref, one_ref, two_ref, out_ref):
    for j in range(3):
        out_ref[j * 192 : j * 192 + 192, :] = upg_ref[:, j * 128 : j * 128 + 128]
    out_ref[576:960, :] = down_ref[:, 0:128]
    out_ref[960:1152, :] = jnp.concatenate([down_ref[0:192, 128:192], down_ref[192:384, 128:192]], axis=1)
    out_ref[1152:1248, :] = gproj_ref[:, 0:128]
    out_ref[1248:1296, :] = jnp.concatenate([gproj_ref[0:48, 128:192], gproj_ref[48:96, 128:192]], axis=1)
    a, b, c = gqkv_ref[0], gqkv_ref[1], gqkv_ref[2]
    out_ref[1296:1488, :] = jnp.concatenate([a, c[:, 0:32]], axis=1)
    out_ref[1488:1680, :] = jnp.concatenate([b, c[:, 32:64]], axis=1)
    out_ref[1680:1728, :] = jnp.concatenate([c[i * 48 : i * 48 + 48, 64:96] for i in range(4)], axis=1)
    rows = []
    for r in range(12):
        pair = table_ref[r * 16 : r * 16 + 13, :]
        rows += [pair[:, 0:128], pair[:, 128:256]]
    none = jnp.zeros((1, 64), F32)
    rows += [one_ref[:, 0:128], jnp.concatenate([one_ref[:, 128:192], none], axis=1)]
    rows += [two_ref[:, 0:128], jnp.concatenate([two_ref[:, 128:192], none], axis=1)]
    rows += [jnp.zeros((4, 128), F32)]
    out_ref[1728:2048, :] = jnp.concatenate(rows, axis=0).astype(BF)


def pack(down, upg, gqkv, gproj, table, one, two):
    return pl.pallas_call(
        pack_kernel, out_shape=shape((2048, 128), BF), compiler_params=VM, name="pack"
    )(down, upg, gqkv, gproj, table, one, two)


def add_kernel(place_ref, got_ref, out_ref):
    bands = [jnp.sum(got_ref[a * 32 : a * 32 + 32].astype(F32), axis=0) for a in range(4)]
    total = bands[0] + bands[1] + bands[2] + bands[3]
    row = place_ref[0] * 16 + lax.broadcasted_iota(I32, (16, 128), 0)
    table = (row >= 1728) & (row < 2040)
    for a in range(4):
        out_ref[a * 32 : a * 32 + 32] = jnp.broadcast_to(jnp.where(table, bands[a], total).astype(BF)[None], (32, 16, 128))


def add(place, got):
    return pl.pallas_call(
        add_kernel,
        out_shape=shape((128, 16, 128), BF),
        in_specs=[pl.BlockSpec(memory_space=pltpu.SMEM), pl.BlockSpec(memory_space=pltpu.VMEM)],
        compiler_params=VM,
        name="add",
    )(place, got)


def unpack_kernel(weight_scale, table_scale, in_ref, qkv_ref, proj_ref, upg_ref, down_ref, gain_ref, table_ref):
    def rows(start, stop):
        return in_ref[start:stop, :].astype(F32) * weight_scale

    for j in range(3):
        upg_ref[:, j * 128 : j * 128 + 128] = rows(j * 192, j * 192 + 192)
    down_ref[:, 0:128] = rows(576, 960)
    tail = rows(960, 1152)
    down_ref[0:192, 128:192] = tail[:, 0:64]
    down_ref[192:384, 128:192] = tail[:, 64:128]
    proj_ref[:, 0:128] = rows(1152, 1248)
    tail = rows(1248, 1296)
    proj_ref[0:48, 128:192] = tail[:, 0:64]
    proj_ref[48:96, 128:192] = tail[:, 64:128]
    first, second, third = rows(1296, 1488), rows(1488, 1680), rows(1680, 1728)
    qkv_ref[0] = first[:, 0:96]
    qkv_ref[1] = second[:, 0:96]
    qkv_ref[2, :, 0:32] = first[:, 96:128]
    qkv_ref[2, :, 32:64] = second[:, 96:128]
    for i in range(4):
        qkv_ref[2, i * 48 : i * 48 + 48, 64:96] = third[:, i * 32 : i * 32 + 32]
    table = in_ref[1728:2048, :].astype(F32)
    for r in range(12):
        for half in range(2):
            piece = table[r * 26 + half * 13 : r * 26 + half * 13 + 13] * table_scale
            for a in range(13):
                start = a * 256 + half * 128
                wide = min(128, 3312 - start)
                table_ref[r // 3, r % 3 : r % 3 + 1, start : start + wide] = piece[a : a + 1, 0:wide]
    gain_ref[...] = table[312:320] * weight_scale


def unpack(weight_scale, table_scale, got):
    return pl.pallas_call(
        functools.partial(unpack_kernel, weight_scale, table_scale),
        out_shape=(
            shape((3, 192, 96), F32),
            shape((96, 192), F32),
            shape((192, 384), F32),
            shape((384, 192), F32),
            shape((8, 128), F32),
            shape((4, 3, 3312), F32),
        ),
        compiler_params=VM,
        name="unpack",
    )(got)


def moved(value, band, sector, half):
    sizes = [lax.axis_size(name) for name in ("lat", "lon", "tp")]
    pairs = []
    for a in range(sizes[0]):
        for b in range(sizes[1]):
            for c in range(sizes[2]):
                source = ((a + band) % sizes[0], (b + sector) % sizes[1], (c + half) % sizes[2])
                pairs.append(tuple((x * sizes[1] + y) * sizes[2] + z for x, y, z in (source, (a, b, c))))
    return lax.ppermute(value, ("lat", "lon", "tp"), pairs)


def shifted_parts(quarters):
    return (
        quarters[3],
        moved(quarters[2], 0, 1, 0),
        moved(quarters[1], 1, 0, 0),
        moved(quarters[0], 1, 1, 0),
    )


def local(
    inputs,
    residual_mid,
    grad_out,
    mask_ids,
    key_valid,
    bias_index,
    pos_bias,
    norm1_gain,
    qkv_weight,
    proj_weight,
    norm2_gain,
    fc1_weight,
    fc2_weight,
):
    levels, lat_cells, lon_cells, channels = inputs.shape
    cell_count = levels * lat_cells * lon_cells
    weight_scale = (cell_count * lax.axis_size("lat") * lax.axis_size("lon")) ** (-0.5)
    table_scale = (lon_cells * lax.axis_size("lon") // 12) ** (-0.5)
    gain1, gain2 = norm1_gain.reshape(1, -1), norm2_gain.reshape(1, -1)

    x = split(inputs.reshape(48, 12, 192))
    xw = shifted_parts(x)
    part2, mid, up, down, upg = mlp(
        residual_mid.reshape(48, 12, 192), grad_out.reshape(48, 12, 192), gain2, fc1_weight, fc2_weight
    )
    other2 = moved(part2, 0, 0, 1)
    main, tail, lo, hi = gather(bias_index, pos_bias.reshape(4, 3, 3312))
    code = mask_ids * 2 + (key_valid > 0).astype(jnp.int32)
    code = code.reshape(4, 2, 2, 3, 2, 6).transpose(0, 2, 4, 1, 3, 5).reshape(4, 1, 144)
    *gm, gain_two = middle(mid, up, part2, other2, gain2)
    gw = shifted_parts(gm)
    low, q, k, v, prob, att = forward(xw, gain1, qkv_weight, main, tail, code)
    part1, score, gqkv, gproj = backward(gw, proj_weight, qkv_weight, low, q, k, v, prob, att)
    other1 = moved(part1, 0, 0, 1)
    table = scatter(score, lo, hi)
    *g, gain_one = meet(part1, other1, xw)
    back = (moved(g[3], -1, -1, 0), moved(g[2], -1, 0, 0), moved(g[1], 0, -1, 0), g[0])
    sums = pack(down, upg, gqkv, gproj, table, gain_one, gain_two).reshape(128, 16, 128)
    place = (lax.axis_index("lat") * lax.axis_size("lon") + lax.axis_index("lon")).reshape(1)
    got = lax.all_to_all(sums, ("lat", "lon"), 0, 0)
    got = lax.all_to_all(add(place, got), ("lat", "lon"), 0, 0)
    qkv_out, proj_out, up_out, down_out, gains, table_out = unpack(
        weight_scale, table_scale, got.reshape(2048, 128)
    )
    result = finish(x, gm, back, gain1).reshape(levels, lat_cells, lon_cells, channels)
    share = channels // lax.axis_size("tp")
    start = lax.axis_index("tp") * share
    gains = gains[0:4].reshape(2, 256)[:, 0:channels]
    mine = lax.dynamic_slice_in_dim(gains, start, share, axis=1)
    return (result, qkv_out, proj_out, up_out, down_out, mine[0], mine[1], table_out[None])


def solution(mesh):
    return jax.shard_map(
        local,
        mesh=mesh,
        in_specs=(
            P(None, "lat", "lon", None),
            P(None, "lat", "lon", None),
            P(None, "lat", "lon", None),
            P(None, "lat", "lon"),
            P(None, "lat", "lon"),
            P(),
            P("lat", None, "tp", None),
            P(),
            P(None, None, "tp"),
            P("tp", None),
            P(),
            P(None, "tp"),
            P("tp", None),
        ),
        out_specs=(
            P(None, "lat", "lon", None),
            P(None, None, "tp"),
            P("tp", None),
            P(None, "tp"),
            P("tp", None),
            P("tp"),
            P("tp"),
            P("lat", None, "tp", None),
        ),
        check_vma=False,
    )
```

```python
import functools

import jax
import jax.numpy as jnp
import numpy as np
from jax import lax
from jax.experimental import pallas as pl
from jax.experimental.pallas import tpu as pltpu
from jax.sharding import PartitionSpec as P

HD = 32
EPSILON = 1e-05
EXCLUDED = -1e30
BF = jnp.bfloat16
F32 = jnp.float32
I32 = jnp.int32
VMEM = pl.BlockSpec(memory_space=pltpu.VMEM)
VM = pltpu.CompilerParams(vmem_limit_bytes=48 * 1024 * 1024)


def cost(microseconds):
    return pl.CostEstimate(flops=0, bytes_accessed=int(microseconds * 3000000), transcendentals=0)


def shape(dims, kind):
    return jax.ShapeDtypeStruct(dims, kind)


def dot_nn(a, b):
    return lax.dot_general(a, b, (((1,), (0,)), ((), ())), preferred_element_type=F32)


def dot_nt(a, b):
    return lax.dot_general(a, b, (((1,), (1,)), ((), ())), preferred_element_type=F32)


def dot_tn(a, b):
    return lax.dot_general(a, b, (((0,), (0,)), ((), ())), preferred_element_type=F32)


def layer_stats(rows):
    mean = jnp.mean(rows, axis=-1, keepdims=True)
    centred = rows - mean
    inverse = lax.rsqrt(jnp.mean(centred * centred, axis=-1, keepdims=True) + EPSILON)
    return centred * inverse, inverse


def norm_backward(grad_normed, gain, normed, inverse):
    scaled = grad_normed * gain
    first = jnp.mean(scaled, axis=-1, keepdims=True)
    second = jnp.mean(scaled * normed, axis=-1, keepdims=True)
    return (scaled - first - normed * second) * inverse


def gelu_pair(pre):
    cdf = 0.5 * (1.0 + lax.erf(pre * 0.7071067811865476))
    pdf = 0.3989422804014327 * jnp.exp(-0.5 * pre * pre)
    return pre * cdf, cdf + pre * pdf


def to_quarters(field_ref, scratch):
    for lat in range(6):
        for half in range(2):
            rows = field_ref[lat, half * 6 : half * 6 + 6].astype(F32).reshape(48, 192)
            start = ((lat // 3) * 2 + half) * 144 + (lat % 3) * 48
            scratch[start : start + 48, :] = rows


def level_order():
    order = np.zeros((144, 144), np.float32)
    for w in range(4):
        for cell in range(18):
            for level in range(2):
                order[w * 36 + cell * 2 + level, cell * 8 + (2 * w + 1 + level) % 8] = 1.0
    return jnp.asarray(order, BF)


def to_windows(parts, order, scratch):
    for s in range(4):
        rows = dot_nn(order, parts[s][...])
        for w in range(4):
            scratch[w * 144 + s * 36 : w * 144 + s * 36 + 36, :] = rows[w * 36 : w * 36 + 36]


def head_kernel(x_ref, mid_ref, up_ref, gain_ref, fc1_ref, fc2_ref,
                o0, o1, o2, o3, part_ref, midq_ref, upq_ref, grads_ref, scratch, mid_s, up_s):
    to_quarters(x_ref, scratch)
    for q, out in enumerate((o0, o1, o2, o3)):
        out[...] = scratch[q * 144 : q * 144 + 144, :].astype(BF)
    to_quarters(mid_ref, mid_s)
    to_quarters(up_ref, up_s)
    mid = mid_s[...]
    up = up_s[...].astype(BF)
    midq_ref[...] = mid.astype(BF)
    upq_ref[...] = up
    normed, _ = layer_stats(mid)
    lowered = (normed * gain_ref[...]).astype(BF)
    pre = dot_nn(lowered, fc1_ref[...])
    active, slopes = gelu_pair(pre)
    grad_pre = (dot_nn(up, fc2_ref[...]) * slopes).astype(BF)
    part_ref[...] = dot_nt(grad_pre, fc1_ref[...]).astype(BF)
    for start, grads in ((0, dot_tn(lowered, grad_pre)), (576, dot_tn(up, active.astype(BF)))):
        for j in range(3):
            grads_ref[start + j * 192 : start + j * 192 + 192, :] = grads[:, j * 128 : j * 128 + 128].astype(BF)


def head(x, mid, up, gain, fc1, fc2):
    return pl.pallas_call(
        head_kernel,
        out_shape=tuple(shape((144, 192), BF) for _ in range(4))
        + (shape((576, 192), BF), shape((576, 192), BF), shape((576, 192), BF), shape((1152, 128), BF)),
        scratch_shapes=[pltpu.VMEM((576, 192), F32)] * 3,
        compiler_params=VM,
        cost_estimate=cost(3),
        name="head",
    )(x, mid, up, gain, fc1, fc2)


def middle_kernel(mid_ref, up_ref, own_ref, other_ref, gain_ref, after_ref, o0, o1, o2, o3, gain_out):
    normed, inverse = layer_stats(mid_ref[...].astype(F32))
    grad = own_ref[...].astype(F32) + other_ref[...].astype(F32)
    gain_out[...] = jnp.sum(grad * normed, axis=0, keepdims=True)
    out = up_ref[...].astype(F32) + norm_backward(grad, gain_ref[...], normed, inverse)
    for q, o in enumerate((o0, o1, o2, o3)):
        o[...] = out[q * 144 : q * 144 + 144].astype(BF)


def middle(mid, up, own, other, gain, after):
    return pl.pallas_call(
        middle_kernel,
        out_shape=tuple(shape((144, 192), BF) for _ in range(4)) + (shape((1, 192), F32),),
        in_specs=[VMEM] * 5 + [pl.BlockSpec(memory_space=pl.ANY)],
        compiler_params=VM,
        cost_estimate=cost(1),
        name="middle",
    )(mid, up, own, other, gain, after)


def window_order():
    canon = np.arange(144).reshape(2, 2, 3, 2, 6).transpose(1, 3, 2, 4, 0).reshape(-1)
    order = np.zeros((144, 144), np.float32)
    order[np.arange(144), canon] = 1.0
    return order


def pack_tail(tail):
    spread = (lax.broadcasted_iota(I32, (16, 128), 1) & 15) == lax.broadcasted_iota(I32, (16, 128), 0)
    wide = dot_nn(tail, spread.astype(F32).astype(BF))
    here = (lax.broadcasted_iota(I32, (144, 128), 1) >> 4) == (lax.broadcasted_iota(I32, (144, 128), 0) & 7)
    wide = jnp.where(here, wide, 0.0).astype(BF)
    rows = (lax.broadcasted_iota(I32, (24, 144), 1) >> 3) == lax.broadcasted_iota(I32, (24, 144), 0)
    return dot_nn(rows.astype(F32).astype(BF), wide)


def one_hot(low):
    return (lax.broadcasted_iota(I32, (256, 128), 0) == low).astype(F32).astype(BF)


def gather_kernel(index_ref, order_ref, bias_ref, main_ref, tail_ref, lo_ref, hi_ref, table, stage):
    index = index_ref[...]
    order = order_ref[...]
    pieces = []
    for part in (index & 127, index >> 7):
        moved = dot_nt(dot_nn(order, part.astype(F32).astype(BF)).astype(BF), order)
        pieces.append((moved[:, 0:128].astype(I32), pack_tail(moved[:, 128:144].astype(BF)).astype(I32)))
    for rows, low, high in ((slice(0, 144), pieces[0][0], pieces[1][0]), (slice(144, 168), pieces[0][1], pieces[1][1])):
        lo_ref[rows, :] = low + (high & 1) * 128
        hi_ref[rows, :] = high >> 1
    table[...] = jnp.zeros((160, 256), F32)
    for r in range(12):
        line = bias_ref[r % 3, r // 3 : r // 3 + 1, :]
        line = line - jnp.max(line, axis=1, keepdims=True)
        for c in range(13):
            wide = min(256, 3312 - c * 256)
            row = c * 8 + r if r < 8 else 104 + (c // 2) * 8 + (c % 2) * 4 + r - 8
            table[row : row + 1, 0:wide] = line[:, c * 256 : c * 256 + wide]
    upper = table[...].astype(BF)
    lower = (table[...] - upper.astype(F32)).astype(BF)
    terms = jnp.concatenate([upper, lower], axis=1)
    half = (lax.broadcasted_iota(I32, (8, 128), 0) >> 2)

    def step(i, _):
        for pair in range(9):
            hot = jnp.concatenate([one_hot(lo_ref[pl.ds(i * 18 + pair * 2 + j, 1), :]) for j in range(2)], axis=1)
            found = dot_nn(terms, jnp.concatenate([hot, hot], axis=0))
            for j in range(2):
                block = i * 18 + pair * 2 + j
                cols = slice(j * 128, j * 128 + 128)
                high = hi_ref[pl.ds(block, 1), :]
                first = jnp.zeros((8, 128), F32)
                for c in range(13):
                    first = jnp.where(high == c, found[c * 8 : c * 8 + 8, cols], first)
                second = jnp.zeros((8, 128), F32)
                shifted = high - half
                for c in range(7):
                    second = jnp.where(shifted == 2 * c, found[104 + c * 8 : 112 + c * 8, cols], second)
                start = pl.multiple_of(block * 16, 16)
                stage[pl.ds(start, 8), :] = first
                stage[pl.ds(start + 8, 8), :] = second + pltpu.roll(second, 4, 0)
        return 0

    lax.fori_loop(0, 9, step, 0)
    for r in range(12):
        main_ref[r] = stage[pl.ds(r, 144, stride=16), :]
        packed = stage[pl.ds(144 * 16 + r, 18, stride=16), :]
        for s in range(8):
            tail_ref[r, pl.ds(s, 18, stride=8), :] = pltpu.roll(packed, 128 - 16 * s, 1) if s else packed


def gather(index, bias):
    return pl.pallas_call(
        gather_kernel,
        out_shape=(
            shape((12, 144, 128), F32),
            shape((12, 144, 128), F32),
            shape((168, 128), I32),
            shape((168, 128), I32),
        ),
        scratch_shapes=[pltpu.VMEM((160, 256), F32), pltpu.VMEM((162 * 16, 128), F32)],
        compiler_params=VM,
        cost_estimate=cost(10),
        name="gather",
    )(index, jnp.asarray(window_order(), BF), bias)


def forward_kernel(x0, x1, x2, x3, order_ref, gain_ref, qkv_ref, main_ref, tail_ref, code_ref,
                   low_ref, q_ref, k_ref, v_ref, prob_ref, att_ref, scratch):
    to_windows((x0, x1, x2, x3), order_ref[...], scratch)
    normed, _ = layer_stats(scratch[...])
    low = (normed * gain_ref[...]).astype(BF)
    low_ref[...] = low
    for j, out in enumerate((q_ref, k_ref, v_ref)):
        out[...] = dot_nn(low, qkv_ref[j]).astype(BF)
    eye = lax.broadcasted_iota(I32, (144, 144), 0) == lax.broadcasted_iota(I32, (144, 144), 1)

    def window(w, _):
        rows = pl.ds(pl.multiple_of(w * 144, 16), 144)
        code = code_ref[w]
        label = code >> 1
        column = jnp.sum(jnp.where(eye, label, 0), axis=1, keepdims=True)
        allowed = eye | ((column == label) & ((code & 1) > 0))
        query, key, value = q_ref[rows, :], k_ref[rows, :], v_ref[rows, :]
        heads = []
        for h in range(3):
            cols = slice(h * HD, h * HD + HD)
            bias = jnp.concatenate([main_ref[w * 3 + h], tail_ref[w * 3 + h][:, 0:16]], axis=1)
            scores = dot_nt(query[:, cols], key[:, cols]) * (HD ** -0.5) + bias
            scores = jnp.where(allowed, scores, EXCLUDED)
            expo = jnp.exp(scores - jnp.max(scores, axis=-1, keepdims=True))
            prob = expo * (1.0 / jnp.sum(expo, axis=-1, keepdims=True))
            prob_ref[w * 3 + h] = prob
            heads.append(dot_nn(prob.astype(BF), value[:, cols]))
        att_ref[rows, :] = jnp.concatenate(heads, axis=1).astype(BF)
        return 0

    lax.fori_loop(0, 4, window, 0)


def forward(x, gain, qkv, main, tail, code):
    return pl.pallas_call(
        forward_kernel,
        out_shape=(
            shape((576, 192), BF),
            shape((576, 96), BF),
            shape((576, 96), BF),
            shape((576, 96), BF),
            shape((12, 144, 144), F32),
            shape((576, 96), BF),
        ),
        scratch_shapes=[pltpu.VMEM((576, 192), F32)],
        compiler_params=VM,
        cost_estimate=cost(5),
        name="forward",
    )(*x, level_order(), gain, qkv, main, tail, code)


def backward_kernel(g0, g1, g2, g3, order_ref, proj_ref, qkv_ref, low_ref, q_ref, k_ref, v_ref, prob_ref, att_ref,
                    part_ref, score_ref, grads_ref, scratch, gatt, gcols):
    to_windows((g0, g1, g2, g3), order_ref[...], scratch)
    grad = scratch[...].astype(BF)
    gproj = dot_tn(att_ref[...], grad).astype(BF)
    grads_ref[0:96, :] = gproj[:, 0:128]
    grads_ref[96:144, :] = jnp.concatenate([gproj[0:48, 128:192], gproj[48:96, 128:192]], axis=1)
    gatt[...] = dot_nt(grad, proj_ref[...]).astype(BF)

    def window(w, _):
        rows = pl.ds(pl.multiple_of(w * 144, 16), 144)
        query, key, value, above = q_ref[rows, :], k_ref[rows, :], v_ref[rows, :], gatt[rows, :]
        queries, keys, values = [], [], []
        for h in range(3):
            cols = slice(h * HD, h * HD + HD)
            prob = prob_ref[w * 3 + h]
            values.append(dot_tn(prob.astype(BF), above[:, cols]))
            grad_prob = dot_nt(above[:, cols], value[:, cols])
            score = prob * (grad_prob - jnp.sum(grad_prob * prob, axis=-1, keepdims=True))
            score_ref[w * 3 + h, 0:144, :] = score[:, 0:128]
            score_ref[w * 3 + h, 144:168, :] = pack_tail(score[:, 128:144].astype(BF))
            low_score = (score * (HD ** -0.5)).astype(BF)
            queries.append(dot_nn(low_score, key[:, cols]))
            keys.append(dot_tn(low_score, query[:, cols]))
        gcols[0, rows, :] = jnp.concatenate(queries, axis=1).astype(BF)
        gcols[1, rows, :] = jnp.concatenate(keys, axis=1).astype(BF)
        gcols[2, rows, :] = jnp.concatenate(values, axis=1).astype(BF)
        return 0

    lax.fori_loop(0, 4, window, 0)
    low = low_ref[...]
    total = None
    gqkv = []
    for j in range(3):
        cols = gcols[j]
        gqkv.append(dot_tn(low, cols).astype(BF))
        term = dot_nt(cols, qkv_ref[j])
        total = term if total is None else total + term
    a, b, c = gqkv
    grads_ref[144:336, :] = jnp.concatenate([a, c[:, 0:32]], axis=1)
    grads_ref[336:528, :] = jnp.concatenate([b, c[:, 32:64]], axis=1)
    grads_ref[528:576, :] = jnp.concatenate([c[i * 48 : i * 48 + 48, 64:96] for i in range(4)], axis=1)
    scratch[...] = total
    for s in range(4):
        pieces = [scratch[w * 144 + s * 36 : w * 144 + s * 36 + 36, :] for w in range(4)]
        piece = jnp.concatenate(pieces, axis=0).astype(BF)
        part_ref[s * 144 : s * 144 + 144, :] = dot_tn(order_ref[...], piece).astype(BF)


def backward(g, proj, qkv, low, q, k, v, prob, att):
    return pl.pallas_call(
        backward_kernel,
        out_shape=(
            shape((576, 192), BF),
            shape((12, 168, 128), F32),
            shape((576, 128), BF),
        ),
        scratch_shapes=[pltpu.VMEM((576, 192), F32), pltpu.VMEM((576, 96), BF), pltpu.VMEM((3, 576, 96), BF)],
        compiler_params=VM,
        cost_estimate=cost(7),
        name="backward",
    )(*g, level_order(), proj, qkv, low, q, k, v, prob, att)


def scatter_kernel(score_ref, lo_ref, hi_ref, out_ref):
    out_ref[...] = jnp.zeros((192, 256), F32)
    place = lax.broadcasted_iota(I32, (16, 128), 0)

    def step(i, _):
        left, right = [], []
        for j in range(18):
            row = pl.ds(i * 18 + j, 1)
            here = place == hi_ref[row, :]
            right.append(one_hot(lo_ref[row, :]))
            left.append(
                jnp.concatenate([jnp.where(here, score_ref[r, row, :], 0.0).astype(BF) for r in range(12)], axis=0)
            )
        out_ref[...] += dot_nt(jnp.concatenate(left, axis=1), jnp.concatenate(right, axis=1))
        return 0

    lax.fori_loop(0, 9, step, 0)


def scatter(score, lo, hi):
    return pl.pallas_call(
        scatter_kernel, out_shape=shape((192, 256), F32), compiler_params=VM, cost_estimate=cost(5), name="scatter"
    )(score, lo, hi)


def meet_kernel(own_ref, other_ref, x0, x1, x2, x3, grads_ref, two_ref, o0, o1, o2, o3, out_ref):
    gain = jnp.zeros((1, 192), F32)
    for s, (x, o) in enumerate(zip((x0, x1, x2, x3), (o0, o1, o2, o3))):
        rows = slice(s * 144, s * 144 + 144)
        grad = own_ref[rows, :].astype(F32) + other_ref[rows, :].astype(F32)
        normed, _ = layer_stats(x[...].astype(F32))
        gain = gain + jnp.sum(grad * normed, axis=0, keepdims=True)
        o[...] = grad.astype(BF)
    out_ref[0:576, :] = grads_ref[...]
    none = jnp.zeros((1, 64), F32)
    rows = []
    for line in (gain, two_ref[...]):
        rows += [line[:, 0:128], jnp.concatenate([line[:, 128:192], none], axis=1)]
    out_ref[576:592, :] = jnp.concatenate(rows + [jnp.zeros((12, 128), F32)], axis=0).astype(BF)


def meet(own, other, x, grads, two):
    return pl.pallas_call(
        meet_kernel,
        out_shape=tuple(shape((144, 192), BF) for _ in range(4)) + (shape((592, 128), BF),),
        compiler_params=VM,
        name="meet",
    )(own, other, *x, grads, two)


def finish_kernel(x0, x1, x2, x3, m0, m1, m2, m3, g0, g1, g2, g3, gain_ref, out_ref):
    for q, (x, m, g) in enumerate(zip((x0, x1, x2, x3), (m0, m1, m2, m3), (g0, g1, g2, g3))):
        normed, inverse = layer_stats(x[...].astype(F32))
        rows = m[...].astype(F32) + norm_backward(g[...].astype(F32), gain_ref[...], normed, inverse)
        for lat in range(3):
            piece = rows[lat * 48 : lat * 48 + 48].reshape(6, 8, 192)
            out_ref[(q // 2) * 3 + lat, (q % 2) * 6 : (q % 2) * 6 + 6] = piece.astype(BF)


def finish(x, m, g, gain):
    return pl.pallas_call(
        finish_kernel, out_shape=shape((6, 12, 8, 192), BF), compiler_params=VM, name="finish"
    )(*x, *m, *g, gain)


def both(own, other):
    return (own.astype(F32) + other.astype(F32)).astype(BF)


def pack_kernel(first_ref, first_other, second_ref, second_other, table_ref, out_ref):
    out_ref[0:1152, :] = both(first_ref[...], first_other[...])
    second = second_ref[...].astype(F32) + second_other[...].astype(F32)
    out_ref[1152:1728, :] = second[0:576].astype(BF)
    rows = []
    for r in range(12):
        pair = table_ref[r * 16 : r * 16 + 13, :]
        rows += [pair[:, 0:128], pair[:, 128:256]]
    out_ref[1728:2048, :] = jnp.concatenate(rows + [second[576:584]], axis=0).astype(BF)


def pack(first, first_other, second, second_other, table):
    return pl.pallas_call(
        pack_kernel, out_shape=shape((2048, 128), BF), compiler_params=VM, cost_estimate=cost(1), name="pack"
    )(first, first_other, second, second_other, table)


def add_kernel(got_ref, out_ref):
    total = got_ref[0].astype(F32)
    for i in range(1, 32):
        total = total + got_ref[i].astype(F32)
    out_ref[...] = jnp.broadcast_to(total.astype(BF)[None], (32, 64, 128))


def add(got):
    return pl.pallas_call(
        add_kernel, out_shape=shape((32, 64, 128), BF), compiler_params=VM, cost_estimate=cost(1), name="add"
    )(got)


def unpack_kernel(weight_scale, table_scale, in_ref, qkv_ref, proj_ref, upg_ref, down_ref, gain_ref, table_ref):
    def rows(start, stop):
        return in_ref[start:stop, :].astype(F32) * weight_scale

    for j in range(3):
        upg_ref[:, j * 128 : j * 128 + 128] = rows(j * 192, j * 192 + 192)
        down_ref[:, j * 128 : j * 128 + 128] = rows(576 + j * 192, 768 + j * 192)
    proj_ref[:, 0:128] = rows(1152, 1248)
    tail = rows(1248, 1296)
    proj_ref[0:48, 128:192] = tail[:, 0:64]
    proj_ref[48:96, 128:192] = tail[:, 64:128]
    first, second, third = rows(1296, 1488), rows(1488, 1680), rows(1680, 1728)
    qkv_ref[0] = first[:, 0:96]
    qkv_ref[1] = second[:, 0:96]
    qkv_ref[2, :, 0:32] = first[:, 96:128]
    qkv_ref[2, :, 32:64] = second[:, 96:128]
    for i in range(4):
        qkv_ref[2, i * 48 : i * 48 + 48, 64:96] = third[:, i * 32 : i * 32 + 32]
    table = in_ref[1728:2048, :].astype(F32)
    for r in range(12):
        for half in range(2):
            piece = table[r * 26 + half * 13 : r * 26 + half * 13 + 13] * table_scale
            for a in range(13):
                start = a * 256 + half * 128
                wide = min(128, 3312 - start)
                table_ref[r % 3, r // 3 : r // 3 + 1, start : start + wide] = piece[a : a + 1, 0:wide]
    gain_ref[...] = table[312:320] * weight_scale


def unpack(weight_scale, table_scale, got):
    return pl.pallas_call(
        functools.partial(unpack_kernel, weight_scale, table_scale),
        out_shape=(
            shape((3, 192, 96), F32),
            shape((96, 192), F32),
            shape((192, 384), F32),
            shape((192, 384), F32),
            shape((8, 128), F32),
            shape((3, 4, 3312), F32),
        ),
        compiler_params=VM,
        name="unpack",
    )(got)


def moved(value, band, sector, half):
    sizes = [lax.axis_size(name) for name in ("lat", "lon", "tp")]
    pairs = []
    for a in range(sizes[0]):
        for b in range(sizes[1]):
            for c in range(sizes[2]):
                source = ((a + band) % sizes[0], (b + sector) % sizes[1], (c + half) % sizes[2])
                pairs.append(tuple((x * sizes[1] + y) * sizes[2] + z for x, y, z in (source, (a, b, c))))
    return lax.ppermute(value, ("lat", "lon", "tp"), pairs)


def swapped(value, bit):
    pairs = [(a, a ^ bit) for a in range(lax.axis_size("lat"))]
    return lax.ppermute(value, "lat", pairs)


def shifted_parts(quarters):
    return (
        quarters[3],
        moved(quarters[2], 0, 1, 0),
        moved(quarters[1], 1, 0, 0),
        moved(quarters[0], 1, 1, 0),
    )


def local(
    inputs,
    residual_mid,
    grad_out,
    mask_ids,
    key_valid,
    bias_index,
    pos_bias,
    norm1_gain,
    qkv_weight,
    proj_weight,
    norm2_gain,
    fc1_weight,
    fc2_weight,
):
    levels, lat_cells, lon_cells, channels = inputs.shape
    cell_count = levels * lat_cells * lon_cells
    weight_scale = (cell_count * lax.axis_size("lat") * lax.axis_size("lon")) ** (-0.5)
    table_scale = (lon_cells * lax.axis_size("lon") // 12) ** (-0.5)
    gain1, gain2 = norm1_gain.reshape(1, -1), norm2_gain.reshape(1, -1)

    def turned(field):
        return field.transpose(1, 2, 0, 3)

    *x, part2, mid, up, first = head(
        turned(inputs), turned(residual_mid), turned(grad_out), gain2, fc1_weight, fc2_weight.T
    )
    other2 = moved(part2, 0, 0, 1)
    xw = shifted_parts(x)
    main, tail, lo, hi = gather(bias_index, pos_bias[0].transpose(1, 0, 2))
    code = mask_ids * 2 + (key_valid > 0).astype(jnp.int32)
    code = code.reshape(4, 2, 2, 3, 2, 6).transpose(0, 2, 4, 3, 5, 1).reshape(4, 1, 144)
    *gm, gain_two = middle(mid, up, part2, other2, gain2, lo)
    gw = shifted_parts(gm)
    first = both(first, swapped(first, 1))
    first_other = swapped(first, 2)
    low, q, k, v, prob, att = forward(xw, gain1, qkv_weight, main, tail, code)
    part1, score, grads = backward(gw, proj_weight, qkv_weight, low, q, k, v, prob, att)
    other1 = moved(part1, 0, 0, 1)
    table = scatter(score, lo, hi)
    *g, second = meet(part1, other1, xw, grads, gain_two)
    second = both(second, swapped(second, 1))
    second_other = swapped(second, 2)
    back = (moved(g[3], -1, -1, 0), moved(g[2], -1, 0, 0), moved(g[1], 0, -1, 0), g[0])
    sums = pack(first, first_other, second, second_other, table).reshape(32, 64, 128)
    got = lax.all_to_all(sums, "lon", 0, 0)
    got = lax.all_to_all(add(got), "lon", 0, 0)
    qkv_out, proj_out, up_out, down_out, gains, table_out = unpack(
        weight_scale, table_scale, got.reshape(2048, 128)
    )
    result = finish(x, gm, back, gain1).transpose(2, 0, 1, 3)
    share = channels // lax.axis_size("tp")
    start = lax.axis_index("tp") * share
    gains = gains[0:4].reshape(2, 256)[:, 0:channels]
    mine = lax.dynamic_slice_in_dim(gains, start, share, axis=1)
    return (result, qkv_out, proj_out, up_out, down_out.T, mine[0], mine[1], table_out.transpose(1, 0, 2)[None])


def solution(mesh):
    return jax.shard_map(
        local,
        mesh=mesh,
        in_specs=(
            P(None, "lat", "lon", None),
            P(None, "lat", "lon", None),
            P(None, "lat", "lon", None),
            P(None, "lat", "lon"),
            P(None, "lat", "lon"),
            P(),
            P("lat", None, "tp", None),
            P(),
            P(None, None, "tp"),
            P("tp", None),
            P(),
            P(None, "tp"),
            P("tp", None),
        ),
        out_specs=(
            P(None, "lat", "lon", None),
            P(None, None, "tp"),
            P("tp", None),
            P(None, "tp"),
            P("tp", None),
            P("tp"),
            P("tp"),
            P("lat", None, "tp", None),
        ),
        check_vma=False,
    )
```

```python
import functools

import jax
import jax.numpy as jnp
import numpy as np
from jax import lax
from jax.experimental import pallas as pl
from jax.experimental.pallas import tpu as pltpu
from jax.sharding import PartitionSpec as P

HD = 32
EPSILON = 1e-05
EXCLUDED = -1e30
BF = jnp.bfloat16
F32 = jnp.float32
I32 = jnp.int32
VMEM = pl.BlockSpec(memory_space=pltpu.VMEM)
VM = pltpu.CompilerParams(vmem_limit_bytes=24 * 1024 * 1024)
ALL = pltpu.CompilerParams(vmem_limit_bytes=63 * 1024 * 1024)
ANY = pl.BlockSpec(memory_space=pl.ANY)


def cost(microseconds):
    return pl.CostEstimate(flops=int(microseconds * 1e9), bytes_accessed=0, transcendentals=0)


def shape(dims, kind):
    return jax.ShapeDtypeStruct(dims, kind)


def dot_nn(a, b):
    return lax.dot_general(a, b, (((1,), (0,)), ((), ())), preferred_element_type=F32)


def dot_nt(a, b):
    return lax.dot_general(a, b, (((1,), (1,)), ((), ())), preferred_element_type=F32)


def dot_tn(a, b):
    return lax.dot_general(a, b, (((0,), (0,)), ((), ())), preferred_element_type=F32)


def layer_stats(rows):
    mean = jnp.mean(rows, axis=-1, keepdims=True)
    centred = rows - mean
    inverse = lax.rsqrt(jnp.mean(centred * centred, axis=-1, keepdims=True) + EPSILON)
    return centred * inverse, inverse


def norm_backward(grad_normed, gain, normed, inverse):
    scaled = grad_normed * gain
    first = jnp.mean(scaled, axis=-1, keepdims=True)
    second = jnp.mean(scaled * normed, axis=-1, keepdims=True)
    return (scaled - first - normed * second) * inverse


def gelu_pair(pre):
    cdf = 0.5 * (1.0 + lax.erf(pre * 0.7071067811865476))
    pdf = 0.3989422804014327 * jnp.exp(-0.5 * pre * pre)
    return pre * cdf, cdf + pre * pdf


def to_quarters(field_ref, scratch):
    for lat in range(6):
        for half in range(2):
            rows = field_ref[lat, half * 6 : half * 6 + 6].astype(F32).reshape(48, 192)
            start = ((lat // 3) * 2 + half) * 144 + (lat % 3) * 48
            scratch[start : start + 48, :] = rows


def level_order():
    order = np.zeros((144, 144), np.float32)
    for w in range(4):
        for cell in range(18):
            for level in range(2):
                order[w * 36 + cell * 2 + level, cell * 8 + (2 * w + 1 + level) % 8] = 1.0
    return jnp.asarray(order, BF)


def to_windows(parts, start, order, scratch):
    for s in range(4):
        rows = dot_nn(order, parts[s][start : start + 144, :])
        for w in range(4):
            scratch[w * 144 + s * 36 : w * 144 + s * 36 + 36, :] = rows[w * 36 : w * 36 + 36]


def head_kernel(mid_hbm, up_hbm, gain_hbm, fc1_hbm, fc2_hbm, part_hbm, grads_hbm,
                mid_ref, up_ref, gain_ref, fc1_ref, fc2_ref, part_ref, grads_ref, mid_s, up_s, sem):
    pairs = ((mid_hbm, mid_ref), (gain_hbm, gain_ref), (fc1_hbm, fc1_ref), (up_hbm, up_ref), (fc2_hbm, fc2_ref))
    copies = [pltpu.make_async_copy(a, b, sem.at[i]) for i, (a, b) in enumerate(pairs)]
    for copy in copies:
        copy.start()
    for copy in copies[:3]:
        copy.wait()
    to_quarters(mid_ref, mid_s)
    normed, _ = layer_stats(mid_s[...])
    lowered = (normed * gain_ref[...]).astype(BF)
    pre = dot_nn(lowered, fc1_ref[...])
    active, slopes = gelu_pair(pre)
    for copy in copies[3:]:
        copy.wait()
    to_quarters(up_ref, up_s)
    up = up_s[...].astype(BF)
    grad_pre = (dot_nn(up, fc2_ref[...]) * slopes).astype(BF)
    part_ref[...] = dot_nt(grad_pre, fc1_ref[...]).astype(BF)
    part_copy = pltpu.make_async_copy(part_ref, part_hbm, sem.at[5])
    part_copy.start()
    for start, grads in ((0, dot_tn(lowered, grad_pre)), (576, dot_tn(up, active.astype(BF)))):
        for j in range(3):
            grads_ref[start + j * 192 : start + j * 192 + 192, :] = grads[:, j * 128 : j * 128 + 128].astype(BF)
    grads_copy = pltpu.make_async_copy(grads_ref, grads_hbm, sem.at[6])
    grads_copy.start()
    part_copy.wait()
    grads_copy.wait()


def head(mid, up, gain, fc1, fc2):
    return pl.pallas_call(
        head_kernel,
        out_shape=(shape((576, 192), BF), shape((1152, 128), BF)),
        in_specs=[ANY] * 5,
        out_specs=(ANY, ANY),
        scratch_shapes=[
            pltpu.VMEM((6, 12, 8, 192), BF),
            pltpu.VMEM((6, 12, 8, 192), BF),
            pltpu.VMEM((1, 192), F32),
            pltpu.VMEM((192, 384), BF),
            pltpu.VMEM((192, 384), BF),
            pltpu.VMEM((576, 192), BF),
            pltpu.VMEM((1152, 128), BF),
            pltpu.VMEM((576, 192), F32),
            pltpu.VMEM((576, 192), F32),
            pltpu.SemaphoreType.DMA((7,)),
        ],
        compiler_params=ALL,
        cost_estimate=cost(3),
        name="head",
    )(mid, up, gain, fc1, fc2)


def middle_kernel(x_ref, mid_ref, up_ref, own_ref, other_ref, gain_ref, after_ref,
                  o0, o1, o2, o3, gain_out, x_s, mid_s, up_s):
    to_quarters(x_ref, x_s)
    to_quarters(mid_ref, mid_s)
    to_quarters(up_ref, up_s)
    normed, inverse = layer_stats(mid_s[...])
    grad = own_ref[...].astype(F32) + other_ref[...].astype(F32)
    gain_out[...] = jnp.sum(grad * normed, axis=0, keepdims=True)
    out = up_s[...] + norm_backward(grad, gain_ref[...], normed, inverse)
    for q, o in enumerate((o0, o1, o2, o3)):
        o[0:144, :] = x_s[q * 144 : q * 144 + 144, :].astype(BF)
        o[144:288, :] = out[q * 144 : q * 144 + 144].astype(BF)


def middle(x, mid, up, own, other, gain, after):
    return pl.pallas_call(
        middle_kernel,
        out_shape=tuple(shape((288, 192), BF) for _ in range(4)) + (shape((1, 192), F32),),
        in_specs=[VMEM] * 6 + [ANY],
        scratch_shapes=[pltpu.VMEM((576, 192), F32)] * 3,
        compiler_params=VM,
        cost_estimate=cost(1),
        name="middle",
    )(x, mid, up, own, other, gain, after)


def window_order():
    canon = np.arange(144).reshape(2, 2, 3, 2, 6).transpose(1, 3, 2, 4, 0).reshape(-1)
    order = np.zeros((144, 144), np.float32)
    order[np.arange(144), canon] = 1.0
    return order


def pack_tail(tail):
    spread = (lax.broadcasted_iota(I32, (16, 128), 1) & 15) == lax.broadcasted_iota(I32, (16, 128), 0)
    wide = dot_nn(tail, spread.astype(F32).astype(BF))
    here = (lax.broadcasted_iota(I32, (144, 128), 1) >> 4) == (lax.broadcasted_iota(I32, (144, 128), 0) & 7)
    wide = jnp.where(here, wide, 0.0).astype(BF)
    rows = (lax.broadcasted_iota(I32, (24, 144), 1) >> 3) == lax.broadcasted_iota(I32, (24, 144), 0)
    return dot_nn(rows.astype(F32).astype(BF), wide)


def one_hot(low):
    rows = lax.broadcasted_iota(I32, (256, 128), 0).astype(F32).astype(BF)
    return jnp.where(rows == low.astype(F32).astype(BF), jnp.ones((), BF), jnp.zeros((), BF))


def look_up(terms, lo_ref, hi_ref, stage, first_block, steps):
    half = (lax.broadcasted_iota(I32, (8, 128), 0) >> 2)

    def step(i, _):
        for pair in range(9):
            base = first_block + i * 18 + pair * 2
            hot = jnp.concatenate([one_hot(lo_ref[pl.ds(base + j, 1), :]) for j in range(2)], axis=1)
            found = dot_nn(terms, jnp.concatenate([hot, hot], axis=0))
            for j in range(2):
                cols = slice(j * 128, j * 128 + 128)
                high = hi_ref[pl.ds(base + j, 1), :]
                first = jnp.zeros((8, 128), F32)
                for c in range(13):
                    first = jnp.where(high == c, found[c * 8 : c * 8 + 8, cols], first)
                second = jnp.zeros((8, 128), F32)
                shifted = high - half
                for c in range(7):
                    second = jnp.where(shifted == 2 * c, found[104 + c * 8 : 112 + c * 8, cols], second)
                start = pl.multiple_of((base + j - first_block) * 16, 16)
                stage[pl.ds(start, 8), :] = first
                stage[pl.ds(start + 8, 8), :] = second + pltpu.roll(second, 4, 0)
        return 0

    lax.fori_loop(0, steps, step, 0)


def gather_first_kernel(index_ref, order_ref, bias_ref, ids_ref, valid_ref,
                        stage, lo_ref, hi_ref, terms_ref, code_ref, table):
    index = index_ref[...]
    order = order_ref[...]
    pieces = []
    for part in (index & 127, index >> 7):
        moved = dot_nt(dot_nn(order, part.astype(F32).astype(BF)).astype(BF), order)
        pieces.append((moved[:, 0:128].astype(I32), pack_tail(moved[:, 128:144].astype(BF)).astype(I32)))
    for rows, low, high in ((slice(0, 144), pieces[0][0], pieces[1][0]), (slice(144, 168), pieces[0][1], pieces[1][1])):
        lo_ref[rows, :] = low + (high & 1) * 128
        hi_ref[rows, :] = high >> 1
    table[...] = jnp.zeros((160, 256), F32)
    for r in range(12):
        line = bias_ref[r % 3, r // 3 : r // 3 + 1, :]
        line = line - jnp.max(line, axis=1, keepdims=True)
        for c in range(13):
            wide = min(256, 3312 - c * 256)
            row = c * 8 + r if r < 8 else 104 + (c // 2) * 8 + (c % 2) * 4 + r - 8
            table[row : row + 1, 0:wide] = line[:, c * 256 : c * 256 + wide]
    upper = table[...].astype(BF)
    terms_ref[:, 0:256] = upper
    terms_ref[:, 256:512] = (table[...] - upper.astype(F32)).astype(BF)
    code = (ids_ref[...] * 2 + (valid_ref[...] > 0).astype(I32)).astype(F32).reshape(48, 12).astype(BF)
    row = lax.broadcasted_iota(I32, (24, 48), 0)
    column = lax.broadcasted_iota(I32, (24, 48), 1)
    lines = []
    for level in range(2):
        pick = ((row >> 2) * 8 + (row & 3) * 2 + level) == column
        picked = dot_nn(pick.astype(F32).astype(BF), code)
        lines += [picked[lat * 4 : lat * 4 + 4] for lat in range(6)]
    lines = jnp.concatenate(lines, axis=1)
    code_ref[...] = dot_nt(lines.astype(BF), order)
    look_up(terms_ref[...], lo_ref, hi_ref, stage, 0, 5)


def gather_first(index, bias, ids, valid):
    return pl.pallas_call(
        gather_first_kernel,
        out_shape=(
            shape((90 * 16, 128), F32),
            shape((168, 128), I32),
            shape((168, 128), I32),
            shape((160, 512), BF),
            shape((4, 144), F32),
        ),
        scratch_shapes=[pltpu.VMEM((160, 256), F32)],
        compiler_params=VM,
        cost_estimate=cost(6),
        name="gather_first",
    )(index, jnp.asarray(window_order(), BF), bias, ids, valid)


def gather_second_kernel(first_stage, lo_ref, hi_ref, terms_ref, after_ref, main_ref, tail_ref, stage):
    look_up(terms_ref[...], lo_ref, hi_ref, stage, 90, 4)
    for r in range(12):
        main_ref[r, 0:90, :] = first_stage[pl.ds(r, 90, stride=16), :]
        main_ref[r, 90:144, :] = stage[pl.ds(r, 54, stride=16), :]
        packed = stage[pl.ds(54 * 16 + r, 18, stride=16), :]
        for s in range(8):
            tail_ref[r, pl.ds(s, 18, stride=8), :] = pltpu.roll(packed, 128 - 16 * s, 1) if s else packed


def gather_second(first_stage, lo, hi, terms, after):
    return pl.pallas_call(
        gather_second_kernel,
        out_shape=(shape((12, 144, 128), F32), shape((12, 144, 128), F32)),
        in_specs=[VMEM] * 4 + [ANY],
        scratch_shapes=[pltpu.VMEM((72 * 16, 128), F32)],
        compiler_params=VM,
        cost_estimate=cost(4),
        name="gather_second",
    )(first_stage, lo, hi, terms, after)


def forward_kernel(x0, x1, x2, x3, order_ref, gain_ref, qkv_ref, main_ref, tail_ref, code_ref,
                   low_ref, q_ref, k_ref, v_ref, prob_ref, att_ref, scratch):
    to_windows((x0, x1, x2, x3), 0, order_ref[...], scratch)
    normed, _ = layer_stats(scratch[...])
    low = (normed * gain_ref[...]).astype(BF)
    low_ref[...] = low
    for j, out in enumerate((q_ref, k_ref, v_ref)):
        out[...] = dot_nn(low, qkv_ref[j]).astype(BF)
    eye = lax.broadcasted_iota(I32, (144, 144), 0) == lax.broadcasted_iota(I32, (144, 144), 1)

    def window(w, _):
        rows = pl.ds(pl.multiple_of(w * 144, 16), 144)
        code = code_ref[pl.ds(w, 1), :].astype(I32)
        label = code >> 1
        column = jnp.sum(jnp.where(eye, label, 0), axis=1, keepdims=True)
        allowed = eye | ((column == label) & ((code & 1) > 0))
        query, key, value = q_ref[rows, :], k_ref[rows, :], v_ref[rows, :]
        heads = []
        for h in range(3):
            cols = slice(h * HD, h * HD + HD)
            bias = jnp.concatenate([main_ref[w * 3 + h], tail_ref[w * 3 + h][:, 0:16]], axis=1)
            scores = dot_nt(query[:, cols], key[:, cols]) * (HD ** -0.5) + bias
            scores = jnp.where(allowed, scores, EXCLUDED)
            expo = jnp.exp(scores - jnp.max(scores, axis=-1, keepdims=True))
            prob = expo * (1.0 / jnp.sum(expo, axis=-1, keepdims=True))
            prob_ref[w * 3 + h] = prob
            heads.append(dot_nn(prob.astype(BF), value[:, cols]))
        att_ref[rows, :] = jnp.concatenate(heads, axis=1).astype(BF)
        return 0

    lax.fori_loop(0, 4, window, 0)


def forward(x, gain, qkv, main, tail, code):
    return pl.pallas_call(
        forward_kernel,
        out_shape=(
            shape((576, 192), BF),
            shape((576, 96), BF),
            shape((576, 96), BF),
            shape((576, 96), BF),
            shape((12, 144, 144), F32),
            shape((576, 96), BF),
        ),
        scratch_shapes=[pltpu.VMEM((576, 192), F32)],
        compiler_params=VM,
        cost_estimate=cost(5),
        name="forward",
    )(*x, level_order(), gain, qkv, main, tail, code)


def backward_kernel(g0, g1, g2, g3, order_ref, proj_ref, qkv_ref, low_ref, q_ref, k_ref, v_ref, prob_ref, att_ref,
                    part_ref, score_ref, grads_ref, scratch, gatt, gcols):
    to_windows((g0, g1, g2, g3), 144, order_ref[...], scratch)
    grad = scratch[...].astype(BF)
    gproj = dot_tn(att_ref[...], grad).astype(BF)
    grads_ref[0:96, :] = gproj[:, 0:128]
    grads_ref[96:144, :] = jnp.concatenate([gproj[0:48, 128:192], gproj[48:96, 128:192]], axis=1)
    gatt[...] = dot_nt(grad, proj_ref[...]).astype(BF)

    def window(w, _):
        rows = pl.ds(pl.multiple_of(w * 144, 16), 144)
        query, key, value, above = q_ref[rows, :], k_ref[rows, :], v_ref[rows, :], gatt[rows, :]
        queries, keys, values = [], [], []
        for h in range(3):
            cols = slice(h * HD, h * HD + HD)
            prob = prob_ref[w * 3 + h]
            values.append(dot_tn(prob.astype(BF), above[:, cols]))
            grad_prob = dot_nt(above[:, cols], value[:, cols])
            score = prob * (grad_prob - jnp.sum(grad_prob * prob, axis=-1, keepdims=True))
            score_ref[w * 3 + h, 0:144, :] = score[:, 0:128]
            score_ref[w * 3 + h, 144:168, :] = pack_tail(score[:, 128:144].astype(BF))
            low_score = (score * (HD ** -0.5)).astype(BF)
            queries.append(dot_nn(low_score, key[:, cols]))
            keys.append(dot_tn(low_score, query[:, cols]))
        gcols[0, rows, :] = jnp.concatenate(queries, axis=1).astype(BF)
        gcols[1, rows, :] = jnp.concatenate(keys, axis=1).astype(BF)
        gcols[2, rows, :] = jnp.concatenate(values, axis=1).astype(BF)
        return 0

    lax.fori_loop(0, 4, window, 0)
    low = low_ref[...]
    total = None
    gqkv = []
    for j in range(3):
        cols = gcols[j]
        gqkv.append(dot_tn(low, cols).astype(BF))
        term = dot_nt(cols, qkv_ref[j])
        total = term if total is None else total + term
    a, b, c = gqkv
    grads_ref[144:336, :] = jnp.concatenate([a, c[:, 0:32]], axis=1)
    grads_ref[336:528, :] = jnp.concatenate([b, c[:, 32:64]], axis=1)
    grads_ref[528:576, :] = jnp.concatenate([c[i * 48 : i * 48 + 48, 64:96] for i in range(4)], axis=1)
    scratch[...] = total
    for s in range(4):
        pieces = [scratch[w * 144 + s * 36 : w * 144 + s * 36 + 36, :] for w in range(4)]
        piece = jnp.concatenate(pieces, axis=0).astype(BF)
        part_ref[s * 144 : s * 144 + 144, :] = dot_tn(order_ref[...], piece).astype(BF)


def backward(g, proj, qkv, low, q, k, v, prob, att):
    return pl.pallas_call(
        backward_kernel,
        out_shape=(
            shape((576, 192), BF),
            shape((12, 168, 128), F32),
            shape((576, 128), BF),
        ),
        scratch_shapes=[pltpu.VMEM((576, 192), F32), pltpu.VMEM((576, 96), BF), pltpu.VMEM((3, 576, 96), BF)],
        compiler_params=VM,
        cost_estimate=cost(7),
        name="backward",
    )(*g, level_order(), proj, qkv, low, q, k, v, prob, att)


def scatter_kernel(score_ref, lo_ref, hi_ref, out_ref):
    out_ref[...] = jnp.zeros((192, 256), F32)
    place = lax.broadcasted_iota(I32, (16, 128), 0)

    def step(i, _):
        left, right = [], []
        for j in range(18):
            row = pl.ds(i * 18 + j, 1)
            here = place == hi_ref[row, :]
            right.append(one_hot(lo_ref[row, :]))
            left.append(
                jnp.concatenate([jnp.where(here, score_ref[r, row, :], 0.0).astype(BF) for r in range(12)], axis=0)
            )
        out_ref[...] += dot_nt(jnp.concatenate(left, axis=1), jnp.concatenate(right, axis=1))
        return 0

    lax.fori_loop(0, 9, step, 0)


def scatter(score, lo, hi):
    return pl.pallas_call(
        scatter_kernel, out_shape=shape((192, 256), F32), compiler_params=VM, cost_estimate=cost(5), name="scatter"
    )(score, lo, hi)


def meet_kernel(own_ref, other_ref, x0, x1, x2, x3, first_ref, second_ref, table_ref, two_ref,
                o0, o1, o2, o3, out_ref):
    gain = jnp.zeros((1, 192), F32)
    for s, (x, o) in enumerate(zip((x0, x1, x2, x3), (o0, o1, o2, o3))):
        rows = slice(s * 144, s * 144 + 144)
        grad = own_ref[rows, :].astype(F32) + other_ref[rows, :].astype(F32)
        normed, _ = layer_stats(x[0:144, :].astype(F32))
        gain = gain + jnp.sum(grad * normed, axis=0, keepdims=True)
        o[...] = grad.astype(BF)
    out_ref[0:1152, :] = first_ref[...]
    out_ref[1152:1728, :] = second_ref[...]
    rows = []
    for r in range(12):
        pair = table_ref[r * 16 : r * 16 + 13, :]
        rows += [pair[:, 0:128], pair[:, 128:256]]
    none = jnp.zeros((1, 64), F32)
    for line in (gain, two_ref[...]):
        rows += [line[:, 0:128], jnp.concatenate([line[:, 128:192], none], axis=1)]
    rows += [jnp.zeros((4, 128), F32)]
    out_ref[1728:2048, :] = jnp.concatenate(rows, axis=0).astype(BF)


def meet(own, other, x, first, second, table, two):
    return pl.pallas_call(
        meet_kernel,
        out_shape=tuple(shape((144, 192), BF) for _ in range(4)) + (shape((2048, 128), BF),),
        compiler_params=VM,
        cost_estimate=cost(1),
        name="meet",
    )(own, other, *x, first, second, table, two)


def finish_kernel(x0, x1, x2, x3, g0, g1, g2, g3, gain_ref, out_ref):
    for q, (x, g) in enumerate(zip((x0, x1, x2, x3), (g0, g1, g2, g3))):
        normed, inverse = layer_stats(x[0:144, :].astype(F32))
        rows = x[144:288, :].astype(F32) + norm_backward(g[...].astype(F32), gain_ref[...], normed, inverse)
        for lat in range(3):
            piece = rows[lat * 48 : lat * 48 + 48].reshape(6, 8, 192)
            out_ref[(q // 2) * 3 + lat, (q % 2) * 6 : (q % 2) * 6 + 6] = piece.astype(BF)


def finish(x, g, gain):
    return pl.pallas_call(
        finish_kernel, out_shape=shape((6, 12, 8, 192), BF), compiler_params=VM, cost_estimate=cost(1), name="finish"
    )(*x, *g, gain)


def add_kernel(got_ref, out_ref):
    total = got_ref[0].astype(F32)
    for i in range(1, 32):
        total = total + got_ref[i].astype(F32)
    out_ref[...] = total.astype(BF)


def add(got):
    return pl.pallas_call(
        add_kernel, out_shape=shape((64, 128), BF), compiler_params=VM, cost_estimate=cost(1), name="add"
    )(got)


def spread_kernel(place_ref, own_ref, a_ref, b_ref, c_ref, out_ref):
    own = own_ref[...].astype(F32)
    total = own + a_ref[...].astype(F32) + b_ref[...].astype(F32) + c_ref[...].astype(F32)
    row = place_ref[0] * 64 + lax.broadcasted_iota(I32, (64, 128), 0)
    table = (row >= 1728) & (row < 2040)
    out_ref[...] = jnp.broadcast_to(jnp.where(table, own, total).astype(BF)[None], (32, 64, 128))


def spread(place, own, a, b, c):
    return pl.pallas_call(
        spread_kernel,
        out_shape=shape((32, 64, 128), BF),
        in_specs=[pl.BlockSpec(memory_space=pltpu.SMEM)] + [VMEM] * 4,
        compiler_params=VM,
        cost_estimate=cost(1),
        name="spread",
    )(place, own, a, b, c)


def unpack_kernel(weight_scale, table_scale, half_ref, in_ref,
                  qkv_ref, proj_ref, upg_ref, down_ref, one_ref, two_ref, table_ref):
    def rows(start, stop):
        return in_ref[start:stop, :].astype(F32) * weight_scale

    for j in range(3):
        upg_ref[:, j * 128 : j * 128 + 128] = rows(j * 192, j * 192 + 192)
        down_ref[:, j * 128 : j * 128 + 128] = rows(576 + j * 192, 768 + j * 192)
    proj_ref[:, 0:128] = rows(1152, 1248)
    tail = rows(1248, 1296)
    proj_ref[0:48, 128:192] = tail[:, 0:64]
    proj_ref[48:96, 128:192] = tail[:, 64:128]
    first, second, third = rows(1296, 1488), rows(1488, 1680), rows(1680, 1728)
    qkv_ref[0] = first[:, 0:96]
    qkv_ref[1] = second[:, 0:96]
    qkv_ref[2, :, 0:32] = first[:, 96:128]
    qkv_ref[2, :, 32:64] = second[:, 96:128]
    for i in range(4):
        qkv_ref[2, i * 48 : i * 48 + 48, 64:96] = third[:, i * 32 : i * 32 + 32]
    table = in_ref[1728:2048, :].astype(F32)
    for r in range(12):
        for half in range(2):
            piece = table[r * 26 + half * 13 : r * 26 + half * 13 + 13] * table_scale
            for a in range(13):
                start = a * 256 + half * 128
                wide = min(128, 3312 - start)
                table_ref[r % 3, r // 3 : r // 3 + 1, start : start + wide] = piece[a : a + 1, 0:wide]
    for start, out in ((312, one_ref), (314, two_ref)):
        line = table[start : start + 1]
        upper = jnp.concatenate([line[:, 96:128], table[start + 1 : start + 2, 0:64]], axis=1)
        out[...] = jnp.where(half_ref[0] == 0, line[:, 0:96], upper) * weight_scale


def unpack(weight_scale, table_scale, half, got):
    return pl.pallas_call(
        functools.partial(unpack_kernel, weight_scale, table_scale),
        out_shape=(
            shape((3, 192, 96), F32),
            shape((96, 192), F32),
            shape((192, 384), F32),
            shape((192, 384), F32),
            shape((1, 96), F32),
            shape((1, 96), F32),
            shape((3, 4, 3312), F32),
        ),
        in_specs=[pl.BlockSpec(memory_space=pltpu.SMEM), VMEM],
        compiler_params=VM,
        name="unpack",
    )(half, got)


def moved(value, band, sector, half):
    sizes = [lax.axis_size(name) for name in ("lat", "lon", "tp")]
    pairs = []
    for a in range(sizes[0]):
        for b in range(sizes[1]):
            for c in range(sizes[2]):
                source = ((a + band) % sizes[0], (b + sector) % sizes[1], (c + half) % sizes[2])
                pairs.append(tuple((x * sizes[1] + y) * sizes[2] + z for x, y, z in (source, (a, b, c))))
    return lax.ppermute(value, ("lat", "lon", "tp"), pairs)


def swapped(value, bit):
    pairs = [(a, a ^ bit) for a in range(lax.axis_size("lat"))]
    return lax.ppermute(value, "lat", pairs)


def shifted_parts(quarters):
    return (
        quarters[3],
        moved(quarters[2], 0, 1, 0),
        moved(quarters[1], 1, 0, 0),
        moved(quarters[0], 1, 1, 0),
    )


def local(
    inputs,
    residual_mid,
    grad_out,
    mask_ids,
    key_valid,
    bias_index,
    pos_bias,
    norm1_gain,
    qkv_weight,
    proj_weight,
    norm2_gain,
    fc1_weight,
    fc2_weight,
):
    levels, lat_cells, lon_cells, channels = inputs.shape
    cell_count = levels * lat_cells * lon_cells
    weight_scale = (cell_count * lax.axis_size("lat") * lax.axis_size("lon")) ** (-0.5)
    table_scale = (lon_cells * lax.axis_size("lon") // 12) ** (-0.5)
    gain1, gain2 = norm1_gain.reshape(1, -1), norm2_gain.reshape(1, -1)

    def turned(field):
        return field.transpose(1, 2, 0, 3)

    x_in, mid_in, up_in = turned(inputs), turned(residual_mid), turned(grad_out)
    part2, first = head(mid_in, up_in, gain2, fc1_weight, fc2_weight.T)
    other2 = moved(part2, 0, 0, 1)
    stage, lo, hi, terms, code = gather_first(
        bias_index, pos_bias[0].transpose(1, 0, 2), mask_ids.transpose(1, 0, 2), key_valid.transpose(1, 0, 2)
    )
    *x, gain_two = middle(x_in, mid_in, up_in, part2, other2, gain2, lo)
    xw = shifted_parts(x)
    main, tail = gather_second(stage, lo, hi, terms, gain_two)
    low, q, k, v, prob, att = forward(xw, gain1, qkv_weight, main, tail, code)
    part1, score, second = backward(xw, proj_weight, qkv_weight, low, q, k, v, prob, att)
    other1 = moved(part1, 0, 0, 1)
    table = scatter(score, lo, hi)
    *g, sums = meet(part1, other1, xw, first, second, table, gain_two)
    back = (moved(g[3], -1, -1, 0), moved(g[2], -1, 0, 0), moved(g[1], 0, -1, 0), g[0])
    own = add(lax.all_to_all(sums.reshape(32, 64, 128), "lon", 0, 0))
    place = lax.axis_index("lon").reshape(1)
    totals = spread(place, own, swapped(own, 1), swapped(own, 2), swapped(own, 3))
    got = lax.all_to_all(totals, "lon", 0, 0)
    qkv_out, proj_out, up_out, down_out, one, two, table_out = unpack(
        weight_scale, table_scale, lax.axis_index("tp").reshape(1), got.reshape(2048, 128)
    )
    result = finish(x, back, gain1).transpose(2, 0, 1, 3)
    return (
        result,
        qkv_out,
        proj_out,
        up_out,
        down_out.T,
        one.reshape(channels // lax.axis_size("tp")),
        two.reshape(channels // lax.axis_size("tp")),
        table_out.transpose(1, 0, 2)[None],
    )


def solution(mesh):
    return jax.shard_map(
        local,
        mesh=mesh,
        in_specs=(
            P(None, "lat", "lon", None),
            P(None, "lat", "lon", None),
            P(None, "lat", "lon", None),
            P(None, "lat", "lon"),
            P(None, "lat", "lon"),
            P(),
            P("lat", None, "tp", None),
            P(),
            P(None, None, "tp"),
            P("tp", None),
            P(),
            P(None, "tp"),
            P("tp", None),
        ),
        out_specs=(
            P(None, "lat", "lon", None),
            P(None, None, "tp"),
            P("tp", None),
            P(None, "tp"),
            P("tp", None),
            P("tp"),
            P("tp"),
            P("lat", None, "tp", None),
        ),
        check_vma=False,
    )
```

```python
import functools

import jax
import jax.numpy as jnp
import numpy as np
from jax import lax
from jax.experimental import pallas as pl
from jax.experimental.pallas import tpu as pltpu
from jax.sharding import PartitionSpec as P

HD = 32
EPSILON = 1e-05
EXCLUDED = -1e30
BF = jnp.bfloat16
F32 = jnp.float32
I32 = jnp.int32
VMEM = pl.BlockSpec(memory_space=pltpu.VMEM)
VM = pltpu.CompilerParams(vmem_limit_bytes=24 * 1024 * 1024)
ALL = pltpu.CompilerParams(vmem_limit_bytes=63 * 1024 * 1024)
ANY = pl.BlockSpec(memory_space=pl.ANY)


def cost(microseconds):
    return pl.CostEstimate(flops=int(microseconds * 1e9), bytes_accessed=0, transcendentals=0)


def shape(dims, kind):
    return jax.ShapeDtypeStruct(dims, kind)


def dot_nn(a, b):
    return lax.dot_general(a, b, (((1,), (0,)), ((), ())), preferred_element_type=F32)


def dot_nt(a, b):
    return lax.dot_general(a, b, (((1,), (1,)), ((), ())), preferred_element_type=F32)


def dot_tn(a, b):
    return lax.dot_general(a, b, (((0,), (0,)), ((), ())), preferred_element_type=F32)


def layer_stats(rows):
    mean = jnp.mean(rows, axis=-1, keepdims=True)
    centred = rows - mean
    inverse = lax.rsqrt(jnp.mean(centred * centred, axis=-1, keepdims=True) + EPSILON)
    return centred * inverse, inverse


def norm_backward(grad_normed, gain, normed, inverse):
    scaled = grad_normed * gain
    first = jnp.mean(scaled, axis=-1, keepdims=True)
    second = jnp.mean(scaled * normed, axis=-1, keepdims=True)
    return (scaled - first - normed * second) * inverse


def gelu_pair(pre):
    cdf = 0.5 * (1.0 + lax.erf(pre * 0.7071067811865476))
    pdf = 0.3989422804014327 * jnp.exp(-0.5 * pre * pre)
    return pre * cdf, cdf + pre * pdf


def to_quarters(field_ref, scratch):
    for lat in range(6):
        for half in range(2):
            rows = field_ref[lat, half * 6 : half * 6 + 6].astype(F32).reshape(48, 192)
            start = ((lat // 3) * 2 + half) * 144 + (lat % 3) * 48
            scratch[start : start + 48, :] = rows


def level_order():
    order = np.zeros((144, 144), np.float32)
    for w in range(4):
        for cell in range(18):
            for level in range(2):
                order[w * 36 + cell * 2 + level, cell * 8 + (2 * w + 1 + level) % 8] = 1.0
    return jnp.asarray(order, BF)


def to_windows(parts, order, scratch):
    for s in range(4):
        rows = dot_nn(order, parts[s][...])
        for w in range(4):
            scratch[w * 144 + s * 36 : w * 144 + s * 36 + 36, :] = rows[w * 36 : w * 36 + 36]


def head_kernel(x_hbm, mid_hbm, up_hbm, gain_hbm, fc1_hbm, fc2_hbm, o0, o1, o2, o3, part_hbm, grads_hbm,
                x_ref, mid_ref, up_ref, gain_ref, fc1_ref, fc2_ref, xq_ref, part_ref, grads_ref, x_s, mid_s, up_s, sem):
    pairs = (
        (mid_hbm, mid_ref),
        (gain_hbm, gain_ref),
        (fc1_hbm, fc1_ref),
        (up_hbm, up_ref),
        (fc2_hbm, fc2_ref),
        (x_hbm, x_ref),
    )
    copies = [pltpu.make_async_copy(a, b, sem.at[i]) for i, (a, b) in enumerate(pairs)]
    for copy in copies:
        copy.start()
    for copy in copies[:3]:
        copy.wait()
    to_quarters(mid_ref, mid_s)
    normed, _ = layer_stats(mid_s[...])
    lowered = (normed * gain_ref[...]).astype(BF)
    pre = dot_nn(lowered, fc1_ref[...])
    active, slopes = gelu_pair(pre)
    for copy in copies[3:]:
        copy.wait()
    to_quarters(x_ref, x_s)
    writes = []
    for q, out in enumerate((o0, o1, o2, o3)):
        xq_ref[q] = x_s[q * 144 : q * 144 + 144, :].astype(BF)
        writes.append(pltpu.make_async_copy(xq_ref.at[q], out, sem.at[8 + q]))
        writes[-1].start()
    to_quarters(up_ref, up_s)
    up = up_s[...].astype(BF)
    grad_pre = (dot_nn(up, fc2_ref[...]) * slopes).astype(BF)
    part_ref[...] = dot_nt(grad_pre, fc1_ref[...]).astype(BF)
    writes.append(pltpu.make_async_copy(part_ref, part_hbm, sem.at[6]))
    writes[-1].start()
    for start, grads in ((0, dot_tn(lowered, grad_pre)), (576, dot_tn(up, active.astype(BF)))):
        for j in range(3):
            grads_ref[start + j * 192 : start + j * 192 + 192, :] = grads[:, j * 128 : j * 128 + 128].astype(BF)
    writes.append(pltpu.make_async_copy(grads_ref, grads_hbm, sem.at[7]))
    writes[-1].start()
    for write in writes:
        write.wait()


def head(x, mid, up, gain, fc1, fc2):
    return pl.pallas_call(
        head_kernel,
        out_shape=tuple(shape((144, 192), BF) for _ in range(4)) + (shape((576, 192), BF), shape((1152, 128), BF)),
        in_specs=[ANY] * 6,
        out_specs=tuple(ANY for _ in range(6)),
        scratch_shapes=[
            pltpu.VMEM((6, 12, 8, 192), BF),
            pltpu.VMEM((6, 12, 8, 192), BF),
            pltpu.VMEM((6, 12, 8, 192), BF),
            pltpu.VMEM((1, 192), F32),
            pltpu.VMEM((192, 384), BF),
            pltpu.VMEM((192, 384), BF),
            pltpu.VMEM((4, 144, 192), BF),
            pltpu.VMEM((576, 192), BF),
            pltpu.VMEM((1152, 128), BF),
            pltpu.VMEM((576, 192), F32),
            pltpu.VMEM((576, 192), F32),
            pltpu.VMEM((576, 192), F32),
            pltpu.SemaphoreType.DMA((12,)),
        ],
        compiler_params=ALL,
        cost_estimate=cost(3),
        name="head",
    )(x, mid, up, gain, fc1, fc2)


def middle_kernel(mid_ref, up_ref, own_ref, other_ref, gain_ref, after_ref, o0, o1, o2, o3, gain_out, mid_s, up_s):
    to_quarters(mid_ref, mid_s)
    to_quarters(up_ref, up_s)
    normed, inverse = layer_stats(mid_s[...])
    grad = own_ref[...].astype(F32) + other_ref[...].astype(F32)
    gain_out[...] = jnp.sum(grad * normed, axis=0, keepdims=True)
    out = up_s[...] + norm_backward(grad, gain_ref[...], normed, inverse)
    for q, o in enumerate((o0, o1, o2, o3)):
        o[...] = out[q * 144 : q * 144 + 144].astype(BF)


def middle(mid, up, own, other, gain, after):
    return pl.pallas_call(
        middle_kernel,
        out_shape=tuple(shape((144, 192), BF) for _ in range(4)) + (shape((1, 192), F32),),
        in_specs=[VMEM] * 5 + [ANY],
        scratch_shapes=[pltpu.VMEM((576, 192), F32)] * 2,
        compiler_params=VM,
        cost_estimate=cost(1),
        name="middle",
    )(mid, up, own, other, gain, after)


def window_order():
    canon = np.arange(144).reshape(2, 2, 3, 2, 6).transpose(1, 3, 2, 4, 0).reshape(-1)
    order = np.zeros((144, 144), np.float32)
    order[np.arange(144), canon] = 1.0
    return order


def pack_tail(tail):
    spread = (lax.broadcasted_iota(I32, (16, 128), 1) & 15) == lax.broadcasted_iota(I32, (16, 128), 0)
    wide = dot_nn(tail, spread.astype(F32).astype(BF))
    here = (lax.broadcasted_iota(I32, (144, 128), 1) >> 4) == (lax.broadcasted_iota(I32, (144, 128), 0) & 7)
    wide = jnp.where(here, wide, 0.0).astype(BF)
    rows = (lax.broadcasted_iota(I32, (24, 144), 1) >> 3) == lax.broadcasted_iota(I32, (24, 144), 0)
    return dot_nn(rows.astype(F32).astype(BF), wide)


def one_hot(low):
    rows = lax.broadcasted_iota(I32, (256, 128), 0).astype(F32).astype(BF)
    return jnp.where(rows == low.astype(F32).astype(BF), jnp.ones((), BF), jnp.zeros((), BF))


def look_up(terms, lo_ref, hi_ref, stage, first_block, steps):
    half = (lax.broadcasted_iota(I32, (8, 128), 0) >> 2)

    def step(i, _):
        for pair in range(9):
            base = first_block + i * 18 + pair * 2
            hot = jnp.concatenate([one_hot(lo_ref[pl.ds(base + j, 1), :]) for j in range(2)], axis=1)
            found = dot_nn(terms, jnp.concatenate([hot, hot], axis=0))
            for j in range(2):
                cols = slice(j * 128, j * 128 + 128)
                high = hi_ref[pl.ds(base + j, 1), :]
                first = jnp.zeros((8, 128), F32)
                for c in range(13):
                    first = jnp.where(high == c, found[c * 8 : c * 8 + 8, cols], first)
                second = jnp.zeros((8, 128), F32)
                shifted = high - half
                for c in range(7):
                    second = jnp.where(shifted == 2 * c, found[104 + c * 8 : 112 + c * 8, cols], second)
                start = pl.multiple_of((base + j - first_block) * 16, 16)
                stage[pl.ds(start, 8), :] = first
                stage[pl.ds(start + 8, 8), :] = second + pltpu.roll(second, 4, 0)
        return 0

    lax.fori_loop(0, steps, step, 0, unroll=True)


def gather_first_kernel(index_ref, order_ref, bias_ref, ids_ref, valid_ref,
                        stage, lo_ref, hi_ref, terms_ref, code_ref, table):
    index = index_ref[...]
    order = order_ref[...]
    pieces = []
    for part in (index & 127, index >> 7):
        moved = dot_nt(dot_nn(order, part.astype(F32).astype(BF)).astype(BF), order)
        pieces.append((moved[:, 0:128].astype(I32), pack_tail(moved[:, 128:144].astype(BF)).astype(I32)))
    for rows, low, high in ((slice(0, 144), pieces[0][0], pieces[1][0]), (slice(144, 168), pieces[0][1], pieces[1][1])):
        lo_ref[rows, :] = low + (high & 1) * 128
        hi_ref[rows, :] = high >> 1
    table[...] = jnp.zeros((160, 256), F32)
    for r in range(12):
        line = bias_ref[r % 3, r // 3 : r // 3 + 1, :]
        line = line - jnp.max(line, axis=1, keepdims=True)
        for c in range(13):
            wide = min(256, 3312 - c * 256)
            row = c * 8 + r if r < 8 else 104 + (c // 2) * 8 + (c % 2) * 4 + r - 8
            table[row : row + 1, 0:wide] = line[:, c * 256 : c * 256 + wide]
    upper = table[...].astype(BF)
    terms_ref[:, 0:256] = upper
    terms_ref[:, 256:512] = (table[...] - upper.astype(F32)).astype(BF)
    code = (ids_ref[...] * 2 + (valid_ref[...] > 0).astype(I32)).astype(F32).reshape(48, 12).astype(BF)
    row = lax.broadcasted_iota(I32, (24, 48), 0)
    column = lax.broadcasted_iota(I32, (24, 48), 1)
    lines = []
    for level in range(2):
        pick = ((row >> 2) * 8 + (row & 3) * 2 + level) == column
        picked = dot_nn(pick.astype(F32).astype(BF), code)
        lines += [picked[lat * 4 : lat * 4 + 4] for lat in range(6)]
    lines = jnp.concatenate(lines, axis=1)
    code_ref[...] = dot_nt(lines.astype(BF), order)
    look_up(terms_ref[...], lo_ref, hi_ref, stage, 0, 5)


def gather_first(index, bias, ids, valid):
    return pl.pallas_call(
        gather_first_kernel,
        out_shape=(
            shape((90 * 16, 128), F32),
            shape((168, 128), I32),
            shape((168, 128), I32),
            shape((160, 512), BF),
            shape((4, 144), F32),
        ),
        scratch_shapes=[pltpu.VMEM((160, 256), F32)],
        compiler_params=VM,
        cost_estimate=cost(6),
        name="gather_first",
    )(index, jnp.asarray(window_order(), BF), bias, ids, valid)


def gather_second_kernel(first_stage, lo_ref, hi_ref, terms_ref, after_ref, main_ref, tail_ref, stage):
    look_up(terms_ref[...], lo_ref, hi_ref, stage, 90, 4)
    for r in range(12):
        main_ref[r, 0:90, :] = first_stage[pl.ds(r, 90, stride=16), :]
        main_ref[r, 90:144, :] = stage[pl.ds(r, 54, stride=16), :]
        packed = stage[pl.ds(54 * 16 + r, 18, stride=16), :]
        for s in range(8):
            tail_ref[r, pl.ds(s, 18, stride=8), :] = pltpu.roll(packed, 128 - 16 * s, 1) if s else packed


def gather_second(first_stage, lo, hi, terms, after):
    return pl.pallas_call(
        gather_second_kernel,
        out_shape=(shape((12, 144, 128), F32), shape((12, 144, 128), F32)),
        in_specs=[VMEM] * 4 + [ANY],
        scratch_shapes=[pltpu.VMEM((72 * 16, 128), F32)],
        compiler_params=VM,
        cost_estimate=cost(4),
        name="gather_second",
    )(first_stage, lo, hi, terms, after)


def forward_kernel(x0, x1, x2, x3, order_ref, gain_ref, qkv_ref, main_ref, tail_ref, code_ref,
                   low_ref, q_ref, k_ref, v_ref, prob_ref, att_ref, scratch):
    to_windows((x0, x1, x2, x3), order_ref[...], scratch)
    normed, _ = layer_stats(scratch[...])
    low = (normed * gain_ref[...]).astype(BF)
    low_ref[...] = low
    for j, out in enumerate((q_ref, k_ref, v_ref)):
        out[...] = dot_nn(low, qkv_ref[j]).astype(BF)
    eye = lax.broadcasted_iota(I32, (144, 144), 0) == lax.broadcasted_iota(I32, (144, 144), 1)

    def window(w, _):
        rows = pl.ds(pl.multiple_of(w * 144, 16), 144)
        code = code_ref[pl.ds(w, 1), :].astype(I32)
        label = code >> 1
        column = jnp.sum(jnp.where(eye, label, 0), axis=1, keepdims=True)
        allowed = eye | ((column == label) & ((code & 1) > 0))
        query, key, value = q_ref[rows, :], k_ref[rows, :], v_ref[rows, :]
        heads = []
        for h in range(3):
            cols = slice(h * HD, h * HD + HD)
            bias = jnp.concatenate([main_ref[w * 3 + h], tail_ref[w * 3 + h][:, 0:16]], axis=1)
            scores = dot_nt(query[:, cols], key[:, cols]) * (HD ** -0.5) + bias
            scores = jnp.where(allowed, scores, EXCLUDED)
            expo = jnp.exp(scores - jnp.max(scores, axis=-1, keepdims=True))
            prob = expo * (1.0 / jnp.sum(expo, axis=-1, keepdims=True))
            prob_ref[w * 3 + h] = prob
            heads.append(dot_nn(prob.astype(BF), value[:, cols]))
        att_ref[rows, :] = jnp.concatenate(heads, axis=1).astype(BF)
        return 0

    lax.fori_loop(0, 4, window, 0, unroll=True)


def forward(x, gain, qkv, main, tail, code):
    return pl.pallas_call(
        forward_kernel,
        out_shape=(
            shape((576, 192), BF),
            shape((576, 96), BF),
            shape((576, 96), BF),
            shape((576, 96), BF),
            shape((12, 144, 144), F32),
            shape((576, 96), BF),
        ),
        scratch_shapes=[pltpu.VMEM((576, 192), F32)],
        compiler_params=VM,
        cost_estimate=cost(5),
        name="forward",
    )(*x, level_order(), gain, qkv, main, tail, code)


def backward_kernel(g0, g1, g2, g3, order_ref, proj_ref, qkv_ref, low_ref, q_ref, k_ref, v_ref, prob_ref, att_ref,
                    part_ref, score_ref, grads_ref, scratch, gatt, gcols):
    to_windows((g0, g1, g2, g3), order_ref[...], scratch)
    grad = scratch[...].astype(BF)
    gproj = dot_tn(att_ref[...], grad).astype(BF)
    grads_ref[0:96, :] = gproj[:, 0:128]
    grads_ref[96:144, :] = jnp.concatenate([gproj[0:48, 128:192], gproj[48:96, 128:192]], axis=1)
    gatt[...] = dot_nt(grad, proj_ref[...]).astype(BF)

    def window(w, _):
        rows = pl.ds(pl.multiple_of(w * 144, 16), 144)
        query, key, value, above = q_ref[rows, :], k_ref[rows, :], v_ref[rows, :], gatt[rows, :]
        queries, keys, values = [], [], []
        for h in range(3):
            cols = slice(h * HD, h * HD + HD)
            prob = prob_ref[w * 3 + h]
            values.append(dot_tn(prob.astype(BF), above[:, cols]))
            grad_prob = dot_nt(above[:, cols], value[:, cols])
            score = prob * (grad_prob - jnp.sum(grad_prob * prob, axis=-1, keepdims=True))
            score_ref[w * 3 + h, 0:144, :] = score[:, 0:128]
            score_ref[w * 3 + h, 144:168, :] = pack_tail(score[:, 128:144].astype(BF))
            low_score = (score * (HD ** -0.5)).astype(BF)
            queries.append(dot_nn(low_score, key[:, cols]))
            keys.append(dot_tn(low_score, query[:, cols]))
        gcols[0, rows, :] = jnp.concatenate(queries, axis=1).astype(BF)
        gcols[1, rows, :] = jnp.concatenate(keys, axis=1).astype(BF)
        gcols[2, rows, :] = jnp.concatenate(values, axis=1).astype(BF)
        return 0

    lax.fori_loop(0, 4, window, 0, unroll=True)
    low = low_ref[...]
    total = None
    gqkv = []
    for j in range(3):
        cols = gcols[j]
        gqkv.append(dot_tn(low, cols).astype(BF))
        term = dot_nt(cols, qkv_ref[j])
        total = term if total is None else total + term
    a, b, c = gqkv
    grads_ref[144:336, :] = jnp.concatenate([a, c[:, 0:32]], axis=1)
    grads_ref[336:528, :] = jnp.concatenate([b, c[:, 32:64]], axis=1)
    grads_ref[528:576, :] = jnp.concatenate([c[i * 48 : i * 48 + 48, 64:96] for i in range(4)], axis=1)
    scratch[...] = total
    for s in range(4):
        pieces = [scratch[w * 144 + s * 36 : w * 144 + s * 36 + 36, :] for w in range(4)]
        piece = jnp.concatenate(pieces, axis=0).astype(BF)
        part_ref[s * 144 : s * 144 + 144, :] = dot_tn(order_ref[...], piece).astype(BF)


def backward(g, proj, qkv, low, q, k, v, prob, att):
    return pl.pallas_call(
        backward_kernel,
        out_shape=(
            shape((576, 192), BF),
            shape((12, 168, 128), F32),
            shape((576, 128), BF),
        ),
        scratch_shapes=[pltpu.VMEM((576, 192), F32), pltpu.VMEM((576, 96), BF), pltpu.VMEM((3, 576, 96), BF)],
        compiler_params=VM,
        cost_estimate=cost(7),
        name="backward",
    )(*g, level_order(), proj, qkv, low, q, k, v, prob, att)


def scatter_kernel(score_ref, lo_ref, hi_ref, out_ref):
    out_ref[...] = jnp.zeros((192, 256), F32)
    place = lax.broadcasted_iota(I32, (16, 128), 0)

    def step(i, _):
        left, right = [], []
        for j in range(18):
            row = pl.ds(i * 18 + j, 1)
            here = place == hi_ref[row, :]
            right.append(one_hot(lo_ref[row, :]))
            left.append(
                jnp.concatenate([jnp.where(here, score_ref[r, row, :], 0.0).astype(BF) for r in range(12)], axis=0)
            )
        out_ref[...] += dot_nt(jnp.concatenate(left, axis=1), jnp.concatenate(right, axis=1))
        return 0

    lax.fori_loop(0, 9, step, 0, unroll=True)


def scatter(score, lo, hi):
    return pl.pallas_call(
        scatter_kernel, out_shape=shape((192, 256), F32), compiler_params=VM, cost_estimate=cost(5), name="scatter"
    )(score, lo, hi)


def meet_kernel(own_ref, other_ref, x0, x1, x2, x3, first_ref, second_ref, table_ref, two_ref,
                o0, o1, o2, o3, out_ref):
    gain = jnp.zeros((1, 192), F32)
    for s, (x, o) in enumerate(zip((x0, x1, x2, x3), (o0, o1, o2, o3))):
        rows = slice(s * 144, s * 144 + 144)
        grad = own_ref[rows, :].astype(F32) + other_ref[rows, :].astype(F32)
        normed, _ = layer_stats(x[...].astype(F32))
        gain = gain + jnp.sum(grad * normed, axis=0, keepdims=True)
        o[...] = grad.astype(BF)
    out_ref[0:1152, :] = first_ref[...]
    out_ref[1152:1728, :] = second_ref[...]
    rows = []
    for r in range(12):
        pair = table_ref[r * 16 : r * 16 + 13, :]
        rows += [pair[:, 0:128], pair[:, 128:256]]
    none = jnp.zeros((1, 64), F32)
    for line in (gain, two_ref[...]):
        rows += [line[:, 0:128], jnp.concatenate([line[:, 128:192], none], axis=1)]
    rows += [jnp.zeros((4, 128), F32)]
    out_ref[1728:2048, :] = jnp.concatenate(rows, axis=0).astype(BF)


def meet(own, other, x, first, second, table, two):
    return pl.pallas_call(
        meet_kernel,
        out_shape=tuple(shape((144, 192), BF) for _ in range(4)) + (shape((2048, 128), BF),),
        compiler_params=VM,
        cost_estimate=cost(1),
        name="meet",
    )(own, other, *x, first, second, table, two)


def finish_kernel(x0, x1, x2, x3, m0, m1, m2, m3, g0, g1, g2, g3, gain_ref, out_ref):
    for q, (x, m, g) in enumerate(zip((x0, x1, x2, x3), (m0, m1, m2, m3), (g0, g1, g2, g3))):
        normed, inverse = layer_stats(x[...].astype(F32))
        rows = m[...].astype(F32) + norm_backward(g[...].astype(F32), gain_ref[...], normed, inverse)
        for lat in range(3):
            piece = rows[lat * 48 : lat * 48 + 48].reshape(6, 8, 192)
            out_ref[(q // 2) * 3 + lat, (q % 2) * 6 : (q % 2) * 6 + 6] = piece.astype(BF)


def finish(x, m, g, gain):
    return pl.pallas_call(
        finish_kernel, out_shape=shape((6, 12, 8, 192), BF), compiler_params=VM, cost_estimate=cost(1), name="finish"
    )(*x, *m, *g, gain)


def add_kernel(got_ref, b0, b1, b2, out_ref):
    total = got_ref[0].astype(F32)
    for i in range(1, 32):
        total = total + got_ref[i].astype(F32)
    out_ref[...] = total.astype(BF)


def add(got, after):
    return pl.pallas_call(
        add_kernel,
        out_shape=shape((64, 128), BF),
        in_specs=[VMEM] + [ANY] * 3,
        compiler_params=VM,
        cost_estimate=cost(1),
        name="add",
    )(got, *after)


def spread_kernel(place_ref, own_ref, a_ref, b_ref, c_ref, after_ref, out_ref):
    own = own_ref[...].astype(F32)
    total = own + a_ref[...].astype(F32) + b_ref[...].astype(F32) + c_ref[...].astype(F32)
    row = place_ref[0] * 64 + lax.broadcasted_iota(I32, (64, 128), 0)
    table = (row >= 1728) & (row < 2040)
    out_ref[...] = jnp.broadcast_to(jnp.where(table, own, total).astype(BF)[None], (32, 64, 128))


def spread(place, own, a, b, c, after):
    return pl.pallas_call(
        spread_kernel,
        out_shape=shape((32, 64, 128), BF),
        in_specs=[pl.BlockSpec(memory_space=pltpu.SMEM)] + [VMEM] * 4 + [ANY],
        compiler_params=VM,
        cost_estimate=cost(1),
        name="spread",
    )(place, own, a, b, c, after)


def unpack_kernel(weight_scale, table_scale, half_ref, in_ref,
                  qkv_ref, proj_ref, upg_ref, down_ref, one_ref, two_ref, table_ref):
    def rows(start, stop):
        return in_ref[start:stop, :].astype(F32) * weight_scale

    for j in range(3):
        upg_ref[:, j * 128 : j * 128 + 128] = rows(j * 192, j * 192 + 192)
        down_ref[:, j * 128 : j * 128 + 128] = rows(576 + j * 192, 768 + j * 192)
    proj_ref[:, 0:128] = rows(1152, 1248)
    tail = rows(1248, 1296)
    proj_ref[0:48, 128:192] = tail[:, 0:64]
    proj_ref[48:96, 128:192] = tail[:, 64:128]
    first, second, third = rows(1296, 1488), rows(1488, 1680), rows(1680, 1728)
    qkv_ref[0] = first[:, 0:96]
    qkv_ref[1] = second[:, 0:96]
    qkv_ref[2, :, 0:32] = first[:, 96:128]
    qkv_ref[2, :, 32:64] = second[:, 96:128]
    for i in range(4):
        qkv_ref[2, i * 48 : i * 48 + 48, 64:96] = third[:, i * 32 : i * 32 + 32]
    table = in_ref[1728:2048, :].astype(F32)
    for r in range(12):
        for half in range(2):
            piece = table[r * 26 + half * 13 : r * 26 + half * 13 + 13] * table_scale
            for a in range(13):
                start = a * 256 + half * 128
                wide = min(128, 3312 - start)
                table_ref[r % 3, r // 3 : r // 3 + 1, start : start + wide] = piece[a : a + 1, 0:wide]
    for start, out in ((312, one_ref), (314, two_ref)):
        line = table[start : start + 1]
        upper = jnp.concatenate([line[:, 96:128], table[start + 1 : start + 2, 0:64]], axis=1)
        out[...] = jnp.where(half_ref[0] == 0, line[:, 0:96], upper) * weight_scale


def unpack(weight_scale, table_scale, half, got):
    return pl.pallas_call(
        functools.partial(unpack_kernel, weight_scale, table_scale),
        out_shape=(
            shape((3, 192, 96), F32),
            shape((96, 192), F32),
            shape((192, 384), F32),
            shape((192, 384), F32),
            shape((1, 96), F32),
            shape((1, 96), F32),
            shape((3, 4, 3312), F32),
        ),
        in_specs=[pl.BlockSpec(memory_space=pltpu.SMEM), VMEM],
        compiler_params=VM,
        name="unpack",
    )(half, got)


def moved(value, band, sector, half):
    sizes = [lax.axis_size(name) for name in ("lat", "lon", "tp")]
    pairs = []
    for a in range(sizes[0]):
        for b in range(sizes[1]):
            for c in range(sizes[2]):
                source = ((a + band) % sizes[0], (b + sector) % sizes[1], (c + half) % sizes[2])
                pairs.append(tuple((x * sizes[1] + y) * sizes[2] + z for x, y, z in (source, (a, b, c))))
    return lax.ppermute(value, ("lat", "lon", "tp"), pairs)


def swapped(value, bit):
    pairs = [(a, a ^ bit) for a in range(lax.axis_size("lat"))]
    return lax.ppermute(value, "lat", pairs)


def shifted_parts(quarters):
    return (
        quarters[3],
        moved(quarters[2], 0, 1, 0),
        moved(quarters[1], 1, 0, 0),
        moved(quarters[0], 1, 1, 0),
    )


def local(
    inputs,
    residual_mid,
    grad_out,
    mask_ids,
    key_valid,
    bias_index,
    pos_bias,
    norm1_gain,
    qkv_weight,
    proj_weight,
    norm2_gain,
    fc1_weight,
    fc2_weight,
):
    levels, lat_cells, lon_cells, channels = inputs.shape
    cell_count = levels * lat_cells * lon_cells
    weight_scale = (cell_count * lax.axis_size("lat") * lax.axis_size("lon")) ** (-0.5)
    table_scale = (lon_cells * lax.axis_size("lon") // 12) ** (-0.5)
    gain1, gain2 = norm1_gain.reshape(1, -1), norm2_gain.reshape(1, -1)

    def turned(field):
        return field.transpose(1, 2, 0, 3)

    x_in, mid_in, up_in = turned(inputs), turned(residual_mid), turned(grad_out)
    *x, part2, first = head(x_in, mid_in, up_in, gain2, fc1_weight, fc2_weight.T)
    other2 = moved(part2, 0, 0, 1)
    xw = shifted_parts(x)
    stage, lo, hi, terms, code = gather_first(
        bias_index, pos_bias[0].transpose(1, 0, 2), mask_ids.transpose(1, 0, 2), key_valid.transpose(1, 0, 2)
    )
    *gm, gain_two = middle(mid_in, up_in, part2, other2, gain2, lo)
    gw = shifted_parts(gm)
    main, tail = gather_second(stage, lo, hi, terms, gain_two)
    low, q, k, v, prob, att = forward(xw, gain1, qkv_weight, main, tail, code)
    part1, score, second = backward(gw, proj_weight, qkv_weight, low, q, k, v, prob, att)
    other1 = moved(part1, 0, 0, 1)
    table = scatter(score, lo, hi)
    *g, sums = meet(part1, other1, xw, first, second, table, gain_two)
    back = (moved(g[3], -1, -1, 0), moved(g[2], -1, 0, 0), moved(g[1], 0, -1, 0), g[0])
    own = add(lax.all_to_all(sums.reshape(32, 64, 128), "lon", 0, 0), back[:3])
    result = finish(x, gm, back, gain1)
    place = lax.axis_index("lon").reshape(1)
    totals = spread(place, own, swapped(own, 1), swapped(own, 2), swapped(own, 3), result)
    got = lax.all_to_all(totals, "lon", 0, 0)
    qkv_out, proj_out, up_out, down_out, one, two, table_out = unpack(
        weight_scale, table_scale, lax.axis_index("tp").reshape(1), got.reshape(2048, 128)
    )
    return (
        result.transpose(2, 0, 1, 3),
        qkv_out,
        proj_out,
        up_out,
        down_out.T,
        one.reshape(channels // lax.axis_size("tp")),
        two.reshape(channels // lax.axis_size("tp")),
        table_out.transpose(1, 0, 2)[None],
    )


def solution(mesh):
    return jax.shard_map(
        local,
        mesh=mesh,
        in_specs=(
            P(None, "lat", "lon", None),
            P(None, "lat", "lon", None),
            P(None, "lat", "lon", None),
            P(None, "lat", "lon"),
            P(None, "lat", "lon"),
            P(),
            P("lat", None, "tp", None),
            P(),
            P(None, None, "tp"),
            P("tp", None),
            P(),
            P(None, "tp"),
            P("tp", None),
        ),
        out_specs=(
            P(None, "lat", "lon", None),
            P(None, None, "tp"),
            P("tp", None),
            P(None, "tp"),
            P("tp", None),
            P("tp"),
            P("tp"),
            P("lat", None, "tp", None),
        ),
        check_vma=False,
    )
```

```python
import functools

import jax
import jax.numpy as jnp
import numpy as np
from jax import lax
from jax.experimental import pallas as pl
from jax.experimental.pallas import tpu as pltpu
from jax.sharding import PartitionSpec as P

HD = 32
EPSILON = 1e-05
EXCLUDED = -1e30
BF = jnp.bfloat16
F32 = jnp.float32
I32 = jnp.int32
VMEM = pl.BlockSpec(memory_space=pltpu.VMEM)
VM = pltpu.CompilerParams(vmem_limit_bytes=24 * 1024 * 1024)
ALL = pltpu.CompilerParams(vmem_limit_bytes=63 * 1024 * 1024)
SMEM = pl.BlockSpec(memory_space=pltpu.SMEM)
ANY = pl.BlockSpec(memory_space=pl.ANY)


def cost(microseconds):
    return pl.CostEstimate(flops=int(microseconds * 1e9), bytes_accessed=0, transcendentals=0)


def shape(dims, kind):
    return jax.ShapeDtypeStruct(dims, kind)


def dot_nn(a, b):
    return lax.dot_general(a, b, (((1,), (0,)), ((), ())), preferred_element_type=F32)


def dot_nt(a, b):
    return lax.dot_general(a, b, (((1,), (1,)), ((), ())), preferred_element_type=F32)


def dot_tn(a, b):
    return lax.dot_general(a, b, (((0,), (0,)), ((), ())), preferred_element_type=F32)


def layer_stats(rows):
    mean = jnp.mean(rows, axis=-1, keepdims=True)
    centred = rows - mean
    inverse = lax.rsqrt(jnp.mean(centred * centred, axis=-1, keepdims=True) + EPSILON)
    return centred * inverse, inverse


def norm_backward(grad_normed, gain, normed, inverse):
    scaled = grad_normed * gain
    first = jnp.mean(scaled, axis=-1, keepdims=True)
    second = jnp.mean(scaled * normed, axis=-1, keepdims=True)
    return (scaled - first - normed * second) * inverse


def gelu_pair(pre):
    cdf = 0.5 * (1.0 + lax.erf(pre * 0.7071067811865476))
    pdf = 0.3989422804014327 * jnp.exp(-0.5 * pre * pre)
    return pre * cdf, cdf + pre * pdf


def to_quarters(field_ref, scratch):
    for lat in range(6):
        for half in range(2):
            rows = field_ref[lat, half * 6 : half * 6 + 6].astype(F32).reshape(48, 192)
            start = ((lat // 3) * 2 + half) * 144 + (lat % 3) * 48
            scratch[start : start + 48, :] = rows


def level_order():
    order = np.zeros((144, 144), np.float32)
    for w in range(4):
        for cell in range(18):
            for level in range(2):
                order[w * 36 + cell * 2 + level, cell * 8 + (2 * w + 1 + level) % 8] = 1.0
    return jnp.asarray(order, BF)


def to_windows(parts, order, scratch):
    for s in range(4):
        rows = dot_nn(order, parts[s][...])
        for w in range(4):
            scratch[w * 144 + s * 36 : w * 144 + s * 36 + 36, :] = rows[w * 36 : w * 36 + 36]


def head_kernel(x_hbm, mid_hbm, up_hbm, gain_hbm, fc1_hbm, fc2_hbm, o0, o1, o2, o3, part_hbm, grads_hbm,
                x_ref, mid_ref, up_ref, gain_ref, fc1_ref, fc2_ref, xq_ref, part_ref, grads_ref, x_s, mid_s, up_s, sem):
    pairs = (
        (mid_hbm, mid_ref),
        (gain_hbm, gain_ref),
        (fc1_hbm, fc1_ref),
        (up_hbm, up_ref),
        (fc2_hbm, fc2_ref),
        (x_hbm, x_ref),
    )
    copies = [pltpu.make_async_copy(a, b, sem.at[i]) for i, (a, b) in enumerate(pairs)]
    for copy in copies:
        copy.start()
    for copy in copies[:3]:
        copy.wait()
    to_quarters(mid_ref, mid_s)
    normed, _ = layer_stats(mid_s[...])
    lowered = (normed * gain_ref[...]).astype(BF)
    pre = dot_nn(lowered, fc1_ref[...])
    active, slopes = gelu_pair(pre)
    for copy in copies[3:]:
        copy.wait()
    to_quarters(x_ref, x_s)
    writes = []
    for q, out in enumerate((o0, o1, o2, o3)):
        xq_ref[q] = x_s[q * 144 : q * 144 + 144, :].astype(BF)
        writes.append(pltpu.make_async_copy(xq_ref.at[q], out, sem.at[8 + q]))
        writes[-1].start()
    to_quarters(up_ref, up_s)
    up = up_s[...].astype(BF)
    grad_pre = (dot_nn(up, fc2_ref[...]) * slopes).astype(BF)
    part_ref[...] = dot_nt(grad_pre, fc1_ref[...]).astype(BF)
    writes.append(pltpu.make_async_copy(part_ref, part_hbm, sem.at[6]))
    writes[-1].start()
    for start, grads in ((0, dot_tn(lowered, grad_pre)), (576, dot_tn(up, active.astype(BF)))):
        for j in range(3):
            grads_ref[start + j * 192 : start + j * 192 + 192, :] = grads[:, j * 128 : j * 128 + 128].astype(BF)
    writes.append(pltpu.make_async_copy(grads_ref, grads_hbm, sem.at[7]))
    writes[-1].start()
    for write in writes:
        write.wait()


def head(x, mid, up, gain, fc1, fc2):
    return pl.pallas_call(
        head_kernel,
        out_shape=tuple(shape((144, 192), BF) for _ in range(4)) + (shape((576, 192), BF), shape((1152, 128), BF)),
        in_specs=[ANY] * 6,
        out_specs=tuple(ANY for _ in range(6)),
        scratch_shapes=[
            pltpu.VMEM((6, 12, 8, 192), BF),
            pltpu.VMEM((6, 12, 8, 192), BF),
            pltpu.VMEM((6, 12, 8, 192), BF),
            pltpu.VMEM((1, 192), F32),
            pltpu.VMEM((192, 384), BF),
            pltpu.VMEM((192, 384), BF),
            pltpu.VMEM((4, 144, 192), BF),
            pltpu.VMEM((576, 192), BF),
            pltpu.VMEM((1152, 128), BF),
            pltpu.VMEM((576, 192), F32),
            pltpu.VMEM((576, 192), F32),
            pltpu.VMEM((576, 192), F32),
            pltpu.SemaphoreType.DMA((12,)),
        ],
        compiler_params=ALL,
        cost_estimate=cost(3),
        name="head",
    )(x, mid, up, gain, fc1, fc2)


def middle_kernel(mid_ref, up_ref, own_ref, other_ref, gain_ref, after_ref, o0, o1, o2, o3, gain_out, mid_s, up_s):
    to_quarters(mid_ref, mid_s)
    to_quarters(up_ref, up_s)
    normed, inverse = layer_stats(mid_s[...])
    grad = own_ref[...].astype(F32) + other_ref[...].astype(F32)
    gain_out[...] = jnp.sum(grad * normed, axis=0, keepdims=True)
    out = up_s[...] + norm_backward(grad, gain_ref[...], normed, inverse)
    for q, o in enumerate((o0, o1, o2, o3)):
        o[...] = out[q * 144 : q * 144 + 144].astype(BF)


def middle(mid, up, own, other, gain, after):
    return pl.pallas_call(
        middle_kernel,
        out_shape=tuple(shape((144, 192), BF) for _ in range(4)) + (shape((1, 192), F32),),
        in_specs=[VMEM] * 5 + [ANY],
        scratch_shapes=[pltpu.VMEM((576, 192), F32)] * 2,
        compiler_params=VM,
        cost_estimate=cost(1),
        name="middle",
    )(mid, up, own, other, gain, after)


def window_order():
    canon = np.arange(144).reshape(2, 2, 3, 2, 6).transpose(1, 3, 2, 4, 0).reshape(-1)
    order = np.zeros((144, 144), np.float32)
    order[np.arange(144), canon] = 1.0
    return order


def pack_tail(tail):
    spread = (lax.broadcasted_iota(I32, (16, 128), 1) & 15) == lax.broadcasted_iota(I32, (16, 128), 0)
    wide = dot_nn(tail, spread.astype(F32).astype(BF))
    here = (lax.broadcasted_iota(I32, (144, 128), 1) >> 4) == (lax.broadcasted_iota(I32, (144, 128), 0) & 7)
    wide = jnp.where(here, wide, 0.0).astype(BF)
    rows = (lax.broadcasted_iota(I32, (24, 144), 1) >> 3) == lax.broadcasted_iota(I32, (24, 144), 0)
    return dot_nn(rows.astype(F32).astype(BF), wide)


def one_hot(low):
    rows = lax.broadcasted_iota(I32, (256, 128), 0).astype(F32).astype(BF)
    return jnp.where(rows == low.astype(F32).astype(BF), jnp.ones((), BF), jnp.zeros((), BF))


def look_up(terms, lo_ref, hi_ref, stage, first_block, steps):
    half = (lax.broadcasted_iota(I32, (8, 128), 0) >> 2)

    def step(i, _):
        for pair in range(9):
            base = first_block + i * 18 + pair * 2
            hot = jnp.concatenate([one_hot(lo_ref[pl.ds(base + j, 1), :]) for j in range(2)], axis=1)
            found = dot_nn(terms, jnp.concatenate([hot, hot], axis=0))
            for j in range(2):
                cols = slice(j * 128, j * 128 + 128)
                high = hi_ref[pl.ds(base + j, 1), :]
                first = jnp.zeros((8, 128), F32)
                for c in range(13):
                    first = jnp.where(high == c, found[c * 8 : c * 8 + 8, cols], first)
                second = jnp.zeros((8, 128), F32)
                shifted = high - half
                for c in range(7):
                    second = jnp.where(shifted == 2 * c, found[104 + c * 8 : 112 + c * 8, cols], second)
                start = pl.multiple_of((base + j - first_block) * 16, 16)
                stage[pl.ds(start, 8), :] = first
                stage[pl.ds(start + 8, 8), :] = second + pltpu.roll(second, 4, 0)
        return 0

    lax.fori_loop(0, steps, step, 0, unroll=True)


def gather_first_kernel(index_ref, order_ref, bias_ref, ids_ref, valid_ref,
                        stage, lo_ref, hi_ref, terms_ref, code_ref, table):
    index = index_ref[...]
    order = order_ref[...]
    pieces = []
    for part in (index & 127, index >> 7):
        moved = dot_nt(dot_nn(order, part.astype(F32).astype(BF)).astype(BF), order)
        pieces.append((moved[:, 0:128].astype(I32), pack_tail(moved[:, 128:144].astype(BF)).astype(I32)))
    for rows, low, high in ((slice(0, 144), pieces[0][0], pieces[1][0]), (slice(144, 168), pieces[0][1], pieces[1][1])):
        lo_ref[rows, :] = low + (high & 1) * 128
        hi_ref[rows, :] = high >> 1
    table[...] = jnp.zeros((160, 256), F32)
    for r in range(12):
        line = bias_ref[r % 3, r // 3 : r // 3 + 1, :]
        line = line - jnp.max(line, axis=1, keepdims=True)
        for c in range(13):
            wide = min(256, 3312 - c * 256)
            row = c * 8 + r if r < 8 else 104 + (c // 2) * 8 + (c % 2) * 4 + r - 8
            table[row : row + 1, 0:wide] = line[:, c * 256 : c * 256 + wide]
    upper = table[...].astype(BF)
    terms_ref[:, 0:256] = upper
    terms_ref[:, 256:512] = (table[...] - upper.astype(F32)).astype(BF)
    code = (ids_ref[...] * 2 + (valid_ref[...] > 0).astype(I32)).astype(F32).reshape(48, 12).astype(BF)
    row = lax.broadcasted_iota(I32, (24, 48), 0)
    column = lax.broadcasted_iota(I32, (24, 48), 1)
    lines = []
    for level in range(2):
        pick = ((row >> 2) * 8 + (row & 3) * 2 + level) == column
        picked = dot_nn(pick.astype(F32).astype(BF), code)
        lines += [picked[lat * 4 : lat * 4 + 4] for lat in range(6)]
    lines = jnp.concatenate(lines, axis=1)
    code_ref[...] = dot_nt(lines.astype(BF), order)
    look_up(terms_ref[...], lo_ref, hi_ref, stage, 0, 5)


def gather_first(index, bias, ids, valid):
    return pl.pallas_call(
        gather_first_kernel,
        out_shape=(
            shape((90 * 16, 128), F32),
            shape((168, 128), I32),
            shape((168, 128), I32),
            shape((160, 512), BF),
            shape((4, 144), F32),
        ),
        scratch_shapes=[pltpu.VMEM((160, 256), F32)],
        compiler_params=VM,
        cost_estimate=cost(6),
        name="gather_first",
    )(index, jnp.asarray(window_order(), BF), bias, ids, valid)


def gather_second_kernel(first_stage, lo_ref, hi_ref, terms_ref, after_ref, main_ref, tail_ref, stage):
    look_up(terms_ref[...], lo_ref, hi_ref, stage, 90, 4)
    for r in range(12):
        main_ref[r, 0:90, :] = first_stage[pl.ds(r, 90, stride=16), :]
        main_ref[r, 90:144, :] = stage[pl.ds(r, 54, stride=16), :]
        packed = stage[pl.ds(54 * 16 + r, 18, stride=16), :]
        for s in range(8):
            tail_ref[r, pl.ds(s, 18, stride=8), :] = pltpu.roll(packed, 128 - 16 * s, 1) if s else packed


def gather_second(first_stage, lo, hi, terms, after):
    return pl.pallas_call(
        gather_second_kernel,
        out_shape=(shape((12, 144, 128), F32), shape((12, 144, 128), F32)),
        in_specs=[VMEM] * 4 + [ANY],
        scratch_shapes=[pltpu.VMEM((72 * 16, 128), F32)],
        compiler_params=VM,
        cost_estimate=cost(4),
        name="gather_second",
    )(first_stage, lo, hi, terms, after)


def forward_kernel(x0, x1, x2, x3, order_ref, gain_ref, qkv_ref, main_ref, tail_ref, code_ref,
                   low_ref, q_ref, k_ref, v_ref, prob_ref, att_ref, scratch):
    to_windows((x0, x1, x2, x3), order_ref[...], scratch)
    normed, _ = layer_stats(scratch[...])
    low = (normed * gain_ref[...]).astype(BF)
    low_ref[...] = low
    for j, out in enumerate((q_ref, k_ref, v_ref)):
        out[...] = dot_nn(low, qkv_ref[j]).astype(BF)
    eye = lax.broadcasted_iota(I32, (144, 144), 0) == lax.broadcasted_iota(I32, (144, 144), 1)

    def window(w, _):
        rows = pl.ds(pl.multiple_of(w * 144, 16), 144)
        code = code_ref[pl.ds(w, 1), :].astype(I32)
        label = code >> 1
        column = jnp.sum(jnp.where(eye, label, 0), axis=1, keepdims=True)
        allowed = eye | ((column == label) & ((code & 1) > 0))
        query, key, value = q_ref[rows, :], k_ref[rows, :], v_ref[rows, :]
        heads = []
        for h in range(3):
            cols = slice(h * HD, h * HD + HD)
            bias = jnp.concatenate([main_ref[w * 3 + h], tail_ref[w * 3 + h][:, 0:16]], axis=1)
            scores = dot_nt(query[:, cols], key[:, cols]) * (HD ** -0.5) + bias
            scores = jnp.where(allowed, scores, EXCLUDED)
            expo = jnp.exp(scores - jnp.max(scores, axis=-1, keepdims=True))
            prob = expo * (1.0 / jnp.sum(expo, axis=-1, keepdims=True))
            prob_ref[w * 3 + h] = prob
            heads.append(dot_nn(prob.astype(BF), value[:, cols]))
        att_ref[rows, :] = jnp.concatenate(heads, axis=1).astype(BF)
        return 0

    lax.fori_loop(0, 4, window, 0, unroll=True)


def forward(x, gain, qkv, main, tail, code):
    return pl.pallas_call(
        forward_kernel,
        out_shape=(
            shape((576, 192), BF),
            shape((576, 96), BF),
            shape((576, 96), BF),
            shape((576, 96), BF),
            shape((12, 144, 144), F32),
            shape((576, 96), BF),
        ),
        scratch_shapes=[pltpu.VMEM((576, 192), F32)],
        compiler_params=VM,
        cost_estimate=cost(5),
        name="forward",
    )(*x, level_order(), gain, qkv, main, tail, code)


def backward_kernel(g0, g1, g2, g3, order_ref, proj_ref, qkv_ref, q_ref, k_ref, v_ref, prob_ref,
                    part_ref, score_ref, gcols, grad_ref, scratch, gatt):
    to_windows((g0, g1, g2, g3), order_ref[...], scratch)
    grad = scratch[...].astype(BF)
    grad_ref[...] = grad
    gatt[...] = dot_nt(grad, proj_ref[...]).astype(BF)

    def window(w, _):
        rows = pl.ds(pl.multiple_of(w * 144, 16), 144)
        query, key, value, above = q_ref[rows, :], k_ref[rows, :], v_ref[rows, :], gatt[rows, :]
        queries, keys, values = [], [], []
        for h in range(3):
            cols = slice(h * HD, h * HD + HD)
            prob = prob_ref[w * 3 + h]
            values.append(dot_tn(prob.astype(BF), above[:, cols]))
            grad_prob = dot_nt(above[:, cols], value[:, cols])
            score = prob * (grad_prob - jnp.sum(grad_prob * prob, axis=-1, keepdims=True))
            score_ref[w * 3 + h] = score
            low_score = (score * (HD ** -0.5)).astype(BF)
            queries.append(dot_nn(low_score, key[:, cols]))
            keys.append(dot_tn(low_score, query[:, cols]))
        gcols[0, rows, :] = jnp.concatenate(queries, axis=1).astype(BF)
        gcols[1, rows, :] = jnp.concatenate(keys, axis=1).astype(BF)
        gcols[2, rows, :] = jnp.concatenate(values, axis=1).astype(BF)
        return 0

    lax.fori_loop(0, 4, window, 0, unroll=True)
    total = None
    for j in range(3):
        term = dot_nt(gcols[j], qkv_ref[j])
        total = term if total is None else total + term
    scratch[...] = total
    for s in range(4):
        pieces = [scratch[w * 144 + s * 36 : w * 144 + s * 36 + 36, :] for w in range(4)]
        piece = jnp.concatenate(pieces, axis=0).astype(BF)
        part_ref[s * 144 : s * 144 + 144, :] = dot_tn(order_ref[...], piece).astype(BF)


def backward(g, proj, qkv, q, k, v, prob):
    return pl.pallas_call(
        backward_kernel,
        out_shape=(
            shape((576, 192), BF),
            shape((12, 144, 144), F32),
            shape((3, 576, 96), BF),
            shape((576, 192), BF),
        ),
        scratch_shapes=[pltpu.VMEM((576, 192), F32), pltpu.VMEM((576, 96), BF)],
        compiler_params=VM,
        cost_estimate=cost(7),
        name="backward",
    )(*g, level_order(), proj, qkv, q, k, v, prob)


def scatter_kernel(score_ref, lo_ref, hi_ref, low_ref, gcols, att_ref, grad_ref, out_ref, grads_ref, tails):
    out_ref[...] = jnp.zeros((192, 256), F32)
    place = lax.broadcasted_iota(I32, (16, 128), 0)
    for r in range(12):
        tails[r] = pack_tail(score_ref[r, :, 128:144].astype(BF))
    for i in range(9):
        left, right = [], []
        for j in range(18):
            row = slice(i * 18 + j, i * 18 + j + 1)
            here = place == hi_ref[row, :]
            right.append(one_hot(lo_ref[row, :]))
            lines = [score_ref[r, row, 0:128] if i < 8 else tails[r, j : j + 1, :] for r in range(12)]
            left.append(jnp.concatenate([jnp.where(here, line, 0.0).astype(BF) for line in lines], axis=0))
        out_ref[...] += dot_nt(jnp.concatenate(left, axis=1), jnp.concatenate(right, axis=1))
    gproj = dot_tn(att_ref[...], grad_ref[...]).astype(BF)
    grads_ref[0:96, :] = gproj[:, 0:128]
    grads_ref[96:144, :] = jnp.concatenate([gproj[0:48, 128:192], gproj[48:96, 128:192]], axis=1)
    low = low_ref[...]
    a, b, c = [dot_tn(low, gcols[j]).astype(BF) for j in range(3)]
    grads_ref[144:336, :] = jnp.concatenate([a, c[:, 0:32]], axis=1)
    grads_ref[336:528, :] = jnp.concatenate([b, c[:, 32:64]], axis=1)
    grads_ref[528:576, :] = jnp.concatenate([c[i * 48 : i * 48 + 48, 64:96] for i in range(4)], axis=1)


def scatter(score, lo, hi, low, gcols, att, grad):
    return pl.pallas_call(
        scatter_kernel,
        out_shape=(shape((192, 256), F32), shape((576, 128), BF)),
        scratch_shapes=[pltpu.VMEM((12, 24, 128), F32)],
        compiler_params=VM,
        cost_estimate=cost(5),
        name="scatter",
    )(score, lo, hi, low, gcols, att, grad)


def meet_kernel(place_ref, own_ref, other_ref, x0, x1, x2, x3, first_ref, second_ref, table_ref, two_ref, out_ref):
    gain = jnp.zeros((1, 192), F32)
    for s, x in enumerate((x0, x1, x2, x3)):
        rows = slice(s * 144, s * 144 + 144)
        grad = own_ref[rows, :].astype(F32) + other_ref[rows, :].astype(F32)
        normed, _ = layer_stats(x[...].astype(F32))
        gain = gain + jnp.sum(grad * normed, axis=0, keepdims=True)
    out_ref[0:1152, :] = first_ref[...]
    out_ref[1152:1728, :] = second_ref[...]
    rows = []
    for r in range(12):
        pair = table_ref[r * 16 : r * 16 + 13, :]
        rows += [pair[:, 0:128], pair[:, 128:256]]
    none = jnp.zeros((1, 64), F32)
    for line in (gain, two_ref[...]):
        rows += [line[:, 0:128], jnp.concatenate([line[:, 128:192], none], axis=1)]
    rows += [jnp.zeros((4, 128), F32)]
    out_ref[1728:2048, :] = jnp.concatenate(rows, axis=0).astype(BF)


def meet(place, own, other, x, first, second, table, two):
    return pl.pallas_call(
        meet_kernel,
        out_shape=shape((2048, 128), BF),
        in_specs=[SMEM] + [VMEM] * 10,
        compiler_params=VM,
        cost_estimate=cost(1),
        name="meet",
    )(place, own, other, *x, first, second, table, two)


def finish_kernel(x0, x1, x2, x3, m0, m1, m2, m3, g0, g1, g2, g3, gain_ref, out_ref, token_ref):
    token_ref[...] = jnp.zeros((8, 128), F32)
    for q, (x, m, g) in enumerate(zip((x0, x1, x2, x3), (m0, m1, m2, m3), (g0, g1, g2, g3))):
        normed, inverse = layer_stats(x[...].astype(F32))
        rows = m[...].astype(F32) + norm_backward(g[0:144, :].astype(F32), gain_ref[...], normed, inverse)
        for lat in range(3):
            piece = rows[lat * 48 : lat * 48 + 48].reshape(6, 8, 192)
            out_ref[(q // 2) * 3 + lat, (q % 2) * 6 : (q % 2) * 6 + 6] = piece.astype(BF)


def finish(x, m, g, gain):
    return pl.pallas_call(
        finish_kernel,
        out_shape=(shape((6, 12, 8, 192), BF), shape((8, 128), F32)),
        compiler_params=VM,
        cost_estimate=cost(1),
        name="finish",
    )(*x, *m, *g, gain)


def add_kernel(got_ref, own_ref, other_ref, out_ref, g0, g1, g2, g3):
    total = got_ref[0].astype(F32)
    for i in range(1, 32):
        total = total + got_ref[i].astype(F32)
    out_ref[...] = total.astype(BF)
    for s, out in enumerate((g0, g1, g2, g3)):
        rows = slice(s * 144, s * 144 + 144)
        out[0:144, :] = (own_ref[rows, :].astype(F32) + other_ref[rows, :].astype(F32)).astype(BF)
    g2[144:208, :] = jnp.concatenate([total, jnp.zeros((64, 64), F32)], axis=1).astype(BF)


def add(got, own, other):
    quarter = shape((144, 192), BF)
    return pl.pallas_call(
        add_kernel,
        out_shape=(shape((64, 128), BF), quarter, quarter, shape((208, 192), BF), quarter),
        compiler_params=VM,
        cost_estimate=cost(1),
        name="add",
    )(got, own, other)


def spread_kernel(place_ref, own_ref, a_ref, b_ref, c_ref, after_ref, out_ref):
    own = own_ref[...].astype(F32)
    total = own + a_ref[144:208, 0:128].astype(F32) + b_ref[...].astype(F32) + c_ref[...].astype(F32)
    row = place_ref[0] * 64 + lax.broadcasted_iota(I32, (64, 128), 0)
    table = (row >= 1728) & (row < 2040)
    out_ref[...] = jnp.broadcast_to(jnp.where(table, own, total).astype(BF)[None], (32, 64, 128))


def spread(place, own, a, b, c, after):
    return pl.pallas_call(
        spread_kernel,
        out_shape=shape((32, 64, 128), BF),
        in_specs=[SMEM] + [VMEM] * 4 + [ANY],
        compiler_params=VM,
        cost_estimate=cost(1),
        name="spread",
    )(place, own, a, b, c, after)


def unpack_kernel(weight_scale, table_scale, place_ref, in_ref,
                  qkv_ref, proj_ref, upg_ref, down_ref, one_ref, two_ref, table_ref):
    def rows(start, stop):
        return in_ref[start:stop, :].astype(F32) * weight_scale

    for j in range(3):
        upg_ref[:, j * 128 : j * 128 + 128] = rows(j * 192, j * 192 + 192)
        down_ref[:, j * 128 : j * 128 + 128] = rows(576 + j * 192, 768 + j * 192)
    proj_ref[:, 0:128] = rows(1152, 1248)
    tail = rows(1248, 1296)
    proj_ref[0:48, 128:192] = tail[:, 0:64]
    proj_ref[48:96, 128:192] = tail[:, 64:128]
    first, second, third = rows(1296, 1488), rows(1488, 1680), rows(1680, 1728)
    qkv_ref[0] = first[:, 0:96]
    qkv_ref[1] = second[:, 0:96]
    qkv_ref[2, :, 0:32] = first[:, 96:128]
    qkv_ref[2, :, 32:64] = second[:, 96:128]
    for i in range(4):
        qkv_ref[2, i * 48 : i * 48 + 48, 64:96] = third[:, i * 32 : i * 32 + 32]
    table = in_ref[1728:2048, :].astype(F32)
    for r in range(12):
        for half in range(2):
            piece = table[r * 26 + half * 13 : r * 26 + half * 13 + 13] * table_scale
            for a in range(13):
                start = a * 256 + half * 128
                wide = min(128, 3312 - start)
                table_ref[r % 3, r // 3 : r // 3 + 1, start : start + wide] = piece[a : a + 1, 0:wide]
    for start, out in ((312, one_ref), (314, two_ref)):
        line = table[start : start + 1]
        upper = jnp.concatenate([line[:, 96:128], table[start + 1 : start + 2, 0:64]], axis=1)
        out[...] = jnp.where(place_ref[1] == 0, line[:, 0:96], upper) * weight_scale


def unpack(weight_scale, table_scale, place, got):
    return pl.pallas_call(
        functools.partial(unpack_kernel, weight_scale, table_scale),
        out_shape=(
            shape((3, 192, 96), F32),
            shape((96, 192), F32),
            shape((192, 384), F32),
            shape((192, 384), F32),
            shape((1, 96), F32),
            shape((1, 96), F32),
            shape((3, 4, 3312), F32),
        ),
        in_specs=[SMEM, VMEM],
        compiler_params=VM,
        name="unpack",
    )(place, got)


def moved(value, band, sector, half):
    sizes = [lax.axis_size(name) for name in ("lat", "lon", "tp")]
    pairs = []
    for a in range(sizes[0]):
        for b in range(sizes[1]):
            for c in range(sizes[2]):
                source = ((a + band) % sizes[0], (b + sector) % sizes[1], (c + half) % sizes[2])
                pairs.append(tuple((x * sizes[1] + y) * sizes[2] + z for x, y, z in (source, (a, b, c))))
    return lax.ppermute(value, ("lat", "lon", "tp"), pairs)


def shifted_parts(quarters):
    return (
        quarters[3],
        moved(quarters[2], 0, 1, 0),
        moved(quarters[1], 1, 0, 0),
        moved(quarters[0], 1, 1, 0),
    )


def local(
    inputs,
    residual_mid,
    grad_out,
    mask_ids,
    key_valid,
    bias_index,
    pos_bias,
    norm1_gain,
    qkv_weight,
    proj_weight,
    norm2_gain,
    fc1_weight,
    fc2_weight,
):
    levels, lat_cells, lon_cells, channels = inputs.shape
    cell_count = levels * lat_cells * lon_cells
    weight_scale = (cell_count * lax.axis_size("lat") * lax.axis_size("lon")) ** (-0.5)
    table_scale = (lon_cells * lax.axis_size("lon") // 12) ** (-0.5)
    gain1, gain2 = norm1_gain.reshape(1, -1), norm2_gain.reshape(1, -1)

    def turned(field):
        return field.transpose(1, 2, 0, 3)

    x_in, mid_in, up_in = turned(inputs), turned(residual_mid), turned(grad_out)
    *x, part2, first = head(x_in, mid_in, up_in, gain2, fc1_weight, fc2_weight.T)
    other2 = moved(part2, 0, 0, 1)
    xw = shifted_parts(x)
    stage, lo, hi, terms, code = gather_first(
        bias_index, pos_bias[0].transpose(1, 0, 2), mask_ids.transpose(1, 0, 2), key_valid.transpose(1, 0, 2)
    )
    *gm, gain_two = middle(mid_in, up_in, part2, other2, gain2, lo)
    gw = shifted_parts(gm)
    main, tail = gather_second(stage, lo, hi, terms, gain_two)
    low, q, k, v, prob, att = forward(xw, gain1, qkv_weight, main, tail, code)
    part1, score, gcols, grad = backward(gw, proj_weight, qkv_weight, q, k, v, prob)
    other1 = moved(part1, 0, 0, 1)
    table, second = scatter(score, lo, hi, low, gcols, att, grad)
    place = jnp.stack([lax.axis_index("lon"), lax.axis_index("tp")])
    sums = meet(place, part1, other1, xw, first, second, table, gain_two)
    own, g0, g1, g2, g3 = add(lax.all_to_all(sums.reshape(32, 64, 128), "lon", 0, 0), part1, other1)
    next_band = moved(g2, -1, 0, 0)
    back = (moved(g3, -1, -1, 0), next_band, moved(g1, 0, -1, 0), g0)
    result, token = finish(x, gm, back, gain1)
    totals = spread(place, own, next_band, moved(own, -2, 0, 0), moved(own, -3, 0, 0), token)
    got = lax.all_to_all(totals, "lon", 0, 0)
    qkv_out, proj_out, up_out, down_out, one, two, table_out = unpack(
        weight_scale, table_scale, place, got.reshape(2048, 128)
    )
    return (
        result.transpose(2, 0, 1, 3),
        qkv_out,
        proj_out,
        up_out,
        down_out.T,
        one.reshape(channels // lax.axis_size("tp")),
        two.reshape(channels // lax.axis_size("tp")),
        table_out.transpose(1, 0, 2)[None],
    )


def solution(mesh):
    return jax.shard_map(
        local,
        mesh=mesh,
        in_specs=(
            P(None, "lat", "lon", None),
            P(None, "lat", "lon", None),
            P(None, "lat", "lon", None),
            P(None, "lat", "lon"),
            P(None, "lat", "lon"),
            P(),
            P("lat", None, "tp", None),
            P(),
            P(None, None, "tp"),
            P("tp", None),
            P(),
            P(None, "tp"),
            P("tp", None),
        ),
        out_specs=(
            P(None, "lat", "lon", None),
            P(None, None, "tp"),
            P("tp", None),
            P(None, "tp"),
            P("tp", None),
            P("tp"),
            P("tp"),
            P("lat", None, "tp", None),
        ),
        check_vma=False,
    )
```

```python
import functools

import jax
import jax.numpy as jnp
import numpy as np
from jax import lax
from jax.experimental import pallas as pl
from jax.experimental.pallas import tpu as pltpu
from jax.sharding import PartitionSpec as P

HD = 32
EPSILON = 1e-05
EXCLUDED = -1e30
BF = jnp.bfloat16
F32 = jnp.float32
I32 = jnp.int32
VMEM = pl.BlockSpec(memory_space=pltpu.VMEM)
VM = pltpu.CompilerParams(vmem_limit_bytes=24 * 1024 * 1024)
ALL = pltpu.CompilerParams(vmem_limit_bytes=63 * 1024 * 1024)
SMEM = pl.BlockSpec(memory_space=pltpu.SMEM)
ANY = pl.BlockSpec(memory_space=pl.ANY)


def cost(microseconds):
    return pl.CostEstimate(flops=int(microseconds * 1e9), bytes_accessed=0, transcendentals=0)


def shape(dims, kind):
    return jax.ShapeDtypeStruct(dims, kind)


def both(own, other):
    return (own.astype(F32) + other.astype(F32)).astype(BF)


def dot_nn(a, b):
    return lax.dot_general(a, b, (((1,), (0,)), ((), ())), preferred_element_type=F32)


def dot_nt(a, b):
    return lax.dot_general(a, b, (((1,), (1,)), ((), ())), preferred_element_type=F32)


def dot_tn(a, b):
    return lax.dot_general(a, b, (((0,), (0,)), ((), ())), preferred_element_type=F32)


def layer_stats(rows):
    mean = jnp.mean(rows, axis=-1, keepdims=True)
    centred = rows - mean
    inverse = lax.rsqrt(jnp.mean(centred * centred, axis=-1, keepdims=True) + EPSILON)
    return centred * inverse, inverse


def norm_backward(grad_normed, gain, normed, inverse):
    scaled = grad_normed * gain
    first = jnp.mean(scaled, axis=-1, keepdims=True)
    second = jnp.mean(scaled * normed, axis=-1, keepdims=True)
    return (scaled - first - normed * second) * inverse


def gelu_pair(pre):
    cdf = 0.5 * (1.0 + lax.erf(pre * 0.7071067811865476))
    pdf = 0.3989422804014327 * jnp.exp(-0.5 * pre * pre)
    return pre * cdf, cdf + pre * pdf


def to_quarters(field_ref, scratch):
    for lat in range(6):
        for half in range(2):
            rows = field_ref[lat, half * 6 : half * 6 + 6].astype(F32).reshape(48, 192)
            start = ((lat // 3) * 2 + half) * 144 + (lat % 3) * 48
            scratch[start : start + 48, :] = rows


def level_order():
    order = np.zeros((144, 144), np.float32)
    for w in range(4):
        for cell in range(18):
            for level in range(2):
                order[w * 36 + cell * 2 + level, cell * 8 + (2 * w + 1 + level) % 8] = 1.0
    return jnp.asarray(order, BF)


def window_parts(own, band, sector):
    return (own[...], sector[0:144, :], band[0:144, :], sector[144:288, :])


def to_windows(parts, order, scratch):
    for s in range(4):
        rows = dot_nn(order, parts[s])
        for w in range(4):
            scratch[w * 144 + s * 36 : w * 144 + s * 36 + 36, :] = rows[w * 36 : w * 36 + 36]


def head_kernel(place_ref, x_hbm, mid_hbm, up_hbm, gain_hbm, fc1_hbm, fc2_hbm, o10, o2, o3, part_hbm, keep_hbm, send_hbm,
                x_ref, mid_ref, up_ref, gain_ref, fc1_ref, fc2_ref, xq_ref, part_ref, grads_ref, x_s, mid_s, up_s, sem):
    pairs = (
        (mid_hbm, mid_ref),
        (gain_hbm, gain_ref),
        (fc1_hbm, fc1_ref),
        (up_hbm, up_ref),
        (fc2_hbm, fc2_ref),
        (x_hbm, x_ref),
    )
    copies = [pltpu.make_async_copy(a, b, sem.at[i]) for i, (a, b) in enumerate(pairs)]
    for copy in copies:
        copy.start()
    for copy in copies[:3]:
        copy.wait()
    to_quarters(mid_ref, mid_s)
    normed, _ = layer_stats(mid_s[...])
    lowered = (normed * gain_ref[...]).astype(BF)
    pre = dot_nn(lowered, fc1_ref[...])
    active, slopes = gelu_pair(pre)
    for copy in copies[3:]:
        copy.wait()
    to_quarters(x_ref, x_s)
    for place, q in enumerate((1, 0, 2, 3)):
        xq_ref[place * 144 : place * 144 + 144, :] = x_s[q * 144 : q * 144 + 144, :].astype(BF)
    writes = []
    for i, (start, size, out) in enumerate(((0, 288, o10), (288, 144, o2), (432, 144, o3))):
        writes.append(pltpu.make_async_copy(xq_ref.at[pl.ds(start, size)], out, sem.at[9 + i]))
        writes[-1].start()
    to_quarters(up_ref, up_s)
    up = up_s[...].astype(BF)
    grad_pre = (dot_nn(up, fc2_ref[...]) * slopes).astype(BF)
    part_ref[...] = dot_nt(grad_pre, fc1_ref[...]).astype(BF)
    writes.append(pltpu.make_async_copy(part_ref, part_hbm, sem.at[6]))
    writes[-1].start()
    for start, grads in ((0, dot_tn(lowered, grad_pre)), (576, dot_tn(up, active.astype(BF)))):
        for j in range(3):
            grads_ref[start + j * 192 : start + j * 192 + 192, :] = grads[:, j * 128 : j * 128 + 128].astype(BF)
    core = place_ref[2]
    for i, (half, out) in enumerate(((core, keep_hbm), (1 - core, send_hbm))):
        piece = grads_ref.at[pl.ds(pl.multiple_of(half * 576, 16), 576)]
        writes.append(pltpu.make_async_copy(piece, out, sem.at[7 + i]))
        writes[-1].start()
    for write in writes:
        write.wait()


def head(place, x, mid, up, gain, fc1, fc2):
    return pl.pallas_call(
        head_kernel,
        out_shape=(
            shape((288, 192), BF),
            shape((144, 192), BF),
            shape((144, 192), BF),
            shape((576, 192), BF),
            shape((576, 128), BF),
            shape((576, 128), BF),
        ),
        in_specs=[SMEM] + [ANY] * 6,
        out_specs=tuple(ANY for _ in range(6)),
        scratch_shapes=[
            pltpu.VMEM((6, 12, 8, 192), BF),
            pltpu.VMEM((6, 12, 8, 192), BF),
            pltpu.VMEM((6, 12, 8, 192), BF),
            pltpu.VMEM((1, 192), F32),
            pltpu.VMEM((192, 384), BF),
            pltpu.VMEM((192, 384), BF),
            pltpu.VMEM((576, 192), BF),
            pltpu.VMEM((576, 192), BF),
            pltpu.VMEM((1152, 128), BF),
            pltpu.VMEM((576, 192), F32),
            pltpu.VMEM((576, 192), F32),
            pltpu.VMEM((576, 192), F32),
            pltpu.SemaphoreType.DMA((12,)),
        ],
        compiler_params=ALL,
        cost_estimate=cost(3),
        name="head",
    )(place, x, mid, up, gain, fc1, fc2)


def middle_kernel(mid_ref, up_ref, own_ref, other_ref, gain_ref, x2_ref, band_ref, after_ref,
                  o10, o2, o3, x_out, gain_out, mid_s, up_s):
    to_quarters(mid_ref, mid_s)
    to_quarters(up_ref, up_s)
    normed, inverse = layer_stats(mid_s[...])
    grad = own_ref[...].astype(F32) + other_ref[...].astype(F32)
    gain_out[...] = jnp.sum(grad * normed, axis=0, keepdims=True)
    out = (up_s[...] + norm_backward(grad, gain_ref[...], normed, inverse)).astype(BF)
    o10[0:144, :] = out[144:288]
    o10[144:288, :] = out[0:144]
    o2[...] = out[288:432]
    o3[...] = out[432:576]
    x_out[0:144, :] = x2_ref[...]
    x_out[144:288, :] = band_ref[144:288, :]


def middle(mid, up, own, other, gain, x2, band, after):
    return pl.pallas_call(
        middle_kernel,
        out_shape=(
            shape((288, 192), BF),
            shape((144, 192), BF),
            shape((144, 192), BF),
            shape((288, 192), BF),
            shape((1, 192), F32),
        ),
        in_specs=[VMEM] * 7 + [ANY],
        scratch_shapes=[pltpu.VMEM((576, 192), F32)] * 2,
        compiler_params=VM,
        cost_estimate=cost(1),
        name="middle",
    )(mid, up, own, other, gain, x2, band, after)


def join_kernel(first_ref, band_ref, out_ref):
    out_ref[0:144, :] = first_ref[...]
    out_ref[144:288, :] = band_ref[144:288, :]


def join(first, band):
    return pl.pallas_call(
        join_kernel, out_shape=shape((288, 192), BF), compiler_params=VM, cost_estimate=cost(0.1), name="join"
    )(first, band)


def window_order():
    canon = np.arange(144).reshape(2, 2, 3, 2, 6).transpose(1, 3, 2, 4, 0).reshape(-1)
    order = np.zeros((144, 144), np.float32)
    order[np.arange(144), canon] = 1.0
    return order


def pack_tail(tail):
    spread = (lax.broadcasted_iota(I32, (16, 128), 1) & 15) == lax.broadcasted_iota(I32, (16, 128), 0)
    wide = dot_nn(tail, spread.astype(F32).astype(BF))
    here = (lax.broadcasted_iota(I32, (144, 128), 1) >> 4) == (lax.broadcasted_iota(I32, (144, 128), 0) & 7)
    wide = jnp.where(here, wide, 0.0).astype(BF)
    rows = (lax.broadcasted_iota(I32, (24, 144), 1) >> 3) == lax.broadcasted_iota(I32, (24, 144), 0)
    return dot_nn(rows.astype(F32).astype(BF), wide)


def one_hot(low):
    rows = lax.broadcasted_iota(I32, (256, 128), 0).astype(F32).astype(BF)
    return jnp.where(rows == low.astype(F32).astype(BF), jnp.ones((), BF), jnp.zeros((), BF))


def look_up(terms, lo_ref, hi_ref, stage, first_block, steps):
    half = (lax.broadcasted_iota(I32, (8, 128), 0) >> 2)

    def step(i, _):
        for pair in range(9):
            base = first_block + i * 18 + pair * 2
            hot = jnp.concatenate([one_hot(lo_ref[pl.ds(base + j, 1), :]) for j in range(2)], axis=1)
            found = dot_nn(terms, jnp.concatenate([hot, hot], axis=0))
            for j in range(2):
                cols = slice(j * 128, j * 128 + 128)
                high = hi_ref[pl.ds(base + j, 1), :]
                first = jnp.zeros((8, 128), F32)
                for c in range(13):
                    first = jnp.where(high == c, found[c * 8 : c * 8 + 8, cols], first)
                second = jnp.zeros((8, 128), F32)
                shifted = high - half
                for c in range(7):
                    second = jnp.where(shifted == 2 * c, found[104 + c * 8 : 112 + c * 8, cols], second)
                start = pl.multiple_of((base + j - first_block) * 16, 16)
                stage[pl.ds(start, 8), :] = first
                stage[pl.ds(start + 8, 8), :] = second + pltpu.roll(second, 4, 0)
        return 0

    lax.fori_loop(0, steps, step, 0, unroll=True)


def gather_first_kernel(index_ref, order_ref, bias_ref, ids_ref, valid_ref,
                        stage, lo_ref, hi_ref, terms_ref, code_ref, table):
    index = index_ref[...]
    order = order_ref[...]
    pieces = []
    for part in (index & 127, index >> 7):
        moved = dot_nt(dot_nn(order, part.astype(F32).astype(BF)).astype(BF), order)
        pieces.append((moved[:, 0:128].astype(I32), pack_tail(moved[:, 128:144].astype(BF)).astype(I32)))
    for rows, low, high in ((slice(0, 144), pieces[0][0], pieces[1][0]), (slice(144, 168), pieces[0][1], pieces[1][1])):
        lo_ref[rows, :] = low + (high & 1) * 128
        hi_ref[rows, :] = high >> 1
    table[...] = jnp.zeros((160, 256), F32)
    for r in range(12):
        line = bias_ref[r % 3, r // 3 : r // 3 + 1, :]
        line = line - jnp.max(line, axis=1, keepdims=True)
        for c in range(13):
            wide = min(256, 3312 - c * 256)
            row = c * 8 + r if r < 8 else 104 + (c // 2) * 8 + (c % 2) * 4 + r - 8
            table[row : row + 1, 0:wide] = line[:, c * 256 : c * 256 + wide]
    upper = table[...].astype(BF)
    terms_ref[:, 0:256] = upper
    terms_ref[:, 256:512] = (table[...] - upper.astype(F32)).astype(BF)
    code = (ids_ref[...] * 2 + (valid_ref[...] > 0).astype(I32)).astype(F32).reshape(48, 12).astype(BF)
    row = lax.broadcasted_iota(I32, (24, 48), 0)
    column = lax.broadcasted_iota(I32, (24, 48), 1)
    lines = []
    for level in range(2):
        pick = ((row >> 2) * 8 + (row & 3) * 2 + level) == column
        picked = dot_nn(pick.astype(F32).astype(BF), code)
        lines += [picked[lat * 4 : lat * 4 + 4] for lat in range(6)]
    lines = jnp.concatenate(lines, axis=1)
    code_ref[...] = dot_nt(lines.astype(BF), order)
    look_up(terms_ref[...], lo_ref, hi_ref, stage, 0, 7)


def gather_first(index, bias, ids, valid):
    return pl.pallas_call(
        gather_first_kernel,
        out_shape=(
            shape((126 * 16, 128), F32),
            shape((168, 128), I32),
            shape((168, 128), I32),
            shape((160, 512), BF),
            shape((4, 144), F32),
        ),
        scratch_shapes=[pltpu.VMEM((160, 256), F32)],
        compiler_params=VM,
        cost_estimate=cost(6),
        name="gather_first",
    )(index, jnp.asarray(window_order(), BF), bias, ids, valid)


def gather_second_kernel(first_stage, lo_ref, hi_ref, terms_ref, after_ref, main_ref, tail_ref, stage):
    look_up(terms_ref[...], lo_ref, hi_ref, stage, 126, 2)
    for r in range(12):
        main_ref[r, 0:126, :] = first_stage[pl.ds(r, 126, stride=16), :]
        main_ref[r, 126:144, :] = stage[pl.ds(r, 18, stride=16), :]
        packed = stage[pl.ds(18 * 16 + r, 18, stride=16), :]
        for s in range(8):
            tail_ref[r, pl.ds(s, 18, stride=8), :] = pltpu.roll(packed, 128 - 16 * s, 1) if s else packed


def gather_second(first_stage, lo, hi, terms, after):
    return pl.pallas_call(
        gather_second_kernel,
        out_shape=(shape((12, 144, 128), F32), shape((12, 144, 128), F32)),
        in_specs=[VMEM] * 4 + [ANY],
        scratch_shapes=[pltpu.VMEM((36 * 16, 128), F32)],
        compiler_params=VM,
        cost_estimate=cost(4),
        name="gather_second",
    )(first_stage, lo, hi, terms, after)


def forward_kernel(own_ref, band_ref, sector_ref, order_ref, gain_ref, qkv_ref, main_ref, tail_ref, code_ref,
                   low_ref, q_ref, k_ref, v_ref, prob_ref, att_ref, scratch):
    to_windows(window_parts(own_ref, band_ref, sector_ref), order_ref[...], scratch)
    normed, _ = layer_stats(scratch[...])
    low = (normed * gain_ref[...]).astype(BF)
    low_ref[...] = low
    for j, out in enumerate((q_ref, k_ref, v_ref)):
        out[...] = dot_nn(low, qkv_ref[j]).astype(BF)
    eye = lax.broadcasted_iota(I32, (144, 144), 0) == lax.broadcasted_iota(I32, (144, 144), 1)

    def window(w, _):
        rows = pl.ds(pl.multiple_of(w * 144, 16), 144)
        code = code_ref[pl.ds(w, 1), :].astype(I32)
        label = code >> 1
        column = jnp.sum(jnp.where(eye, label, 0), axis=1, keepdims=True)
        allowed = eye | ((column == label) & ((code & 1) > 0))
        query, key, value = q_ref[rows, :], k_ref[rows, :], v_ref[rows, :]
        heads = []
        for h in range(3):
            cols = slice(h * HD, h * HD + HD)
            bias = jnp.concatenate([main_ref[w * 3 + h], tail_ref[w * 3 + h][:, 0:16]], axis=1)
            scores = dot_nt(query[:, cols], key[:, cols]) * (HD ** -0.5) + bias
            scores = jnp.where(allowed, scores, EXCLUDED)
            expo = jnp.exp(scores - jnp.max(scores, axis=-1, keepdims=True))
            prob = expo * (1.0 / jnp.sum(expo, axis=-1, keepdims=True))
            prob_ref[w * 3 + h] = prob
            heads.append(dot_nn(prob.astype(BF), value[:, cols]))
        att_ref[rows, :] = jnp.concatenate(heads, axis=1).astype(BF)
        return 0

    lax.fori_loop(0, 4, window, 0, unroll=True)


def forward(x, gain, qkv, main, tail, code):
    return pl.pallas_call(
        forward_kernel,
        out_shape=(
            shape((576, 192), BF),
            shape((576, 96), BF),
            shape((576, 96), BF),
            shape((576, 96), BF),
            shape((12, 144, 144), F32),
            shape((576, 96), BF),
        ),
        scratch_shapes=[pltpu.VMEM((576, 192), F32)],
        compiler_params=VM,
        cost_estimate=cost(5),
        name="forward",
    )(*x, level_order(), gain, qkv, main, tail, code)


def backward_kernel(own_ref, band_ref, sector_ref, order_ref, proj_ref, qkv_ref, q_ref, k_ref, v_ref, prob_ref,
                    part_ref, score_ref, gcols, grad_ref, scratch, gatt):
    to_windows(window_parts(own_ref, band_ref, sector_ref), order_ref[...], scratch)
    grad = scratch[...].astype(BF)
    grad_ref[...] = grad
    gatt[...] = dot_nt(grad, proj_ref[...]).astype(BF)

    def window(w, _):
        rows = pl.ds(pl.multiple_of(w * 144, 16), 144)
        query, key, value, above = q_ref[rows, :], k_ref[rows, :], v_ref[rows, :], gatt[rows, :]
        queries, keys, values = [], [], []
        for h in range(3):
            cols = slice(h * HD, h * HD + HD)
            prob = prob_ref[w * 3 + h]
            values.append(dot_tn(prob.astype(BF), above[:, cols]))
            grad_prob = dot_nt(above[:, cols], value[:, cols])
            score = prob * (grad_prob - jnp.sum(grad_prob * prob, axis=-1, keepdims=True))
            score_ref[w * 3 + h] = score
            low_score = (score * (HD ** -0.5)).astype(BF)
            queries.append(dot_nn(low_score, key[:, cols]))
            keys.append(dot_tn(low_score, query[:, cols]))
        gcols[0, rows, :] = jnp.concatenate(queries, axis=1).astype(BF)
        gcols[1, rows, :] = jnp.concatenate(keys, axis=1).astype(BF)
        gcols[2, rows, :] = jnp.concatenate(values, axis=1).astype(BF)
        return 0

    lax.fori_loop(0, 4, window, 0, unroll=True)
    total = None
    for j in range(3):
        term = dot_nt(gcols[j], qkv_ref[j])
        total = term if total is None else total + term
    scratch[...] = total
    for s in range(4):
        pieces = [scratch[w * 144 + s * 36 : w * 144 + s * 36 + 36, :] for w in range(4)]
        piece = jnp.concatenate(pieces, axis=0).astype(BF)
        part_ref[s * 144 : s * 144 + 144, :] = dot_tn(order_ref[...], piece).astype(BF)


def backward(g, proj, qkv, q, k, v, prob):
    return pl.pallas_call(
        backward_kernel,
        out_shape=(
            shape((576, 192), BF),
            shape((12, 144, 144), F32),
            shape((3, 576, 96), BF),
            shape((576, 192), BF),
        ),
        scratch_shapes=[pltpu.VMEM((576, 192), F32), pltpu.VMEM((576, 96), BF)],
        compiler_params=VM,
        cost_estimate=cost(7),
        name="backward",
    )(*g, level_order(), proj, qkv, q, k, v, prob)


def scatter_kernel(place_ref, score_ref, lo_ref, hi_ref, low_ref, gcols, att_ref, grad_ref,
                   out_ref, keep_ref, send_ref, grads_ref, tails):
    out_ref[...] = jnp.zeros((192, 256), F32)
    place = lax.broadcasted_iota(I32, (16, 128), 0)
    for r in range(12):
        tails[r] = pack_tail(score_ref[r, :, 128:144].astype(BF))
    for i in range(9):
        left, right = [], []
        for j in range(18):
            row = slice(i * 18 + j, i * 18 + j + 1)
            here = place == hi_ref[row, :]
            right.append(one_hot(lo_ref[row, :]))
            lines = [score_ref[r, row, 0:128] if i < 8 else tails[r, j : j + 1, :] for r in range(12)]
            left.append(jnp.concatenate([jnp.where(here, line, 0.0).astype(BF) for line in lines], axis=0))
        out_ref[...] += dot_nt(jnp.concatenate(left, axis=1), jnp.concatenate(right, axis=1))
    gproj = dot_tn(att_ref[...], grad_ref[...]).astype(BF)
    grads_ref[0:96, :] = gproj[:, 0:128]
    grads_ref[96:144, :] = jnp.concatenate([gproj[0:48, 128:192], gproj[48:96, 128:192]], axis=1)
    low = low_ref[...]
    a, b, c = [dot_tn(low, gcols[j]).astype(BF) for j in range(3)]
    grads_ref[144:336, :] = jnp.concatenate([a, c[:, 0:32]], axis=1)
    grads_ref[336:528, :] = jnp.concatenate([b, c[:, 32:64]], axis=1)
    grads_ref[528:576, :] = jnp.concatenate([c[i * 48 : i * 48 + 48, 64:96] for i in range(4)], axis=1)
    core = place_ref[2]
    keep_ref[...] = grads_ref[pl.ds(pl.multiple_of(core * 288, 16), 288), :]
    send_ref[...] = grads_ref[pl.ds(pl.multiple_of((1 - core) * 288, 16), 288), :]


def scatter(place, score, lo, hi, low, gcols, att, grad):
    return pl.pallas_call(
        scatter_kernel,
        out_shape=(shape((192, 256), F32), shape((288, 128), BF), shape((288, 128), BF)),
        in_specs=[SMEM] + [VMEM] * 7,
        scratch_shapes=[pltpu.VMEM((576, 128), BF), pltpu.VMEM((12, 24, 128), F32)],
        compiler_params=VM,
        cost_estimate=cost(5),
        name="scatter",
    )(place, score, lo, hi, low, gcols, att, grad)


def meet_kernel(own_ref, other_ref, x_own, x_band, x_sector, first_ref, first_other, second_ref, second_other,
                table_ref, two_ref, out_ref):
    gain = jnp.zeros((1, 192), F32)
    for s, x in enumerate(window_parts(x_own, x_band, x_sector)):
        rows = slice(s * 144, s * 144 + 144)
        grad = own_ref[rows, :].astype(F32) + other_ref[rows, :].astype(F32)
        normed, _ = layer_stats(x.astype(F32))
        gain = gain + jnp.sum(grad * normed, axis=0, keepdims=True)
    out_ref[0:576, :] = both(first_ref[...], first_other[...])
    out_ref[576:864, :] = both(second_ref[...], second_other[...])
    rows = []
    for r in range(12):
        pair = table_ref[r * 16 : r * 16 + 13, :]
        rows += [pair[:, 0:128], pair[:, 128:256]]
    none = jnp.zeros((1, 64), F32)
    for line in (gain, two_ref[...]):
        rows += [line[:, 0:128], jnp.concatenate([line[:, 128:192], none], axis=1)]
    rows += [jnp.zeros((100, 128), F32)]
    out_ref[864:1280, :] = jnp.concatenate(rows, axis=0).astype(BF)


def meet(own, other, x, first, first_other, second, second_other, table, two):
    return pl.pallas_call(
        meet_kernel,
        out_shape=shape((1280, 128), BF),
        compiler_params=VM,
        cost_estimate=cost(1),
        name="meet",
    )(own, other, *x, first, first_other, second, second_other, table, two)


def finish_kernel(x10, x2, x3, m10, m2, m3, g0, g1, g2, g3, gain_ref, out_ref, token_ref):
    token_ref[...] = jnp.zeros((8, 128), F32)
    xs = (x10[144:288, :], x10[0:144, :], x2[...], x3[...])
    ms = (m10[144:288, :], m10[0:144, :], m2[...], m3[...])
    for q, (x, m, g) in enumerate(zip(xs, ms, (g0, g1, g2, g3))):
        normed, inverse = layer_stats(x.astype(F32))
        rows = m.astype(F32) + norm_backward(g[...].astype(F32), gain_ref[...], normed, inverse)
        for lat in range(3):
            piece = rows[lat * 48 : lat * 48 + 48].reshape(6, 8, 192)
            out_ref[(q // 2) * 3 + lat, (q % 2) * 6 : (q % 2) * 6 + 6] = piece.astype(BF)


def finish(x, m, g, gain):
    return pl.pallas_call(
        finish_kernel,
        out_shape=(shape((6, 12, 8, 192), BF), shape((8, 128), F32)),
        compiler_params=VM,
        cost_estimate=cost(1),
        name="finish",
    )(*x, *m, *g, gain)


def add_kernel(got_ref, own_ref, other_ref, out_ref, g0, g1, g2, g3):
    total = got_ref[0].astype(F32)
    for i in range(1, 32):
        total = total + got_ref[i].astype(F32)
    out_ref[...] = total.astype(BF)
    for s, out in enumerate((g0, g1, g2, g3)):
        rows = slice(s * 144, s * 144 + 144)
        out[...] = both(own_ref[rows, :], other_ref[rows, :])


def add(got, own, other):
    return pl.pallas_call(
        add_kernel,
        out_shape=(shape((40, 128), BF),) + tuple(shape((144, 192), BF) for _ in range(4)),
        compiler_params=VM,
        cost_estimate=cost(1),
        name="add",
    )(got, own, other)


def spread_kernel(place_ref, own_ref, other_ref, after_ref, out_ref):
    own = own_ref[...].astype(F32)
    row = place_ref[0] * 40 + lax.broadcasted_iota(I32, (40, 128), 0)
    table = (row >= 864) & (row < 1176)
    total = own + jnp.where(table, 0.0, other_ref[...].astype(F32))
    out_ref[...] = jnp.broadcast_to(total.astype(BF)[None], (32, 40, 128))


def spread(place, own, other, after):
    return pl.pallas_call(
        spread_kernel,
        out_shape=shape((32, 40, 128), BF),
        in_specs=[SMEM] + [VMEM] * 2 + [ANY],
        compiler_params=VM,
        cost_estimate=cost(1),
        name="spread",
    )(place, own, other, after)


def unpack_kernel(weight_scale, table_scale, place_ref, own_ref, other_ref,
                  qkv_ref, proj_ref, upg_ref, down_ref, one_ref, two_ref, table_ref):
    swap = place_ref[2] == 1
    own, other = own_ref[0:864, :].astype(F32) * weight_scale, other_ref[0:864, :].astype(F32) * weight_scale
    lower, upper = jnp.where(swap, other, own), jnp.where(swap, own, other)
    for j in range(3):
        upg_ref[:, j * 128 : j * 128 + 128] = lower[j * 192 : j * 192 + 192]
        down_ref[:, j * 128 : j * 128 + 128] = upper[j * 192 : j * 192 + 192]
    second = jnp.concatenate([lower[576:864], upper[576:864]], axis=0)
    proj_ref[:, 0:128] = second[0:96]
    proj_ref[0:48, 128:192] = second[96:144, 0:64]
    proj_ref[48:96, 128:192] = second[96:144, 64:128]
    qkv_ref[0] = second[144:336, 0:96]
    qkv_ref[1] = second[336:528, 0:96]
    qkv_ref[2, :, 0:32] = second[144:336, 96:128]
    qkv_ref[2, :, 32:64] = second[336:528, 96:128]
    for i in range(4):
        qkv_ref[2, i * 48 : i * 48 + 48, 64:96] = second[528:576, i * 32 : i * 32 + 32]
    table = own_ref[864:1184, :].astype(F32)
    for r in range(12):
        for half in range(2):
            piece = table[r * 26 + half * 13 : r * 26 + half * 13 + 13] * table_scale
            for a in range(13):
                start = a * 256 + half * 128
                wide = min(128, 3312 - start)
                table_ref[r % 3, r // 3 : r // 3 + 1, start : start + wide] = piece[a : a + 1, 0:wide]
    gains = table[304:320] + other_ref[1168:1184, :].astype(F32)
    for start, out in ((8, one_ref), (10, two_ref)):
        line = gains[start : start + 1]
        later = jnp.concatenate([line[:, 96:128], gains[start + 1 : start + 2, 0:64]], axis=1)
        out[...] = jnp.where(place_ref[1] == 0, line[:, 0:96], later) * weight_scale


def unpack(weight_scale, table_scale, place, got, other):
    return pl.pallas_call(
        functools.partial(unpack_kernel, weight_scale, table_scale),
        out_shape=(
            shape((3, 192, 96), F32),
            shape((96, 192), F32),
            shape((192, 384), F32),
            shape((192, 384), F32),
            shape((1, 96), F32),
            shape((1, 96), F32),
            shape((3, 4, 3312), F32),
        ),
        in_specs=[SMEM, VMEM, VMEM],
        compiler_params=VM,
        name="unpack",
    )(place, got, other)


def moved(value, band, sector, half):
    sizes = [lax.axis_size(name) for name in ("lat", "lon", "tp")]
    pairs = []
    for a in range(sizes[0]):
        for b in range(sizes[1]):
            for c in range(sizes[2]):
                source = ((a + band) % sizes[0], (b + sector) % sizes[1], (c + half) % sizes[2])
                pairs.append(tuple((x * sizes[1] + y) * sizes[2] + z for x, y, z in (source, (a, b, c))))
    return lax.ppermute(value, ("lat", "lon", "tp"), pairs)


def other_core(value):
    return lax.ppermute(value, "lat", [(a, a ^ 1) for a in range(lax.axis_size("lat"))])


def local(
    inputs,
    residual_mid,
    grad_out,
    mask_ids,
    key_valid,
    bias_index,
    pos_bias,
    norm1_gain,
    qkv_weight,
    proj_weight,
    norm2_gain,
    fc1_weight,
    fc2_weight,
):
    levels, lat_cells, lon_cells, channels = inputs.shape
    cell_count = levels * lat_cells * lon_cells
    weight_scale = (cell_count * lax.axis_size("lat") * lax.axis_size("lon")) ** (-0.5)
    table_scale = (lon_cells * lax.axis_size("lon") // 12) ** (-0.5)
    gain1, gain2 = norm1_gain.reshape(1, -1), norm2_gain.reshape(1, -1)

    def turned(field):
        return field.transpose(1, 2, 0, 3)

    x_in, mid_in, up_in = turned(inputs), turned(residual_mid), turned(grad_out)
    place = jnp.stack([lax.axis_index("lon"), lax.axis_index("tp"), lax.axis_index("lat") % 2])
    x10, x2, x3, part2, first, first_send = head(place, x_in, mid_in, up_in, gain2, fc1_weight, fc2_weight.T)
    other2 = moved(part2, 0, 0, 1)
    x_band = moved(x10, 1, 0, 0)
    stage, lo, hi, terms, code = gather_first(
        bias_index, pos_bias[0].transpose(1, 0, 2), mask_ids.transpose(1, 0, 2), key_valid.transpose(1, 0, 2)
    )
    m10, m2, m3, x_next, gain_two = middle(mid_in, up_in, part2, other2, gain2, x2, x_band, lo)
    m_band = moved(m10, 1, 0, 0)
    x_sector = moved(x_next, 0, 1, 0)
    main, tail = gather_second(stage, lo, hi, terms, gain_two)
    m_sector = moved(join(m2, m_band), 0, 1, 0)
    xw = (x3, x_band, x_sector)
    low, q, k, v, prob, att = forward(xw, gain1, qkv_weight, main, tail, code)
    part1, score, gcols, grad = backward((m3, m_band, m_sector), proj_weight, qkv_weight, q, k, v, prob)
    other1 = moved(part1, 0, 0, 1)
    table, second, second_send = scatter(place, score, lo, hi, low, gcols, att, grad)
    sums = meet(
        part1, other1, xw, first, other_core(first_send), second, other_core(second_send), table, gain_two
    )
    own, g0, g1, g2, g3 = add(lax.all_to_all(sums.reshape(32, 40, 128), "lon", 0, 0), part1, other1)
    across = moved(own, 2, 0, 0)
    back = (moved(g3, -1, -1, 0), moved(g2, -1, 0, 0), moved(g1, 0, -1, 0), g0)
    result, token = finish((x10, x2, x3), (m10, m2, m3), back, gain1)
    totals = spread(place, own, across, token)
    got = lax.all_to_all(totals, "lon", 0, 0).reshape(1280, 128)
    qkv_out, proj_out, up_out, down_out, one, two, table_out = unpack(
        weight_scale, table_scale, place, got, other_core(got)
    )
    return (
        result.transpose(2, 0, 1, 3),
        qkv_out,
        proj_out,
        up_out,
        down_out.T,
        one.reshape(channels // lax.axis_size("tp")),
        two.reshape(channels // lax.axis_size("tp")),
        table_out.transpose(1, 0, 2)[None],
    )


def solution(mesh):
    return jax.shard_map(
        local,
        mesh=mesh,
        in_specs=(
            P(None, "lat", "lon", None),
            P(None, "lat", "lon", None),
            P(None, "lat", "lon", None),
            P(None, "lat", "lon"),
            P(None, "lat", "lon"),
            P(),
            P("lat", None, "tp", None),
            P(),
            P(None, None, "tp"),
            P("tp", None),
            P(),
            P(None, "tp"),
            P("tp", None),
        ),
        out_specs=(
            P(None, "lat", "lon", None),
            P(None, None, "tp"),
            P("tp", None),
            P(None, "tp"),
            P("tp", None),
            P("tp"),
            P("tp"),
            P("lat", None, "tp", None),
        ),
        check_vma=False,
    )
```

```python
import functools

import jax
import jax.numpy as jnp
import numpy as np
from jax import lax
from jax.experimental import pallas as pl
from jax.experimental.pallas import tpu as pltpu
from jax.sharding import PartitionSpec as P

HD = 32
EPSILON = 1e-05
EXCLUDED = -1e30
BF = jnp.bfloat16
F32 = jnp.float32
I32 = jnp.int32
VMEM = pl.BlockSpec(memory_space=pltpu.VMEM)
VM = pltpu.CompilerParams(vmem_limit_bytes=24 * 1024 * 1024)
ALL = pltpu.CompilerParams(vmem_limit_bytes=63 * 1024 * 1024)
SMEM = pl.BlockSpec(memory_space=pltpu.SMEM)
ANY = pl.BlockSpec(memory_space=pl.ANY)


def cost(microseconds):
    return pl.CostEstimate(flops=int(microseconds * 1e9), bytes_accessed=0, transcendentals=0)


def shape(dims, kind):
    return jax.ShapeDtypeStruct(dims, kind)


def both(own, other):
    return (own.astype(F32) + other.astype(F32)).astype(BF)


def dot_nn(a, b):
    return lax.dot_general(a, b, (((1,), (0,)), ((), ())), preferred_element_type=F32)


def dot_nt(a, b):
    return lax.dot_general(a, b, (((1,), (1,)), ((), ())), preferred_element_type=F32)


def dot_tn(a, b):
    return lax.dot_general(a, b, (((0,), (0,)), ((), ())), preferred_element_type=F32)


def layer_stats(rows):
    mean = jnp.mean(rows, axis=-1, keepdims=True)
    centred = rows - mean
    inverse = lax.rsqrt(jnp.mean(centred * centred, axis=-1, keepdims=True) + EPSILON)
    return centred * inverse, inverse


def norm_backward(grad_normed, gain, normed, inverse):
    scaled = grad_normed * gain
    first = jnp.mean(scaled, axis=-1, keepdims=True)
    second = jnp.mean(scaled * normed, axis=-1, keepdims=True)
    return (scaled - first - normed * second) * inverse


def gelu_pair(pre):
    cdf = 0.5 * (1.0 + lax.erf(pre * 0.7071067811865476))
    pdf = 0.3989422804014327 * jnp.exp(-0.5 * pre * pre)
    return pre * cdf, cdf + pre * pdf


def to_quarters(field_ref, scratch):
    for lat in range(6):
        for half in range(2):
            rows = field_ref[lat, half * 6 : half * 6 + 6].astype(F32).reshape(48, 192)
            start = ((lat // 3) * 2 + half) * 144 + (lat % 3) * 48
            scratch[start : start + 48, :] = rows


def level_order():
    order = np.zeros((144, 144), np.float32)
    for w in range(4):
        for cell in range(18):
            for level in range(2):
                order[w * 36 + cell * 2 + level, cell * 8 + (2 * w + 1 + level) % 8] = 1.0
    return jnp.asarray(order, BF)


def to_windows(parts, order, scratch):
    for s in range(4):
        rows = dot_nn(order, parts[s][...])
        for w in range(4):
            scratch[w * 144 + s * 36 : w * 144 + s * 36 + 36, :] = rows[w * 36 : w * 36 + 36]


def head_kernel(x_hbm, mid_hbm, up_hbm, gain_hbm, fc1_hbm, fc2_hbm, o0, o1, o2, o3, part_hbm, keep_hbm, send_hbm,
                x_ref, mid_ref, up_ref, gain_ref, fc1_ref, fc2_ref, xq_ref, part_ref, grads_ref, x_s, mid_s, up_s, sem):
    pairs = (
        (mid_hbm, mid_ref),
        (gain_hbm, gain_ref),
        (fc1_hbm, fc1_ref),
        (up_hbm, up_ref),
        (fc2_hbm, fc2_ref),
        (x_hbm, x_ref),
    )
    copies = [pltpu.make_async_copy(a, b, sem.at[i]) for i, (a, b) in enumerate(pairs)]
    for copy in copies:
        copy.start()
    for copy in copies[:3]:
        copy.wait()
    to_quarters(mid_ref, mid_s)
    normed, _ = layer_stats(mid_s[...])
    lowered = (normed * gain_ref[...]).astype(BF)
    pre = dot_nn(lowered, fc1_ref[...])
    active, slopes = gelu_pair(pre)
    for copy in copies[3:]:
        copy.wait()
    to_quarters(x_ref, x_s)
    writes = []
    for q, out in enumerate((o0, o1, o2, o3)):
        xq_ref[q] = x_s[q * 144 : q * 144 + 144, :].astype(BF)
        writes.append(pltpu.make_async_copy(xq_ref.at[q], out, sem.at[8 + q]))
        writes[-1].start()
    to_quarters(up_ref, up_s)
    up = up_s[...].astype(BF)
    grad_pre = (dot_nn(up, fc2_ref[...]) * slopes).astype(BF)
    part_ref[...] = dot_nt(grad_pre, fc1_ref[...]).astype(BF)
    writes.append(pltpu.make_async_copy(part_ref, part_hbm, sem.at[6]))
    writes[-1].start()
    for start, grads in ((0, dot_tn(lowered, grad_pre)), (576, dot_tn(up, active.astype(BF)))):
        for j in range(3):
            grads_ref[start + j * 192 : start + j * 192 + 192, :] = grads[:, j * 128 : j * 128 + 128].astype(BF)
    core = lax.rem(lax.axis_index("lat"), 2)
    for i, (half, out) in enumerate(((core, keep_hbm), (1 - core, send_hbm))):
        piece = grads_ref.at[pl.ds(pl.multiple_of(half * 576, 16), 576)]
        writes.append(pltpu.make_async_copy(piece, out, sem.at[12 + i]))
        writes[-1].start()
    for write in writes:
        write.wait()


def head(x, mid, up, gain, fc1, fc2):
    return pl.pallas_call(
        head_kernel,
        out_shape=tuple(shape((144, 192), BF) for _ in range(4))
        + (shape((576, 192), BF), shape((576, 128), BF), shape((576, 128), BF)),
        in_specs=[ANY] * 6,
        out_specs=tuple(ANY for _ in range(7)),
        scratch_shapes=[
            pltpu.VMEM((6, 12, 8, 192), BF),
            pltpu.VMEM((6, 12, 8, 192), BF),
            pltpu.VMEM((6, 12, 8, 192), BF),
            pltpu.VMEM((1, 192), F32),
            pltpu.VMEM((192, 384), BF),
            pltpu.VMEM((192, 384), BF),
            pltpu.VMEM((4, 144, 192), BF),
            pltpu.VMEM((576, 192), BF),
            pltpu.VMEM((1152, 128), BF),
            pltpu.VMEM((576, 192), F32),
            pltpu.VMEM((576, 192), F32),
            pltpu.VMEM((576, 192), F32),
            pltpu.SemaphoreType.DMA((14,)),
        ],
        compiler_params=ALL,
        cost_estimate=cost(3),
        name="head",
    )(x, mid, up, gain, fc1, fc2)


def middle_kernel(mid_ref, up_ref, own_ref, other_ref, gain_ref, after_ref, o0, o1, o2, o3, gain_out, mid_s, up_s):
    to_quarters(mid_ref, mid_s)
    to_quarters(up_ref, up_s)
    normed, inverse = layer_stats(mid_s[...])
    grad = own_ref[...].astype(F32) + other_ref[...].astype(F32)
    gain_out[...] = jnp.sum(grad * normed, axis=0, keepdims=True)
    out = up_s[...] + norm_backward(grad, gain_ref[...], normed, inverse)
    for q, o in enumerate((o0, o1, o2, o3)):
        o[...] = out[q * 144 : q * 144 + 144].astype(BF)


def middle(mid, up, own, other, gain, after):
    return pl.pallas_call(
        middle_kernel,
        out_shape=tuple(shape((144, 192), BF) for _ in range(4)) + (shape((1, 192), F32),),
        in_specs=[VMEM] * 5 + [ANY],
        scratch_shapes=[pltpu.VMEM((576, 192), F32)] * 2,
        compiler_params=VM,
        cost_estimate=cost(1),
        name="middle",
    )(mid, up, own, other, gain, after)


def window_order():
    canon = np.arange(144).reshape(2, 2, 3, 2, 6).transpose(1, 3, 2, 4, 0).reshape(-1)
    order = np.zeros((144, 144), np.float32)
    order[np.arange(144), canon] = 1.0
    return order


def pack_tail(tail):
    spread = (lax.broadcasted_iota(I32, (16, 128), 1) & 15) == lax.broadcasted_iota(I32, (16, 128), 0)
    wide = dot_nn(tail, spread.astype(F32).astype(BF))
    here = (lax.broadcasted_iota(I32, (144, 128), 1) >> 4) == (lax.broadcasted_iota(I32, (144, 128), 0) & 7)
    wide = jnp.where(here, wide, 0.0).astype(BF)
    rows = (lax.broadcasted_iota(I32, (24, 144), 1) >> 3) == lax.broadcasted_iota(I32, (24, 144), 0)
    return dot_nn(rows.astype(F32).astype(BF), wide)


def one_hot(low):
    rows = lax.broadcasted_iota(I32, (256, 128), 0).astype(F32).astype(BF)
    return jnp.where(rows == low.astype(F32).astype(BF), jnp.ones((), BF), jnp.zeros((), BF))


def look_up(terms, lo_ref, hi_ref, stage, first_block, steps):
    half = (lax.broadcasted_iota(I32, (8, 128), 0) >> 2)

    def step(i, _):
        for pair in range(9):
            base = first_block + i * 18 + pair * 2
            hot = jnp.concatenate([one_hot(lo_ref[pl.ds(base + j, 1), :]) for j in range(2)], axis=1)
            found = dot_nn(terms, jnp.concatenate([hot, hot], axis=0))
            for j in range(2):
                cols = slice(j * 128, j * 128 + 128)
                high = hi_ref[pl.ds(base + j, 1), :]
                first = jnp.zeros((8, 128), F32)
                for c in range(13):
                    first = jnp.where(high == c, found[c * 8 : c * 8 + 8, cols], first)
                second = jnp.zeros((8, 128), F32)
                shifted = high - half
                for c in range(7):
                    second = jnp.where(shifted == 2 * c, found[104 + c * 8 : 112 + c * 8, cols], second)
                start = pl.multiple_of((base + j - first_block) * 16, 16)
                stage[pl.ds(start, 8), :] = first
                stage[pl.ds(start + 8, 8), :] = second + pltpu.roll(second, 4, 0)
        return 0

    lax.fori_loop(0, steps, step, 0, unroll=True)


def gather_first_kernel(index_ref, order_ref, bias_ref, ids_ref, valid_ref,
                        stage, lo_ref, hi_ref, terms_ref, code_ref, table):
    index = index_ref[...]
    order = order_ref[...]
    pieces = []
    for part in (index & 127, index >> 7):
        moved = dot_nt(dot_nn(order, part.astype(F32).astype(BF)).astype(BF), order)
        pieces.append((moved[:, 0:128].astype(I32), pack_tail(moved[:, 128:144].astype(BF)).astype(I32)))
    for rows, low, high in ((slice(0, 144), pieces[0][0], pieces[1][0]), (slice(144, 168), pieces[0][1], pieces[1][1])):
        lo_ref[rows, :] = low + (high & 1) * 128
        hi_ref[rows, :] = high >> 1
    table[...] = jnp.zeros((160, 256), F32)
    for r in range(12):
        line = bias_ref[r % 3, r // 3 : r // 3 + 1, :]
        line = line - jnp.max(line, axis=1, keepdims=True)
        for c in range(13):
            wide = min(256, 3312 - c * 256)
            row = c * 8 + r if r < 8 else 104 + (c // 2) * 8 + (c % 2) * 4 + r - 8
            table[row : row + 1, 0:wide] = line[:, c * 256 : c * 256 + wide]
    upper = table[...].astype(BF)
    terms_ref[:, 0:256] = upper
    terms_ref[:, 256:512] = (table[...] - upper.astype(F32)).astype(BF)
    code = (ids_ref[...] * 2 + (valid_ref[...] > 0).astype(I32)).astype(F32).reshape(48, 12).astype(BF)
    row = lax.broadcasted_iota(I32, (24, 48), 0)
    column = lax.broadcasted_iota(I32, (24, 48), 1)
    lines = []
    for level in range(2):
        pick = ((row >> 2) * 8 + (row & 3) * 2 + level) == column
        picked = dot_nn(pick.astype(F32).astype(BF), code)
        lines += [picked[lat * 4 : lat * 4 + 4] for lat in range(6)]
    lines = jnp.concatenate(lines, axis=1)
    code_ref[...] = dot_nt(lines.astype(BF), order)
    look_up(terms_ref[...], lo_ref, hi_ref, stage, 0, 5)


def gather_first(index, bias, ids, valid):
    return pl.pallas_call(
        gather_first_kernel,
        out_shape=(
            shape((90 * 16, 128), F32),
            shape((168, 128), I32),
            shape((168, 128), I32),
            shape((160, 512), BF),
            shape((4, 144), F32),
        ),
        scratch_shapes=[pltpu.VMEM((160, 256), F32)],
        compiler_params=VM,
        cost_estimate=cost(0.5),
        name="gather_first",
    )(index, jnp.asarray(window_order(), BF), bias, ids, valid)


def gather_second_kernel(first_stage, lo_ref, hi_ref, terms_ref, a0, a1, a2, a3, main_ref, tail_ref, stage):
    look_up(terms_ref[...], lo_ref, hi_ref, stage, 90, 4)
    for r in range(12):
        main_ref[r, 0:90, :] = first_stage[pl.ds(r, 90, stride=16), :]
        main_ref[r, 90:144, :] = stage[pl.ds(r, 54, stride=16), :]
        packed = stage[pl.ds(54 * 16 + r, 18, stride=16), :]
        for s in range(8):
            tail_ref[r, pl.ds(s, 18, stride=8), :] = pltpu.roll(packed, 128 - 16 * s, 1) if s else packed


def gather_second(first_stage, lo, hi, terms, after):
    return pl.pallas_call(
        gather_second_kernel,
        out_shape=(shape((12, 144, 128), F32), shape((12, 144, 128), F32)),
        in_specs=[VMEM] * 4 + [ANY] * 4,
        scratch_shapes=[pltpu.VMEM((72 * 16, 128), F32)],
        compiler_params=VM,
        cost_estimate=cost(4),
        name="gather_second",
    )(first_stage, lo, hi, terms, *after)


def forward_kernel(x0, x1, x2, x3, order_ref, gain_ref, qkv_ref, main_ref, tail_ref, code_ref,
                   low_ref, q_ref, k_ref, v_ref, prob_ref, att_ref, scratch):
    to_windows((x0, x1, x2, x3), order_ref[...], scratch)
    normed, _ = layer_stats(scratch[...])
    low = (normed * gain_ref[...]).astype(BF)
    low_ref[...] = low
    for j, out in enumerate((q_ref, k_ref, v_ref)):
        out[...] = dot_nn(low, qkv_ref[j]).astype(BF)
    eye = lax.broadcasted_iota(I32, (144, 144), 0) == lax.broadcasted_iota(I32, (144, 144), 1)

    def window(w, _):
        rows = pl.ds(pl.multiple_of(w * 144, 16), 144)
        code = code_ref[pl.ds(w, 1), :].astype(I32)
        label = code >> 1
        column = jnp.sum(jnp.where(eye, label, 0), axis=1, keepdims=True)
        allowed = eye | ((column == label) & ((code & 1) > 0))
        query, key, value = q_ref[rows, :], k_ref[rows, :], v_ref[rows, :]
        heads = []
        for h in range(3):
            cols = slice(h * HD, h * HD + HD)
            bias = jnp.concatenate([main_ref[w * 3 + h], tail_ref[w * 3 + h][:, 0:16]], axis=1)
            scores = dot_nt(query[:, cols], key[:, cols]) * (HD ** -0.5) + bias
            scores = jnp.where(allowed, scores, EXCLUDED)
            expo = jnp.exp(scores - jnp.max(scores, axis=-1, keepdims=True))
            prob = expo * (1.0 / jnp.sum(expo, axis=-1, keepdims=True))
            prob_ref[w * 3 + h] = prob
            heads.append(dot_nn(prob.astype(BF), value[:, cols]))
        att_ref[rows, :] = jnp.concatenate(heads, axis=1).astype(BF)
        return 0

    lax.fori_loop(0, 4, window, 0, unroll=True)


def forward(x, gain, qkv, main, tail, code):
    return pl.pallas_call(
        forward_kernel,
        out_shape=(
            shape((576, 192), BF),
            shape((576, 96), BF),
            shape((576, 96), BF),
            shape((576, 96), BF),
            shape((12, 144, 144), F32),
            shape((576, 96), BF),
        ),
        scratch_shapes=[pltpu.VMEM((576, 192), F32)],
        compiler_params=VM,
        cost_estimate=cost(5),
        name="forward",
    )(*x, level_order(), gain, qkv, main, tail, code)


def backward_kernel(g0, g1, g2, g3, order_ref, proj_ref, qkv_ref, q_ref, k_ref, v_ref, prob_ref,
                    part_ref, score_ref, gcols, grad_ref, scratch, gatt):
    to_windows((g0, g1, g2, g3), order_ref[...], scratch)
    grad = scratch[...].astype(BF)
    grad_ref[...] = grad
    gatt[...] = dot_nt(grad, proj_ref[...]).astype(BF)

    def window(w, _):
        rows = pl.ds(pl.multiple_of(w * 144, 16), 144)
        query, key, value, above = q_ref[rows, :], k_ref[rows, :], v_ref[rows, :], gatt[rows, :]
        queries, keys, values = [], [], []
        for h in range(3):
            cols = slice(h * HD, h * HD + HD)
            prob = prob_ref[w * 3 + h]
            values.append(dot_tn(prob.astype(BF), above[:, cols]))
            grad_prob = dot_nt(above[:, cols], value[:, cols])
            score = prob * (grad_prob - jnp.sum(grad_prob * prob, axis=-1, keepdims=True))
            score_ref[w * 3 + h] = score
            low_score = (score * (HD ** -0.5)).astype(BF)
            queries.append(dot_nn(low_score, key[:, cols]))
            keys.append(dot_tn(low_score, query[:, cols]))
        gcols[0, rows, :] = jnp.concatenate(queries, axis=1).astype(BF)
        gcols[1, rows, :] = jnp.concatenate(keys, axis=1).astype(BF)
        gcols[2, rows, :] = jnp.concatenate(values, axis=1).astype(BF)
        return 0

    lax.fori_loop(0, 4, window, 0, unroll=True)
    total = None
    for j in range(3):
        term = dot_nt(gcols[j], qkv_ref[j])
        total = term if total is None else total + term
    scratch[...] = total
    for s in range(4):
        pieces = [scratch[w * 144 + s * 36 : w * 144 + s * 36 + 36, :] for w in range(4)]
        piece = jnp.concatenate(pieces, axis=0).astype(BF)
        part_ref[s * 144 : s * 144 + 144, :] = dot_tn(order_ref[...], piece).astype(BF)


def backward(g, proj, qkv, q, k, v, prob):
    return pl.pallas_call(
        backward_kernel,
        out_shape=(
            shape((576, 192), BF),
            shape((12, 144, 144), F32),
            shape((3, 576, 96), BF),
            shape((576, 192), BF),
        ),
        scratch_shapes=[pltpu.VMEM((576, 192), F32), pltpu.VMEM((576, 96), BF)],
        compiler_params=VM,
        cost_estimate=cost(7),
        name="backward",
    )(*g, level_order(), proj, qkv, q, k, v, prob)


def scatter_kernel(score_ref, lo_ref, hi_ref, low_ref, gcols, att_ref, grad_ref,
                   out_ref, keep_ref, send_ref, grads_ref, tails):
    out_ref[...] = jnp.zeros((192, 256), F32)
    place = lax.broadcasted_iota(I32, (16, 128), 0)
    for r in range(12):
        tails[r] = pack_tail(score_ref[r, :, 128:144].astype(BF))
    for i in range(9):
        left, right = [], []
        for j in range(18):
            row = slice(i * 18 + j, i * 18 + j + 1)
            here = place == hi_ref[row, :]
            right.append(one_hot(lo_ref[row, :]))
            lines = [score_ref[r, row, 0:128] if i < 8 else tails[r, j : j + 1, :] for r in range(12)]
            left.append(jnp.concatenate([jnp.where(here, line, 0.0).astype(BF) for line in lines], axis=0))
        out_ref[...] += dot_nt(jnp.concatenate(left, axis=1), jnp.concatenate(right, axis=1))
    gproj = dot_tn(att_ref[...], grad_ref[...]).astype(BF)
    grads_ref[0:96, :] = gproj[:, 0:128]
    grads_ref[96:144, :] = jnp.concatenate([gproj[0:48, 128:192], gproj[48:96, 128:192]], axis=1)
    low = low_ref[...]
    a, b, c = [dot_tn(low, gcols[j]).astype(BF) for j in range(3)]
    grads_ref[144:336, :] = jnp.concatenate([a, c[:, 0:32]], axis=1)
    grads_ref[336:528, :] = jnp.concatenate([b, c[:, 32:64]], axis=1)
    grads_ref[528:576, :] = jnp.concatenate([c[i * 48 : i * 48 + 48, 64:96] for i in range(4)], axis=1)
    core = lax.rem(lax.axis_index("lat"), 2)
    keep_ref[...] = grads_ref[pl.ds(pl.multiple_of(core * 288, 16), 288), :]
    send_ref[...] = grads_ref[pl.ds(pl.multiple_of((1 - core) * 288, 16), 288), :]


def scatter(score, lo, hi, low, gcols, att, grad):
    return pl.pallas_call(
        scatter_kernel,
        out_shape=(shape((192, 256), F32), shape((288, 128), BF), shape((288, 128), BF)),
        scratch_shapes=[pltpu.VMEM((576, 128), BF), pltpu.VMEM((12, 24, 128), F32)],
        compiler_params=VM,
        cost_estimate=cost(5),
        name="scatter",
    )(score, lo, hi, low, gcols, att, grad)


def meet_kernel(own_ref, other_ref, x0, x1, x2, x3, first_ref, first_other, second_ref, second_other,
                table_ref, two_ref, out_ref):
    gain = jnp.zeros((1, 192), F32)
    for s, x in enumerate((x0, x1, x2, x3)):
        rows = slice(s * 144, s * 144 + 144)
        grad = own_ref[rows, :].astype(F32) + other_ref[rows, :].astype(F32)
        normed, _ = layer_stats(x[...].astype(F32))
        gain = gain + jnp.sum(grad * normed, axis=0, keepdims=True)
    out_ref[0:576, :] = both(first_ref[...], first_other[...])
    out_ref[576:864, :] = both(second_ref[...], second_other[...])
    rows = []
    for r in range(12):
        pair = table_ref[r * 16 : r * 16 + 13, :]
        rows += [pair[:, 0:128], pair[:, 128:256]]
    none = jnp.zeros((1, 64), F32)
    for line in (gain, two_ref[...]):
        rows += [line[:, 0:128], jnp.concatenate([line[:, 128:192], none], axis=1)]
    rows += [jnp.zeros((100, 128), F32)]
    out_ref[864:1280, :] = jnp.concatenate(rows, axis=0).astype(BF)


def meet(own, other, x, first, first_other, second, second_other, table, two):
    return pl.pallas_call(
        meet_kernel,
        out_shape=shape((1280, 128), BF),
        compiler_params=VM,
        cost_estimate=cost(1),
        name="meet",
    )(own, other, *x, first, first_other, second, second_other, table, two)


def finish_kernel(x0, x1, x2, x3, m0, m1, m2, m3, g_own, band, sector, gain_ref, after_ref, out_ref):
    gs = (sector[144:288, :], band[0:144, :], sector[0:144, :], g_own[...])
    for q, (x, m, g) in enumerate(zip((x0, x1, x2, x3), (m0, m1, m2, m3), gs)):
        normed, inverse = layer_stats(x[...].astype(F32))
        rows = m[...].astype(F32) + norm_backward(g.astype(F32), gain_ref[...], normed, inverse)
        for lat in range(3):
            piece = rows[lat * 48 : lat * 48 + 48].reshape(6, 8, 192)
            out_ref[(q // 2) * 3 + lat, (q % 2) * 6 : (q % 2) * 6 + 6] = piece.astype(BF)


def finish(x, m, g, gain, after):
    return pl.pallas_call(
        finish_kernel,
        out_shape=shape((6, 12, 8, 192), BF),
        in_specs=[VMEM] * 12 + [ANY],
        compiler_params=VM,
        cost_estimate=cost(1),
        name="finish",
    )(*x, *m, *g, gain, after)


def add_kernel(got_ref, own_ref, other_ref, out_ref, g0, g1, g23):
    total = got_ref[0].astype(F32)
    for i in range(1, 32):
        total = total + got_ref[i].astype(F32)
    out_ref[...] = total.astype(BF)
    g0[...] = both(own_ref[0:144, :], other_ref[0:144, :])
    g1[...] = both(own_ref[144:288, :], other_ref[144:288, :])
    g23[...] = both(own_ref[288:576, :], other_ref[288:576, :])


def add(got, own, other):
    return pl.pallas_call(
        add_kernel,
        out_shape=(shape((40, 128), BF), shape((144, 192), BF), shape((144, 192), BF), shape((288, 192), BF)),
        compiler_params=VM,
        cost_estimate=cost(1),
        name="add",
    )(got, own, other)


def spread_kernel(own_ref, other_ref, g1, band, out_ref, next_ref):
    own = own_ref[...].astype(F32)
    row = lax.axis_index("lon") * 40 + lax.broadcasted_iota(I32, (40, 128), 0)
    table = (row >= 864) & (row < 1176)
    total = own + jnp.where(table, 0.0, other_ref[...].astype(F32))
    out_ref[...] = jnp.broadcast_to(total.astype(BF)[None], (32, 40, 128))
    next_ref[0:144, :] = g1[...]
    next_ref[144:288, :] = band[144:288, :]


def spread(own, other, g1, band):
    return pl.pallas_call(
        spread_kernel,
        out_shape=(shape((32, 40, 128), BF), shape((288, 192), BF)),
        compiler_params=VM,
        cost_estimate=cost(1),
        name="spread",
    )(own, other, g1, band)


def unpack_kernel(weight_scale, table_scale, own_ref, other_ref,
                  qkv_ref, proj_ref, upg_ref, down_ref, one_ref, two_ref, table_ref):
    swap = lax.rem(lax.axis_index("lat"), 2) == 1
    own, other = own_ref[0:864, :].astype(F32) * weight_scale, other_ref[0:864, :].astype(F32) * weight_scale
    lower, upper = jnp.where(swap, other, own), jnp.where(swap, own, other)
    for j in range(3):
        upg_ref[:, j * 128 : j * 128 + 128] = lower[j * 192 : j * 192 + 192]
        down_ref[:, j * 128 : j * 128 + 128] = upper[j * 192 : j * 192 + 192]
    second = jnp.concatenate([lower[576:864], upper[576:864]], axis=0)
    proj_ref[:, 0:128] = second[0:96]
    proj_ref[0:48, 128:192] = second[96:144, 0:64]
    proj_ref[48:96, 128:192] = second[96:144, 64:128]
    qkv_ref[0] = second[144:336, 0:96]
    qkv_ref[1] = second[336:528, 0:96]
    qkv_ref[2, :, 0:32] = second[144:336, 96:128]
    qkv_ref[2, :, 32:64] = second[336:528, 96:128]
    for i in range(4):
        qkv_ref[2, i * 48 : i * 48 + 48, 64:96] = second[528:576, i * 32 : i * 32 + 32]
    table = own_ref[864:1184, :].astype(F32)
    for r in range(12):
        for half in range(2):
            piece = table[r * 26 + half * 13 : r * 26 + half * 13 + 13] * table_scale
            for a in range(13):
                start = a * 256 + half * 128
                wide = min(128, 3312 - start)
                table_ref[r % 3, r // 3 : r // 3 + 1, start : start + wide] = piece[a : a + 1, 0:wide]
    gains = table[304:320] + other_ref[1168:1184, :].astype(F32)
    for start, out in ((8, one_ref), (10, two_ref)):
        line = gains[start : start + 1]
        later = jnp.concatenate([line[:, 96:128], gains[start + 1 : start + 2, 0:64]], axis=1)
        out[...] = jnp.where(lax.axis_index("tp") == 0, line[:, 0:96], later) * weight_scale


def unpack(weight_scale, table_scale, got, other):
    return pl.pallas_call(
        functools.partial(unpack_kernel, weight_scale, table_scale),
        out_shape=(
            shape((3, 192, 96), F32),
            shape((96, 192), F32),
            shape((192, 384), F32),
            shape((192, 384), F32),
            shape((1, 96), F32),
            shape((1, 96), F32),
            shape((3, 4, 3312), F32),
        ),
        compiler_params=VM,
        name="unpack",
    )(got, other)


def moved(value, band, sector, half):
    sizes = [lax.axis_size(name) for name in ("lat", "lon", "tp")]
    pairs = []
    for a in range(sizes[0]):
        for b in range(sizes[1]):
            for c in range(sizes[2]):
                source = ((a + band) % sizes[0], (b + sector) % sizes[1], (c + half) % sizes[2])
                pairs.append(tuple((x * sizes[1] + y) * sizes[2] + z for x, y, z in (source, (a, b, c))))
    return lax.ppermute(value, ("lat", "lon", "tp"), pairs)


def shifted_parts(quarters):
    return (
        quarters[3],
        moved(quarters[2], 0, 1, 0),
        moved(quarters[1], 1, 0, 0),
        moved(quarters[0], 1, 1, 0),
    )


def other_core(value):
    return lax.ppermute(value, "lat", [(a, a ^ 1) for a in range(lax.axis_size("lat"))])


def local(
    inputs,
    residual_mid,
    grad_out,
    mask_ids,
    key_valid,
    bias_index,
    pos_bias,
    norm1_gain,
    qkv_weight,
    proj_weight,
    norm2_gain,
    fc1_weight,
    fc2_weight,
):
    levels, lat_cells, lon_cells, channels = inputs.shape
    cell_count = levels * lat_cells * lon_cells
    weight_scale = (cell_count * lax.axis_size("lat") * lax.axis_size("lon")) ** (-0.5)
    table_scale = (lon_cells * lax.axis_size("lon") // 12) ** (-0.5)
    gain1, gain2 = norm1_gain.reshape(1, -1), norm2_gain.reshape(1, -1)

    def turned(field):
        return field.transpose(1, 2, 0, 3)

    x_in, mid_in, up_in = turned(inputs), turned(residual_mid), turned(grad_out)
    *x, part2, first, first_send = head(x_in, mid_in, up_in, gain2, fc1_weight, fc2_weight.T)
    other2 = moved(part2, 0, 0, 1)
    xw = shifted_parts(x)
    stage, lo, hi, terms, code = gather_first(
        bias_index, pos_bias[0].transpose(1, 0, 2), mask_ids.transpose(1, 0, 2), key_valid.transpose(1, 0, 2)
    )
    *gm, gain_two = middle(mid_in, up_in, part2, other2, gain2, lo)
    gw = shifted_parts(gm)
    main, tail = gather_second(stage, lo, hi, terms, (gain_two, *xw[1:]))
    low, q, k, v, prob, att = forward(xw, gain1, qkv_weight, main, tail, code)
    part1, score, gcols, grad = backward(gw, proj_weight, qkv_weight, q, k, v, prob)
    other1 = moved(part1, 0, 0, 1)
    table, second, second_send = scatter(score, lo, hi, low, gcols, att, grad)
    sums = meet(
        part1, other1, xw, first, other_core(first_send), second, other_core(second_send), table, gain_two
    )
    own, g0, g1, g23 = add(lax.all_to_all(sums.reshape(32, 40, 128), "lon", 0, 0), part1, other1)
    g_band = moved(g23, -1, 0, 0)
    totals, g_next = spread(own, moved(own, 2, 0, 0), g1, g_band)
    got = lax.all_to_all(totals, "lon", 0, 0).reshape(1280, 128)
    g_sector = moved(g_next, 0, -1, 0)
    qkv_out, proj_out, up_out, down_out, one, two, table_out = unpack(
        weight_scale, table_scale, got, other_core(got)
    )
    result = finish(x, gm, (g0, g_band, g_sector), gain1, one)
    return (
        result.transpose(2, 0, 1, 3),
        qkv_out,
        proj_out,
        up_out,
        down_out.T,
        one.reshape(channels // lax.axis_size("tp")),
        two.reshape(channels // lax.axis_size("tp")),
        table_out.transpose(1, 0, 2)[None],
    )


def solution(mesh):
    return jax.shard_map(
        local,
        mesh=mesh,
        in_specs=(
            P(None, "lat", "lon", None),
            P(None, "lat", "lon", None),
            P(None, "lat", "lon", None),
            P(None, "lat", "lon"),
            P(None, "lat", "lon"),
            P(),
            P("lat", None, "tp", None),
            P(),
            P(None, None, "tp"),
            P("tp", None),
            P(),
            P(None, "tp"),
            P("tp", None),
        ),
        out_specs=(
            P(None, "lat", "lon", None),
            P(None, None, "tp"),
            P("tp", None),
            P(None, "tp"),
            P("tp", None),
            P("tp"),
            P("tp"),
            P("lat", None, "tp", None),
        ),
        check_vma=False,
    )
```

```python
import functools

import jax
import jax.numpy as jnp
import numpy as np
from jax import lax
from jax.experimental import pallas as pl
from jax.experimental.pallas import tpu as pltpu
from jax.sharding import PartitionSpec as P

HD = 32
EPSILON = 1e-05
EXCLUDED = -1e30
BF = jnp.bfloat16
F32 = jnp.float32
I32 = jnp.int32
VMEM = pl.BlockSpec(memory_space=pltpu.VMEM)
VM = pltpu.CompilerParams(vmem_limit_bytes=24 * 1024 * 1024)
ALL = pltpu.CompilerParams(vmem_limit_bytes=63 * 1024 * 1024)
SMEM = pl.BlockSpec(memory_space=pltpu.SMEM)
ANY = pl.BlockSpec(memory_space=pl.ANY)


def cost(microseconds):
    return pl.CostEstimate(flops=int(microseconds * 1e9), bytes_accessed=0, transcendentals=0)


def shape(dims, kind):
    return jax.ShapeDtypeStruct(dims, kind)


def both(own, other):
    return (own.astype(F32) + other.astype(F32)).astype(BF)


def dot_nn(a, b):
    return lax.dot_general(a, b, (((1,), (0,)), ((), ())), preferred_element_type=F32)


def dot_nt(a, b):
    return lax.dot_general(a, b, (((1,), (1,)), ((), ())), preferred_element_type=F32)


def dot_tn(a, b):
    return lax.dot_general(a, b, (((0,), (0,)), ((), ())), preferred_element_type=F32)


def layer_stats(rows):
    mean = jnp.mean(rows, axis=-1, keepdims=True)
    centred = rows - mean
    inverse = lax.rsqrt(jnp.mean(centred * centred, axis=-1, keepdims=True) + EPSILON)
    return centred * inverse, inverse


def norm_backward(grad_normed, gain, normed, inverse):
    scaled = grad_normed * gain
    first = jnp.mean(scaled, axis=-1, keepdims=True)
    second = jnp.mean(scaled * normed, axis=-1, keepdims=True)
    return (scaled - first - normed * second) * inverse


def gelu_pair(pre):
    cdf = 0.5 * (1.0 + lax.erf(pre * 0.7071067811865476))
    pdf = 0.3989422804014327 * jnp.exp(-0.5 * pre * pre)
    return pre * cdf, cdf + pre * pdf


def to_quarters(field_ref, scratch):
    for lat in range(6):
        for half in range(2):
            rows = field_ref[lat, half * 6 : half * 6 + 6].astype(F32).reshape(48, 192)
            start = ((lat // 3) * 2 + half) * 144 + (lat % 3) * 48
            scratch[start : start + 48, :] = rows


def level_order():
    order = np.zeros((144, 144), np.float32)
    for w in range(4):
        for cell in range(18):
            for level in range(2):
                order[w * 36 + cell * 2 + level, cell * 8 + (2 * w + 1 + level) % 8] = 1.0
    return jnp.asarray(order, BF)


def to_windows(parts, order, scratch):
    for s in range(4):
        rows = dot_nn(order, parts[s][...])
        for w in range(4):
            scratch[w * 144 + s * 36 : w * 144 + s * 36 + 36, :] = rows[w * 36 : w * 36 + 36]


def head_kernel(x_hbm, mid_hbm, up_hbm, gain_hbm, fc1_hbm, fc2_hbm, o0, o1, o2, o3, part_hbm, keep_hbm, send_hbm,
                x_ref, mid_ref, up_ref, gain_ref, fc1_ref, fc2_ref, xq_ref, part_ref, grads_ref, x_s, mid_s, up_s, sem):
    pairs = (
        (mid_hbm, mid_ref),
        (gain_hbm, gain_ref),
        (fc1_hbm, fc1_ref),
        (up_hbm, up_ref),
        (fc2_hbm, fc2_ref),
        (x_hbm, x_ref),
    )
    copies = [pltpu.make_async_copy(a, b, sem.at[i]) for i, (a, b) in enumerate(pairs)]
    for copy in copies:
        copy.start()
    for copy in copies[:3]:
        copy.wait()
    to_quarters(mid_ref, mid_s)
    normed, _ = layer_stats(mid_s[...])
    lowered = (normed * gain_ref[...]).astype(BF)
    pre = dot_nn(lowered, fc1_ref[...])
    active, slopes = gelu_pair(pre)
    for copy in copies[3:]:
        copy.wait()
    to_quarters(x_ref, x_s)
    writes = []
    for q, out in enumerate((o0, o1, o2, o3)):
        xq_ref[q] = x_s[q * 144 : q * 144 + 144, :].astype(BF)
        writes.append(pltpu.make_async_copy(xq_ref.at[q], out, sem.at[8 + q]))
        writes[-1].start()
    to_quarters(up_ref, up_s)
    up = up_s[...].astype(BF)
    grad_pre = (dot_nn(up, fc2_ref[...]) * slopes).astype(BF)
    part_ref[...] = dot_nt(grad_pre, fc1_ref[...]).astype(BF)
    writes.append(pltpu.make_async_copy(part_ref, part_hbm, sem.at[6]))
    writes[-1].start()
    for start, grads in ((0, dot_tn(lowered, grad_pre)), (576, dot_tn(up, active.astype(BF)))):
        for j in range(3):
            grads_ref[start + j * 192 : start + j * 192 + 192, :] = grads[:, j * 128 : j * 128 + 128].astype(BF)
    core = lax.rem(lax.axis_index("lat"), 2)
    for i, (half, out) in enumerate(((core, keep_hbm), (1 - core, send_hbm))):
        piece = grads_ref.at[pl.ds(pl.multiple_of(half * 576, 16), 576)]
        writes.append(pltpu.make_async_copy(piece, out, sem.at[12 + i]))
        writes[-1].start()
    for write in writes:
        write.wait()


def head(x, mid, up, gain, fc1, fc2):
    return pl.pallas_call(
        head_kernel,
        out_shape=tuple(shape((144, 192), BF) for _ in range(4))
        + (shape((576, 192), BF), shape((576, 128), BF), shape((576, 128), BF)),
        in_specs=[ANY] * 6,
        out_specs=tuple(ANY for _ in range(7)),
        scratch_shapes=[
            pltpu.VMEM((6, 12, 8, 192), BF),
            pltpu.VMEM((6, 12, 8, 192), BF),
            pltpu.VMEM((6, 12, 8, 192), BF),
            pltpu.VMEM((1, 192), F32),
            pltpu.VMEM((192, 384), BF),
            pltpu.VMEM((192, 384), BF),
            pltpu.VMEM((4, 144, 192), BF),
            pltpu.VMEM((576, 192), BF),
            pltpu.VMEM((1152, 128), BF),
            pltpu.VMEM((576, 192), F32),
            pltpu.VMEM((576, 192), F32),
            pltpu.VMEM((576, 192), F32),
            pltpu.SemaphoreType.DMA((14,)),
        ],
        compiler_params=ALL,
        cost_estimate=cost(3),
        name="head",
    )(x, mid, up, gain, fc1, fc2)


def middle_kernel(mid_ref, up_ref, own_ref, other_ref, gain_ref, after_ref, o0, o1, o2, o3, gain_out, mid_s, up_s):
    to_quarters(mid_ref, mid_s)
    to_quarters(up_ref, up_s)
    normed, inverse = layer_stats(mid_s[...])
    grad = own_ref[...].astype(F32) + other_ref[...].astype(F32)
    gain_out[...] = jnp.sum(grad * normed, axis=0, keepdims=True)
    out = up_s[...] + norm_backward(grad, gain_ref[...], normed, inverse)
    for q, o in enumerate((o0, o1, o2, o3)):
        o[...] = out[q * 144 : q * 144 + 144].astype(BF)


def middle(mid, up, own, other, gain, after):
    return pl.pallas_call(
        middle_kernel,
        out_shape=tuple(shape((144, 192), BF) for _ in range(4)) + (shape((1, 192), F32),),
        in_specs=[VMEM] * 5 + [ANY],
        scratch_shapes=[pltpu.VMEM((576, 192), F32)] * 2,
        compiler_params=VM,
        cost_estimate=cost(1),
        name="middle",
    )(mid, up, own, other, gain, after)


def window_order():
    canon = np.arange(144).reshape(2, 2, 3, 2, 6).transpose(1, 3, 2, 4, 0).reshape(-1)
    order = np.zeros((144, 144), np.float32)
    order[np.arange(144), canon] = 1.0
    return order


def pack_tail(tail):
    spread = (lax.broadcasted_iota(I32, (16, 128), 1) & 15) == lax.broadcasted_iota(I32, (16, 128), 0)
    wide = dot_nn(tail, spread.astype(F32).astype(BF))
    here = (lax.broadcasted_iota(I32, (144, 128), 1) >> 4) == (lax.broadcasted_iota(I32, (144, 128), 0) & 7)
    wide = jnp.where(here, wide, 0.0).astype(BF)
    rows = (lax.broadcasted_iota(I32, (24, 144), 1) >> 3) == lax.broadcasted_iota(I32, (24, 144), 0)
    return dot_nn(rows.astype(F32).astype(BF), wide)


def one_hot(low):
    rows = lax.broadcasted_iota(I32, (256, 128), 0).astype(F32).astype(BF)
    return jnp.where(rows == low.astype(F32).astype(BF), jnp.ones((), BF), jnp.zeros((), BF))


def look_up(terms, lo_ref, hi_ref, stage, first_block, steps):
    half = (lax.broadcasted_iota(I32, (8, 128), 0) >> 2)

    def step(i, _):
        for pair in range(9):
            base = first_block + i * 18 + pair * 2
            hot = jnp.concatenate([one_hot(lo_ref[pl.ds(base + j, 1), :]) for j in range(2)], axis=1)
            found = dot_nn(terms, jnp.concatenate([hot, hot], axis=0))
            for j in range(2):
                cols = slice(j * 128, j * 128 + 128)
                high = hi_ref[pl.ds(base + j, 1), :]
                first = jnp.zeros((8, 128), F32)
                for c in range(13):
                    first = jnp.where(high == c, found[c * 8 : c * 8 + 8, cols], first)
                second = jnp.zeros((8, 128), F32)
                shifted = high - half
                for c in range(7):
                    second = jnp.where(shifted == 2 * c, found[104 + c * 8 : 112 + c * 8, cols], second)
                start = pl.multiple_of((base + j - first_block) * 16, 16)
                stage[pl.ds(start, 8), :] = first
                stage[pl.ds(start + 8, 8), :] = second + pltpu.roll(second, 4, 0)
        return 0

    lax.fori_loop(0, steps, step, 0, unroll=True)


def gather_first_kernel(index_ref, order_ref, bias_ref, ids_ref, valid_ref,
                        stage, lo_ref, hi_ref, terms_ref, code_ref, table):
    index = index_ref[...]
    order = order_ref[...]
    pieces = []
    for part in (index & 127, index >> 7):
        moved = dot_nt(dot_nn(order, part.astype(F32).astype(BF)).astype(BF), order)
        pieces.append((moved[:, 0:128].astype(I32), pack_tail(moved[:, 128:144].astype(BF)).astype(I32)))
    for rows, low, high in ((slice(0, 144), pieces[0][0], pieces[1][0]), (slice(144, 168), pieces[0][1], pieces[1][1])):
        lo_ref[rows, :] = low + (high & 1) * 128
        hi_ref[rows, :] = high >> 1
    table[...] = jnp.zeros((160, 256), F32)
    for r in range(12):
        line = bias_ref[r % 3, r // 3 : r // 3 + 1, :]
        line = line - jnp.max(line, axis=1, keepdims=True)
        for c in range(13):
            wide = min(256, 3312 - c * 256)
            row = c * 8 + r if r < 8 else 104 + (c // 2) * 8 + (c % 2) * 4 + r - 8
            table[row : row + 1, 0:wide] = line[:, c * 256 : c * 256 + wide]
    upper = table[...].astype(BF)
    terms_ref[:, 0:256] = upper
    terms_ref[:, 256:512] = (table[...] - upper.astype(F32)).astype(BF)
    code = (ids_ref[...] * 2 + (valid_ref[...] > 0).astype(I32)).astype(F32).reshape(48, 12).astype(BF)
    row = lax.broadcasted_iota(I32, (24, 48), 0)
    column = lax.broadcasted_iota(I32, (24, 48), 1)
    lines = []
    for level in range(2):
        pick = ((row >> 2) * 8 + (row & 3) * 2 + level) == column
        picked = dot_nn(pick.astype(F32).astype(BF), code)
        lines += [picked[lat * 4 : lat * 4 + 4] for lat in range(6)]
    lines = jnp.concatenate(lines, axis=1)
    code_ref[...] = dot_nt(lines.astype(BF), order)
    look_up(terms_ref[...], lo_ref, hi_ref, stage, 0, 5)


def gather_first(index, bias, ids, valid):
    return pl.pallas_call(
        gather_first_kernel,
        out_shape=(
            shape((90 * 16, 128), F32),
            shape((168, 128), I32),
            shape((168, 128), I32),
            shape((160, 512), BF),
            shape((4, 144), F32),
        ),
        scratch_shapes=[pltpu.VMEM((160, 256), F32)],
        compiler_params=VM,
        cost_estimate=cost(0.5),
        name="gather_first",
    )(index, jnp.asarray(window_order(), BF), bias, ids, valid)


def gather_second_kernel(first_stage, lo_ref, hi_ref, terms_ref, a0, a1, a2, a3, main_ref, tail_ref, stage):
    look_up(terms_ref[...], lo_ref, hi_ref, stage, 90, 4)
    for r in range(12):
        main_ref[r, 0:90, :] = first_stage[pl.ds(r, 90, stride=16), :]
        main_ref[r, 90:144, :] = stage[pl.ds(r, 54, stride=16), :]
        packed = stage[pl.ds(54 * 16 + r, 18, stride=16), :]
        for s in range(8):
            tail_ref[r, pl.ds(s, 18, stride=8), :] = pltpu.roll(packed, 128 - 16 * s, 1) if s else packed


def gather_second(first_stage, lo, hi, terms, after):
    return pl.pallas_call(
        gather_second_kernel,
        out_shape=(shape((12, 144, 128), F32), shape((12, 144, 128), F32)),
        in_specs=[VMEM] * 4 + [ANY] * 4,
        scratch_shapes=[pltpu.VMEM((72 * 16, 128), F32)],
        compiler_params=VM,
        cost_estimate=cost(4),
        name="gather_second",
    )(first_stage, lo, hi, terms, *after)


def forward_kernel(x0, x1, x2, x3, order_ref, gain_ref, qkv_ref, main_ref, tail_ref, code_ref,
                   low_ref, q_ref, k_ref, v_ref, prob_ref, att_ref, scratch):
    to_windows((x0, x1, x2, x3), order_ref[...], scratch)
    normed, _ = layer_stats(scratch[...])
    low = (normed * gain_ref[...]).astype(BF)
    low_ref[...] = low
    for j, out in enumerate((q_ref, k_ref, v_ref)):
        out[...] = dot_nn(low, qkv_ref[j]).astype(BF)
    eye = lax.broadcasted_iota(I32, (144, 144), 0) == lax.broadcasted_iota(I32, (144, 144), 1)

    def window(w, _):
        rows = pl.ds(pl.multiple_of(w * 144, 16), 144)
        code = code_ref[pl.ds(w, 1), :].astype(I32)
        label = code >> 1
        column = jnp.sum(jnp.where(eye, label, 0), axis=1, keepdims=True)
        allowed = eye | ((column == label) & ((code & 1) > 0))
        query, key, value = q_ref[rows, :], k_ref[rows, :], v_ref[rows, :]
        heads = []
        for h in range(3):
            cols = slice(h * HD, h * HD + HD)
            bias = jnp.concatenate([main_ref[w * 3 + h], tail_ref[w * 3 + h][:, 0:16]], axis=1)
            scores = dot_nt(query[:, cols], key[:, cols]) * (HD ** -0.5) + bias
            scores = jnp.where(allowed, scores, EXCLUDED)
            expo = jnp.exp(scores - jnp.max(scores, axis=-1, keepdims=True))
            prob = expo * (1.0 / jnp.sum(expo, axis=-1, keepdims=True))
            prob_ref[w * 3 + h] = prob
            heads.append(dot_nn(prob.astype(BF), value[:, cols]))
        att_ref[rows, :] = jnp.concatenate(heads, axis=1).astype(BF)
        return 0

    lax.fori_loop(0, 4, window, 0, unroll=True)


def forward(x, gain, qkv, main, tail, code):
    return pl.pallas_call(
        forward_kernel,
        out_shape=(
            shape((576, 192), BF),
            shape((576, 96), BF),
            shape((576, 96), BF),
            shape((576, 96), BF),
            shape((12, 144, 144), F32),
            shape((576, 96), BF),
        ),
        scratch_shapes=[pltpu.VMEM((576, 192), F32)],
        compiler_params=VM,
        cost_estimate=cost(5),
        name="forward",
    )(*x, level_order(), gain, qkv, main, tail, code)


def backward_kernel(g0, g1, g2, g3, order_ref, proj_ref, qkv_ref, q_ref, k_ref, v_ref, prob_ref,
                    part_ref, score_ref, gcols, grad_ref, scratch, gatt):
    to_windows((g0, g1, g2, g3), order_ref[...], scratch)
    grad = scratch[...].astype(BF)
    grad_ref[...] = grad
    gatt[...] = dot_nt(grad, proj_ref[...]).astype(BF)

    def window(w, _):
        rows = pl.ds(pl.multiple_of(w * 144, 16), 144)
        query, key, value, above = q_ref[rows, :], k_ref[rows, :], v_ref[rows, :], gatt[rows, :]
        queries, keys, values = [], [], []
        for h in range(3):
            cols = slice(h * HD, h * HD + HD)
            prob = prob_ref[w * 3 + h]
            values.append(dot_tn(prob.astype(BF), above[:, cols]))
            grad_prob = dot_nt(above[:, cols], value[:, cols])
            score = prob * (grad_prob - jnp.sum(grad_prob * prob, axis=-1, keepdims=True))
            score_ref[w * 3 + h] = score
            low_score = (score * (HD ** -0.5)).astype(BF)
            queries.append(dot_nn(low_score, key[:, cols]))
            keys.append(dot_tn(low_score, query[:, cols]))
        gcols[0, rows, :] = jnp.concatenate(queries, axis=1).astype(BF)
        gcols[1, rows, :] = jnp.concatenate(keys, axis=1).astype(BF)
        gcols[2, rows, :] = jnp.concatenate(values, axis=1).astype(BF)
        return 0

    lax.fori_loop(0, 4, window, 0, unroll=True)
    total = None
    for j in range(3):
        term = dot_nt(gcols[j], qkv_ref[j])
        total = term if total is None else total + term
    scratch[...] = total
    for s in range(4):
        pieces = [scratch[w * 144 + s * 36 : w * 144 + s * 36 + 36, :] for w in range(4)]
        piece = jnp.concatenate(pieces, axis=0).astype(BF)
        part_ref[s * 144 : s * 144 + 144, :] = dot_tn(order_ref[...], piece).astype(BF)


def backward(g, proj, qkv, q, k, v, prob):
    return pl.pallas_call(
        backward_kernel,
        out_shape=(
            shape((576, 192), BF),
            shape((12, 144, 144), F32),
            shape((3, 576, 96), BF),
            shape((576, 192), BF),
        ),
        scratch_shapes=[pltpu.VMEM((576, 192), F32), pltpu.VMEM((576, 96), BF)],
        compiler_params=VM,
        cost_estimate=cost(7),
        name="backward",
    )(*g, level_order(), proj, qkv, q, k, v, prob)


def scatter_kernel(score_ref, lo_ref, hi_ref, low_ref, gcols, att_ref, grad_ref,
                   out_ref, keep_ref, send_ref, grads_ref, tails):
    out_ref[...] = jnp.zeros((192, 256), F32)
    place = lax.broadcasted_iota(I32, (16, 128), 0)
    for r in range(12):
        tails[r] = pack_tail(score_ref[r, :, 128:144].astype(BF))
    for i in range(9):
        left, right = [], []
        for j in range(18):
            row = slice(i * 18 + j, i * 18 + j + 1)
            here = place == hi_ref[row, :]
            right.append(one_hot(lo_ref[row, :]))
            lines = [score_ref[r, row, 0:128] if i < 8 else tails[r, j : j + 1, :] for r in range(12)]
            left.append(jnp.concatenate([jnp.where(here, line, 0.0).astype(BF) for line in lines], axis=0))
        out_ref[...] += dot_nt(jnp.concatenate(left, axis=1), jnp.concatenate(right, axis=1))
    gproj = dot_tn(att_ref[...], grad_ref[...]).astype(BF)
    grads_ref[0:96, :] = gproj[:, 0:128]
    grads_ref[96:144, :] = jnp.concatenate([gproj[0:48, 128:192], gproj[48:96, 128:192]], axis=1)
    low = low_ref[...]
    a, b, c = [dot_tn(low, gcols[j]).astype(BF) for j in range(3)]
    grads_ref[144:336, :] = jnp.concatenate([a, c[:, 0:32]], axis=1)
    grads_ref[336:528, :] = jnp.concatenate([b, c[:, 32:64]], axis=1)
    grads_ref[528:576, :] = jnp.concatenate([c[i * 48 : i * 48 + 48, 64:96] for i in range(4)], axis=1)
    core = lax.rem(lax.axis_index("lat"), 2)
    keep_ref[...] = grads_ref[pl.ds(pl.multiple_of(core * 288, 16), 288), :]
    send_ref[...] = grads_ref[pl.ds(pl.multiple_of((1 - core) * 288, 16), 288), :]


def scatter(score, lo, hi, low, gcols, att, grad):
    return pl.pallas_call(
        scatter_kernel,
        out_shape=(shape((192, 256), F32), shape((288, 128), BF), shape((288, 128), BF)),
        scratch_shapes=[pltpu.VMEM((576, 128), BF), pltpu.VMEM((12, 24, 128), F32)],
        compiler_params=VM,
        cost_estimate=cost(5),
        name="scatter",
    )(score, lo, hi, low, gcols, att, grad)


def meet_kernel(own_ref, other_ref, x0, x1, x2, x3, first_ref, first_other, second_ref, second_other,
                table_ref, two_ref, out_ref, g0, g1, g2, g3):
    gain = jnp.zeros((1, 192), F32)
    for s, x in enumerate((x0, x1, x2, x3)):
        rows = slice(s * 144, s * 144 + 144)
        grad = own_ref[rows, :].astype(F32) + other_ref[rows, :].astype(F32)
        normed, _ = layer_stats(x[...].astype(F32))
        gain = gain + jnp.sum(grad * normed, axis=0, keepdims=True)
        (g0, g1, g2, g3)[s][...] = grad.astype(BF)
    out_ref[0:576, :] = both(first_ref[...], first_other[...])
    out_ref[576:864, :] = both(second_ref[...], second_other[...])
    rows = []
    for r in range(12):
        pair = table_ref[r * 16 : r * 16 + 13, :]
        rows += [pair[:, 0:128], pair[:, 128:256]]
    none = jnp.zeros((1, 64), F32)
    for line in (gain, two_ref[...]):
        rows += [line[:, 0:128], jnp.concatenate([line[:, 128:192], none], axis=1)]
    rows += [jnp.zeros((100, 128), F32)]
    out_ref[864:1280, :] = jnp.concatenate(rows, axis=0).astype(BF)


def meet(own, other, x, first, first_other, second, second_other, table, two):
    return pl.pallas_call(
        meet_kernel,
        out_shape=(
            shape((1280, 128), BF),
            shape((144, 192), BF),
            shape((144, 192), BF),
            shape((144, 192), BF),
            shape((144, 192), BF),
        ),
        compiler_params=VM,
        cost_estimate=cost(1),
        name="meet",
    )(own, other, *x, first, first_other, second, second_other, table, two)


def finish_kernel(x0, x1, x2, x3, m0, m1, m2, m3, g0, g1, g2, g3, gain_ref, out_ref):
    for q, (x, m, g) in enumerate(zip((x0, x1, x2, x3), (m0, m1, m2, m3), (g0, g1, g2, g3))):
        normed, inverse = layer_stats(x[...].astype(F32))
        rows = m[...].astype(F32) + norm_backward(g[...].astype(F32), gain_ref[...], normed, inverse)
        for lat in range(3):
            piece = rows[lat * 48 : lat * 48 + 48].reshape(6, 8, 192)
            out_ref[(q // 2) * 3 + lat, (q % 2) * 6 : (q % 2) * 6 + 6] = piece.astype(BF)


def finish(x, m, g, gain):
    return pl.pallas_call(
        finish_kernel,
        out_shape=shape((6, 12, 8, 192), BF),
        compiler_params=VM,
        cost_estimate=cost(1),
        name="finish",
    )(*x, *m, *g, gain)


def add_kernel(got_ref, b0, b1, b2, out_ref):
    total = got_ref[0].astype(F32)
    for i in range(1, 32):
        total = total + got_ref[i].astype(F32)
    out_ref[...] = total.astype(BF)


def add(got, after):
    return pl.pallas_call(
        add_kernel,
        out_shape=shape((40, 128), BF),
        in_specs=[VMEM] + [ANY] * 3,
        compiler_params=VM,
        cost_estimate=cost(1),
        name="add",
    )(got, *after)


def spread_kernel(own_ref, other_ref, out_ref):
    own = own_ref[...].astype(F32)
    row = lax.axis_index("lon") * 40 + lax.broadcasted_iota(I32, (40, 128), 0)
    table = (row >= 864) & (row < 1176)
    total = own + jnp.where(table, 0.0, other_ref[...].astype(F32))
    out_ref[...] = jnp.broadcast_to(total.astype(BF)[None], (32, 40, 128))


def spread(own, other):
    return pl.pallas_call(
        spread_kernel, out_shape=shape((32, 40, 128), BF), compiler_params=VM, cost_estimate=cost(1), name="spread"
    )(own, other)


def unpack_kernel(weight_scale, table_scale, own_ref, other_ref,
                  qkv_ref, proj_ref, upg_ref, down_ref, one_ref, two_ref, table_ref):
    swap = lax.rem(lax.axis_index("lat"), 2) == 1
    own, other = own_ref[0:864, :].astype(F32) * weight_scale, other_ref[0:864, :].astype(F32) * weight_scale
    lower, upper = jnp.where(swap, other, own), jnp.where(swap, own, other)
    for j in range(3):
        upg_ref[:, j * 128 : j * 128 + 128] = lower[j * 192 : j * 192 + 192]
        down_ref[:, j * 128 : j * 128 + 128] = upper[j * 192 : j * 192 + 192]
    second = jnp.concatenate([lower[576:864], upper[576:864]], axis=0)
    proj_ref[:, 0:128] = second[0:96]
    proj_ref[0:48, 128:192] = second[96:144, 0:64]
    proj_ref[48:96, 128:192] = second[96:144, 64:128]
    qkv_ref[0] = second[144:336, 0:96]
    qkv_ref[1] = second[336:528, 0:96]
    qkv_ref[2, :, 0:32] = second[144:336, 96:128]
    qkv_ref[2, :, 32:64] = second[336:528, 96:128]
    for i in range(4):
        qkv_ref[2, i * 48 : i * 48 + 48, 64:96] = second[528:576, i * 32 : i * 32 + 32]
    table = own_ref[864:1184, :].astype(F32)
    for r in range(12):
        for half in range(2):
            piece = table[r * 26 + half * 13 : r * 26 + half * 13 + 13] * table_scale
            for a in range(13):
                start = a * 256 + half * 128
                wide = min(128, 3312 - start)
                table_ref[r % 3, r // 3 : r // 3 + 1, start : start + wide] = piece[a : a + 1, 0:wide]
    gains = table[304:320] + other_ref[1168:1184, :].astype(F32)
    for start, out in ((8, one_ref), (10, two_ref)):
        line = gains[start : start + 1]
        later = jnp.concatenate([line[:, 96:128], gains[start + 1 : start + 2, 0:64]], axis=1)
        out[...] = jnp.where(lax.axis_index("tp") == 0, line[:, 0:96], later) * weight_scale


def unpack(weight_scale, table_scale, got, other):
    return pl.pallas_call(
        functools.partial(unpack_kernel, weight_scale, table_scale),
        out_shape=(
            shape((3, 192, 96), F32),
            shape((96, 192), F32),
            shape((192, 384), F32),
            shape((192, 384), F32),
            shape((1, 96), F32),
            shape((1, 96), F32),
            shape((3, 4, 3312), F32),
        ),
        compiler_params=VM,
        name="unpack",
    )(got, other)


def moved(value, band, sector, half):
    sizes = [lax.axis_size(name) for name in ("lat", "lon", "tp")]
    pairs = []
    for a in range(sizes[0]):
        for b in range(sizes[1]):
            for c in range(sizes[2]):
                source = ((a + band) % sizes[0], (b + sector) % sizes[1], (c + half) % sizes[2])
                pairs.append(tuple((x * sizes[1] + y) * sizes[2] + z for x, y, z in (source, (a, b, c))))
    return lax.ppermute(value, ("lat", "lon", "tp"), pairs)


def shifted_parts(quarters):
    return (
        quarters[3],
        moved(quarters[2], 0, 1, 0),
        moved(quarters[1], 1, 0, 0),
        moved(quarters[0], 1, 1, 0),
    )


def other_core(value):
    return lax.ppermute(value, "lat", [(a, a ^ 1) for a in range(lax.axis_size("lat"))])


def local(
    inputs,
    residual_mid,
    grad_out,
    mask_ids,
    key_valid,
    bias_index,
    pos_bias,
    norm1_gain,
    qkv_weight,
    proj_weight,
    norm2_gain,
    fc1_weight,
    fc2_weight,
):
    levels, lat_cells, lon_cells, channels = inputs.shape
    cell_count = levels * lat_cells * lon_cells
    weight_scale = (cell_count * lax.axis_size("lat") * lax.axis_size("lon")) ** (-0.5)
    table_scale = (lon_cells * lax.axis_size("lon") // 12) ** (-0.5)
    gain1, gain2 = norm1_gain.reshape(1, -1), norm2_gain.reshape(1, -1)

    def turned(field):
        return field.transpose(1, 2, 0, 3)

    x_in, mid_in, up_in = turned(inputs), turned(residual_mid), turned(grad_out)
    *x, part2, first, first_send = head(x_in, mid_in, up_in, gain2, fc1_weight, fc2_weight.T)
    other2 = moved(part2, 0, 0, 1)
    xw = shifted_parts(x)
    stage, lo, hi, terms, code = gather_first(
        bias_index, pos_bias[0].transpose(1, 0, 2), mask_ids.transpose(1, 0, 2), key_valid.transpose(1, 0, 2)
    )
    *gm, gain_two = middle(mid_in, up_in, part2, other2, gain2, lo)
    gw = shifted_parts(gm)
    main, tail = gather_second(stage, lo, hi, terms, (gain_two, *xw[1:]))
    low, q, k, v, prob, att = forward(xw, gain1, qkv_weight, main, tail, code)
    part1, score, gcols, grad = backward(gw, proj_weight, qkv_weight, q, k, v, prob)
    other1 = moved(part1, 0, 0, 1)
    table, second, second_send = scatter(score, lo, hi, low, gcols, att, grad)
    sums, *g = meet(
        part1, other1, xw, first, other_core(first_send), second, other_core(second_send), table, gain_two
    )
    back = (moved(g[3], -1, -1, 0), moved(g[2], -1, 0, 0), moved(g[1], 0, -1, 0), g[0])
    own = add(lax.all_to_all(sums.reshape(32, 40, 128), "lon", 0, 0), back[:3])
    totals = spread(own, moved(own, 2, 0, 0))
    result = finish(x, gm, back, gain1)
    got = lax.all_to_all(totals, "lon", 0, 0).reshape(1280, 128)
    qkv_out, proj_out, up_out, down_out, one, two, table_out = unpack(
        weight_scale, table_scale, got, other_core(got)
    )
    return (
        result.transpose(2, 0, 1, 3),
        qkv_out,
        proj_out,
        up_out,
        down_out.T,
        one.reshape(channels // lax.axis_size("tp")),
        two.reshape(channels // lax.axis_size("tp")),
        table_out.transpose(1, 0, 2)[None],
    )


def solution(mesh):
    return jax.shard_map(
        local,
        mesh=mesh,
        in_specs=(
            P(None, "lat", "lon", None),
            P(None, "lat", "lon", None),
            P(None, "lat", "lon", None),
            P(None, "lat", "lon"),
            P(None, "lat", "lon"),
            P(),
            P("lat", None, "tp", None),
            P(),
            P(None, None, "tp"),
            P("tp", None),
            P(),
            P(None, "tp"),
            P("tp", None),
        ),
        out_specs=(
            P(None, "lat", "lon", None),
            P(None, None, "tp"),
            P("tp", None),
            P(None, "tp"),
            P("tp", None),
            P("tp"),
            P("tp"),
            P("lat", None, "tp", None),
        ),
        check_vma=False,
    )
```

```python
import functools

import jax
import jax.numpy as jnp
import numpy as np
from jax import lax
from jax.experimental import pallas as pl
from jax.experimental.pallas import tpu as pltpu
from jax.sharding import PartitionSpec as P

HD = 32
EPSILON = 1e-05
EXCLUDED = -1e30
BF = jnp.bfloat16
F32 = jnp.float32
I32 = jnp.int32
VMEM = pl.BlockSpec(memory_space=pltpu.VMEM)
VM = pltpu.CompilerParams(vmem_limit_bytes=24 * 1024 * 1024)
ALL = pltpu.CompilerParams(vmem_limit_bytes=63 * 1024 * 1024)
SMEM = pl.BlockSpec(memory_space=pltpu.SMEM)
ANY = pl.BlockSpec(memory_space=pl.ANY)


def cost(microseconds):
    return pl.CostEstimate(flops=int(microseconds * 1e9), bytes_accessed=0, transcendentals=0)


def shape(dims, kind):
    return jax.ShapeDtypeStruct(dims, kind)


def both(own, other):
    return (own.astype(F32) + other.astype(F32)).astype(BF)


def dot_nn(a, b):
    return lax.dot_general(a, b, (((1,), (0,)), ((), ())), preferred_element_type=F32)


def dot_nt(a, b):
    return lax.dot_general(a, b, (((1,), (1,)), ((), ())), preferred_element_type=F32)


def dot_tn(a, b):
    return lax.dot_general(a, b, (((0,), (0,)), ((), ())), preferred_element_type=F32)


def layer_stats(rows):
    mean = jnp.mean(rows, axis=-1, keepdims=True)
    centred = rows - mean
    inverse = lax.rsqrt(jnp.mean(centred * centred, axis=-1, keepdims=True) + EPSILON)
    return centred * inverse, inverse


def norm_backward(grad_normed, gain, normed, inverse):
    scaled = grad_normed * gain
    first = jnp.mean(scaled, axis=-1, keepdims=True)
    second = jnp.mean(scaled * normed, axis=-1, keepdims=True)
    return (scaled - first - normed * second) * inverse


def gelu_pair(pre):
    cdf = 0.5 * (1.0 + lax.erf(pre * 0.7071067811865476))
    pdf = 0.3989422804014327 * jnp.exp(-0.5 * pre * pre)
    return pre * cdf, cdf + pre * pdf


def to_quarters(field_ref, scratch):
    for lat in range(6):
        for half in range(2):
            rows = field_ref[lat, half * 6 : half * 6 + 6].astype(F32).reshape(48, 192)
            start = ((lat // 3) * 2 + half) * 144 + (lat % 3) * 48
            scratch[start : start + 48, :] = rows


def level_order():
    order = np.zeros((144, 144), np.float32)
    for w in range(4):
        for cell in range(18):
            for level in range(2):
                order[w * 36 + cell * 2 + level, cell * 8 + (2 * w + 1 + level) % 8] = 1.0
    return jnp.asarray(order, BF)


def to_windows(parts, order, scratch):
    for s in range(4):
        rows = dot_nn(order, parts[s][...])
        for w in range(4):
            scratch[w * 144 + s * 36 : w * 144 + s * 36 + 36, :] = rows[w * 36 : w * 36 + 36]


def head_kernel(x_hbm, mid_hbm, up_hbm, gain_hbm, fc1_hbm, fc2_hbm, o0, o1, o2, o3, part_hbm, keep_hbm, send_hbm,
                x_ref, mid_ref, up_ref, gain_ref, fc1_ref, fc2_ref, xq_ref, part_ref, grads_ref, x_s, mid_s, up_s, sem):
    pairs = (
        (mid_hbm, mid_ref),
        (gain_hbm, gain_ref),
        (fc1_hbm, fc1_ref),
        (up_hbm, up_ref),
        (fc2_hbm, fc2_ref),
        (x_hbm, x_ref),
    )
    copies = [pltpu.make_async_copy(a, b, sem.at[i]) for i, (a, b) in enumerate(pairs)]
    for copy in copies:
        copy.start()
    for copy in copies[:3]:
        copy.wait()
    to_quarters(mid_ref, mid_s)
    normed, _ = layer_stats(mid_s[...])
    lowered = (normed * gain_ref[...]).astype(BF)
    pre = dot_nn(lowered, fc1_ref[...])
    active, slopes = gelu_pair(pre)
    for copy in copies[3:]:
        copy.wait()
    to_quarters(x_ref, x_s)
    writes = []
    for q, out in enumerate((o0, o1, o2, o3)):
        xq_ref[q] = x_s[q * 144 : q * 144 + 144, :].astype(BF)
        writes.append(pltpu.make_async_copy(xq_ref.at[q], out, sem.at[8 + q]))
        writes[-1].start()
    to_quarters(up_ref, up_s)
    up = up_s[...].astype(BF)
    grad_pre = (dot_nn(up, fc2_ref[...]) * slopes).astype(BF)
    part_ref[...] = dot_nt(grad_pre, fc1_ref[...]).astype(BF)
    writes.append(pltpu.make_async_copy(part_ref, part_hbm, sem.at[6]))
    writes[-1].start()
    for start, grads in ((0, dot_tn(lowered, grad_pre)), (576, dot_tn(up, active.astype(BF)))):
        for j in range(3):
            grads_ref[start + j * 192 : start + j * 192 + 192, :] = grads[:, j * 128 : j * 128 + 128].astype(BF)
    core = lax.rem(lax.axis_index("lat"), 2)
    for i, (half, out) in enumerate(((core, keep_hbm), (1 - core, send_hbm))):
        piece = grads_ref.at[pl.ds(pl.multiple_of(half * 576, 16), 576)]
        writes.append(pltpu.make_async_copy(piece, out, sem.at[12 + i]))
        writes[-1].start()
    for write in writes:
        write.wait()


def head(x, mid, up, gain, fc1, fc2):
    return pl.pallas_call(
        head_kernel,
        out_shape=tuple(shape((144, 192), BF) for _ in range(4))
        + (shape((576, 192), BF), shape((576, 128), BF), shape((576, 128), BF)),
        in_specs=[ANY] * 6,
        out_specs=tuple(ANY for _ in range(7)),
        scratch_shapes=[
            pltpu.VMEM((6, 12, 8, 192), BF),
            pltpu.VMEM((6, 12, 8, 192), BF),
            pltpu.VMEM((6, 12, 8, 192), BF),
            pltpu.VMEM((1, 192), F32),
            pltpu.VMEM((192, 384), BF),
            pltpu.VMEM((192, 384), BF),
            pltpu.VMEM((4, 144, 192), BF),
            pltpu.VMEM((576, 192), BF),
            pltpu.VMEM((1152, 128), BF),
            pltpu.VMEM((576, 192), F32),
            pltpu.VMEM((576, 192), F32),
            pltpu.VMEM((576, 192), F32),
            pltpu.SemaphoreType.DMA((14,)),
        ],
        compiler_params=ALL,
        cost_estimate=cost(3),
        name="head",
    )(x, mid, up, gain, fc1, fc2)


def middle_kernel(mid_ref, up_ref, own_ref, other_ref, gain_ref, after_ref, o0, o1, o2, o3, gain_out, mid_s, up_s):
    to_quarters(mid_ref, mid_s)
    to_quarters(up_ref, up_s)
    normed, inverse = layer_stats(mid_s[...])
    grad = own_ref[...].astype(F32) + other_ref[...].astype(F32)
    gain_out[...] = jnp.sum(grad * normed, axis=0, keepdims=True)
    out = up_s[...] + norm_backward(grad, gain_ref[...], normed, inverse)
    for q, o in enumerate((o0, o1, o2, o3)):
        o[...] = out[q * 144 : q * 144 + 144].astype(BF)


def middle(mid, up, own, other, gain, after):
    return pl.pallas_call(
        middle_kernel,
        out_shape=tuple(shape((144, 192), BF) for _ in range(4)) + (shape((1, 192), F32),),
        in_specs=[VMEM] * 5 + [ANY],
        scratch_shapes=[pltpu.VMEM((576, 192), F32)] * 2,
        compiler_params=VM,
        cost_estimate=cost(1),
        name="middle",
    )(mid, up, own, other, gain, after)


def window_order():
    canon = np.arange(144).reshape(2, 2, 3, 2, 6).transpose(1, 3, 2, 4, 0).reshape(-1)
    order = np.zeros((144, 144), np.float32)
    order[np.arange(144), canon] = 1.0
    return order


def pack_tail(tail):
    spread = (lax.broadcasted_iota(I32, (16, 128), 1) & 15) == lax.broadcasted_iota(I32, (16, 128), 0)
    wide = dot_nn(tail, spread.astype(F32).astype(BF))
    here = (lax.broadcasted_iota(I32, (144, 128), 1) >> 4) == (lax.broadcasted_iota(I32, (144, 128), 0) & 7)
    wide = jnp.where(here, wide, 0.0).astype(BF)
    rows = (lax.broadcasted_iota(I32, (24, 144), 1) >> 3) == lax.broadcasted_iota(I32, (24, 144), 0)
    return dot_nn(rows.astype(F32).astype(BF), wide)


def one_hot(low):
    rows = lax.broadcasted_iota(I32, (256, 128), 0).astype(F32).astype(BF)
    return jnp.where(rows == low.astype(F32).astype(BF), jnp.ones((), BF), jnp.zeros((), BF))


def look_up(terms, lo_ref, hi_ref, stage, first_block, steps):
    half = (lax.broadcasted_iota(I32, (8, 128), 0) >> 2)

    def step(i, _):
        for pair in range(9):
            base = first_block + i * 18 + pair * 2
            hot = jnp.concatenate([one_hot(lo_ref[pl.ds(base + j, 1), :]) for j in range(2)], axis=1)
            found = dot_nn(terms, jnp.concatenate([hot, hot], axis=0))
            for j in range(2):
                cols = slice(j * 128, j * 128 + 128)
                high = hi_ref[pl.ds(base + j, 1), :]
                first = jnp.zeros((8, 128), F32)
                for c in range(13):
                    first = jnp.where(high == c, found[c * 8 : c * 8 + 8, cols], first)
                second = jnp.zeros((8, 128), F32)
                shifted = high - half
                for c in range(7):
                    second = jnp.where(shifted == 2 * c, found[104 + c * 8 : 112 + c * 8, cols], second)
                start = pl.multiple_of((base + j - first_block) * 16, 16)
                stage[pl.ds(start, 8), :] = first
                stage[pl.ds(start + 8, 8), :] = second + pltpu.roll(second, 4, 0)
        return 0

    lax.fori_loop(0, steps, step, 0, unroll=True)


def gather_first_kernel(index_ref, order_ref, bias_ref, ids_ref, valid_ref,
                        stage, lo_ref, hi_ref, terms_ref, code_ref, table):
    index = index_ref[...]
    order = order_ref[...]
    pieces = []
    for part in (index & 127, index >> 7):
        moved = dot_nt(dot_nn(order, part.astype(F32).astype(BF)).astype(BF), order)
        pieces.append((moved[:, 0:128].astype(I32), pack_tail(moved[:, 128:144].astype(BF)).astype(I32)))
    for rows, low, high in ((slice(0, 144), pieces[0][0], pieces[1][0]), (slice(144, 168), pieces[0][1], pieces[1][1])):
        lo_ref[rows, :] = low + (high & 1) * 128
        hi_ref[rows, :] = high >> 1
    table[...] = jnp.zeros((160, 256), F32)
    for r in range(12):
        line = bias_ref[r % 3, r // 3 : r // 3 + 1, :]
        line = line - jnp.max(line, axis=1, keepdims=True)
        for c in range(13):
            wide = min(256, 3312 - c * 256)
            row = c * 8 + r if r < 8 else 104 + (c // 2) * 8 + (c % 2) * 4 + r - 8
            table[row : row + 1, 0:wide] = line[:, c * 256 : c * 256 + wide]
    upper = table[...].astype(BF)
    terms_ref[:, 0:256] = upper
    terms_ref[:, 256:512] = (table[...] - upper.astype(F32)).astype(BF)
    code = (ids_ref[...] * 2 + (valid_ref[...] > 0).astype(I32)).astype(F32).reshape(48, 12).astype(BF)
    row = lax.broadcasted_iota(I32, (24, 48), 0)
    column = lax.broadcasted_iota(I32, (24, 48), 1)
    lines = []
    for level in range(2):
        pick = ((row >> 2) * 8 + (row & 3) * 2 + level) == column
        picked = dot_nn(pick.astype(F32).astype(BF), code)
        lines += [picked[lat * 4 : lat * 4 + 4] for lat in range(6)]
    lines = jnp.concatenate(lines, axis=1)
    code_ref[...] = dot_nt(lines.astype(BF), order)
    look_up(terms_ref[...], lo_ref, hi_ref, stage, 0, 5)


def gather_first(index, bias, ids, valid):
    return pl.pallas_call(
        gather_first_kernel,
        out_shape=(
            shape((90 * 16, 128), F32),
            shape((168, 128), I32),
            shape((168, 128), I32),
            shape((160, 512), BF),
            shape((4, 144), F32),
        ),
        scratch_shapes=[pltpu.VMEM((160, 256), F32)],
        compiler_params=VM,
        cost_estimate=cost(0.5),
        name="gather_first",
    )(index, jnp.asarray(window_order(), BF), bias, ids, valid)


def gather_second_kernel(first_stage, lo_ref, hi_ref, terms_ref, a0, a1, a2, a3, main_ref, tail_ref, stage):
    look_up(terms_ref[...], lo_ref, hi_ref, stage, 90, 4)
    for r in range(12):
        main_ref[r, 0:90, :] = first_stage[pl.ds(r, 90, stride=16), :]
        main_ref[r, 90:144, :] = stage[pl.ds(r, 54, stride=16), :]
        packed = stage[pl.ds(54 * 16 + r, 18, stride=16), :]
        for s in range(8):
            tail_ref[r, pl.ds(s, 18, stride=8), :] = pltpu.roll(packed, 128 - 16 * s, 1) if s else packed


def gather_second(first_stage, lo, hi, terms, after):
    return pl.pallas_call(
        gather_second_kernel,
        out_shape=(shape((12, 144, 128), F32), shape((12, 144, 128), F32)),
        in_specs=[VMEM] * 4 + [ANY] * 4,
        scratch_shapes=[pltpu.VMEM((72 * 16, 128), F32)],
        compiler_params=VM,
        cost_estimate=cost(4),
        name="gather_second",
    )(first_stage, lo, hi, terms, *after)


def forward_kernel(x0, x1, x2, x3, order_ref, gain_ref, qkv_ref, main_ref, tail_ref, code_ref,
                   low_ref, q_ref, k_ref, v_ref, prob_ref, att_ref, scratch):
    to_windows((x0, x1, x2, x3), order_ref[...], scratch)
    normed, _ = layer_stats(scratch[...])
    low = (normed * gain_ref[...]).astype(BF)
    low_ref[...] = low
    for j, out in enumerate((q_ref, k_ref, v_ref)):
        out[...] = dot_nn(low, qkv_ref[j]).astype(BF)
    eye = lax.broadcasted_iota(I32, (144, 144), 0) == lax.broadcasted_iota(I32, (144, 144), 1)

    def window(w, _):
        rows = pl.ds(pl.multiple_of(w * 144, 16), 144)
        code = code_ref[pl.ds(w, 1), :].astype(I32)
        label = code >> 1
        column = jnp.sum(jnp.where(eye, label, 0), axis=1, keepdims=True)
        allowed = eye | ((column == label) & ((code & 1) > 0))
        query, key, value = q_ref[rows, :], k_ref[rows, :], v_ref[rows, :]
        heads = []
        for h in range(3):
            cols = slice(h * HD, h * HD + HD)
            bias = jnp.concatenate([main_ref[w * 3 + h], tail_ref[w * 3 + h][:, 0:16]], axis=1)
            scores = dot_nt(query[:, cols], key[:, cols]) * (HD ** -0.5) + bias
            scores = jnp.where(allowed, scores, EXCLUDED)
            expo = jnp.exp(scores - jnp.max(scores, axis=-1, keepdims=True))
            prob = expo * (1.0 / jnp.sum(expo, axis=-1, keepdims=True))
            prob_ref[w * 3 + h] = prob
            heads.append(dot_nn(prob.astype(BF), value[:, cols]))
        att_ref[rows, :] = jnp.concatenate(heads, axis=1).astype(BF)
        return 0

    lax.fori_loop(0, 4, window, 0, unroll=True)


def forward(x, gain, qkv, main, tail, code):
    return pl.pallas_call(
        forward_kernel,
        out_shape=(
            shape((576, 192), BF),
            shape((576, 96), BF),
            shape((576, 96), BF),
            shape((576, 96), BF),
            shape((12, 144, 144), F32),
            shape((576, 96), BF),
        ),
        scratch_shapes=[pltpu.VMEM((576, 192), F32)],
        compiler_params=VM,
        cost_estimate=cost(5),
        name="forward",
    )(*x, level_order(), gain, qkv, main, tail, code)


def backward_kernel(g0, g1, g2, g3, order_ref, proj_ref, qkv_ref, q_ref, k_ref, v_ref, prob_ref,
                    part_ref, score_ref, end_ref, gcols, grad_ref, scratch, gatt):
    to_windows((g0, g1, g2, g3), order_ref[...], scratch)
    grad = scratch[...].astype(BF)
    grad_ref[...] = grad
    gatt[...] = dot_nt(grad, proj_ref[...]).astype(BF)

    def window(w, _):
        rows = pl.ds(pl.multiple_of(w * 144, 16), 144)
        query, key, value, above = q_ref[rows, :], k_ref[rows, :], v_ref[rows, :], gatt[rows, :]
        queries, keys, values = [], [], []
        for h in range(3):
            cols = slice(h * HD, h * HD + HD)
            prob = prob_ref[w * 3 + h]
            values.append(dot_tn(above[:, cols], prob.astype(BF)))
            grad_prob = dot_nt(above[:, cols], value[:, cols])
            score = prob * (grad_prob - jnp.sum(grad_prob * prob, axis=-1, keepdims=True))
            score_ref[w * 3 + h] = score[:, 0:128]
            end_ref[w * 3 + h, :, 0:16] = score[:, 128:144]
            low_score = (score * (HD ** -0.5)).astype(BF)
            queries.append(dot_nn(low_score, key[:, cols]))
            keys.append(dot_tn(query[:, cols], low_score))
        gcols[0, rows, :] = jnp.concatenate(queries, axis=1).astype(BF)
        gcols[1, rows, :] = jnp.concatenate(keys, axis=0).T.astype(BF)
        gcols[2, rows, :] = jnp.concatenate(values, axis=0).T.astype(BF)
        return 0

    lax.fori_loop(0, 4, window, 0, unroll=True)
    total = None
    for j in range(3):
        term = dot_nt(gcols[j], qkv_ref[j])
        total = term if total is None else total + term
    scratch[...] = total
    for s in range(4):
        pieces = [scratch[w * 144 + s * 36 : w * 144 + s * 36 + 36, :] for w in range(4)]
        piece = jnp.concatenate(pieces, axis=0).astype(BF)
        part_ref[s * 144 : s * 144 + 144, :] = dot_tn(order_ref[...], piece).astype(BF)


def backward(g, proj, qkv, q, k, v, prob):
    return pl.pallas_call(
        backward_kernel,
        out_shape=(
            shape((576, 192), BF),
            shape((12, 144, 128), F32),
            shape((12, 144, 128), F32),
            shape((3, 576, 96), BF),
            shape((576, 192), BF),
        ),
        scratch_shapes=[pltpu.VMEM((576, 192), F32), pltpu.VMEM((576, 96), BF)],
        compiler_params=VM,
        cost_estimate=cost(7),
        name="backward",
    )(*g, level_order(), proj, qkv, q, k, v, prob)


def scatter_kernel(score_ref, end_ref, lo_ref, hi_ref, after_ref, out_ref, tails):
    total = jnp.zeros((256, 192), F32)
    place = lax.broadcasted_iota(I32, (16, 128), 0)
    group = lax.broadcasted_iota(I32, (18, 128), 1) >> 4
    for r in range(12):
        packed = end_ref[r, pl.ds(0, 18, stride=8), :]
        for j in range(1, 8):
            moved_on = pltpu.roll(end_ref[r, pl.ds(j, 18, stride=8), :], 16 * j, 1)
            packed = jnp.where(group == j, moved_on, packed)
        tails[r, 0:18, :] = packed
    for i in range(9):
        left, right = [], []
        for j in range(18):
            row = slice(i * 18 + j, i * 18 + j + 1)
            here = place == hi_ref[row, :]
            right.append(one_hot(lo_ref[row, :]))
            lines = [score_ref[r, row, :] if i < 8 else tails[r, j : j + 1, :] for r in range(12)]
            left.append(jnp.concatenate([jnp.where(here, line, 0.0).astype(BF) for line in lines], axis=0))
        total = total + dot_nt(jnp.concatenate(right, axis=1), jnp.concatenate(left, axis=1))
    out_ref[...] = total.T


def scatter(score, end, lo, hi, after):
    return pl.pallas_call(
        scatter_kernel,
        out_shape=shape((192, 256), F32),
        in_specs=[VMEM] * 4 + [ANY],
        scratch_shapes=[pltpu.VMEM((12, 24, 128), F32)],
        compiler_params=VM,
        cost_estimate=cost(4),
        name="scatter",
    )(score, end, lo, hi, after)


def weigh_kernel(low_ref, gcols, att_ref, grad_ref, keep_ref, send_ref, grads_ref):
    gproj = dot_tn(att_ref[...], grad_ref[...]).astype(BF)
    grads_ref[0:96, :] = gproj[:, 0:128]
    grads_ref[96:144, :] = jnp.concatenate([gproj[0:48, 128:192], gproj[48:96, 128:192]], axis=1)
    low = low_ref[...]
    a, b, c = [dot_tn(low, gcols[j]).astype(BF) for j in range(3)]
    grads_ref[144:336, :] = jnp.concatenate([a, c[:, 0:32]], axis=1)
    grads_ref[336:528, :] = jnp.concatenate([b, c[:, 32:64]], axis=1)
    grads_ref[528:576, :] = jnp.concatenate([c[i * 48 : i * 48 + 48, 64:96] for i in range(4)], axis=1)
    core = lax.rem(lax.axis_index("lat"), 2)
    keep_ref[...] = grads_ref[pl.ds(pl.multiple_of(core * 288, 16), 288), :]
    send_ref[...] = grads_ref[pl.ds(pl.multiple_of((1 - core) * 288, 16), 288), :]


def weigh(low, gcols, att, grad):
    return pl.pallas_call(
        weigh_kernel,
        out_shape=(shape((288, 128), BF), shape((288, 128), BF)),
        scratch_shapes=[pltpu.VMEM((576, 128), BF)],
        compiler_params=VM,
        cost_estimate=cost(0.5),
        name="weigh",
    )(low, gcols, att, grad)


def gain_rows(line):
    none = jnp.zeros((1, 64), F32)
    return [line[:, 0:128], jnp.concatenate([line[:, 128:192], none], axis=1)]


def pack_kernel(first_ref, first_other, second_ref, second_other, table_ref, gain_ref, out_ref):
    out_ref[0:576, :] = both(first_ref[...], first_other[...])
    out_ref[576:864, :] = both(second_ref[...], second_other[...])
    rows = []
    for r in range(12):
        pair = table_ref[r * 16 : r * 16 + 13, :]
        rows += [pair[:, 0:128], pair[:, 128:256]]
    rows += gain_rows(gain_ref[...]) + [jnp.zeros((102, 128), F32)]
    out_ref[864:1280, :] = jnp.concatenate(rows, axis=0).astype(BF)


def pack(first, first_other, second, second_other, table, gain):
    return pl.pallas_call(
        pack_kernel, out_shape=shape((1280, 128), BF), compiler_params=VM, cost_estimate=cost(1), name="pack"
    )(first, first_other, second, second_other, table, gain)


def meet_kernel(own_ref, other_ref, x0, x1, x2, x3, g0, g1, g2, g3, gain_out):
    gain = jnp.zeros((1, 192), F32)
    for s, (x, g) in enumerate(zip((x0, x1, x2, x3), (g0, g1, g2, g3))):
        rows = slice(s * 144, s * 144 + 144)
        grad = own_ref[rows, :].astype(F32) + other_ref[rows, :].astype(F32)
        normed, _ = layer_stats(x[...].astype(F32))
        gain = gain + jnp.sum(grad * normed, axis=0, keepdims=True)
        g[...] = grad.astype(BF)
    gain_out[...] = jnp.concatenate(gain_rows(gain) + [jnp.zeros((6, 128), F32)], axis=0)


def meet(own, other, x):
    return pl.pallas_call(
        meet_kernel,
        out_shape=tuple(shape((144, 192), BF) for _ in range(4)) + (shape((8, 128), F32),),
        compiler_params=VM,
        cost_estimate=cost(1),
        name="meet",
    )(own, other, *x)


def finish_kernel(x0, x1, x2, x3, m0, m1, m2, m3, g0, g1, g2, g3, gain_ref, out_ref):
    for q, (x, m, g) in enumerate(zip((x0, x1, x2, x3), (m0, m1, m2, m3), (g0, g1, g2, g3))):
        normed, inverse = layer_stats(x[...].astype(F32))
        rows = m[...].astype(F32) + norm_backward(g[...].astype(F32), gain_ref[...], normed, inverse)
        for lat in range(3):
            piece = rows[lat * 48 : lat * 48 + 48].reshape(6, 8, 192)
            out_ref[(q // 2) * 3 + lat, (q % 2) * 6 : (q % 2) * 6 + 6] = piece.astype(BF)


def finish(x, m, g, gain):
    return pl.pallas_call(
        finish_kernel,
        out_shape=shape((6, 12, 8, 192), BF),
        compiler_params=VM,
        cost_estimate=cost(1),
        name="finish",
    )(*x, *m, *g, gain)


def add_kernel(got_ref, gain_ref, b0, b1, b2, out_ref):
    total = got_ref[0].astype(F32)
    for i in range(1, 32):
        total = total + got_ref[i].astype(F32)
    out_ref[...] = jnp.concatenate([total, gain_ref[...]], axis=0).astype(BF)


def add(got, gain, after):
    return pl.pallas_call(
        add_kernel,
        out_shape=shape((48, 128), BF),
        in_specs=[VMEM] * 2 + [ANY] * 3,
        compiler_params=VM,
        cost_estimate=cost(1),
        name="add",
    )(got, gain, *after)


def spread_kernel(own_ref, other_ref, out_ref):
    own = own_ref[...].astype(F32)
    place = lax.broadcasted_iota(I32, (48, 128), 0)
    row = lax.axis_index("lon") * 40 + place
    table = (row >= 864) & (row < 1176) & (place < 40)
    total = own + jnp.where(table, 0.0, other_ref[...].astype(F32))
    out_ref[...] = jnp.broadcast_to(total.astype(BF)[None], (32, 48, 128))


def spread(own, other):
    return pl.pallas_call(
        spread_kernel, out_shape=shape((32, 48, 128), BF), compiler_params=VM, cost_estimate=cost(1), name="spread"
    )(own, other)


def unpack_kernel(weight_scale, table_scale, own_ref, other_ref,
                  qkv_ref, proj_ref, upg_ref, down_ref, one_ref, two_ref, table_ref):
    swap = lax.rem(lax.axis_index("lat"), 2) == 1
    fields = []
    gain = jnp.zeros((8, 128), F32)
    for ref in (own_ref, other_ref):
        pieces = [ref[c].astype(F32) for c in range(32)]
        fields.append(jnp.concatenate([piece[0:40] for piece in pieces], axis=0))
        for piece in pieces:
            gain = gain + piece[40:48]
    own, other = fields[0][0:864] * weight_scale, fields[1][0:864] * weight_scale
    lower, upper = jnp.where(swap, other, own), jnp.where(swap, own, other)
    for j in range(3):
        upg_ref[:, j * 128 : j * 128 + 128] = lower[j * 192 : j * 192 + 192]
        down_ref[:, j * 128 : j * 128 + 128] = upper[j * 192 : j * 192 + 192]
    second = jnp.concatenate([lower[576:864], upper[576:864]], axis=0)
    proj_ref[:, 0:128] = second[0:96]
    proj_ref[0:48, 128:192] = second[96:144, 0:64]
    proj_ref[48:96, 128:192] = second[96:144, 64:128]
    qkv_ref[0] = second[144:336, 0:96]
    qkv_ref[1] = second[336:528, 0:96]
    qkv_ref[2, :, 0:32] = second[144:336, 96:128]
    qkv_ref[2, :, 32:64] = second[336:528, 96:128]
    for i in range(4):
        qkv_ref[2, i * 48 : i * 48 + 48, 64:96] = second[528:576, i * 32 : i * 32 + 32]
    table = fields[0][864:1176]
    for r in range(12):
        for half in range(2):
            piece = table[r * 26 + half * 13 : r * 26 + half * 13 + 13] * table_scale
            for a in range(13):
                start = a * 256 + half * 128
                wide = min(128, 3312 - start)
                table_ref[r % 3, r // 3 : r // 3 + 1, start : start + wide] = piece[a : a + 1, 0:wide]
    for rows, out in ((gain, one_ref), (fields[0][1176:1184] + fields[1][1176:1184], two_ref)):
        line = rows[0:1]
        later = jnp.concatenate([line[:, 96:128], rows[1:2, 0:64]], axis=1)
        out[...] = jnp.where(lax.axis_index("tp") == 0, line[:, 0:96], later) * weight_scale


def unpack(weight_scale, table_scale, got, other):
    return pl.pallas_call(
        functools.partial(unpack_kernel, weight_scale, table_scale),
        out_shape=(
            shape((3, 192, 96), F32),
            shape((96, 192), F32),
            shape((192, 384), F32),
            shape((192, 384), F32),
            shape((1, 96), F32),
            shape((1, 96), F32),
            shape((3, 4, 3312), F32),
        ),
        compiler_params=VM,
        name="unpack",
    )(got, other)


def moved(value, band, sector, half):
    sizes = [lax.axis_size(name) for name in ("lat", "lon", "tp")]
    pairs = []
    for a in range(sizes[0]):
        for b in range(sizes[1]):
            for c in range(sizes[2]):
                source = ((a + band) % sizes[0], (b + sector) % sizes[1], (c + half) % sizes[2])
                pairs.append(tuple((x * sizes[1] + y) * sizes[2] + z for x, y, z in (source, (a, b, c))))
    return lax.ppermute(value, ("lat", "lon", "tp"), pairs)


def shifted_parts(quarters):
    return (
        quarters[3],
        moved(quarters[2], 0, 1, 0),
        moved(quarters[1], 1, 0, 0),
        moved(quarters[0], 1, 1, 0),
    )


def other_core(value):
    return lax.ppermute(value, "lat", [(a, a ^ 1) for a in range(lax.axis_size("lat"))])


def local(
    inputs,
    residual_mid,
    grad_out,
    mask_ids,
    key_valid,
    bias_index,
    pos_bias,
    norm1_gain,
    qkv_weight,
    proj_weight,
    norm2_gain,
    fc1_weight,
    fc2_weight,
):
    levels, lat_cells, lon_cells, channels = inputs.shape
    cell_count = levels * lat_cells * lon_cells
    weight_scale = (cell_count * lax.axis_size("lat") * lax.axis_size("lon")) ** (-0.5)
    table_scale = (lon_cells * lax.axis_size("lon") // 12) ** (-0.5)
    gain1, gain2 = norm1_gain.reshape(1, -1), norm2_gain.reshape(1, -1)

    def turned(field):
        return field.transpose(1, 2, 0, 3)

    x_in, mid_in, up_in = turned(inputs), turned(residual_mid), turned(grad_out)
    *x, part2, first, first_send = head(x_in, mid_in, up_in, gain2, fc1_weight, fc2_weight.T)
    other2 = moved(part2, 0, 0, 1)
    xw = shifted_parts(x)
    stage, lo, hi, terms, code = gather_first(
        bias_index, pos_bias[0].transpose(1, 0, 2), mask_ids.transpose(1, 0, 2), key_valid.transpose(1, 0, 2)
    )
    *gm, gain_two = middle(mid_in, up_in, part2, other2, gain2, lo)
    gw = shifted_parts(gm)
    main, tail = gather_second(stage, lo, hi, terms, (gain_two, *xw[1:]))
    low, q, k, v, prob, att = forward(xw, gain1, qkv_weight, main, tail, code)
    part1, score, end, gcols, grad = backward(gw, proj_weight, qkv_weight, q, k, v, prob)
    other1 = moved(part1, 0, 0, 1)
    second, second_send = weigh(low, gcols, att, grad)
    table = scatter(score, end, lo, hi, second)
    sums = pack(first, other_core(first_send), second, other_core(second_send), table, gain_two)
    *g, gain_one = meet(part1, other1, xw)
    back = (moved(g[3], -1, -1, 0), moved(g[2], -1, 0, 0), moved(g[1], 0, -1, 0), g[0])
    own = add(lax.all_to_all(sums.reshape(32, 40, 128), "lon", 0, 0), gain_one, back[:3])
    totals = spread(own, moved(own, 2, 0, 0))
    result = finish(x, gm, back, gain1)
    got = lax.all_to_all(totals, "lon", 0, 0)
    qkv_out, proj_out, up_out, down_out, one, two, table_out = unpack(
        weight_scale, table_scale, got, other_core(got)
    )
    return (
        result.transpose(2, 0, 1, 3),
        qkv_out,
        proj_out,
        up_out,
        down_out.T,
        one.reshape(channels // lax.axis_size("tp")),
        two.reshape(channels // lax.axis_size("tp")),
        table_out.transpose(1, 0, 2)[None],
    )


def solution(mesh):
    return jax.shard_map(
        local,
        mesh=mesh,
        in_specs=(
            P(None, "lat", "lon", None),
            P(None, "lat", "lon", None),
            P(None, "lat", "lon", None),
            P(None, "lat", "lon"),
            P(None, "lat", "lon"),
            P(),
            P("lat", None, "tp", None),
            P(),
            P(None, None, "tp"),
            P("tp", None),
            P(),
            P(None, "tp"),
            P("tp", None),
        ),
        out_specs=(
            P(None, "lat", "lon", None),
            P(None, None, "tp"),
            P("tp", None),
            P(None, "tp"),
            P("tp", None),
            P("tp"),
            P("tp"),
            P("lat", None, "tp", None),
        ),
        check_vma=False,
    )
```

```python
import functools

import jax
import jax.numpy as jnp
import numpy as np
from jax import lax
from jax.experimental import pallas as pl
from jax.experimental.pallas import tpu as pltpu
from jax.sharding import PartitionSpec as P

HD = 32
EPSILON = 1e-05
EXCLUDED = -1e30
BF = jnp.bfloat16
F32 = jnp.float32
I32 = jnp.int32
VMEM = pl.BlockSpec(memory_space=pltpu.VMEM)
VM = pltpu.CompilerParams(vmem_limit_bytes=24 * 1024 * 1024)
ALL = pltpu.CompilerParams(vmem_limit_bytes=63 * 1024 * 1024)
SMEM = pl.BlockSpec(memory_space=pltpu.SMEM)
ANY = pl.BlockSpec(memory_space=pl.ANY)


def cost(microseconds):
    return pl.CostEstimate(flops=int(microseconds * 1e9), bytes_accessed=0, transcendentals=0)


def shape(dims, kind):
    return jax.ShapeDtypeStruct(dims, kind)


def both(own, other):
    return (own.astype(F32) + other.astype(F32)).astype(BF)


def dot_nn(a, b):
    return lax.dot_general(a, b, (((1,), (0,)), ((), ())), preferred_element_type=F32)


def dot_nt(a, b):
    return lax.dot_general(a, b, (((1,), (1,)), ((), ())), preferred_element_type=F32)


def dot_tn(a, b):
    return lax.dot_general(a, b, (((0,), (0,)), ((), ())), preferred_element_type=F32)


def layer_stats(rows):
    mean = jnp.mean(rows, axis=-1, keepdims=True)
    centred = rows - mean
    inverse = lax.rsqrt(jnp.mean(centred * centred, axis=-1, keepdims=True) + EPSILON)
    return centred * inverse, inverse


def norm_backward(grad_normed, gain, normed, inverse):
    scaled = grad_normed * gain
    first = jnp.mean(scaled, axis=-1, keepdims=True)
    second = jnp.mean(scaled * normed, axis=-1, keepdims=True)
    return (scaled - first - normed * second) * inverse


def gelu_pair(pre):
    cdf = 0.5 * (1.0 + lax.erf(pre * 0.7071067811865476))
    pdf = 0.3989422804014327 * jnp.exp(-0.5 * pre * pre)
    return pre * cdf, cdf + pre * pdf


def to_quarters(field_ref, scratch):
    for lat in range(6):
        for half in range(2):
            rows = field_ref[lat, half * 6 : half * 6 + 6].astype(F32).reshape(48, 192)
            start = ((lat // 3) * 2 + half) * 144 + (lat % 3) * 48
            scratch[start : start + 48, :] = rows


def level_order():
    order = np.zeros((144, 144), np.float32)
    for w in range(4):
        for cell in range(18):
            for level in range(2):
                order[w * 36 + cell * 2 + level, cell * 8 + (2 * w + 1 + level) % 8] = 1.0
    return jnp.asarray(order, BF)


def to_windows(parts, order, scratch):
    for s in range(4):
        rows = dot_nn(order, parts[s][...])
        for w in range(4):
            scratch[w * 144 + s * 36 : w * 144 + s * 36 + 36, :] = rows[w * 36 : w * 36 + 36]


def head_kernel(x_hbm, mid_hbm, up_hbm, gain_hbm, fc1_hbm, fc2_hbm, o0, o1, o2, o3, part_hbm, keep_hbm, send_hbm,
                x_ref, mid_ref, up_ref, gain_ref, fc1_ref, fc2_ref, xq_ref, part_ref, grads_ref, x_s, mid_s, up_s, sem):
    pairs = (
        (mid_hbm, mid_ref),
        (gain_hbm, gain_ref),
        (fc1_hbm, fc1_ref),
        (up_hbm, up_ref),
        (fc2_hbm, fc2_ref),
        (x_hbm, x_ref),
    )
    copies = [pltpu.make_async_copy(a, b, sem.at[i]) for i, (a, b) in enumerate(pairs)]
    for copy in copies:
        copy.start()
    for copy in copies[:3]:
        copy.wait()
    to_quarters(mid_ref, mid_s)
    normed, _ = layer_stats(mid_s[...])
    lowered = (normed * gain_ref[...]).astype(BF)
    pre = dot_nn(lowered, fc1_ref[...])
    active, slopes = gelu_pair(pre)
    for copy in copies[3:]:
        copy.wait()
    to_quarters(x_ref, x_s)
    writes = []
    for q, out in enumerate((o0, o1, o2, o3)):
        xq_ref[q] = x_s[q * 144 : q * 144 + 144, :].astype(BF)
        writes.append(pltpu.make_async_copy(xq_ref.at[q], out, sem.at[8 + q]))
        writes[-1].start()
    to_quarters(up_ref, up_s)
    up = up_s[...].astype(BF)
    grad_pre = (dot_nn(up, fc2_ref[...]) * slopes).astype(BF)
    part_ref[...] = dot_nt(grad_pre, fc1_ref[...]).astype(BF)
    writes.append(pltpu.make_async_copy(part_ref, part_hbm, sem.at[6]))
    writes[-1].start()
    for start, grads in ((0, dot_tn(lowered, grad_pre)), (576, dot_tn(up, active.astype(BF)))):
        for j in range(3):
            grads_ref[start + j * 192 : start + j * 192 + 192, :] = grads[:, j * 128 : j * 128 + 128].astype(BF)
    core = lax.rem(lax.axis_index("lat"), 2)
    for i, (half, out) in enumerate(((core, keep_hbm), (1 - core, send_hbm))):
        piece = grads_ref.at[pl.ds(pl.multiple_of(half * 576, 16), 576)]
        writes.append(pltpu.make_async_copy(piece, out, sem.at[12 + i]))
        writes[-1].start()
    for write in writes:
        write.wait()


def head(x, mid, up, gain, fc1, fc2):
    return pl.pallas_call(
        head_kernel,
        out_shape=tuple(shape((144, 192), BF) for _ in range(4))
        + (shape((576, 192), BF), shape((576, 128), BF), shape((576, 128), BF)),
        in_specs=[ANY] * 6,
        out_specs=tuple(ANY for _ in range(7)),
        scratch_shapes=[
            pltpu.VMEM((6, 12, 8, 192), BF),
            pltpu.VMEM((6, 12, 8, 192), BF),
            pltpu.VMEM((6, 12, 8, 192), BF),
            pltpu.VMEM((1, 192), F32),
            pltpu.VMEM((192, 384), BF),
            pltpu.VMEM((192, 384), BF),
            pltpu.VMEM((4, 144, 192), BF),
            pltpu.VMEM((576, 192), BF),
            pltpu.VMEM((1152, 128), BF),
            pltpu.VMEM((576, 192), F32),
            pltpu.VMEM((576, 192), F32),
            pltpu.VMEM((576, 192), F32),
            pltpu.SemaphoreType.DMA((14,)),
        ],
        compiler_params=ALL,
        cost_estimate=cost(3),
        name="head",
    )(x, mid, up, gain, fc1, fc2)


def middle_kernel(mid_ref, up_ref, own_ref, other_ref, gain_ref, after_ref, o0, o1, o2, o3, gain_out, mid_s, up_s):
    to_quarters(mid_ref, mid_s)
    to_quarters(up_ref, up_s)
    normed, inverse = layer_stats(mid_s[...])
    grad = own_ref[...].astype(F32) + other_ref[...].astype(F32)
    gain_out[...] = jnp.sum(grad * normed, axis=0, keepdims=True)
    out = up_s[...] + norm_backward(grad, gain_ref[...], normed, inverse)
    for q, o in enumerate((o0, o1, o2, o3)):
        o[...] = out[q * 144 : q * 144 + 144].astype(BF)


def middle(mid, up, own, other, gain, after):
    return pl.pallas_call(
        middle_kernel,
        out_shape=tuple(shape((144, 192), BF) for _ in range(4)) + (shape((1, 192), F32),),
        in_specs=[VMEM] * 5 + [ANY],
        scratch_shapes=[pltpu.VMEM((576, 192), F32)] * 2,
        compiler_params=VM,
        cost_estimate=cost(1),
        name="middle",
    )(mid, up, own, other, gain, after)


def window_order():
    canon = np.arange(144).reshape(2, 2, 3, 2, 6).transpose(1, 3, 2, 4, 0).reshape(-1)
    order = np.zeros((144, 144), np.float32)
    order[np.arange(144), canon] = 1.0
    return order


def pack_tail(tail):
    spread = (lax.broadcasted_iota(I32, (16, 128), 1) & 15) == lax.broadcasted_iota(I32, (16, 128), 0)
    wide = dot_nn(tail, spread.astype(F32).astype(BF))
    here = (lax.broadcasted_iota(I32, (144, 128), 1) >> 4) == (lax.broadcasted_iota(I32, (144, 128), 0) & 7)
    wide = jnp.where(here, wide, 0.0).astype(BF)
    rows = (lax.broadcasted_iota(I32, (24, 144), 1) >> 3) == lax.broadcasted_iota(I32, (24, 144), 0)
    return dot_nn(rows.astype(F32).astype(BF), wide)


def one_hot(low):
    rows = lax.broadcasted_iota(I32, (256, 128), 0).astype(F32).astype(BF)
    return jnp.where(rows == low.astype(F32).astype(BF), jnp.ones((), BF), jnp.zeros((), BF))


def look_up(terms, lo_ref, hi_ref, stage, first_block, steps):
    half = (lax.broadcasted_iota(I32, (8, 128), 0) >> 2)

    def step(i, _):
        for pair in range(9):
            base = first_block + i * 18 + pair * 2
            hot = jnp.concatenate([one_hot(lo_ref[pl.ds(base + j, 1), :]) for j in range(2)], axis=1)
            found = dot_nn(terms, jnp.concatenate([hot, hot], axis=0))
            for j in range(2):
                cols = slice(j * 128, j * 128 + 128)
                high = hi_ref[pl.ds(base + j, 1), :]
                first = jnp.zeros((8, 128), F32)
                for c in range(13):
                    first = jnp.where(high == c, found[c * 8 : c * 8 + 8, cols], first)
                second = jnp.zeros((8, 128), F32)
                shifted = high - half
                for c in range(7):
                    second = jnp.where(shifted == 2 * c, found[104 + c * 8 : 112 + c * 8, cols], second)
                start = pl.multiple_of((base + j - first_block) * 16, 16)
                stage[pl.ds(start, 8), :] = first
                stage[pl.ds(start + 8, 8), :] = second + pltpu.roll(second, 4, 0)
        return 0

    lax.fori_loop(0, steps, step, 0, unroll=True)


def gather_first_kernel(index_ref, order_ref, bias_ref, ids_ref, valid_ref,
                        stage, lo_ref, hi_ref, terms_ref, code_ref, table):
    index = index_ref[...]
    order = order_ref[...]
    pieces = []
    for part in (index & 127, index >> 7):
        moved = dot_nt(dot_nn(order, part.astype(F32).astype(BF)).astype(BF), order)
        pieces.append((moved[:, 0:128].astype(I32), pack_tail(moved[:, 128:144].astype(BF)).astype(I32)))
    for rows, low, high in ((slice(0, 144), pieces[0][0], pieces[1][0]), (slice(144, 168), pieces[0][1], pieces[1][1])):
        lo_ref[rows, :] = low + (high & 1) * 128
        hi_ref[rows, :] = high >> 1
    table[...] = jnp.zeros((160, 256), F32)
    for r in range(12):
        line = bias_ref[r % 3, r // 3 : r // 3 + 1, :]
        line = line - jnp.max(line, axis=1, keepdims=True)
        for c in range(13):
            wide = min(256, 3312 - c * 256)
            row = c * 8 + r if r < 8 else 104 + (c // 2) * 8 + (c % 2) * 4 + r - 8
            table[row : row + 1, 0:wide] = line[:, c * 256 : c * 256 + wide]
    upper = table[...].astype(BF)
    terms_ref[:, 0:256] = upper
    terms_ref[:, 256:512] = (table[...] - upper.astype(F32)).astype(BF)
    code = (ids_ref[...] * 2 + (valid_ref[...] > 0).astype(I32)).astype(F32).reshape(48, 12).astype(BF)
    row = lax.broadcasted_iota(I32, (24, 48), 0)
    column = lax.broadcasted_iota(I32, (24, 48), 1)
    lines = []
    for level in range(2):
        pick = ((row >> 2) * 8 + (row & 3) * 2 + level) == column
        picked = dot_nn(pick.astype(F32).astype(BF), code)
        lines += [picked[lat * 4 : lat * 4 + 4] for lat in range(6)]
    lines = jnp.concatenate(lines, axis=1)
    code_ref[...] = dot_nt(lines.astype(BF), order)
    look_up(terms_ref[...], lo_ref, hi_ref, stage, 0, 5)


def gather_first(index, bias, ids, valid):
    return pl.pallas_call(
        gather_first_kernel,
        out_shape=(
            shape((90 * 16, 128), F32),
            shape((168, 128), I32),
            shape((168, 128), I32),
            shape((160, 512), BF),
            shape((4, 144), F32),
        ),
        scratch_shapes=[pltpu.VMEM((160, 256), F32)],
        compiler_params=VM,
        cost_estimate=cost(0.5),
        name="gather_first",
    )(index, jnp.asarray(window_order(), BF), bias, ids, valid)


def gather_second_kernel(first_stage, lo_ref, hi_ref, terms_ref, a0, a1, a2, a3, main_ref, tail_ref, stage):
    look_up(terms_ref[...], lo_ref, hi_ref, stage, 90, 4)
    for r in range(12):
        main_ref[r, 0:90, :] = first_stage[pl.ds(r, 90, stride=16), :]
        main_ref[r, 90:144, :] = stage[pl.ds(r, 54, stride=16), :]
        packed = stage[pl.ds(54 * 16 + r, 18, stride=16), :]
        for s in range(8):
            tail_ref[r, pl.ds(s, 18, stride=8), :] = pltpu.roll(packed, 128 - 16 * s, 1) if s else packed


def gather_second(first_stage, lo, hi, terms, after):
    return pl.pallas_call(
        gather_second_kernel,
        out_shape=(shape((12, 144, 128), F32), shape((12, 144, 128), F32)),
        in_specs=[VMEM] * 4 + [ANY] * 4,
        scratch_shapes=[pltpu.VMEM((72 * 16, 128), F32)],
        compiler_params=VM,
        cost_estimate=cost(4),
        name="gather_second",
    )(first_stage, lo, hi, terms, *after)


def forward_kernel(x0, x1, x2, x3, order_ref, gain_ref, qkv_ref, main_ref, tail_ref, code_ref,
                   low_ref, q_ref, k_ref, v_ref, prob_ref, att_ref, scratch):
    to_windows((x0, x1, x2, x3), order_ref[...], scratch)
    normed, _ = layer_stats(scratch[...])
    low = (normed * gain_ref[...]).astype(BF)
    low_ref[...] = low
    for j, out in enumerate((q_ref, k_ref, v_ref)):
        out[...] = dot_nn(low, qkv_ref[j]).astype(BF)
    eye = lax.broadcasted_iota(I32, (144, 144), 0) == lax.broadcasted_iota(I32, (144, 144), 1)

    def window(w, _):
        rows = pl.ds(pl.multiple_of(w * 144, 16), 144)
        code = code_ref[pl.ds(w, 1), :].astype(I32)
        label = code >> 1
        column = jnp.sum(jnp.where(eye, label, 0), axis=1, keepdims=True)
        allowed = eye | ((column == label) & ((code & 1) > 0))
        query, key, value = q_ref[rows, :], k_ref[rows, :], v_ref[rows, :]
        heads = []
        for h in range(3):
            cols = slice(h * HD, h * HD + HD)
            bias = jnp.concatenate([main_ref[w * 3 + h], tail_ref[w * 3 + h][:, 0:16]], axis=1)
            scores = dot_nt(query[:, cols], key[:, cols]) * (HD ** -0.5) + bias
            scores = jnp.where(allowed, scores, EXCLUDED)
            expo = jnp.exp(scores - jnp.max(scores, axis=-1, keepdims=True))
            prob = expo * (1.0 / jnp.sum(expo, axis=-1, keepdims=True))
            prob_ref[w * 3 + h] = prob
            heads.append(dot_nn(prob.astype(BF), value[:, cols]))
        att_ref[rows, :] = jnp.concatenate(heads, axis=1).astype(BF)
        return 0

    lax.fori_loop(0, 4, window, 0, unroll=True)


def forward(x, gain, qkv, main, tail, code):
    return pl.pallas_call(
        forward_kernel,
        out_shape=(
            shape((576, 192), BF),
            shape((576, 96), BF),
            shape((576, 96), BF),
            shape((576, 96), BF),
            shape((12, 144, 144), F32),
            shape((576, 96), BF),
        ),
        scratch_shapes=[pltpu.VMEM((576, 192), F32)],
        compiler_params=VM,
        cost_estimate=cost(5),
        name="forward",
    )(*x, level_order(), gain, qkv, main, tail, code)


def backward_kernel(g0, g1, g2, g3, order_ref, proj_ref, qkv_ref, q_ref, k_ref, v_ref, prob_ref,
                    part_ref, score_ref, end_ref, gcols, grad_ref, scratch, gatt):
    to_windows((g0, g1, g2, g3), order_ref[...], scratch)
    grad = scratch[...].astype(BF)
    grad_ref[...] = grad
    gatt[...] = dot_nt(grad, proj_ref[...]).astype(BF)

    def window(w, _):
        rows = pl.ds(pl.multiple_of(w * 144, 16), 144)
        query, key, value, above = q_ref[rows, :], k_ref[rows, :], v_ref[rows, :], gatt[rows, :]
        queries, keys, values = [], [], []
        for h in range(3):
            cols = slice(h * HD, h * HD + HD)
            prob = prob_ref[w * 3 + h]
            values.append(dot_tn(above[:, cols], prob.astype(BF)))
            grad_prob = dot_nt(above[:, cols], value[:, cols])
            score = prob * (grad_prob - jnp.sum(grad_prob * prob, axis=-1, keepdims=True))
            score_ref[w * 3 + h] = score[:, 0:128]
            end_ref[w * 3 + h, :, 0:16] = score[:, 128:144]
            low_score = (score * (HD ** -0.5)).astype(BF)
            queries.append(dot_nn(low_score, key[:, cols]))
            keys.append(dot_tn(query[:, cols], low_score))
        gcols[0, rows, :] = jnp.concatenate(queries, axis=1).astype(BF)
        gcols[1, rows, :] = jnp.concatenate(keys, axis=0).T.astype(BF)
        gcols[2, rows, :] = jnp.concatenate(values, axis=0).T.astype(BF)
        return 0

    lax.fori_loop(0, 4, window, 0, unroll=True)
    total = None
    for j in range(3):
        term = dot_nt(gcols[j], qkv_ref[j])
        total = term if total is None else total + term
    scratch[...] = total
    for s in range(4):
        pieces = [scratch[w * 144 + s * 36 : w * 144 + s * 36 + 36, :] for w in range(4)]
        piece = jnp.concatenate(pieces, axis=0).astype(BF)
        part_ref[s * 144 : s * 144 + 144, :] = dot_tn(order_ref[...], piece).astype(BF)


def backward(g, proj, qkv, q, k, v, prob):
    return pl.pallas_call(
        backward_kernel,
        out_shape=(
            shape((576, 192), BF),
            shape((12, 144, 128), F32),
            shape((12, 144, 128), F32),
            shape((3, 576, 96), BF),
            shape((576, 192), BF),
        ),
        scratch_shapes=[pltpu.VMEM((576, 192), F32), pltpu.VMEM((576, 96), BF)],
        compiler_params=VM,
        cost_estimate=cost(7),
        name="backward",
    )(*g, level_order(), proj, qkv, q, k, v, prob)


def scatter_kernel(score_ref, end_ref, lo_ref, hi_ref, after_ref, out_ref, tails):
    total = jnp.zeros((256, 192), F32)
    place = lax.broadcasted_iota(I32, (16, 128), 0)
    group = lax.broadcasted_iota(I32, (18, 128), 1) >> 4
    for r in range(12):
        packed = end_ref[r, pl.ds(0, 18, stride=8), :]
        for j in range(1, 8):
            moved_on = pltpu.roll(end_ref[r, pl.ds(j, 18, stride=8), :], 16 * j, 1)
            packed = jnp.where(group == j, moved_on, packed)
        tails[r, 0:18, :] = packed
    for i in range(9):
        left, right = [], []
        for j in range(18):
            row = slice(i * 18 + j, i * 18 + j + 1)
            here = place == hi_ref[row, :]
            right.append(one_hot(lo_ref[row, :]))
            lines = [score_ref[r, row, :] if i < 8 else tails[r, j : j + 1, :] for r in range(12)]
            left.append(jnp.concatenate([jnp.where(here, line, 0.0).astype(BF) for line in lines], axis=0))
        total = total + dot_nt(jnp.concatenate(right, axis=1), jnp.concatenate(left, axis=1))
    out_ref[...] = total.T


def scatter(score, end, lo, hi, after):
    return pl.pallas_call(
        scatter_kernel,
        out_shape=shape((192, 256), F32),
        in_specs=[VMEM] * 4 + [ANY],
        scratch_shapes=[pltpu.VMEM((12, 24, 128), F32)],
        compiler_params=VM,
        cost_estimate=cost(4),
        name="scatter",
    )(score, end, lo, hi, after)


def weigh_kernel(low_ref, gcols, att_ref, grad_ref, first_ref, keep_ref, send_ref, grads_ref):
    gproj = dot_tn(att_ref[...], grad_ref[...]).astype(BF)
    grads_ref[0:96, :] = gproj[:, 0:128]
    grads_ref[96:144, :] = jnp.concatenate([gproj[0:48, 128:192], gproj[48:96, 128:192]], axis=1)
    low = low_ref[...]
    a, b, c = [dot_tn(low, gcols[j]).astype(BF) for j in range(3)]
    grads_ref[144:336, :] = jnp.concatenate([a, c[:, 0:32]], axis=1)
    grads_ref[336:528, :] = jnp.concatenate([b, c[:, 32:64]], axis=1)
    grads_ref[528:576, :] = jnp.concatenate([c[i * 48 : i * 48 + 48, 64:96] for i in range(4)], axis=1)
    core = lax.rem(lax.axis_index("lat"), 2)
    keep_ref[...] = grads_ref[pl.ds(pl.multiple_of(core * 288, 16), 288), :]
    send_ref[0:576, :] = first_ref[...]
    send_ref[576:864, :] = grads_ref[pl.ds(pl.multiple_of((1 - core) * 288, 16), 288), :]


def weigh(low, gcols, att, grad, first):
    return pl.pallas_call(
        weigh_kernel,
        out_shape=(shape((288, 128), BF), shape((864, 128), BF)),
        scratch_shapes=[pltpu.VMEM((576, 128), BF)],
        compiler_params=VM,
        cost_estimate=cost(0.5),
        name="weigh",
    )(low, gcols, att, grad, first)


def gain_rows(line):
    none = jnp.zeros((1, 64), F32)
    return [line[:, 0:128], jnp.concatenate([line[:, 128:192], none], axis=1)]


def pack_kernel(first_ref, second_ref, other_ref, table_ref, gain_ref, out_ref):
    out_ref[0:576, :] = both(first_ref[...], other_ref[0:576, :])
    out_ref[576:864, :] = both(second_ref[...], other_ref[576:864, :])
    rows = []
    for r in range(12):
        pair = table_ref[r * 16 : r * 16 + 13, :]
        rows += [pair[:, 0:128], pair[:, 128:256]]
    rows += gain_rows(gain_ref[...]) + [jnp.zeros((102, 128), F32)]
    out_ref[864:1280, :] = jnp.concatenate(rows, axis=0).astype(BF)


def pack(first, second, other, table, gain):
    return pl.pallas_call(
        pack_kernel, out_shape=shape((1280, 128), BF), compiler_params=VM, cost_estimate=cost(1), name="pack"
    )(first, second, other, table, gain)


def meet_kernel(own_ref, other_ref, x0, x1, x2, x3, g0, g1, g2, g3, gain_out):
    gain = jnp.zeros((1, 192), F32)
    for s, (x, g) in enumerate(zip((x0, x1, x2, x3), (g0, g1, g2, g3))):
        rows = slice(s * 144, s * 144 + 144)
        grad = own_ref[rows, :].astype(F32) + other_ref[rows, :].astype(F32)
        normed, _ = layer_stats(x[...].astype(F32))
        gain = gain + jnp.sum(grad * normed, axis=0, keepdims=True)
        g[...] = grad.astype(BF)
    gain_out[...] = jnp.concatenate(gain_rows(gain) + [jnp.zeros((6, 128), F32)], axis=0)


def meet(own, other, x):
    return pl.pallas_call(
        meet_kernel,
        out_shape=tuple(shape((144, 192), BF) for _ in range(4)) + (shape((8, 128), F32),),
        compiler_params=VM,
        cost_estimate=cost(60),
        name="meet",
    )(own, other, *x)


def finish_kernel(x0, x1, x2, x3, m0, m1, m2, m3, g0, g1, g2, g3, gain_ref, out_ref):
    for q, (x, m, g) in enumerate(zip((x0, x1, x2, x3), (m0, m1, m2, m3), (g0, g1, g2, g3))):
        normed, inverse = layer_stats(x[...].astype(F32))
        rows = m[...].astype(F32) + norm_backward(g[...].astype(F32), gain_ref[...], normed, inverse)
        for lat in range(3):
            piece = rows[lat * 48 : lat * 48 + 48].reshape(6, 8, 192)
            out_ref[(q // 2) * 3 + lat, (q % 2) * 6 : (q % 2) * 6 + 6] = piece.astype(BF)


def finish(x, m, g, gain):
    return pl.pallas_call(
        finish_kernel,
        out_shape=shape((6, 12, 8, 192), BF),
        compiler_params=VM,
        cost_estimate=cost(1),
        name="finish",
    )(*x, *m, *g, gain)


def add_kernel(got_ref, gain_ref, b0, b1, b2, out_ref):
    total = got_ref[0].astype(F32)
    for i in range(1, 32):
        total = total + got_ref[i].astype(F32)
    out_ref[...] = jnp.concatenate([total, gain_ref[...]], axis=0).astype(BF)


def add(got, gain, after):
    return pl.pallas_call(
        add_kernel,
        out_shape=shape((48, 128), BF),
        in_specs=[VMEM] * 2 + [ANY] * 3,
        compiler_params=VM,
        cost_estimate=cost(1),
        name="add",
    )(got, gain, *after)


def spread_kernel(own_ref, other_ref, out_ref):
    own = own_ref[...].astype(F32)
    place = lax.broadcasted_iota(I32, (48, 128), 0)
    row = lax.axis_index("lon") * 40 + place
    table = (row >= 864) & (row < 1176) & (place < 40)
    total = own + jnp.where(table, 0.0, other_ref[...].astype(F32))
    out_ref[...] = jnp.broadcast_to(total.astype(BF)[None], (32, 48, 128))


def spread(own, other):
    return pl.pallas_call(
        spread_kernel, out_shape=shape((32, 48, 128), BF), compiler_params=VM, cost_estimate=cost(1), name="spread"
    )(own, other)


def unpack_kernel(weight_scale, table_scale, own_ref, other_ref,
                  qkv_ref, proj_ref, upg_ref, down_ref, one_ref, two_ref, table_ref):
    swap = lax.rem(lax.axis_index("lat"), 2) == 1
    fields = []
    gain = jnp.zeros((8, 128), F32)
    for ref in (own_ref, other_ref):
        pieces = [ref[c].astype(F32) for c in range(32)]
        fields.append(jnp.concatenate([piece[0:40] for piece in pieces], axis=0))
        for piece in pieces:
            gain = gain + piece[40:48]
    own, other = fields[0][0:864] * weight_scale, fields[1][0:864] * weight_scale
    lower, upper = jnp.where(swap, other, own), jnp.where(swap, own, other)
    for j in range(3):
        upg_ref[:, j * 128 : j * 128 + 128] = lower[j * 192 : j * 192 + 192]
        down_ref[:, j * 128 : j * 128 + 128] = upper[j * 192 : j * 192 + 192]
    second = jnp.concatenate([lower[576:864], upper[576:864]], axis=0)
    proj_ref[:, 0:128] = second[0:96]
    proj_ref[0:48, 128:192] = second[96:144, 0:64]
    proj_ref[48:96, 128:192] = second[96:144, 64:128]
    qkv_ref[0] = second[144:336, 0:96]
    qkv_ref[1] = second[336:528, 0:96]
    qkv_ref[2, :, 0:32] = second[144:336, 96:128]
    qkv_ref[2, :, 32:64] = second[336:528, 96:128]
    for i in range(4):
        qkv_ref[2, i * 48 : i * 48 + 48, 64:96] = second[528:576, i * 32 : i * 32 + 32]
    table = fields[0][864:1176]
    for r in range(12):
        for half in range(2):
            piece = table[r * 26 + half * 13 : r * 26 + half * 13 + 13] * table_scale
            for a in range(13):
                start = a * 256 + half * 128
                wide = min(128, 3312 - start)
                table_ref[r % 3, r // 3 : r // 3 + 1, start : start + wide] = piece[a : a + 1, 0:wide]
    for rows, out in ((gain, one_ref), (fields[0][1176:1184] + fields[1][1176:1184], two_ref)):
        line = rows[0:1]
        later = jnp.concatenate([line[:, 96:128], rows[1:2, 0:64]], axis=1)
        out[...] = jnp.where(lax.axis_index("tp") == 0, line[:, 0:96], later) * weight_scale


def unpack(weight_scale, table_scale, got, other):
    return pl.pallas_call(
        functools.partial(unpack_kernel, weight_scale, table_scale),
        out_shape=(
            shape((3, 192, 96), F32),
            shape((96, 192), F32),
            shape((192, 384), F32),
            shape((192, 384), F32),
            shape((1, 96), F32),
            shape((1, 96), F32),
            shape((3, 4, 3312), F32),
        ),
        compiler_params=VM,
        name="unpack",
    )(got, other)


def moved(value, band, sector, half):
    sizes = [lax.axis_size(name) for name in ("lat", "lon", "tp")]
    pairs = []
    for a in range(sizes[0]):
        for b in range(sizes[1]):
            for c in range(sizes[2]):
                source = ((a + band) % sizes[0], (b + sector) % sizes[1], (c + half) % sizes[2])
                pairs.append(tuple((x * sizes[1] + y) * sizes[2] + z for x, y, z in (source, (a, b, c))))
    return lax.ppermute(value, ("lat", "lon", "tp"), pairs)


def shifted_parts(quarters):
    return (
        quarters[3],
        moved(quarters[2], 0, 1, 0),
        moved(quarters[1], 1, 0, 0),
        moved(quarters[0], 1, 1, 0),
    )


def other_core(value):
    return lax.ppermute(value, "lat", [(a, a ^ 1) for a in range(lax.axis_size("lat"))])


def local(
    inputs,
    residual_mid,
    grad_out,
    mask_ids,
    key_valid,
    bias_index,
    pos_bias,
    norm1_gain,
    qkv_weight,
    proj_weight,
    norm2_gain,
    fc1_weight,
    fc2_weight,
):
    levels, lat_cells, lon_cells, channels = inputs.shape
    cell_count = levels * lat_cells * lon_cells
    weight_scale = (cell_count * lax.axis_size("lat") * lax.axis_size("lon")) ** (-0.5)
    table_scale = (lon_cells * lax.axis_size("lon") // 12) ** (-0.5)
    gain1, gain2 = norm1_gain.reshape(1, -1), norm2_gain.reshape(1, -1)

    def turned(field):
        return field.transpose(1, 2, 0, 3)

    x_in, mid_in, up_in = turned(inputs), turned(residual_mid), turned(grad_out)
    *x, part2, first, first_send = head(x_in, mid_in, up_in, gain2, fc1_weight, fc2_weight.T)
    other2 = moved(part2, 0, 0, 1)
    xw = shifted_parts(x)
    stage, lo, hi, terms, code = gather_first(
        bias_index, pos_bias[0].transpose(1, 0, 2), mask_ids.transpose(1, 0, 2), key_valid.transpose(1, 0, 2)
    )
    *gm, gain_two = middle(mid_in, up_in, part2, other2, gain2, lo)
    gw = shifted_parts(gm)
    main, tail = gather_second(stage, lo, hi, terms, (gain_two, *xw[1:]))
    low, q, k, v, prob, att = forward(xw, gain1, qkv_weight, main, tail, code)
    part1, score, end, gcols, grad = backward(gw, proj_weight, qkv_weight, q, k, v, prob)
    other1 = moved(part1, 0, 0, 1)
    second, send = weigh(low, gcols, att, grad, first_send)
    table = scatter(score, end, lo, hi, second)
    sums = pack(first, second, other_core(send), table, gain_two)
    *g, gain_one = meet(part1, other1, xw)
    back = (moved(g[3], -1, -1, 0), moved(g[2], -1, 0, 0), moved(g[1], 0, -1, 0), g[0])
    own = add(lax.all_to_all(sums.reshape(32, 40, 128), "lon", 0, 0), gain_one, back[:3])
    totals = spread(own, moved(own, 2, 0, 0))
    result = finish(x, gm, back, gain1)
    got = lax.all_to_all(totals, "lon", 0, 0)
    qkv_out, proj_out, up_out, down_out, one, two, table_out = unpack(
        weight_scale, table_scale, got, other_core(got)
    )
    return (
        result.transpose(2, 0, 1, 3),
        qkv_out,
        proj_out,
        up_out,
        down_out.T,
        one.reshape(channels // lax.axis_size("tp")),
        two.reshape(channels // lax.axis_size("tp")),
        table_out.transpose(1, 0, 2)[None],
    )


def solution(mesh):
    return jax.shard_map(
        local,
        mesh=mesh,
        in_specs=(
            P(None, "lat", "lon", None),
            P(None, "lat", "lon", None),
            P(None, "lat", "lon", None),
            P(None, "lat", "lon"),
            P(None, "lat", "lon"),
            P(),
            P("lat", None, "tp", None),
            P(),
            P(None, None, "tp"),
            P("tp", None),
            P(),
            P(None, "tp"),
            P("tp", None),
        ),
        out_specs=(
            P(None, "lat", "lon", None),
            P(None, None, "tp"),
            P("tp", None),
            P(None, "tp"),
            P("tp", None),
            P("tp"),
            P("tp"),
            P("lat", None, "tp", None),
        ),
        check_vma=False,
    )
```

```python
import functools

import jax
import jax.numpy as jnp
import numpy as np
from jax import lax
from jax.experimental import pallas as pl
from jax.experimental.pallas import tpu as pltpu
from jax.sharding import PartitionSpec as P

HD = 32
EPSILON = 1e-05
EXCLUDED = -1e30
BF = jnp.bfloat16
F32 = jnp.float32
I32 = jnp.int32
VMEM = pl.BlockSpec(memory_space=pltpu.VMEM)
VM = pltpu.CompilerParams(vmem_limit_bytes=24 * 1024 * 1024)
ALL = pltpu.CompilerParams(vmem_limit_bytes=63 * 1024 * 1024)
SMEM = pl.BlockSpec(memory_space=pltpu.SMEM)
ANY = pl.BlockSpec(memory_space=pl.ANY)


def cost(microseconds):
    return pl.CostEstimate(flops=int(microseconds * 1e9), bytes_accessed=0, transcendentals=0)


def shape(dims, kind):
    return jax.ShapeDtypeStruct(dims, kind)


def both(own, other):
    return (own.astype(F32) + other.astype(F32)).astype(BF)


def fold(rows):
    return jnp.concatenate(
        [rows[:, 0:128], jnp.concatenate([rows[0:288, 128:192], rows[288:576, 128:192]], axis=1)], axis=0
    )


def unfold(rows):
    return jnp.concatenate(
        [rows[0:576], jnp.concatenate([rows[576:864, 0:64], rows[576:864, 64:128]], axis=0)], axis=1
    )


def dot_nn(a, b):
    return lax.dot_general(a, b, (((1,), (0,)), ((), ())), preferred_element_type=F32)


def dot_nt(a, b):
    return lax.dot_general(a, b, (((1,), (1,)), ((), ())), preferred_element_type=F32)


def dot_tn(a, b):
    return lax.dot_general(a, b, (((0,), (0,)), ((), ())), preferred_element_type=F32)


def layer_stats(rows):
    mean = jnp.mean(rows, axis=-1, keepdims=True)
    centred = rows - mean
    inverse = lax.rsqrt(jnp.mean(centred * centred, axis=-1, keepdims=True) + EPSILON)
    return centred * inverse, inverse


def norm_backward(grad_normed, gain, normed, inverse):
    scaled = grad_normed * gain
    first = jnp.mean(scaled, axis=-1, keepdims=True)
    second = jnp.mean(scaled * normed, axis=-1, keepdims=True)
    return (scaled - first - normed * second) * inverse


def gelu_pair(pre):
    cdf = 0.5 * (1.0 + lax.erf(pre * 0.7071067811865476))
    pdf = 0.3989422804014327 * jnp.exp(-0.5 * pre * pre)
    return pre * cdf, cdf + pre * pdf


def to_quarters(field_ref, scratch):
    for lat in range(6):
        for half in range(2):
            rows = field_ref[lat, half * 6 : half * 6 + 6].astype(F32).reshape(48, 192)
            start = ((lat // 3) * 2 + half) * 144 + (lat % 3) * 48
            scratch[start : start + 48, :] = rows


def level_order():
    order = np.zeros((144, 144), np.float32)
    for w in range(4):
        for cell in range(18):
            for level in range(2):
                order[w * 36 + cell * 2 + level, cell * 8 + (2 * w + 1 + level) % 8] = 1.0
    return jnp.asarray(order, BF)


def to_windows(parts, order, scratch):
    for s in range(4):
        rows = dot_nn(order, parts[s])
        for w in range(4):
            scratch[w * 144 + s * 36 : w * 144 + s * 36 + 36, :] = rows[w * 36 : w * 36 + 36]


def window_parts(own, band, sector):
    return (own[...], sector[0:144, :], band[0:144, :], sector[144:288, :])


def head_kernel(x_hbm, mid_hbm, up_hbm, gain_hbm, fc1_hbm, fc2_hbm, o10, o2, o3, part_hbm, keep_hbm, send_hbm,
                x_ref, mid_ref, up_ref, gain_ref, fc1_ref, fc2_ref, xq_ref, part_ref, grads_ref, x_s, mid_s, up_s, sem):
    pairs = (
        (mid_hbm, mid_ref),
        (gain_hbm, gain_ref),
        (fc1_hbm, fc1_ref),
        (up_hbm, up_ref),
        (fc2_hbm, fc2_ref),
        (x_hbm, x_ref),
    )
    copies = [pltpu.make_async_copy(a, b, sem.at[i]) for i, (a, b) in enumerate(pairs)]
    for copy in copies:
        copy.start()
    for copy in copies[:3]:
        copy.wait()
    to_quarters(mid_ref, mid_s)
    normed, _ = layer_stats(mid_s[...])
    lowered = (normed * gain_ref[...]).astype(BF)
    pre = dot_nn(lowered, fc1_ref[...])
    active, slopes = gelu_pair(pre)
    for copy in copies[3:]:
        copy.wait()
    to_quarters(x_ref, x_s)
    for place, q in enumerate((1, 0, 2, 3)):
        xq_ref[place * 144 : place * 144 + 144, :] = x_s[q * 144 : q * 144 + 144, :].astype(BF)
    writes = []
    for i, (start, size, out) in enumerate(((0, 288, o10), (288, 144, o2), (432, 144, o3))):
        writes.append(pltpu.make_async_copy(xq_ref.at[pl.ds(start, size)], out, sem.at[8 + i]))
        writes[-1].start()
    to_quarters(up_ref, up_s)
    up = up_s[...].astype(BF)
    grad_pre = (dot_nn(up, fc2_ref[...]) * slopes).astype(BF)
    part_ref[...] = fold(dot_nt(grad_pre, fc1_ref[...]).astype(BF))
    writes.append(pltpu.make_async_copy(part_ref, part_hbm, sem.at[6]))
    writes[-1].start()
    for start, grads in ((0, dot_tn(lowered, grad_pre)), (576, dot_tn(up, active.astype(BF)))):
        for j in range(3):
            grads_ref[start + j * 192 : start + j * 192 + 192, :] = grads[:, j * 128 : j * 128 + 128].astype(BF)
    core = lax.rem(lax.axis_index("lat"), 2)
    for i, (half, out) in enumerate(((core, keep_hbm), (1 - core, send_hbm))):
        piece = grads_ref.at[pl.ds(pl.multiple_of(half * 576, 16), 576)]
        writes.append(pltpu.make_async_copy(piece, out, sem.at[12 + i]))
        writes[-1].start()
    for write in writes:
        write.wait()


def head(x, mid, up, gain, fc1, fc2):
    return pl.pallas_call(
        head_kernel,
        out_shape=(
            shape((288, 192), BF),
            shape((144, 192), BF),
            shape((144, 192), BF),
            shape((864, 128), BF),
            shape((576, 128), BF),
            shape((576, 128), BF),
        ),
        in_specs=[ANY] * 6,
        out_specs=tuple(ANY for _ in range(6)),
        scratch_shapes=[
            pltpu.VMEM((6, 12, 8, 192), BF),
            pltpu.VMEM((6, 12, 8, 192), BF),
            pltpu.VMEM((6, 12, 8, 192), BF),
            pltpu.VMEM((1, 192), F32),
            pltpu.VMEM((192, 384), BF),
            pltpu.VMEM((192, 384), BF),
            pltpu.VMEM((576, 192), BF),
            pltpu.VMEM((864, 128), BF),
            pltpu.VMEM((1152, 128), BF),
            pltpu.VMEM((576, 192), F32),
            pltpu.VMEM((576, 192), F32),
            pltpu.VMEM((576, 192), F32),
            pltpu.SemaphoreType.DMA((14,)),
        ],
        compiler_params=ALL,
        cost_estimate=cost(3),
        name="head",
    )(x, mid, up, gain, fc1, fc2)


def middle_kernel(mid_ref, up_ref, own_ref, other_ref, gain_ref, x2_ref, band_ref, after_ref,
                  o0, o1, o2, o3, gain_out, x_out, mid_s, up_s):
    x_out[0:144, :] = x2_ref[...]
    x_out[144:288, :] = band_ref[144:288, :]
    to_quarters(mid_ref, mid_s)
    to_quarters(up_ref, up_s)
    normed, inverse = layer_stats(mid_s[...])
    grad = unfold(own_ref[...].astype(F32) + other_ref[...].astype(F32))
    gain_out[...] = jnp.sum(grad * normed, axis=0, keepdims=True)
    out = up_s[...] + norm_backward(grad, gain_ref[...], normed, inverse)
    for q, o in enumerate((o0, o1, o2, o3)):
        o[...] = out[q * 144 : q * 144 + 144].astype(BF)


def middle(mid, up, own, other, gain, x2, band, after):
    return pl.pallas_call(
        middle_kernel,
        out_shape=tuple(shape((144, 192), BF) for _ in range(4)) + (shape((1, 192), F32), shape((288, 192), BF)),
        in_specs=[VMEM] * 7 + [ANY],
        scratch_shapes=[pltpu.VMEM((576, 192), F32)] * 2,
        compiler_params=VM,
        cost_estimate=cost(1),
        name="middle",
    )(mid, up, own, other, gain, x2, band, after)


def window_order():
    canon = np.arange(144).reshape(2, 2, 3, 2, 6).transpose(1, 3, 2, 4, 0).reshape(-1)
    order = np.zeros((144, 144), np.float32)
    order[np.arange(144), canon] = 1.0
    return order


def pack_tail(tail):
    spread = (lax.broadcasted_iota(I32, (16, 128), 1) & 15) == lax.broadcasted_iota(I32, (16, 128), 0)
    wide = dot_nn(tail, spread.astype(F32).astype(BF))
    here = (lax.broadcasted_iota(I32, (144, 128), 1) >> 4) == (lax.broadcasted_iota(I32, (144, 128), 0) & 7)
    wide = jnp.where(here, wide, 0.0).astype(BF)
    rows = (lax.broadcasted_iota(I32, (24, 144), 1) >> 3) == lax.broadcasted_iota(I32, (24, 144), 0)
    return dot_nn(rows.astype(F32).astype(BF), wide)


def one_hot(low):
    rows = lax.broadcasted_iota(I32, (256, 128), 0).astype(F32).astype(BF)
    return jnp.where(rows == low.astype(F32).astype(BF), jnp.ones((), BF), jnp.zeros((), BF))


def look_up(terms, lo_ref, hi_ref, stage, first_block, steps):
    half = (lax.broadcasted_iota(I32, (8, 128), 0) >> 2)

    def step(i, _):
        for pair in range(9):
            base = first_block + i * 18 + pair * 2
            hot = jnp.concatenate([one_hot(lo_ref[pl.ds(base + j, 1), :]) for j in range(2)], axis=1)
            found = dot_nn(terms, jnp.concatenate([hot, hot], axis=0))
            for j in range(2):
                cols = slice(j * 128, j * 128 + 128)
                high = hi_ref[pl.ds(base + j, 1), :]
                first = jnp.zeros((8, 128), F32)
                for c in range(13):
                    first = jnp.where(high == c, found[c * 8 : c * 8 + 8, cols], first)
                second = jnp.zeros((8, 128), F32)
                shifted = high - half
                for c in range(7):
                    second = jnp.where(shifted == 2 * c, found[104 + c * 8 : 112 + c * 8, cols], second)
                start = pl.multiple_of((base + j - first_block) * 16, 16)
                stage[pl.ds(start, 8), :] = first
                stage[pl.ds(start + 8, 8), :] = second + pltpu.roll(second, 4, 0)
        return 0

    lax.fori_loop(0, steps, step, 0, unroll=True)


def gather_first_kernel(index_ref, order_ref, bias_ref, ids_ref, valid_ref,
                        stage, lo_ref, hi_ref, terms_ref, code_ref, table):
    index = index_ref[...]
    order = order_ref[...]
    pieces = []
    for part in (index & 127, index >> 7):
        moved = dot_nt(dot_nn(order, part.astype(F32).astype(BF)).astype(BF), order)
        pieces.append((moved[:, 0:128].astype(I32), pack_tail(moved[:, 128:144].astype(BF)).astype(I32)))
    for rows, low, high in ((slice(0, 144), pieces[0][0], pieces[1][0]), (slice(144, 168), pieces[0][1], pieces[1][1])):
        lo_ref[rows, :] = low + (high & 1) * 128
        hi_ref[rows, :] = high >> 1
    table[...] = jnp.zeros((160, 256), F32)
    for r in range(12):
        line = bias_ref[r % 3, r // 3 : r // 3 + 1, :]
        line = line - jnp.max(line, axis=1, keepdims=True)
        for c in range(13):
            wide = min(256, 3312 - c * 256)
            row = c * 8 + r if r < 8 else 104 + (c // 2) * 8 + (c % 2) * 4 + r - 8
            table[row : row + 1, 0:wide] = line[:, c * 256 : c * 256 + wide]
    upper = table[...].astype(BF)
    terms_ref[:, 0:256] = upper
    terms_ref[:, 256:512] = (table[...] - upper.astype(F32)).astype(BF)
    code = (ids_ref[...] * 2 + (valid_ref[...] > 0).astype(I32)).astype(F32).reshape(48, 12).astype(BF)
    row = lax.broadcasted_iota(I32, (24, 48), 0)
    column = lax.broadcasted_iota(I32, (24, 48), 1)
    lines = []
    for level in range(2):
        pick = ((row >> 2) * 8 + (row & 3) * 2 + level) == column
        picked = dot_nn(pick.astype(F32).astype(BF), code)
        lines += [picked[lat * 4 : lat * 4 + 4] for lat in range(6)]
    lines = jnp.concatenate(lines, axis=1)
    code_ref[...] = dot_nt(lines.astype(BF), order)
    look_up(terms_ref[...], lo_ref, hi_ref, stage, 0, 7)


def gather_first(index, bias, ids, valid):
    return pl.pallas_call(
        gather_first_kernel,
        out_shape=(
            shape((126 * 16, 128), F32),
            shape((168, 128), I32),
            shape((168, 128), I32),
            shape((160, 512), BF),
            shape((4, 144), F32),
        ),
        scratch_shapes=[pltpu.VMEM((160, 256), F32)],
        compiler_params=VM,
        cost_estimate=cost(0.5),
        name="gather_first",
    )(index, jnp.asarray(window_order(), BF), bias, ids, valid)


def gather_second_kernel(first_stage, lo_ref, hi_ref, terms_ref, a0, a1, main_ref, tail_ref, stage):
    look_up(terms_ref[...], lo_ref, hi_ref, stage, 126, 2)
    for r in range(12):
        main_ref[r, 0:126, :] = first_stage[pl.ds(r, 126, stride=16), :]
        main_ref[r, 126:144, :] = stage[pl.ds(r, 18, stride=16), :]
        packed = stage[pl.ds(18 * 16 + r, 18, stride=16), :]
        for s in range(8):
            tail_ref[r, pl.ds(s, 18, stride=8), :] = pltpu.roll(packed, 128 - 16 * s, 1) if s else packed


def gather_second(first_stage, lo, hi, terms, after):
    return pl.pallas_call(
        gather_second_kernel,
        out_shape=(shape((12, 144, 128), F32), shape((12, 144, 128), F32)),
        in_specs=[VMEM] * 4 + [ANY] * 2,
        scratch_shapes=[pltpu.VMEM((36 * 16, 128), F32)],
        compiler_params=VM,
        cost_estimate=cost(0.2),
        name="gather_second",
    )(first_stage, lo, hi, terms, *after)


def forward_kernel(own_ref, band_ref, sector_ref, order_ref, gain_ref, qkv_ref, main_ref, tail_ref, code_ref,
                   low_ref, q_ref, k_ref, v_ref, prob_ref, att_ref, scratch):
    to_windows(window_parts(own_ref, band_ref, sector_ref), order_ref[...], scratch)
    normed, _ = layer_stats(scratch[...])
    low = (normed * gain_ref[...]).astype(BF)
    low_ref[...] = low
    for j, out in enumerate((q_ref, k_ref, v_ref)):
        out[...] = dot_nn(low, qkv_ref[j]).astype(BF)
    eye = lax.broadcasted_iota(I32, (144, 144), 0) == lax.broadcasted_iota(I32, (144, 144), 1)

    def window(w, _):
        rows = pl.ds(pl.multiple_of(w * 144, 16), 144)
        code = code_ref[pl.ds(w, 1), :].astype(I32)
        label = code >> 1
        column = jnp.sum(jnp.where(eye, label, 0), axis=1, keepdims=True)
        allowed = eye | ((column == label) & ((code & 1) > 0))
        query, key, value = q_ref[rows, :], k_ref[rows, :], v_ref[rows, :]
        heads = []
        for h in range(3):
            cols = slice(h * HD, h * HD + HD)
            bias = jnp.concatenate([main_ref[w * 3 + h], tail_ref[w * 3 + h][:, 0:16]], axis=1)
            scores = dot_nt(query[:, cols], key[:, cols]) * (HD ** -0.5) + bias
            scores = jnp.where(allowed, scores, EXCLUDED)
            expo = jnp.exp(scores - jnp.max(scores, axis=-1, keepdims=True))
            prob = expo * (1.0 / jnp.sum(expo, axis=-1, keepdims=True))
            prob_ref[w * 3 + h] = prob
            heads.append(dot_nn(prob.astype(BF), value[:, cols]))
        att_ref[rows, :] = jnp.concatenate(heads, axis=1).astype(BF)
        return 0

    lax.fori_loop(0, 4, window, 0, unroll=True)


def forward(x, gain, qkv, main, tail, code):
    return pl.pallas_call(
        forward_kernel,
        out_shape=(
            shape((576, 192), BF),
            shape((576, 96), BF),
            shape((576, 96), BF),
            shape((576, 96), BF),
            shape((12, 144, 144), F32),
            shape((576, 96), BF),
        ),
        scratch_shapes=[pltpu.VMEM((576, 192), F32)],
        compiler_params=VM,
        cost_estimate=cost(5),
        name="forward",
    )(*x, level_order(), gain, qkv, main, tail, code)


def backward_kernel(g0, g1, g2, g3, order_ref, proj_ref, qkv_ref, q_ref, k_ref, v_ref, prob_ref,
                    part_ref, score_ref, end_ref, gcols, grad_ref, scratch, gatt):
    to_windows((g0[...], g1[...], g2[...], g3[...]), order_ref[...], scratch)
    grad = scratch[...].astype(BF)
    grad_ref[...] = grad
    gatt[...] = dot_nt(grad, proj_ref[...]).astype(BF)

    def window(w, _):
        rows = pl.ds(pl.multiple_of(w * 144, 16), 144)
        query, key, value, above = q_ref[rows, :], k_ref[rows, :], v_ref[rows, :], gatt[rows, :]
        queries, keys, values = [], [], []
        for h in range(3):
            cols = slice(h * HD, h * HD + HD)
            prob = prob_ref[w * 3 + h]
            values.append(dot_tn(above[:, cols], prob.astype(BF)))
            grad_prob = dot_nt(above[:, cols], value[:, cols])
            score = prob * (grad_prob - jnp.sum(grad_prob * prob, axis=-1, keepdims=True))
            score_ref[w * 3 + h] = score[:, 0:128]
            end_ref[w * 3 + h, :, 0:16] = score[:, 128:144]
            low_score = (score * (HD ** -0.5)).astype(BF)
            queries.append(dot_nn(low_score, key[:, cols]))
            keys.append(dot_tn(query[:, cols], low_score))
        gcols[0, rows, :] = jnp.concatenate(queries, axis=1).astype(BF)
        gcols[1, rows, :] = jnp.concatenate(keys, axis=0).T.astype(BF)
        gcols[2, rows, :] = jnp.concatenate(values, axis=0).T.astype(BF)
        return 0

    lax.fori_loop(0, 4, window, 0, unroll=True)
    total = None
    for j in range(3):
        term = dot_nt(gcols[j], qkv_ref[j])
        total = term if total is None else total + term
    scratch[...] = total
    moved_back = []
    for s in range(4):
        pieces = [scratch[w * 144 + s * 36 : w * 144 + s * 36 + 36, :] for w in range(4)]
        piece = jnp.concatenate(pieces, axis=0).astype(BF)
        moved_back.append(dot_tn(order_ref[...], piece).astype(BF))
    part_ref[...] = fold(jnp.concatenate(moved_back, axis=0))


def backward(g, proj, qkv, q, k, v, prob):
    return pl.pallas_call(
        backward_kernel,
        out_shape=(
            shape((864, 128), BF),
            shape((12, 144, 128), F32),
            shape((12, 144, 128), F32),
            shape((3, 576, 96), BF),
            shape((576, 192), BF),
        ),
        scratch_shapes=[pltpu.VMEM((576, 192), F32), pltpu.VMEM((576, 96), BF)],
        compiler_params=VM,
        cost_estimate=cost(7),
        name="backward",
    )(*g, level_order(), proj, qkv, q, k, v, prob)


def scatter_kernel(score_ref, end_ref, lo_ref, hi_ref, after_ref, out_ref, tails):
    total = jnp.zeros((256, 192), F32)
    place = lax.broadcasted_iota(I32, (16, 128), 0)
    group = lax.broadcasted_iota(I32, (18, 128), 1) >> 4
    for r in range(12):
        packed = end_ref[r, pl.ds(0, 18, stride=8), :]
        for j in range(1, 8):
            moved_on = pltpu.roll(end_ref[r, pl.ds(j, 18, stride=8), :], 16 * j, 1)
            packed = jnp.where(group == j, moved_on, packed)
        tails[r, 0:18, :] = packed
    for i in range(9):
        left, right = [], []
        for j in range(18):
            row = slice(i * 18 + j, i * 18 + j + 1)
            here = place == hi_ref[row, :]
            right.append(one_hot(lo_ref[row, :]))
            lines = [score_ref[r, row, :] if i < 8 else tails[r, j : j + 1, :] for r in range(12)]
            left.append(jnp.concatenate([jnp.where(here, line, 0.0).astype(BF) for line in lines], axis=0))
        total = total + dot_nt(jnp.concatenate(right, axis=1), jnp.concatenate(left, axis=1))
    out_ref[...] = total.T


def scatter(score, end, lo, hi, after):
    return pl.pallas_call(
        scatter_kernel,
        out_shape=shape((192, 256), F32),
        in_specs=[VMEM] * 4 + [ANY],
        scratch_shapes=[pltpu.VMEM((12, 24, 128), F32)],
        compiler_params=VM,
        cost_estimate=cost(4),
        name="scatter",
    )(score, end, lo, hi, after)


def weigh_kernel(low_ref, gcols, att_ref, grad_ref, first_ref, keep_ref, send_ref, grads_ref):
    gproj = dot_tn(att_ref[...], grad_ref[...]).astype(BF)
    grads_ref[0:96, :] = gproj[:, 0:128]
    grads_ref[96:144, :] = jnp.concatenate([gproj[0:48, 128:192], gproj[48:96, 128:192]], axis=1)
    low = low_ref[...]
    a, b, c = [dot_tn(low, gcols[j]).astype(BF) for j in range(3)]
    grads_ref[144:336, :] = jnp.concatenate([a, c[:, 0:32]], axis=1)
    grads_ref[336:528, :] = jnp.concatenate([b, c[:, 32:64]], axis=1)
    grads_ref[528:576, :] = jnp.concatenate([c[i * 48 : i * 48 + 48, 64:96] for i in range(4)], axis=1)
    core = lax.rem(lax.axis_index("lat"), 2)
    keep_ref[...] = grads_ref[pl.ds(pl.multiple_of(core * 288, 16), 288), :]
    send_ref[0:576, :] = first_ref[...]
    send_ref[576:864, :] = grads_ref[pl.ds(pl.multiple_of((1 - core) * 288, 16), 288), :]


def weigh(low, gcols, att, grad, first):
    return pl.pallas_call(
        weigh_kernel,
        out_shape=(shape((288, 128), BF), shape((864, 128), BF)),
        scratch_shapes=[pltpu.VMEM((576, 128), BF)],
        compiler_params=VM,
        cost_estimate=cost(0.5),
        name="weigh",
    )(low, gcols, att, grad, first)


def gain_rows(line):
    none = jnp.zeros((1, 64), F32)
    return [line[:, 0:128], jnp.concatenate([line[:, 128:192], none], axis=1)]


def pack_kernel(first_ref, second_ref, other_ref, table_ref, gain_ref, out_ref):
    out_ref[0:576, :] = both(first_ref[...], other_ref[0:576, :])
    out_ref[576:864, :] = both(second_ref[...], other_ref[576:864, :])
    rows = []
    for r in range(12):
        pair = table_ref[r * 16 : r * 16 + 13, :]
        rows += [pair[:, 0:128], pair[:, 128:256]]
    rows += gain_rows(gain_ref[...]) + [jnp.zeros((102, 128), F32)]
    out_ref[864:1280, :] = jnp.concatenate(rows, axis=0).astype(BF)


def pack(first, second, other, table, gain):
    return pl.pallas_call(
        pack_kernel, out_shape=shape((1280, 128), BF), compiler_params=VM, cost_estimate=cost(1), name="pack"
    )(first, second, other, table, gain)


def meet_kernel(own_ref, other_ref, x_own, x_band, x_sector, g0, g1, g2, g3, gain_out):
    gain = jnp.zeros((1, 192), F32)
    total = unfold(own_ref[...].astype(F32) + other_ref[...].astype(F32))
    for s, (x, g) in enumerate(zip(window_parts(x_own, x_band, x_sector), (g0, g1, g2, g3))):
        grad = total[s * 144 : s * 144 + 144]
        normed, _ = layer_stats(x.astype(F32))
        gain = gain + jnp.sum(grad * normed, axis=0, keepdims=True)
        g[...] = grad.astype(BF)
    gain_out[...] = jnp.concatenate(gain_rows(gain) + [jnp.zeros((6, 128), F32)], axis=0)


def meet(own, other, x):
    return pl.pallas_call(
        meet_kernel,
        out_shape=tuple(shape((144, 192), BF) for _ in range(4)) + (shape((8, 128), F32),),
        compiler_params=VM,
        cost_estimate=cost(60),
        name="meet",
    )(own, other, *x)


def finish_kernel(x10, x2, x3, m0, m1, m2, m3, g0, g1, g2, g3, gain_ref, out_ref, token_ref):
    token_ref[...] = jnp.zeros((8, 128), F32)
    xs = (x10[144:288, :], x10[0:144, :], x2[...], x3[...])
    for q, (x, m, g) in enumerate(zip(xs, (m0, m1, m2, m3), (g0, g1, g2, g3))):
        normed, inverse = layer_stats(x.astype(F32))
        rows = m[...].astype(F32) + norm_backward(g[...].astype(F32), gain_ref[...], normed, inverse)
        for lat in range(3):
            piece = rows[lat * 48 : lat * 48 + 48].reshape(6, 8, 192)
            out_ref[(q // 2) * 3 + lat, (q % 2) * 6 : (q % 2) * 6 + 6] = piece.astype(BF)


def finish(x, m, g, gain):
    return pl.pallas_call(
        finish_kernel,
        out_shape=(shape((6, 12, 8, 192), BF), shape((8, 128), F32)),
        compiler_params=VM,
        cost_estimate=cost(1),
        name="finish",
    )(*x, *m, *g, gain)


def add_kernel(got_ref, gain_ref, b0, b1, b2, out_ref):
    total = got_ref[0].astype(F32)
    for i in range(1, 32):
        total = total + got_ref[i].astype(F32)
    out_ref[...] = jnp.concatenate([total, gain_ref[...]], axis=0).astype(BF)


def add(got, gain, after):
    return pl.pallas_call(
        add_kernel,
        out_shape=shape((48, 128), BF),
        in_specs=[VMEM] * 2 + [ANY] * 3,
        compiler_params=VM,
        cost_estimate=cost(1),
        name="add",
    )(got, gain, *after)


def spread_kernel(own_ref, other_ref, after_ref, out_ref):
    own = own_ref[...].astype(F32)
    place = lax.broadcasted_iota(I32, (48, 128), 0)
    row = lax.axis_index("lon") * 40 + place
    table = (row >= 864) & (row < 1176) & (place < 40)
    total = own + jnp.where(table, 0.0, other_ref[...].astype(F32))
    out_ref[...] = jnp.broadcast_to(total.astype(BF)[None], (32, 48, 128))


def spread(own, other, after):
    return pl.pallas_call(
        spread_kernel,
        out_shape=shape((32, 48, 128), BF),
        in_specs=[VMEM] * 2 + [ANY],
        compiler_params=VM,
        cost_estimate=cost(1),
        name="spread",
    )(own, other, after)


def table_kernel(table_scale, got_ref, table_ref):
    rows = jnp.concatenate([got_ref[c].astype(F32)[0:40] for c in range(21, 30)], axis=0)[24:336] * table_scale
    for r in range(12):
        for a in range(26):
            row, wide = r * 26 + (a % 2) * 13 + a // 2, min(128, 3312 - a * 128)
            table_ref[r % 3, r // 3 : r // 3 + 1, a * 128 : a * 128 + wide] = rows[row : row + 1, 0:wide]


def unpack_table(table_scale, got):
    return pl.pallas_call(
        functools.partial(table_kernel, table_scale),
        out_shape=shape((3, 4, 3312), F32),
        compiler_params=VM,
        cost_estimate=cost(0.5),
        name="table",
    )(got)


def unpack_kernel(weight_scale, own_ref, other_ref, qkv_ref, proj_ref, upg_ref, down_ref, one_ref, two_ref):
    swap = lax.rem(lax.axis_index("lat"), 2) == 1
    fields = []
    gain = jnp.zeros((8, 128), F32)
    for ref in (own_ref, other_ref):
        pieces = [ref[c].astype(F32) for c in range(32)]
        fields.append(jnp.concatenate([piece[0:40] for piece in pieces], axis=0))
        for piece in pieces:
            gain = gain + piece[40:48]
    own, other = fields[0][0:864] * weight_scale, fields[1][0:864] * weight_scale
    lower, upper = jnp.where(swap, other, own), jnp.where(swap, own, other)
    for j in range(3):
        upg_ref[:, j * 128 : j * 128 + 128] = lower[j * 192 : j * 192 + 192]
        down_ref[:, j * 128 : j * 128 + 128] = upper[j * 192 : j * 192 + 192]
    second = jnp.concatenate([lower[576:864], upper[576:864]], axis=0)
    proj_ref[:, 0:128] = second[0:96]
    proj_ref[0:48, 128:192] = second[96:144, 0:64]
    proj_ref[48:96, 128:192] = second[96:144, 64:128]
    qkv_ref[0] = second[144:336, 0:96]
    qkv_ref[1] = second[336:528, 0:96]
    qkv_ref[2, :, 0:32] = second[144:336, 96:128]
    qkv_ref[2, :, 32:64] = second[336:528, 96:128]
    for i in range(4):
        qkv_ref[2, i * 48 : i * 48 + 48, 64:96] = second[528:576, i * 32 : i * 32 + 32]
    for rows, out in ((gain, one_ref), (fields[0][1176:1184] + fields[1][1176:1184], two_ref)):
        line = rows[0:1]
        later = jnp.concatenate([line[:, 96:128], rows[1:2, 0:64]], axis=1)
        out[...] = jnp.where(lax.axis_index("tp") == 0, line[:, 0:96], later) * weight_scale


def unpack(weight_scale, got, other):
    return pl.pallas_call(
        functools.partial(unpack_kernel, weight_scale),
        out_shape=(
            shape((3, 192, 96), F32),
            shape((96, 192), F32),
            shape((192, 384), F32),
            shape((192, 384), F32),
            shape((1, 96), F32),
            shape((1, 96), F32),
        ),
        compiler_params=VM,
        name="unpack",
    )(got, other)


def moved(value, band, sector, half):
    sizes = [lax.axis_size(name) for name in ("lat", "lon", "tp")]
    pairs = []
    for a in range(sizes[0]):
        for b in range(sizes[1]):
            for c in range(sizes[2]):
                source = ((a + band) % sizes[0], (b + sector) % sizes[1], (c + half) % sizes[2])
                pairs.append(tuple((x * sizes[1] + y) * sizes[2] + z for x, y, z in (source, (a, b, c))))
    return lax.ppermute(value, ("lat", "lon", "tp"), pairs)


def shifted_parts(quarters):
    return (
        quarters[3],
        moved(quarters[2], 0, 1, 0),
        moved(quarters[1], 1, 0, 0),
        moved(quarters[0], 1, 1, 0),
    )


def other_core(value):
    return lax.ppermute(value, "lat", [(a, a ^ 1) for a in range(lax.axis_size("lat"))])


def local(
    inputs,
    residual_mid,
    grad_out,
    mask_ids,
    key_valid,
    bias_index,
    pos_bias,
    norm1_gain,
    qkv_weight,
    proj_weight,
    norm2_gain,
    fc1_weight,
    fc2_weight,
):
    levels, lat_cells, lon_cells, channels = inputs.shape
    cell_count = levels * lat_cells * lon_cells
    weight_scale = (cell_count * lax.axis_size("lat") * lax.axis_size("lon")) ** (-0.5)
    table_scale = (lon_cells * lax.axis_size("lon") // 12) ** (-0.5)
    gain1, gain2 = norm1_gain.reshape(1, -1), norm2_gain.reshape(1, -1)

    def turned(field):
        return field.transpose(1, 2, 0, 3)

    x_in, mid_in, up_in = turned(inputs), turned(residual_mid), turned(grad_out)
    x10, x2, x3, part2, first, first_send = head(x_in, mid_in, up_in, gain2, fc1_weight, fc2_weight.T)
    other2 = moved(part2, 0, 0, 1)
    x_band = moved(x10, 1, 0, 0)
    stage, lo, hi, terms, code = gather_first(
        bias_index, pos_bias[0].transpose(1, 0, 2), mask_ids.transpose(1, 0, 2), key_valid.transpose(1, 0, 2)
    )
    *gm, gain_two, x_next = middle(mid_in, up_in, part2, other2, gain2, x2, x_band, lo)
    x_sector = moved(x_next, 0, 1, 0)
    xw = (x3, x_band, x_sector)
    gw = shifted_parts(gm)
    main, tail = gather_second(stage, lo, hi, terms, (gain_two, x_band))
    low, q, k, v, prob, att = forward(xw, gain1, qkv_weight, main, tail, code)
    part1, score, end, gcols, grad = backward(gw, proj_weight, qkv_weight, q, k, v, prob)
    other1 = moved(part1, 0, 0, 1)
    second, send = weigh(low, gcols, att, grad, first_send)
    table = scatter(score, end, lo, hi, second)
    sums = pack(first, second, other_core(send), table, gain_two)
    *g, gain_one = meet(part1, other1, xw)
    back = (moved(g[3], -1, -1, 0), moved(g[2], -1, 0, 0), moved(g[1], 0, -1, 0), g[0])
    own = add(lax.all_to_all(sums.reshape(32, 40, 128), "lon", 0, 0), gain_one, back[:3])
    result, token = finish((x10, x2, x3), gm, back, gain1)
    totals = spread(own, moved(own, 2, 0, 0), token)
    got = lax.all_to_all(totals, "lon", 0, 0)
    table_out = unpack_table(table_scale, got)
    qkv_out, proj_out, up_out, down_out, one, two = unpack(weight_scale, got, other_core(got))
    return (
        result.transpose(2, 0, 1, 3),
        qkv_out,
        proj_out,
        up_out,
        down_out.T,
        one.reshape(channels // lax.axis_size("tp")),
        two.reshape(channels // lax.axis_size("tp")),
        table_out.transpose(1, 0, 2)[None],
    )


def solution(mesh):
    return jax.shard_map(
        local,
        mesh=mesh,
        in_specs=(
            P(None, "lat", "lon", None),
            P(None, "lat", "lon", None),
            P(None, "lat", "lon", None),
            P(None, "lat", "lon"),
            P(None, "lat", "lon"),
            P(),
            P("lat", None, "tp", None),
            P(),
            P(None, None, "tp"),
            P("tp", None),
            P(),
            P(None, "tp"),
            P("tp", None),
        ),
        out_specs=(
            P(None, "lat", "lon", None),
            P(None, None, "tp"),
            P("tp", None),
            P(None, "tp"),
            P("tp", None),
            P("tp"),
            P("tp"),
            P("lat", None, "tp", None),
        ),
        check_vma=False,
    )
```

```python
import functools

import jax
import jax.numpy as jnp
import numpy as np
from jax import lax
from jax.experimental import pallas as pl
from jax.experimental.pallas import tpu as pltpu
from jax.sharding import PartitionSpec as P

HD = 32
EPSILON = 1e-05
EXCLUDED = -1e30
BF = jnp.bfloat16
F32 = jnp.float32
I32 = jnp.int32
VMEM = pl.BlockSpec(memory_space=pltpu.VMEM)
VM = pltpu.CompilerParams(vmem_limit_bytes=24 * 1024 * 1024)
ALL = pltpu.CompilerParams(vmem_limit_bytes=63 * 1024 * 1024)
SMEM = pl.BlockSpec(memory_space=pltpu.SMEM)
ANY = pl.BlockSpec(memory_space=pl.ANY)


def cost(microseconds):
    return pl.CostEstimate(flops=int(microseconds * 1e9), bytes_accessed=0, transcendentals=0)


def shape(dims, kind):
    return jax.ShapeDtypeStruct(dims, kind)


def both(own, other):
    return (own.astype(F32) + other.astype(F32)).astype(BF)


def dot_nn(a, b):
    return lax.dot_general(a, b, (((1,), (0,)), ((), ())), preferred_element_type=F32)


def dot_nt(a, b):
    return lax.dot_general(a, b, (((1,), (1,)), ((), ())), preferred_element_type=F32)


def dot_tn(a, b):
    return lax.dot_general(a, b, (((0,), (0,)), ((), ())), preferred_element_type=F32)


def layer_stats(rows):
    mean = jnp.mean(rows, axis=-1, keepdims=True)
    centred = rows - mean
    inverse = lax.rsqrt(jnp.mean(centred * centred, axis=-1, keepdims=True) + EPSILON)
    return centred * inverse, inverse


def norm_backward(grad_normed, gain, normed, inverse):
    scaled = grad_normed * gain
    first = jnp.mean(scaled, axis=-1, keepdims=True)
    second = jnp.mean(scaled * normed, axis=-1, keepdims=True)
    return (scaled - first - normed * second) * inverse


def gelu_pair(pre):
    cdf = 0.5 * (1.0 + lax.erf(pre * 0.7071067811865476))
    pdf = 0.3989422804014327 * jnp.exp(-0.5 * pre * pre)
    return pre * cdf, cdf + pre * pdf


def to_quarters(field_ref, scratch):
    for lat in range(6):
        for half in range(2):
            rows = field_ref[lat, half * 6 : half * 6 + 6].astype(F32).reshape(48, 192)
            start = ((lat // 3) * 2 + half) * 144 + (lat % 3) * 48
            scratch[start : start + 48, :] = rows


def level_order():
    order = np.zeros((144, 144), np.float32)
    for w in range(4):
        for cell in range(18):
            for level in range(2):
                order[w * 36 + cell * 2 + level, cell * 8 + (2 * w + 1 + level) % 8] = 1.0
    return jnp.asarray(order, BF)


def to_windows(parts, order, scratch):
    for s in range(4):
        rows = dot_nn(order, parts[s][...])
        for w in range(4):
            scratch[w * 144 + s * 36 : w * 144 + s * 36 + 36, :] = rows[w * 36 : w * 36 + 36]


def head_kernel(mid_hbm, up_hbm, gain_hbm, fc1_hbm, fc2_hbm, part_hbm, keep_hbm, send_hbm,
                mid_ref, up_ref, gain_ref, fc1_ref, fc2_ref, part_ref, grads_ref, mid_s, up_s, sem):
    pairs = (
        (mid_hbm, mid_ref),
        (gain_hbm, gain_ref),
        (fc1_hbm, fc1_ref),
        (up_hbm, up_ref),
        (fc2_hbm, fc2_ref),
    )
    copies = [pltpu.make_async_copy(a, b, sem.at[i]) for i, (a, b) in enumerate(pairs)]
    for copy in copies:
        copy.start()
    for copy in copies[:3]:
        copy.wait()
    to_quarters(mid_ref, mid_s)
    normed, _ = layer_stats(mid_s[...])
    lowered = (normed * gain_ref[...]).astype(BF)
    pre = dot_nn(lowered, fc1_ref[...])
    active, slopes = gelu_pair(pre)
    for copy in copies[3:]:
        copy.wait()
    writes = []
    to_quarters(up_ref, up_s)
    up = up_s[...].astype(BF)
    grad_pre = (dot_nn(up, fc2_ref[...]) * slopes).astype(BF)
    part_ref[...] = dot_nt(grad_pre, fc1_ref[...]).astype(BF)
    writes.append(pltpu.make_async_copy(part_ref, part_hbm, sem.at[6]))
    writes[-1].start()
    for start, grads in ((0, dot_tn(lowered, grad_pre)), (576, dot_tn(up, active.astype(BF)))):
        for j in range(3):
            grads_ref[start + j * 192 : start + j * 192 + 192, :] = grads[:, j * 128 : j * 128 + 128].astype(BF)
    core = lax.rem(lax.axis_index("lat"), 2)
    for i, (half, out) in enumerate(((core, keep_hbm), (1 - core, send_hbm))):
        piece = grads_ref.at[pl.ds(pl.multiple_of(half * 576, 16), 576)]
        writes.append(pltpu.make_async_copy(piece, out, sem.at[7 + i]))
        writes[-1].start()
    for write in writes:
        write.wait()


def head(mid, up, gain, fc1, fc2):
    return pl.pallas_call(
        head_kernel,
        out_shape=(shape((576, 192), BF), shape((576, 128), BF), shape((576, 128), BF)),
        in_specs=[ANY] * 5,
        out_specs=(ANY, ANY, ANY),
        scratch_shapes=[
            pltpu.VMEM((6, 12, 8, 192), BF),
            pltpu.VMEM((6, 12, 8, 192), BF),
            pltpu.VMEM((1, 192), F32),
            pltpu.VMEM((192, 384), BF),
            pltpu.VMEM((192, 384), BF),
            pltpu.VMEM((576, 192), BF),
            pltpu.VMEM((1152, 128), BF),
            pltpu.VMEM((576, 192), F32),
            pltpu.VMEM((576, 192), F32),
            pltpu.SemaphoreType.DMA((9,)),
        ],
        compiler_params=ALL,
        cost_estimate=cost(3),
        name="head",
    )(mid, up, gain, fc1, fc2)


def middle_kernel(mid_ref, up_ref, own_ref, other_ref, gain_ref, after_ref, o0, o1, o2, o3, gain_out, mid_s, up_s):
    to_quarters(mid_ref, mid_s)
    to_quarters(up_ref, up_s)
    normed, inverse = layer_stats(mid_s[...])
    grad = own_ref[...].astype(F32) + other_ref[...].astype(F32)
    gain_out[...] = jnp.sum(grad * normed, axis=0, keepdims=True)
    out = up_s[...] + norm_backward(grad, gain_ref[...], normed, inverse)
    for q, o in enumerate((o0, o1, o2, o3)):
        o[...] = out[q * 144 : q * 144 + 144].astype(BF)


def middle(mid, up, own, other, gain, after):
    return pl.pallas_call(
        middle_kernel,
        out_shape=tuple(shape((144, 192), BF) for _ in range(4)) + (shape((1, 192), F32),),
        in_specs=[VMEM] * 5 + [ANY],
        scratch_shapes=[pltpu.VMEM((576, 192), F32)] * 2,
        compiler_params=VM,
        cost_estimate=cost(1),
        name="middle",
    )(mid, up, own, other, gain, after)


def window_order():
    canon = np.arange(144).reshape(2, 2, 3, 2, 6).transpose(1, 3, 2, 4, 0).reshape(-1)
    order = np.zeros((144, 144), np.float32)
    order[np.arange(144), canon] = 1.0
    return order


def pack_tail(tail):
    spread = (lax.broadcasted_iota(I32, (16, 128), 1) & 15) == lax.broadcasted_iota(I32, (16, 128), 0)
    wide = dot_nn(tail, spread.astype(F32).astype(BF))
    here = (lax.broadcasted_iota(I32, (144, 128), 1) >> 4) == (lax.broadcasted_iota(I32, (144, 128), 0) & 7)
    wide = jnp.where(here, wide, 0.0).astype(BF)
    rows = (lax.broadcasted_iota(I32, (24, 144), 1) >> 3) == lax.broadcasted_iota(I32, (24, 144), 0)
    return dot_nn(rows.astype(F32).astype(BF), wide)


def one_hot(low):
    rows = lax.broadcasted_iota(I32, (256, 128), 0).astype(F32).astype(BF)
    return jnp.where(rows == low.astype(F32).astype(BF), jnp.ones((), BF), jnp.zeros((), BF))


def look_up(terms, lo_ref, hi_ref, stage, first_block, steps):
    half = (lax.broadcasted_iota(I32, (8, 128), 0) >> 2)

    def step(i, _):
        for pair in range(9):
            base = first_block + i * 18 + pair * 2
            hot = jnp.concatenate([one_hot(lo_ref[pl.ds(base + j, 1), :]) for j in range(2)], axis=1)
            found = dot_nn(terms, jnp.concatenate([hot, hot], axis=0))
            for j in range(2):
                cols = slice(j * 128, j * 128 + 128)
                high = hi_ref[pl.ds(base + j, 1), :]
                first = jnp.zeros((8, 128), F32)
                for c in range(13):
                    first = jnp.where(high == c, found[c * 8 : c * 8 + 8, cols], first)
                second = jnp.zeros((8, 128), F32)
                shifted = high - half
                for c in range(7):
                    second = jnp.where(shifted == 2 * c, found[104 + c * 8 : 112 + c * 8, cols], second)
                start = pl.multiple_of((base + j - first_block) * 16, 16)
                stage[pl.ds(start, 8), :] = first
                stage[pl.ds(start + 8, 8), :] = second + pltpu.roll(second, 4, 0)
        return 0

    lax.fori_loop(0, steps, step, 0, unroll=True)


def gather_first_kernel(index_ref, order_ref, bias_ref, ids_ref, valid_ref, x_ref,
                        stage, lo_ref, hi_ref, terms_ref, code_ref, o0, o1, o2, o3, table, x_s):
    to_quarters(x_ref, x_s)
    for q, out in enumerate((o0, o1, o2, o3)):
        out[...] = x_s[q * 144 : q * 144 + 144, :].astype(BF)
    index = index_ref[...]
    order = order_ref[...]
    pieces = []
    for part in (index & 127, index >> 7):
        moved = dot_nt(dot_nn(order, part.astype(F32).astype(BF)).astype(BF), order)
        pieces.append((moved[:, 0:128].astype(I32), pack_tail(moved[:, 128:144].astype(BF)).astype(I32)))
    for rows, low, high in ((slice(0, 144), pieces[0][0], pieces[1][0]), (slice(144, 168), pieces[0][1], pieces[1][1])):
        lo_ref[rows, :] = low + (high & 1) * 128
        hi_ref[rows, :] = high >> 1
    table[...] = jnp.zeros((160, 256), F32)
    for r in range(12):
        line = bias_ref[r % 3, r // 3 : r // 3 + 1, :]
        line = line - jnp.max(line, axis=1, keepdims=True)
        for c in range(13):
            wide = min(256, 3312 - c * 256)
            row = c * 8 + r if r < 8 else 104 + (c // 2) * 8 + (c % 2) * 4 + r - 8
            table[row : row + 1, 0:wide] = line[:, c * 256 : c * 256 + wide]
    upper = table[...].astype(BF)
    terms_ref[:, 0:256] = upper
    terms_ref[:, 256:512] = (table[...] - upper.astype(F32)).astype(BF)
    code = (ids_ref[...] * 2 + (valid_ref[...] > 0).astype(I32)).astype(F32).reshape(48, 12).astype(BF)
    row = lax.broadcasted_iota(I32, (24, 48), 0)
    column = lax.broadcasted_iota(I32, (24, 48), 1)
    lines = []
    for level in range(2):
        pick = ((row >> 2) * 8 + (row & 3) * 2 + level) == column
        picked = dot_nn(pick.astype(F32).astype(BF), code)
        lines += [picked[lat * 4 : lat * 4 + 4] for lat in range(6)]
    lines = jnp.concatenate(lines, axis=1)
    code_ref[...] = dot_nt(lines.astype(BF), order)
    look_up(terms_ref[...], lo_ref, hi_ref, stage, 0, 5)


def gather_first(index, bias, ids, valid, x):
    return pl.pallas_call(
        gather_first_kernel,
        out_shape=(
            shape((90 * 16, 128), F32),
            shape((168, 128), I32),
            shape((168, 128), I32),
            shape((160, 512), BF),
            shape((4, 144), F32),
        )
        + tuple(shape((144, 192), BF) for _ in range(4)),
        scratch_shapes=[pltpu.VMEM((160, 256), F32), pltpu.VMEM((576, 192), F32)],
        compiler_params=VM,
        cost_estimate=cost(0.5),
        name="gather_first",
    )(index, jnp.asarray(window_order(), BF), bias, ids, valid, x)


def gather_second_kernel(first_stage, lo_ref, hi_ref, terms_ref, a0, a1, a2, a3, main_ref, tail_ref, stage):
    look_up(terms_ref[...], lo_ref, hi_ref, stage, 90, 4)
    for r in range(12):
        main_ref[r, 0:90, :] = first_stage[pl.ds(r, 90, stride=16), :]
        main_ref[r, 90:144, :] = stage[pl.ds(r, 54, stride=16), :]
        packed = stage[pl.ds(54 * 16 + r, 18, stride=16), :]
        for s in range(8):
            tail_ref[r, pl.ds(s, 18, stride=8), :] = pltpu.roll(packed, 128 - 16 * s, 1) if s else packed


def gather_second(first_stage, lo, hi, terms, after):
    return pl.pallas_call(
        gather_second_kernel,
        out_shape=(shape((12, 144, 128), F32), shape((12, 144, 128), F32)),
        in_specs=[VMEM] * 4 + [ANY] * 4,
        scratch_shapes=[pltpu.VMEM((72 * 16, 128), F32)],
        compiler_params=VM,
        cost_estimate=cost(4),
        name="gather_second",
    )(first_stage, lo, hi, terms, *after)


def forward_kernel(x0, x1, x2, x3, order_ref, gain_ref, qkv_ref, main_ref, tail_ref, code_ref,
                   low_ref, q_ref, k_ref, v_ref, prob_ref, att_ref, scratch):
    to_windows((x0, x1, x2, x3), order_ref[...], scratch)
    normed, _ = layer_stats(scratch[...])
    low = (normed * gain_ref[...]).astype(BF)
    low_ref[...] = low
    for j, out in enumerate((q_ref, k_ref, v_ref)):
        out[...] = dot_nn(low, qkv_ref[j]).astype(BF)
    eye = lax.broadcasted_iota(I32, (144, 144), 0) == lax.broadcasted_iota(I32, (144, 144), 1)

    def window(w, _):
        rows = pl.ds(pl.multiple_of(w * 144, 16), 144)
        code = code_ref[pl.ds(w, 1), :].astype(I32)
        label = code >> 1
        column = jnp.sum(jnp.where(eye, label, 0), axis=1, keepdims=True)
        allowed = eye | ((column == label) & ((code & 1) > 0))
        query, key, value = q_ref[rows, :], k_ref[rows, :], v_ref[rows, :]
        heads = []
        for h in range(3):
            cols = slice(h * HD, h * HD + HD)
            bias = jnp.concatenate([main_ref[w * 3 + h], tail_ref[w * 3 + h][:, 0:16]], axis=1)
            scores = dot_nt(query[:, cols], key[:, cols]) * (HD ** -0.5) + bias
            scores = jnp.where(allowed, scores, EXCLUDED)
            expo = jnp.exp(scores - jnp.max(scores, axis=-1, keepdims=True))
            prob = expo * (1.0 / jnp.sum(expo, axis=-1, keepdims=True))
            prob_ref[w * 3 + h] = prob
            heads.append(dot_nn(prob.astype(BF), value[:, cols]))
        att_ref[rows, :] = jnp.concatenate(heads, axis=1).astype(BF)
        return 0

    lax.fori_loop(0, 4, window, 0, unroll=True)


def forward(x, gain, qkv, main, tail, code):
    return pl.pallas_call(
        forward_kernel,
        out_shape=(
            shape((576, 192), BF),
            shape((576, 96), BF),
            shape((576, 96), BF),
            shape((576, 96), BF),
            shape((12, 144, 144), F32),
            shape((576, 96), BF),
        ),
        scratch_shapes=[pltpu.VMEM((576, 192), F32)],
        compiler_params=VM,
        cost_estimate=cost(5),
        name="forward",
    )(*x, level_order(), gain, qkv, main, tail, code)


def backward_kernel(g0, g1, g2, g3, order_ref, proj_ref, qkv_ref, q_ref, k_ref, v_ref, prob_ref,
                    part_ref, score_ref, end_ref, gcols, grad_ref, scratch, gatt):
    to_windows((g0, g1, g2, g3), order_ref[...], scratch)
    grad = scratch[...].astype(BF)
    grad_ref[...] = grad
    gatt[...] = dot_nt(grad, proj_ref[...]).astype(BF)

    def window(w, _):
        rows = pl.ds(pl.multiple_of(w * 144, 16), 144)
        query, key, value, above = q_ref[rows, :], k_ref[rows, :], v_ref[rows, :], gatt[rows, :]
        queries, keys, values = [], [], []
        for h in range(3):
            cols = slice(h * HD, h * HD + HD)
            prob = prob_ref[w * 3 + h]
            values.append(dot_tn(above[:, cols], prob.astype(BF)))
            grad_prob = dot_nt(above[:, cols], value[:, cols])
            score = prob * (grad_prob - jnp.sum(grad_prob * prob, axis=-1, keepdims=True))
            score_ref[w * 3 + h] = score[:, 0:128]
            end_ref[w * 3 + h, :, 0:16] = score[:, 128:144]
            low_score = (score * (HD ** -0.5)).astype(BF)
            queries.append(dot_nn(low_score, key[:, cols]))
            keys.append(dot_tn(query[:, cols], low_score))
        gcols[0, rows, :] = jnp.concatenate(queries, axis=1).astype(BF)
        gcols[1, rows, :] = jnp.concatenate(keys, axis=0).T.astype(BF)
        gcols[2, rows, :] = jnp.concatenate(values, axis=0).T.astype(BF)
        return 0

    lax.fori_loop(0, 4, window, 0, unroll=True)
    total = None
    for j in range(3):
        term = dot_nt(gcols[j], qkv_ref[j])
        total = term if total is None else total + term
    scratch[...] = total
    for s in range(4):
        pieces = [scratch[w * 144 + s * 36 : w * 144 + s * 36 + 36, :] for w in range(4)]
        piece = jnp.concatenate(pieces, axis=0).astype(BF)
        part_ref[s * 144 : s * 144 + 144, :] = dot_tn(order_ref[...], piece).astype(BF)


def backward(g, proj, qkv, q, k, v, prob):
    return pl.pallas_call(
        backward_kernel,
        out_shape=(
            shape((576, 192), BF),
            shape((12, 144, 128), F32),
            shape((12, 144, 128), F32),
            shape((3, 576, 96), BF),
            shape((576, 192), BF),
        ),
        scratch_shapes=[pltpu.VMEM((576, 192), F32), pltpu.VMEM((576, 96), BF)],
        compiler_params=VM,
        cost_estimate=cost(7),
        name="backward",
    )(*g, level_order(), proj, qkv, q, k, v, prob)


def scatter_kernel(score_ref, end_ref, lo_ref, hi_ref, after_ref, out_ref, tails):
    total = jnp.zeros((256, 192), F32)
    place = lax.broadcasted_iota(I32, (16, 128), 0)
    group = lax.broadcasted_iota(I32, (18, 128), 1) >> 4
    for r in range(12):
        packed = end_ref[r, pl.ds(0, 18, stride=8), :]
        for j in range(1, 8):
            moved_on = pltpu.roll(end_ref[r, pl.ds(j, 18, stride=8), :], 16 * j, 1)
            packed = jnp.where(group == j, moved_on, packed)
        tails[r, 0:18, :] = packed
    for i in range(9):
        left, right = [], []
        for j in range(18):
            row = slice(i * 18 + j, i * 18 + j + 1)
            here = place == hi_ref[row, :]
            right.append(one_hot(lo_ref[row, :]))
            lines = [score_ref[r, row, :] if i < 8 else tails[r, j : j + 1, :] for r in range(12)]
            left.append(jnp.concatenate([jnp.where(here, line, 0.0).astype(BF) for line in lines], axis=0))
        total = total + dot_nt(jnp.concatenate(right, axis=1), jnp.concatenate(left, axis=1))
    out_ref[...] = total.T


def scatter(score, end, lo, hi, after):
    return pl.pallas_call(
        scatter_kernel,
        out_shape=shape((192, 256), F32),
        in_specs=[VMEM] * 4 + [ANY],
        scratch_shapes=[pltpu.VMEM((12, 24, 128), F32)],
        compiler_params=VM,
        cost_estimate=cost(4),
        name="scatter",
    )(score, end, lo, hi, after)


def weigh_kernel(low_ref, gcols, att_ref, grad_ref, first_ref, keep_ref, send_ref, grads_ref):
    gproj = dot_tn(att_ref[...], grad_ref[...]).astype(BF)
    grads_ref[0:96, :] = gproj[:, 0:128]
    grads_ref[96:144, :] = jnp.concatenate([gproj[0:48, 128:192], gproj[48:96, 128:192]], axis=1)
    low = low_ref[...]
    a, b, c = [dot_tn(low, gcols[j]).astype(BF) for j in range(3)]
    grads_ref[144:336, :] = jnp.concatenate([a, c[:, 0:32]], axis=1)
    grads_ref[336:528, :] = jnp.concatenate([b, c[:, 32:64]], axis=1)
    grads_ref[528:576, :] = jnp.concatenate([c[i * 48 : i * 48 + 48, 64:96] for i in range(4)], axis=1)
    core = lax.rem(lax.axis_index("lat"), 2)
    keep_ref[...] = grads_ref[pl.ds(pl.multiple_of(core * 288, 16), 288), :]
    send_ref[0:576, :] = first_ref[...]
    send_ref[576:864, :] = grads_ref[pl.ds(pl.multiple_of((1 - core) * 288, 16), 288), :]


def weigh(low, gcols, att, grad, first):
    return pl.pallas_call(
        weigh_kernel,
        out_shape=(shape((288, 128), BF), shape((864, 128), BF)),
        scratch_shapes=[pltpu.VMEM((576, 128), BF)],
        compiler_params=VM,
        cost_estimate=cost(0.5),
        name="weigh",
    )(low, gcols, att, grad, first)


def gain_rows(line):
    none = jnp.zeros((1, 64), F32)
    return [line[:, 0:128], jnp.concatenate([line[:, 128:192], none], axis=1)]


def pack_kernel(first_ref, second_ref, other_ref, table_ref, gain_ref, out_ref):
    out_ref[0:576, :] = both(first_ref[...], other_ref[0:576, :])
    out_ref[576:864, :] = both(second_ref[...], other_ref[576:864, :])
    rows = []
    for r in range(12):
        pair = table_ref[r * 16 : r * 16 + 13, :]
        rows += [pair[:, 0:128], pair[:, 128:256]]
    rows += gain_rows(gain_ref[...]) + [jnp.zeros((102, 128), F32)]
    out_ref[864:1280, :] = jnp.concatenate(rows, axis=0).astype(BF)


def pack(first, second, other, table, gain):
    return pl.pallas_call(
        pack_kernel, out_shape=shape((1280, 128), BF), compiler_params=VM, cost_estimate=cost(1), name="pack"
    )(first, second, other, table, gain)


def meet_kernel(own_ref, other_ref, x0, x1, x2, x3, g0, g1, g2, g3, gain_out):
    gain = jnp.zeros((1, 192), F32)
    for s, (x, g) in enumerate(zip((x0, x1, x2, x3), (g0, g1, g2, g3))):
        rows = slice(s * 144, s * 144 + 144)
        grad = own_ref[rows, :].astype(F32) + other_ref[rows, :].astype(F32)
        normed, _ = layer_stats(x[...].astype(F32))
        gain = gain + jnp.sum(grad * normed, axis=0, keepdims=True)
        g[...] = grad.astype(BF)
    gain_out[...] = jnp.concatenate(gain_rows(gain) + [jnp.zeros((6, 128), F32)], axis=0)


def meet(own, other, x):
    return pl.pallas_call(
        meet_kernel,
        out_shape=tuple(shape((144, 192), BF) for _ in range(4)) + (shape((8, 128), F32),),
        compiler_params=VM,
        cost_estimate=cost(60),
        name="meet",
    )(own, other, *x)


def finish_kernel(x0, x1, x2, x3, m0, m1, m2, m3, g0, g1, g2, g3, gain_ref, out_ref):
    for q, (x, m, g) in enumerate(zip((x0, x1, x2, x3), (m0, m1, m2, m3), (g0, g1, g2, g3))):
        normed, inverse = layer_stats(x[...].astype(F32))
        rows = m[...].astype(F32) + norm_backward(g[...].astype(F32), gain_ref[...], normed, inverse)
        for lat in range(3):
            piece = rows[lat * 48 : lat * 48 + 48].reshape(6, 8, 192)
            out_ref[(q // 2) * 3 + lat, (q % 2) * 6 : (q % 2) * 6 + 6] = piece.astype(BF)


def finish(x, m, g, gain):
    return pl.pallas_call(
        finish_kernel,
        out_shape=shape((6, 12, 8, 192), BF),
        compiler_params=VM,
        cost_estimate=cost(1),
        name="finish",
    )(*x, *m, *g, gain)


def add_kernel(got_ref, gain_ref, b0, b1, b2, out_ref):
    total = got_ref[0].astype(F32)
    for i in range(1, 32):
        total = total + got_ref[i].astype(F32)
    out_ref[...] = jnp.concatenate([total, gain_ref[...]], axis=0).astype(BF)


def add(got, gain, after):
    return pl.pallas_call(
        add_kernel,
        out_shape=shape((48, 128), BF),
        in_specs=[VMEM] * 2 + [ANY] * 3,
        compiler_params=VM,
        cost_estimate=cost(1),
        name="add",
    )(got, gain, *after)


def spread_kernel(own_ref, other_ref, out_ref):
    own = own_ref[...].astype(F32)
    place = lax.broadcasted_iota(I32, (48, 128), 0)
    row = lax.axis_index("lon") * 40 + place
    table = (row >= 864) & (row < 1176) & (place < 40)
    total = own + jnp.where(table, 0.0, other_ref[...].astype(F32))
    out_ref[...] = jnp.broadcast_to(total.astype(BF)[None], (32, 48, 128))


def spread(own, other):
    return pl.pallas_call(
        spread_kernel, out_shape=shape((32, 48, 128), BF), compiler_params=VM, cost_estimate=cost(1), name="spread"
    )(own, other)


def unpack_kernel(weight_scale, table_scale, own_ref, other_ref,
                  qkv_ref, proj_ref, upg_ref, down_ref, one_ref, two_ref, table_ref):
    swap = lax.rem(lax.axis_index("lat"), 2) == 1
    fields = []
    gain = jnp.zeros((8, 128), F32)
    for ref in (own_ref, other_ref):
        pieces = [ref[c].astype(F32) for c in range(32)]
        fields.append(jnp.concatenate([piece[0:40] for piece in pieces], axis=0))
        for piece in pieces:
            gain = gain + piece[40:48]
    own, other = fields[0][0:864] * weight_scale, fields[1][0:864] * weight_scale
    lower, upper = jnp.where(swap, other, own), jnp.where(swap, own, other)
    for j in range(3):
        upg_ref[:, j * 128 : j * 128 + 128] = lower[j * 192 : j * 192 + 192]
        down_ref[:, j * 128 : j * 128 + 128] = upper[j * 192 : j * 192 + 192]
    second = jnp.concatenate([lower[576:864], upper[576:864]], axis=0)
    proj_ref[:, 0:128] = second[0:96]
    proj_ref[0:48, 128:192] = second[96:144, 0:64]
    proj_ref[48:96, 128:192] = second[96:144, 64:128]
    qkv_ref[0] = second[144:336, 0:96]
    qkv_ref[1] = second[336:528, 0:96]
    qkv_ref[2, :, 0:32] = second[144:336, 96:128]
    qkv_ref[2, :, 32:64] = second[336:528, 96:128]
    for i in range(4):
        qkv_ref[2, i * 48 : i * 48 + 48, 64:96] = second[528:576, i * 32 : i * 32 + 32]
    table = fields[0][864:1176]
    for r in range(12):
        for half in range(2):
            piece = table[r * 26 + half * 13 : r * 26 + half * 13 + 13] * table_scale
            for a in range(13):
                start = a * 256 + half * 128
                wide = min(128, 3312 - start)
                table_ref[r % 3, r // 3 : r // 3 + 1, start : start + wide] = piece[a : a + 1, 0:wide]
    for rows, out in ((gain, one_ref), (fields[0][1176:1184] + fields[1][1176:1184], two_ref)):
        line = rows[0:1]
        later = jnp.concatenate([line[:, 96:128], rows[1:2, 0:64]], axis=1)
        out[...] = jnp.where(lax.axis_index("tp") == 0, line[:, 0:96], later) * weight_scale


def unpack(weight_scale, table_scale, got, other):
    return pl.pallas_call(
        functools.partial(unpack_kernel, weight_scale, table_scale),
        out_shape=(
            shape((3, 192, 96), F32),
            shape((96, 192), F32),
            shape((192, 384), F32),
            shape((192, 384), F32),
            shape((1, 96), F32),
            shape((1, 96), F32),
            shape((3, 4, 3312), F32),
        ),
        compiler_params=VM,
        name="unpack",
    )(got, other)


def moved(value, band, sector, half):
    sizes = [lax.axis_size(name) for name in ("lat", "lon", "tp")]
    pairs = []
    for a in range(sizes[0]):
        for b in range(sizes[1]):
            for c in range(sizes[2]):
                source = ((a + band) % sizes[0], (b + sector) % sizes[1], (c + half) % sizes[2])
                pairs.append(tuple((x * sizes[1] + y) * sizes[2] + z for x, y, z in (source, (a, b, c))))
    return lax.ppermute(value, ("lat", "lon", "tp"), pairs)


def shifted_parts(quarters):
    return (
        quarters[3],
        moved(quarters[2], 0, 1, 0),
        moved(quarters[1], 1, 0, 0),
        moved(quarters[0], 1, 1, 0),
    )


def other_core(value):
    return lax.ppermute(value, "lat", [(a, a ^ 1) for a in range(lax.axis_size("lat"))])


def local(
    inputs,
    residual_mid,
    grad_out,
    mask_ids,
    key_valid,
    bias_index,
    pos_bias,
    norm1_gain,
    qkv_weight,
    proj_weight,
    norm2_gain,
    fc1_weight,
    fc2_weight,
):
    levels, lat_cells, lon_cells, channels = inputs.shape
    cell_count = levels * lat_cells * lon_cells
    weight_scale = (cell_count * lax.axis_size("lat") * lax.axis_size("lon")) ** (-0.5)
    table_scale = (lon_cells * lax.axis_size("lon") // 12) ** (-0.5)
    gain1, gain2 = norm1_gain.reshape(1, -1), norm2_gain.reshape(1, -1)

    def turned(field):
        return field.transpose(1, 2, 0, 3)

    x_in, mid_in, up_in = turned(inputs), turned(residual_mid), turned(grad_out)
    part2, first, first_send = head(mid_in, up_in, gain2, fc1_weight, fc2_weight.T)
    other2 = moved(part2, 0, 0, 1)
    stage, lo, hi, terms, code, *x = gather_first(
        bias_index, pos_bias[0].transpose(1, 0, 2), mask_ids.transpose(1, 0, 2), key_valid.transpose(1, 0, 2), x_in
    )
    xw = shifted_parts(x)
    *gm, gain_two = middle(mid_in, up_in, part2, other2, gain2, lo)
    gw = shifted_parts(gm)
    main, tail = gather_second(stage, lo, hi, terms, (gain_two, *xw[1:]))
    low, q, k, v, prob, att = forward(xw, gain1, qkv_weight, main, tail, code)
    part1, score, end, gcols, grad = backward(gw, proj_weight, qkv_weight, q, k, v, prob)
    other1 = moved(part1, 0, 0, 1)
    second, send = weigh(low, gcols, att, grad, first_send)
    table = scatter(score, end, lo, hi, second)
    sums = pack(first, second, other_core(send), table, gain_two)
    *g, gain_one = meet(part1, other1, xw)
    back = (moved(g[3], -1, -1, 0), moved(g[2], -1, 0, 0), moved(g[1], 0, -1, 0), g[0])
    own = add(lax.all_to_all(sums.reshape(32, 40, 128), "lon", 0, 0), gain_one, back[:3])
    totals = spread(own, moved(own, 2, 0, 0))
    result = finish(x, gm, back, gain1)
    got = lax.all_to_all(totals, "lon", 0, 0)
    qkv_out, proj_out, up_out, down_out, one, two, table_out = unpack(
        weight_scale, table_scale, got, other_core(got)
    )
    return (
        result.transpose(2, 0, 1, 3),
        qkv_out,
        proj_out,
        up_out,
        down_out.T,
        one.reshape(channels // lax.axis_size("tp")),
        two.reshape(channels // lax.axis_size("tp")),
        table_out.transpose(1, 0, 2)[None],
    )


def solution(mesh):
    return jax.shard_map(
        local,
        mesh=mesh,
        in_specs=(
            P(None, "lat", "lon", None),
            P(None, "lat", "lon", None),
            P(None, "lat", "lon", None),
            P(None, "lat", "lon"),
            P(None, "lat", "lon"),
            P(),
            P("lat", None, "tp", None),
            P(),
            P(None, None, "tp"),
            P("tp", None),
            P(),
            P(None, "tp"),
            P("tp", None),
        ),
        out_specs=(
            P(None, "lat", "lon", None),
            P(None, None, "tp"),
            P("tp", None),
            P(None, "tp"),
            P("tp", None),
            P("tp"),
            P("tp"),
            P("lat", None, "tp", None),
        ),
        check_vma=False,
    )
```

```python
import functools

import jax
import jax.numpy as jnp
import numpy as np
from jax import lax
from jax.experimental import pallas as pl
from jax.experimental.pallas import tpu as pltpu
from jax.sharding import PartitionSpec as P

HD = 32
EPSILON = 1e-05
EXCLUDED = -1e30
BF = jnp.bfloat16
F32 = jnp.float32
I32 = jnp.int32
VMEM = pl.BlockSpec(memory_space=pltpu.VMEM)
VM = pltpu.CompilerParams(vmem_limit_bytes=24 * 1024 * 1024)
ALL = pltpu.CompilerParams(vmem_limit_bytes=63 * 1024 * 1024)
SMEM = pl.BlockSpec(memory_space=pltpu.SMEM)
ANY = pl.BlockSpec(memory_space=pl.ANY)


def cost(microseconds):
    return pl.CostEstimate(flops=int(microseconds * 1e9), bytes_accessed=0, transcendentals=0)


def shape(dims, kind):
    return jax.ShapeDtypeStruct(dims, kind)


def both(own, other):
    return (own.astype(F32) + other.astype(F32)).astype(BF)


def dot_nn(a, b):
    return lax.dot_general(a, b, (((1,), (0,)), ((), ())), preferred_element_type=F32)


def dot_nt(a, b):
    return lax.dot_general(a, b, (((1,), (1,)), ((), ())), preferred_element_type=F32)


def dot_tn(a, b):
    return lax.dot_general(a, b, (((0,), (0,)), ((), ())), preferred_element_type=F32)


def layer_stats(rows):
    mean = jnp.mean(rows, axis=-1, keepdims=True)
    centred = rows - mean
    inverse = lax.rsqrt(jnp.mean(centred * centred, axis=-1, keepdims=True) + EPSILON)
    return centred * inverse, inverse


def norm_backward(grad_normed, gain, normed, inverse):
    scaled = grad_normed * gain
    first = jnp.mean(scaled, axis=-1, keepdims=True)
    second = jnp.mean(scaled * normed, axis=-1, keepdims=True)
    return (scaled - first - normed * second) * inverse


def gelu_pair(pre):
    cdf = 0.5 * (1.0 + lax.erf(pre * 0.7071067811865476))
    pdf = 0.3989422804014327 * jnp.exp(-0.5 * pre * pre)
    return pre * cdf, cdf + pre * pdf


def to_quarters(field_ref, scratch):
    for lat in range(6):
        for half in range(2):
            rows = field_ref[lat, half * 6 : half * 6 + 6].astype(F32).reshape(48, 192)
            start = ((lat // 3) * 2 + half) * 144 + (lat % 3) * 48
            scratch[start : start + 48, :] = rows


def level_order():
    order = np.zeros((144, 144), np.float32)
    for w in range(4):
        for cell in range(18):
            for level in range(2):
                order[w * 36 + cell * 2 + level, cell * 8 + (2 * w + 1 + level) % 8] = 1.0
    return jnp.asarray(order, BF)


def to_windows(parts, order, scratch):
    for s in range(4):
        rows = dot_nn(order, parts[s][...])
        for w in range(4):
            scratch[w * 144 + s * 36 : w * 144 + s * 36 + 36, :] = rows[w * 36 : w * 36 + 36]


def head_kernel(mid_hbm, up_hbm, gain_hbm, fc1_hbm, fc2_hbm, part_hbm, keep_hbm, send_hbm,
                mid_ref, up_ref, gain_ref, fc1_ref, fc2_ref, part_ref, grads_ref, mid_s, up_s, sem):
    pairs = (
        (mid_hbm, mid_ref),
        (gain_hbm, gain_ref),
        (fc1_hbm, fc1_ref),
        (up_hbm, up_ref),
        (fc2_hbm, fc2_ref),
    )
    copies = [pltpu.make_async_copy(a, b, sem.at[i]) for i, (a, b) in enumerate(pairs)]
    for copy in copies:
        copy.start()
    for copy in copies[:3]:
        copy.wait()
    to_quarters(mid_ref, mid_s)
    normed, _ = layer_stats(mid_s[...])
    lowered = (normed * gain_ref[...]).astype(BF)
    pre = dot_nn(lowered, fc1_ref[...])
    active, slopes = gelu_pair(pre)
    for copy in copies[3:]:
        copy.wait()
    writes = []
    to_quarters(up_ref, up_s)
    up = up_s[...].astype(BF)
    grad_pre = (dot_nn(up, fc2_ref[...]) * slopes).astype(BF)
    part_ref[...] = dot_nt(grad_pre, fc1_ref[...]).astype(BF)
    writes.append(pltpu.make_async_copy(part_ref, part_hbm, sem.at[6]))
    writes[-1].start()
    for start, grads in ((0, dot_tn(lowered, grad_pre)), (576, dot_tn(up, active.astype(BF)))):
        for j in range(3):
            grads_ref[start + j * 192 : start + j * 192 + 192, :] = grads[:, j * 128 : j * 128 + 128].astype(BF)
    core = lax.rem(lax.axis_index("lat"), 2)
    for i, (half, out) in enumerate(((core, keep_hbm), (1 - core, send_hbm))):
        piece = grads_ref.at[pl.ds(pl.multiple_of(half * 576, 16), 576)]
        writes.append(pltpu.make_async_copy(piece, out, sem.at[7 + i]))
        writes[-1].start()
    for write in writes:
        write.wait()


def head(mid, up, gain, fc1, fc2):
    return pl.pallas_call(
        head_kernel,
        out_shape=(shape((576, 192), BF), shape((576, 128), BF), shape((576, 128), BF)),
        in_specs=[ANY] * 5,
        out_specs=(ANY, ANY, ANY),
        scratch_shapes=[
            pltpu.VMEM((6, 12, 8, 192), BF),
            pltpu.VMEM((6, 12, 8, 192), BF),
            pltpu.VMEM((1, 192), F32),
            pltpu.VMEM((192, 384), BF),
            pltpu.VMEM((192, 384), BF),
            pltpu.VMEM((576, 192), BF),
            pltpu.VMEM((1152, 128), BF),
            pltpu.VMEM((576, 192), F32),
            pltpu.VMEM((576, 192), F32),
            pltpu.SemaphoreType.DMA((9,)),
        ],
        compiler_params=ALL,
        cost_estimate=cost(3),
        name="head",
    )(mid, up, gain, fc1, fc2)


def middle_kernel(mid_ref, up_ref, own_ref, other_ref, gain_ref, after_ref, o0, o1, o2, o3, gain_out, mid_s, up_s):
    to_quarters(mid_ref, mid_s)
    to_quarters(up_ref, up_s)
    normed, inverse = layer_stats(mid_s[...])
    grad = own_ref[...].astype(F32) + other_ref[...].astype(F32)
    gain_out[...] = jnp.sum(grad * normed, axis=0, keepdims=True)
    out = up_s[...] + norm_backward(grad, gain_ref[...], normed, inverse)
    for q, o in enumerate((o0, o1, o2, o3)):
        o[...] = out[q * 144 : q * 144 + 144].astype(BF)


def middle(mid, up, own, other, gain, after):
    return pl.pallas_call(
        middle_kernel,
        out_shape=tuple(shape((144, 192), BF) for _ in range(4)) + (shape((1, 192), F32),),
        in_specs=[VMEM] * 5 + [ANY],
        scratch_shapes=[pltpu.VMEM((576, 192), F32)] * 2,
        compiler_params=VM,
        cost_estimate=cost(1),
        name="middle",
    )(mid, up, own, other, gain, after)


def window_order():
    canon = np.arange(144).reshape(2, 2, 3, 2, 6).transpose(1, 3, 2, 4, 0).reshape(-1)
    order = np.zeros((144, 144), np.float32)
    order[np.arange(144), canon] = 1.0
    return order


def pack_tail(tail):
    spread = (lax.broadcasted_iota(I32, (16, 128), 1) & 15) == lax.broadcasted_iota(I32, (16, 128), 0)
    wide = dot_nn(tail, spread.astype(F32).astype(BF))
    here = (lax.broadcasted_iota(I32, (144, 128), 1) >> 4) == (lax.broadcasted_iota(I32, (144, 128), 0) & 7)
    wide = jnp.where(here, wide, 0.0).astype(BF)
    rows = (lax.broadcasted_iota(I32, (24, 144), 1) >> 3) == lax.broadcasted_iota(I32, (24, 144), 0)
    return dot_nn(rows.astype(F32).astype(BF), wide)


def one_hot(low):
    rows = lax.broadcasted_iota(I32, (256, 128), 0).astype(F32).astype(BF)
    return jnp.where(rows == low.astype(F32).astype(BF), jnp.ones((), BF), jnp.zeros((), BF))


def look_up(terms, lo_ref, hi_ref, stage, first_block, steps):
    half = (lax.broadcasted_iota(I32, (8, 128), 0) >> 2)

    def step(i, _):
        for pair in range(9):
            base = first_block + i * 18 + pair * 2
            hot = jnp.concatenate([one_hot(lo_ref[pl.ds(base + j, 1), :]) for j in range(2)], axis=1)
            found = dot_nn(terms, jnp.concatenate([hot, hot], axis=0))
            for j in range(2):
                cols = slice(j * 128, j * 128 + 128)
                high = hi_ref[pl.ds(base + j, 1), :]
                first = jnp.zeros((8, 128), F32)
                for c in range(13):
                    first = jnp.where(high == c, found[c * 8 : c * 8 + 8, cols], first)
                second = jnp.zeros((8, 128), F32)
                shifted = high - half
                for c in range(7):
                    second = jnp.where(shifted == 2 * c, found[104 + c * 8 : 112 + c * 8, cols], second)
                start = pl.multiple_of((base + j - first_block) * 16, 16)
                stage[pl.ds(start, 8), :] = first
                stage[pl.ds(start + 8, 8), :] = second + pltpu.roll(second, 4, 0)
        return 0

    lax.fori_loop(0, steps, step, 0, unroll=True)


def gather_first_kernel(index_ref, order_ref, bias_ref, ids_ref, valid_ref, x_ref,
                        stage, lo_ref, hi_ref, terms_ref, code_ref, o0, o1, o2, o3, table, x_s):
    to_quarters(x_ref, x_s)
    for q, out in enumerate((o0, o1, o2, o3)):
        out[...] = x_s[q * 144 : q * 144 + 144, :].astype(BF)
    index = index_ref[...]
    order = order_ref[...]
    pieces = []
    for part in (index & 127, index >> 7):
        moved = dot_nt(dot_nn(order, part.astype(F32).astype(BF)).astype(BF), order)
        pieces.append((moved[:, 0:128].astype(I32), pack_tail(moved[:, 128:144].astype(BF)).astype(I32)))
    for rows, low, high in ((slice(0, 144), pieces[0][0], pieces[1][0]), (slice(144, 168), pieces[0][1], pieces[1][1])):
        lo_ref[rows, :] = low + (high & 1) * 128
        hi_ref[rows, :] = high >> 1
    table[...] = jnp.zeros((160, 256), F32)
    for r in range(12):
        line = bias_ref[r % 3, r // 3 : r // 3 + 1, :]
        line = line - jnp.max(line, axis=1, keepdims=True)
        for c in range(13):
            wide = min(256, 3312 - c * 256)
            row = c * 8 + r if r < 8 else 104 + (c // 2) * 8 + (c % 2) * 4 + r - 8
            table[row : row + 1, 0:wide] = line[:, c * 256 : c * 256 + wide]
    upper = table[...].astype(BF)
    terms_ref[:, 0:256] = upper
    terms_ref[:, 256:512] = (table[...] - upper.astype(F32)).astype(BF)
    code = (ids_ref[...] * 2 + (valid_ref[...] > 0).astype(I32)).astype(F32).reshape(48, 12).astype(BF)
    row = lax.broadcasted_iota(I32, (24, 48), 0)
    column = lax.broadcasted_iota(I32, (24, 48), 1)
    lines = []
    for level in range(2):
        pick = ((row >> 2) * 8 + (row & 3) * 2 + level) == column
        picked = dot_nn(pick.astype(F32).astype(BF), code)
        lines += [picked[lat * 4 : lat * 4 + 4] for lat in range(6)]
    lines = jnp.concatenate(lines, axis=1)
    code_ref[...] = dot_nt(lines.astype(BF), order)
    look_up(terms_ref[...], lo_ref, hi_ref, stage, 0, 7)


def gather_first(index, bias, ids, valid, x):
    return pl.pallas_call(
        gather_first_kernel,
        out_shape=(
            shape((126 * 16, 128), F32),
            shape((168, 128), I32),
            shape((168, 128), I32),
            shape((160, 512), BF),
            shape((4, 144), F32),
        )
        + tuple(shape((144, 192), BF) for _ in range(4)),
        scratch_shapes=[pltpu.VMEM((160, 256), F32), pltpu.VMEM((576, 192), F32)],
        compiler_params=VM,
        cost_estimate=cost(0.5),
        name="gather_first",
    )(index, jnp.asarray(window_order(), BF), bias, ids, valid, x)


def gather_second_kernel(first_stage, lo_ref, hi_ref, terms_ref, a0, a1, a2, a3, main_ref, tail_ref, stage):
    look_up(terms_ref[...], lo_ref, hi_ref, stage, 126, 2)
    for r in range(12):
        main_ref[r, 0:126, :] = first_stage[pl.ds(r, 126, stride=16), :]
        main_ref[r, 126:144, :] = stage[pl.ds(r, 18, stride=16), :]
        packed = stage[pl.ds(18 * 16 + r, 18, stride=16), :]
        for s in range(8):
            tail_ref[r, pl.ds(s, 18, stride=8), :] = pltpu.roll(packed, 128 - 16 * s, 1) if s else packed


def gather_second(first_stage, lo, hi, terms, after):
    return pl.pallas_call(
        gather_second_kernel,
        out_shape=(shape((12, 144, 128), F32), shape((12, 144, 128), F32)),
        in_specs=[VMEM] * 4 + [ANY] * 4,
        scratch_shapes=[pltpu.VMEM((36 * 16, 128), F32)],
        compiler_params=VM,
        cost_estimate=cost(4),
        name="gather_second",
    )(first_stage, lo, hi, terms, *after)


def forward_kernel(x0, x1, x2, x3, order_ref, gain_ref, qkv_ref, main_ref, tail_ref, code_ref,
                   low_ref, q_ref, k_ref, v_ref, prob_ref, att_ref, scratch):
    to_windows((x0, x1, x2, x3), order_ref[...], scratch)
    normed, _ = layer_stats(scratch[...])
    low = (normed * gain_ref[...]).astype(BF)
    low_ref[...] = low
    for j, out in enumerate((q_ref, k_ref, v_ref)):
        out[...] = dot_nn(low, qkv_ref[j]).astype(BF)
    eye = lax.broadcasted_iota(I32, (144, 144), 0) == lax.broadcasted_iota(I32, (144, 144), 1)

    def window(w, _):
        rows = pl.ds(pl.multiple_of(w * 144, 16), 144)
        code = code_ref[pl.ds(w, 1), :].astype(I32)
        label = code >> 1
        column = jnp.sum(jnp.where(eye, label, 0), axis=1, keepdims=True)
        allowed = eye | ((column == label) & ((code & 1) > 0))
        query, key, value = q_ref[rows, :], k_ref[rows, :], v_ref[rows, :]
        heads = []
        for h in range(3):
            cols = slice(h * HD, h * HD + HD)
            bias = jnp.concatenate([main_ref[w * 3 + h], tail_ref[w * 3 + h][:, 0:16]], axis=1)
            scores = dot_nt(query[:, cols], key[:, cols]) * (HD ** -0.5) + bias
            scores = jnp.where(allowed, scores, EXCLUDED)
            expo = jnp.exp(scores - jnp.max(scores, axis=-1, keepdims=True))
            prob = expo * (1.0 / jnp.sum(expo, axis=-1, keepdims=True))
            prob_ref[w * 3 + h] = prob
            heads.append(dot_nn(prob.astype(BF), value[:, cols]))
        att_ref[rows, :] = jnp.concatenate(heads, axis=1).astype(BF)
        return 0

    lax.fori_loop(0, 4, window, 0, unroll=True)


def forward(x, gain, qkv, main, tail, code):
    return pl.pallas_call(
        forward_kernel,
        out_shape=(
            shape((576, 192), BF),
            shape((576, 96), BF),
            shape((576, 96), BF),
            shape((576, 96), BF),
            shape((12, 144, 144), F32),
            shape((576, 96), BF),
        ),
        scratch_shapes=[pltpu.VMEM((576, 192), F32)],
        compiler_params=VM,
        cost_estimate=cost(5),
        name="forward",
    )(*x, level_order(), gain, qkv, main, tail, code)


def backward_kernel(g0, g1, g2, g3, order_ref, proj_ref, qkv_ref, q_ref, k_ref, v_ref, prob_ref,
                    part_ref, score_ref, end_ref, gcols, grad_ref, scratch, gatt):
    to_windows((g0, g1, g2, g3), order_ref[...], scratch)
    grad = scratch[...].astype(BF)
    grad_ref[...] = grad
    gatt[...] = dot_nt(grad, proj_ref[...]).astype(BF)

    def window(w, _):
        rows = pl.ds(pl.multiple_of(w * 144, 16), 144)
        query, key, value, above = q_ref[rows, :], k_ref[rows, :], v_ref[rows, :], gatt[rows, :]
        queries, keys, values = [], [], []
        for h in range(3):
            cols = slice(h * HD, h * HD + HD)
            prob = prob_ref[w * 3 + h]
            values.append(dot_tn(above[:, cols], prob.astype(BF)))
            grad_prob = dot_nt(above[:, cols], value[:, cols])
            score = prob * (grad_prob - jnp.sum(grad_prob * prob, axis=-1, keepdims=True))
            score_ref[w * 3 + h] = score[:, 0:128]
            end_ref[w * 3 + h, :, 0:16] = score[:, 128:144]
            low_score = (score * (HD ** -0.5)).astype(BF)
            queries.append(dot_nn(low_score, key[:, cols]))
            keys.append(dot_tn(query[:, cols], low_score))
        gcols[0, rows, :] = jnp.concatenate(queries, axis=1).astype(BF)
        gcols[1, rows, :] = jnp.concatenate(keys, axis=0).T.astype(BF)
        gcols[2, rows, :] = jnp.concatenate(values, axis=0).T.astype(BF)
        return 0

    lax.fori_loop(0, 4, window, 0, unroll=True)
    total = None
    for j in range(3):
        term = dot_nt(gcols[j], qkv_ref[j])
        total = term if total is None else total + term
    scratch[...] = total
    for s in range(4):
        pieces = [scratch[w * 144 + s * 36 : w * 144 + s * 36 + 36, :] for w in range(4)]
        piece = jnp.concatenate(pieces, axis=0).astype(BF)
        part_ref[s * 144 : s * 144 + 144, :] = dot_tn(order_ref[...], piece).astype(BF)


def backward(g, proj, qkv, q, k, v, prob):
    return pl.pallas_call(
        backward_kernel,
        out_shape=(
            shape((576, 192), BF),
            shape((12, 144, 128), F32),
            shape((12, 144, 128), F32),
            shape((3, 576, 96), BF),
            shape((576, 192), BF),
        ),
        scratch_shapes=[pltpu.VMEM((576, 192), F32), pltpu.VMEM((576, 96), BF)],
        compiler_params=VM,
        cost_estimate=cost(7),
        name="backward",
    )(*g, level_order(), proj, qkv, q, k, v, prob)


def scatter_kernel(score_ref, end_ref, lo_ref, hi_ref, after_ref, out_ref, tails):
    total = jnp.zeros((256, 192), F32)
    place = lax.broadcasted_iota(I32, (16, 128), 0)
    group = lax.broadcasted_iota(I32, (18, 128), 1) >> 4
    for r in range(12):
        packed = end_ref[r, pl.ds(0, 18, stride=8), :]
        for j in range(1, 8):
            moved_on = pltpu.roll(end_ref[r, pl.ds(j, 18, stride=8), :], 16 * j, 1)
            packed = jnp.where(group == j, moved_on, packed)
        tails[r, 0:18, :] = packed
    for i in range(9):
        left, right = [], []
        for j in range(18):
            row = slice(i * 18 + j, i * 18 + j + 1)
            here = place == hi_ref[row, :]
            right.append(one_hot(lo_ref[row, :]))
            lines = [score_ref[r, row, :] if i < 8 else tails[r, j : j + 1, :] for r in range(12)]
            left.append(jnp.concatenate([jnp.where(here, line, 0.0).astype(BF) for line in lines], axis=0))
        total = total + dot_nt(jnp.concatenate(right, axis=1), jnp.concatenate(left, axis=1))
    out_ref[...] = total.T


def scatter(score, end, lo, hi, after):
    return pl.pallas_call(
        scatter_kernel,
        out_shape=shape((192, 256), F32),
        in_specs=[VMEM] * 4 + [ANY],
        scratch_shapes=[pltpu.VMEM((12, 24, 128), F32)],
        compiler_params=VM,
        cost_estimate=cost(4),
        name="scatter",
    )(score, end, lo, hi, after)


def weigh_kernel(low_ref, gcols, att_ref, grad_ref, first_ref, keep_ref, send_ref, grads_ref):
    gproj = dot_tn(att_ref[...], grad_ref[...]).astype(BF)
    grads_ref[0:96, :] = gproj[:, 0:128]
    grads_ref[96:144, :] = jnp.concatenate([gproj[0:48, 128:192], gproj[48:96, 128:192]], axis=1)
    low = low_ref[...]
    a, b, c = [dot_tn(low, gcols[j]).astype(BF) for j in range(3)]
    grads_ref[144:336, :] = jnp.concatenate([a, c[:, 0:32]], axis=1)
    grads_ref[336:528, :] = jnp.concatenate([b, c[:, 32:64]], axis=1)
    grads_ref[528:576, :] = jnp.concatenate([c[i * 48 : i * 48 + 48, 64:96] for i in range(4)], axis=1)
    core = lax.rem(lax.axis_index("lat"), 2)
    keep_ref[...] = grads_ref[pl.ds(pl.multiple_of(core * 288, 16), 288), :]
    send_ref[0:576, :] = first_ref[...]
    send_ref[576:864, :] = grads_ref[pl.ds(pl.multiple_of((1 - core) * 288, 16), 288), :]


def weigh(low, gcols, att, grad, first):
    return pl.pallas_call(
        weigh_kernel,
        out_shape=(shape((288, 128), BF), shape((864, 128), BF)),
        scratch_shapes=[pltpu.VMEM((576, 128), BF)],
        compiler_params=VM,
        cost_estimate=cost(0.5),
        name="weigh",
    )(low, gcols, att, grad, first)


def gain_rows(line):
    none = jnp.zeros((1, 64), F32)
    return [line[:, 0:128], jnp.concatenate([line[:, 128:192], none], axis=1)]


def pack_kernel(first_ref, second_ref, other_ref, table_ref, gain_ref, out_ref):
    out_ref[0:576, :] = both(first_ref[...], other_ref[0:576, :])
    out_ref[576:864, :] = both(second_ref[...], other_ref[576:864, :])
    rows = []
    for r in range(12):
        pair = table_ref[r * 16 : r * 16 + 13, :]
        rows += [pair[:, 0:128], pair[:, 128:256]]
    rows += gain_rows(gain_ref[...]) + [jnp.zeros((102, 128), F32)]
    out_ref[864:1280, :] = jnp.concatenate(rows, axis=0).astype(BF)


def pack(first, second, other, table, gain):
    return pl.pallas_call(
        pack_kernel, out_shape=shape((1280, 128), BF), compiler_params=VM, cost_estimate=cost(1), name="pack"
    )(first, second, other, table, gain)


def meet_kernel(own_ref, other_ref, x0, x1, x2, x3, g0, g1, g2, g3, gain_out):
    gain = jnp.zeros((1, 192), F32)
    for s, (x, g) in enumerate(zip((x0, x1, x2, x3), (g0, g1, g2, g3))):
        rows = slice(s * 144, s * 144 + 144)
        grad = own_ref[rows, :].astype(F32) + other_ref[rows, :].astype(F32)
        normed, _ = layer_stats(x[...].astype(F32))
        gain = gain + jnp.sum(grad * normed, axis=0, keepdims=True)
        g[...] = grad.astype(BF)
    gain_out[...] = jnp.concatenate(gain_rows(gain) + [jnp.zeros((6, 128), F32)], axis=0)


def meet(own, other, x):
    return pl.pallas_call(
        meet_kernel,
        out_shape=tuple(shape((144, 192), BF) for _ in range(4)) + (shape((8, 128), F32),),
        compiler_params=VM,
        cost_estimate=cost(60),
        name="meet",
    )(own, other, *x)


def finish_kernel(x0, x1, x2, x3, m0, m1, m2, m3, g0, g1, g2, g3, gain_ref, out_ref):
    for q, (x, m, g) in enumerate(zip((x0, x1, x2, x3), (m0, m1, m2, m3), (g0, g1, g2, g3))):
        normed, inverse = layer_stats(x[...].astype(F32))
        rows = m[...].astype(F32) + norm_backward(g[...].astype(F32), gain_ref[...], normed, inverse)
        for lat in range(3):
            piece = rows[lat * 48 : lat * 48 + 48].reshape(6, 8, 192)
            out_ref[(q // 2) * 3 + lat, (q % 2) * 6 : (q % 2) * 6 + 6] = piece.astype(BF)


def finish(x, m, g, gain):
    return pl.pallas_call(
        finish_kernel,
        out_shape=shape((6, 12, 8, 192), BF),
        compiler_params=VM,
        cost_estimate=cost(1),
        name="finish",
    )(*x, *m, *g, gain)


def add_kernel(got_ref, gain_ref, b0, b1, b2, out_ref):
    total = got_ref[0].astype(F32)
    for i in range(1, 32):
        total = total + got_ref[i].astype(F32)
    out_ref[...] = jnp.concatenate([total, gain_ref[...]], axis=0).astype(BF)


def add(got, gain, after):
    return pl.pallas_call(
        add_kernel,
        out_shape=shape((48, 128), BF),
        in_specs=[VMEM] * 2 + [ANY] * 3,
        compiler_params=VM,
        cost_estimate=cost(1),
        name="add",
    )(got, gain, *after)


def spread_kernel(own_ref, other_ref, out_ref):
    own = own_ref[...].astype(F32)
    place = lax.broadcasted_iota(I32, (48, 128), 0)
    row = lax.axis_index("lon") * 40 + place
    table = (row >= 864) & (row < 1176) & (place < 40)
    total = own + jnp.where(table, 0.0, other_ref[...].astype(F32))
    out_ref[...] = jnp.broadcast_to(total.astype(BF)[None], (32, 48, 128))


def spread(own, other):
    return pl.pallas_call(
        spread_kernel, out_shape=shape((32, 48, 128), BF), compiler_params=VM, cost_estimate=cost(1), name="spread"
    )(own, other)


def unpack_kernel(weight_scale, table_scale, own_ref, other_ref,
                  qkv_ref, proj_ref, upg_ref, down_ref, one_ref, two_ref, table_ref):
    swap = lax.rem(lax.axis_index("lat"), 2) == 1
    fields = []
    gain = jnp.zeros((8, 128), F32)
    for ref in (own_ref, other_ref):
        pieces = [ref[c].astype(F32) for c in range(32)]
        fields.append(jnp.concatenate([piece[0:40] for piece in pieces], axis=0))
        for piece in pieces:
            gain = gain + piece[40:48]
    own, other = fields[0][0:864] * weight_scale, fields[1][0:864] * weight_scale
    lower, upper = jnp.where(swap, other, own), jnp.where(swap, own, other)
    for j in range(3):
        upg_ref[:, j * 128 : j * 128 + 128] = lower[j * 192 : j * 192 + 192]
        down_ref[:, j * 128 : j * 128 + 128] = upper[j * 192 : j * 192 + 192]
    second = jnp.concatenate([lower[576:864], upper[576:864]], axis=0)
    proj_ref[:, 0:128] = second[0:96]
    proj_ref[0:48, 128:192] = second[96:144, 0:64]
    proj_ref[48:96, 128:192] = second[96:144, 64:128]
    qkv_ref[0] = second[144:336, 0:96]
    qkv_ref[1] = second[336:528, 0:96]
    qkv_ref[2, :, 0:32] = second[144:336, 96:128]
    qkv_ref[2, :, 32:64] = second[336:528, 96:128]
    for i in range(4):
        qkv_ref[2, i * 48 : i * 48 + 48, 64:96] = second[528:576, i * 32 : i * 32 + 32]
    table = fields[0][864:1176]
    for r in range(12):
        for half in range(2):
            piece = table[r * 26 + half * 13 : r * 26 + half * 13 + 13] * table_scale
            for a in range(13):
                start = a * 256 + half * 128
                wide = min(128, 3312 - start)
                table_ref[r % 3, r // 3 : r // 3 + 1, start : start + wide] = piece[a : a + 1, 0:wide]
    for rows, out in ((gain, one_ref), (fields[0][1176:1184] + fields[1][1176:1184], two_ref)):
        line = rows[0:1]
        later = jnp.concatenate([line[:, 96:128], rows[1:2, 0:64]], axis=1)
        out[...] = jnp.where(lax.axis_index("tp") == 0, line[:, 0:96], later) * weight_scale


def unpack(weight_scale, table_scale, got, other):
    return pl.pallas_call(
        functools.partial(unpack_kernel, weight_scale, table_scale),
        out_shape=(
            shape((3, 192, 96), F32),
            shape((96, 192), F32),
            shape((192, 384), F32),
            shape((192, 384), F32),
            shape((1, 96), F32),
            shape((1, 96), F32),
            shape((3, 4, 3312), F32),
        ),
        compiler_params=VM,
        name="unpack",
    )(got, other)


def moved(value, band, sector, half):
    sizes = [lax.axis_size(name) for name in ("lat", "lon", "tp")]
    pairs = []
    for a in range(sizes[0]):
        for b in range(sizes[1]):
            for c in range(sizes[2]):
                source = ((a + band) % sizes[0], (b + sector) % sizes[1], (c + half) % sizes[2])
                pairs.append(tuple((x * sizes[1] + y) * sizes[2] + z for x, y, z in (source, (a, b, c))))
    return lax.ppermute(value, ("lat", "lon", "tp"), pairs)


def shifted_parts(quarters):
    return (
        quarters[3],
        moved(quarters[2], 0, 1, 0),
        moved(quarters[1], 1, 0, 0),
        moved(quarters[0], 1, 1, 0),
    )


def other_core(value):
    return lax.ppermute(value, "lat", [(a, a ^ 1) for a in range(lax.axis_size("lat"))])


def local(
    inputs,
    residual_mid,
    grad_out,
    mask_ids,
    key_valid,
    bias_index,
    pos_bias,
    norm1_gain,
    qkv_weight,
    proj_weight,
    norm2_gain,
    fc1_weight,
    fc2_weight,
):
    levels, lat_cells, lon_cells, channels = inputs.shape
    cell_count = levels * lat_cells * lon_cells
    weight_scale = (cell_count * lax.axis_size("lat") * lax.axis_size("lon")) ** (-0.5)
    table_scale = (lon_cells * lax.axis_size("lon") // 12) ** (-0.5)
    gain1, gain2 = norm1_gain.reshape(1, -1), norm2_gain.reshape(1, -1)

    def turned(field):
        return field.transpose(1, 2, 0, 3)

    x_in, mid_in, up_in = turned(inputs), turned(residual_mid), turned(grad_out)
    part2, first, first_send = head(mid_in, up_in, gain2, fc1_weight, fc2_weight.T)
    other2 = moved(part2, 0, 0, 1)
    stage, lo, hi, terms, code, *x = gather_first(
        bias_index, pos_bias[0].transpose(1, 0, 2), mask_ids.transpose(1, 0, 2), key_valid.transpose(1, 0, 2), x_in
    )
    xw = shifted_parts(x)
    *gm, gain_two = middle(mid_in, up_in, part2, other2, gain2, lo)
    gw = shifted_parts(gm)
    main, tail = gather_second(stage, lo, hi, terms, (gain_two, *xw[1:]))
    low, q, k, v, prob, att = forward(xw, gain1, qkv_weight, main, tail, code)
    part1, score, end, gcols, grad = backward(gw, proj_weight, qkv_weight, q, k, v, prob)
    other1 = moved(part1, 0, 0, 1)
    second, send = weigh(low, gcols, att, grad, first_send)
    table = scatter(score, end, lo, hi, second)
    sums = pack(first, second, other_core(send), table, gain_two)
    *g, gain_one = meet(part1, other1, xw)
    back = (moved(g[3], -1, -1, 0), moved(g[2], -1, 0, 0), moved(g[1], 0, -1, 0), g[0])
    own = add(lax.all_to_all(sums.reshape(32, 40, 128), "lon", 0, 0), gain_one, back[:3])
    totals = spread(own, moved(own, 2, 0, 0))
    result = finish(x, gm, back, gain1)
    got = lax.all_to_all(totals, "lon", 0, 0)
    qkv_out, proj_out, up_out, down_out, one, two, table_out = unpack(
        weight_scale, table_scale, got, other_core(got)
    )
    return (
        result.transpose(2, 0, 1, 3),
        qkv_out,
        proj_out,
        up_out,
        down_out.T,
        one.reshape(channels // lax.axis_size("tp")),
        two.reshape(channels // lax.axis_size("tp")),
        table_out.transpose(1, 0, 2)[None],
    )


def solution(mesh):
    return jax.shard_map(
        local,
        mesh=mesh,
        in_specs=(
            P(None, "lat", "lon", None),
            P(None, "lat", "lon", None),
            P(None, "lat", "lon", None),
            P(None, "lat", "lon"),
            P(None, "lat", "lon"),
            P(),
            P("lat", None, "tp", None),
            P(),
            P(None, None, "tp"),
            P("tp", None),
            P(),
            P(None, "tp"),
            P("tp", None),
        ),
        out_specs=(
            P(None, "lat", "lon", None),
            P(None, None, "tp"),
            P("tp", None),
            P(None, "tp"),
            P("tp", None),
            P("tp"),
            P("tp"),
            P("lat", None, "tp", None),
        ),
        check_vma=False,
    )
```

```python
import functools

import jax
import jax.numpy as jnp
import numpy as np
from jax import lax
from jax.experimental import pallas as pl
from jax.experimental.pallas import tpu as pltpu
from jax.sharding import PartitionSpec as P

HD = 32
EPSILON = 1e-05
EXCLUDED = -1e30
BF = jnp.bfloat16
F32 = jnp.float32
I32 = jnp.int32
VMEM = pl.BlockSpec(memory_space=pltpu.VMEM)
VM = pltpu.CompilerParams(vmem_limit_bytes=24 * 1024 * 1024)
ALL = pltpu.CompilerParams(vmem_limit_bytes=63 * 1024 * 1024)
SMEM = pl.BlockSpec(memory_space=pltpu.SMEM)
ANY = pl.BlockSpec(memory_space=pl.ANY)


def cost(microseconds):
    return pl.CostEstimate(flops=int(microseconds * 1e9), bytes_accessed=0, transcendentals=0)


def shape(dims, kind):
    return jax.ShapeDtypeStruct(dims, kind)


def both(own, other):
    return (own.astype(F32) + other.astype(F32)).astype(BF)


def fold(rows):
    return jnp.concatenate(
        [rows[:, 0:128], jnp.concatenate([rows[0:72, 128:192], rows[72:144, 128:192]], axis=1)], axis=0
    )


def unfold(rows):
    return jnp.concatenate(
        [rows[0:144], jnp.concatenate([rows[144:216, 0:64], rows[144:216, 64:128]], axis=0)], axis=1
    )


def dot_nn(a, b):
    return lax.dot_general(a, b, (((1,), (0,)), ((), ())), preferred_element_type=F32)


def dot_nt(a, b):
    return lax.dot_general(a, b, (((1,), (1,)), ((), ())), preferred_element_type=F32)


def dot_tn(a, b):
    return lax.dot_general(a, b, (((0,), (0,)), ((), ())), preferred_element_type=F32)


def layer_stats(rows):
    mean = jnp.mean(rows, axis=-1, keepdims=True)
    centred = rows - mean
    inverse = lax.rsqrt(jnp.mean(centred * centred, axis=-1, keepdims=True) + EPSILON)
    return centred * inverse, inverse


def norm_backward(grad_normed, gain, normed, inverse):
    scaled = grad_normed * gain
    first = jnp.mean(scaled, axis=-1, keepdims=True)
    second = jnp.mean(scaled * normed, axis=-1, keepdims=True)
    return (scaled - first - normed * second) * inverse


def gelu_pair(pre):
    cdf = 0.5 * (1.0 + lax.erf(pre * 0.7071067811865476))
    pdf = 0.3989422804014327 * jnp.exp(-0.5 * pre * pre)
    return pre * cdf, cdf + pre * pdf


def to_quarters(field_ref, scratch):
    for lat in range(6):
        for half in range(2):
            rows = field_ref[lat, half * 6 : half * 6 + 6].astype(F32).reshape(48, 192)
            start = ((lat // 3) * 2 + half) * 144 + (lat % 3) * 48
            scratch[start : start + 48, :] = rows


def level_order():
    order = np.zeros((144, 144), np.float32)
    for w in range(4):
        for cell in range(18):
            for level in range(2):
                order[w * 36 + cell * 2 + level, cell * 8 + (2 * w + 1 + level) % 8] = 1.0
    return jnp.asarray(order, BF)


def to_windows(parts, order, scratch):
    for s in range(4):
        rows = dot_nn(order, parts[s][...])
        for w in range(4):
            scratch[w * 144 + s * 36 : w * 144 + s * 36 + 36, :] = rows[w * 36 : w * 36 + 36]


def head_kernel(mid_hbm, up_hbm, gain_hbm, fc1_hbm, fc2_hbm, part_hbm, keep_hbm, send_hbm,
                mid_ref, up_ref, gain_ref, fc1_ref, fc2_ref, part_ref, grads_ref, mid_s, up_s, sem):
    pairs = (
        (mid_hbm, mid_ref),
        (gain_hbm, gain_ref),
        (fc1_hbm, fc1_ref),
        (up_hbm, up_ref),
        (fc2_hbm, fc2_ref),
    )
    copies = [pltpu.make_async_copy(a, b, sem.at[i]) for i, (a, b) in enumerate(pairs)]
    for copy in copies:
        copy.start()
    for copy in copies[:3]:
        copy.wait()
    to_quarters(mid_ref, mid_s)
    normed, _ = layer_stats(mid_s[...])
    lowered = (normed * gain_ref[...]).astype(BF)
    pre = dot_nn(lowered, fc1_ref[...])
    active, slopes = gelu_pair(pre)
    for copy in copies[3:]:
        copy.wait()
    writes = []
    to_quarters(up_ref, up_s)
    up = up_s[...].astype(BF)
    grad_pre = (dot_nn(up, fc2_ref[...]) * slopes).astype(BF)
    part_ref[...] = dot_nt(grad_pre, fc1_ref[...]).astype(BF)
    writes.append(pltpu.make_async_copy(part_ref, part_hbm, sem.at[6]))
    writes[-1].start()
    for start, grads in ((0, dot_tn(lowered, grad_pre)), (576, dot_tn(up, active.astype(BF)))):
        for j in range(3):
            grads_ref[start + j * 192 : start + j * 192 + 192, :] = grads[:, j * 128 : j * 128 + 128].astype(BF)
    core = lax.rem(lax.axis_index("lat"), 2)
    for i, (half, out) in enumerate(((core, keep_hbm), (1 - core, send_hbm))):
        piece = grads_ref.at[pl.ds(pl.multiple_of(half * 576, 16), 576)]
        writes.append(pltpu.make_async_copy(piece, out, sem.at[7 + i]))
        writes[-1].start()
    for write in writes:
        write.wait()


def head(mid, up, gain, fc1, fc2):
    return pl.pallas_call(
        head_kernel,
        out_shape=(shape((576, 192), BF), shape((576, 128), BF), shape((576, 128), BF)),
        in_specs=[ANY] * 5,
        out_specs=(ANY, ANY, ANY),
        scratch_shapes=[
            pltpu.VMEM((6, 12, 8, 192), BF),
            pltpu.VMEM((6, 12, 8, 192), BF),
            pltpu.VMEM((1, 192), F32),
            pltpu.VMEM((192, 384), BF),
            pltpu.VMEM((192, 384), BF),
            pltpu.VMEM((576, 192), BF),
            pltpu.VMEM((1152, 128), BF),
            pltpu.VMEM((576, 192), F32),
            pltpu.VMEM((576, 192), F32),
            pltpu.SemaphoreType.DMA((9,)),
        ],
        compiler_params=ALL,
        cost_estimate=cost(3),
        name="head",
    )(mid, up, gain, fc1, fc2)


def middle_kernel(mid_ref, up_ref, own_ref, other_ref, gain_ref, after_ref, o0, o1, o2, o3, gain_out, mid_s, up_s):
    to_quarters(mid_ref, mid_s)
    to_quarters(up_ref, up_s)
    normed, inverse = layer_stats(mid_s[...])
    grad = own_ref[...].astype(F32) + other_ref[...].astype(F32)
    gain_out[...] = jnp.sum(grad * normed, axis=0, keepdims=True)
    out = up_s[...] + norm_backward(grad, gain_ref[...], normed, inverse)
    for q, o in enumerate((o0, o1, o2, o3)):
        o[...] = out[q * 144 : q * 144 + 144].astype(BF)


def middle(mid, up, own, other, gain, after):
    return pl.pallas_call(
        middle_kernel,
        out_shape=tuple(shape((144, 192), BF) for _ in range(4)) + (shape((1, 192), F32),),
        in_specs=[VMEM] * 5 + [ANY],
        scratch_shapes=[pltpu.VMEM((576, 192), F32)] * 2,
        compiler_params=VM,
        cost_estimate=cost(1),
        name="middle",
    )(mid, up, own, other, gain, after)


def window_order():
    canon = np.arange(144).reshape(2, 2, 3, 2, 6).transpose(1, 3, 2, 4, 0).reshape(-1)
    order = np.zeros((144, 144), np.float32)
    order[np.arange(144), canon] = 1.0
    return order


def pack_tail(tail):
    spread = (lax.broadcasted_iota(I32, (16, 128), 1) & 15) == lax.broadcasted_iota(I32, (16, 128), 0)
    wide = dot_nn(tail, spread.astype(F32).astype(BF))
    here = (lax.broadcasted_iota(I32, (144, 128), 1) >> 4) == (lax.broadcasted_iota(I32, (144, 128), 0) & 7)
    wide = jnp.where(here, wide, 0.0).astype(BF)
    rows = (lax.broadcasted_iota(I32, (24, 144), 1) >> 3) == lax.broadcasted_iota(I32, (24, 144), 0)
    return dot_nn(rows.astype(F32).astype(BF), wide)


def one_hot(low):
    rows = lax.broadcasted_iota(I32, (256, 128), 0).astype(F32).astype(BF)
    return jnp.where(rows == low.astype(F32).astype(BF), jnp.ones((), BF), jnp.zeros((), BF))


def look_up(terms, lo_ref, hi_ref, stage, first_block, steps):
    half = (lax.broadcasted_iota(I32, (8, 128), 0) >> 2)

    def step(i, _):
        for pair in range(9):
            base = first_block + i * 18 + pair * 2
            hot = jnp.concatenate([one_hot(lo_ref[pl.ds(base + j, 1), :]) for j in range(2)], axis=1)
            found = dot_nn(terms, jnp.concatenate([hot, hot], axis=0))
            for j in range(2):
                cols = slice(j * 128, j * 128 + 128)
                high = hi_ref[pl.ds(base + j, 1), :]
                first = jnp.zeros((8, 128), F32)
                for c in range(13):
                    first = jnp.where(high == c, found[c * 8 : c * 8 + 8, cols], first)
                second = jnp.zeros((8, 128), F32)
                shifted = high - half
                for c in range(7):
                    second = jnp.where(shifted == 2 * c, found[104 + c * 8 : 112 + c * 8, cols], second)
                start = pl.multiple_of((base + j - first_block) * 16, 16)
                stage[pl.ds(start, 8), :] = first
                stage[pl.ds(start + 8, 8), :] = second + pltpu.roll(second, 4, 0)
        return 0

    lax.fori_loop(0, steps, step, 0, unroll=True)


def gather_first_kernel(index_ref, order_ref, bias_ref, ids_ref, valid_ref, x_ref,
                        stage, lo_ref, hi_ref, terms_ref, code_ref, o0, o1, o2, o3, table, x_s):
    to_quarters(x_ref, x_s)
    for q, out in enumerate((o0, o1, o2, o3)):
        out[...] = x_s[q * 144 : q * 144 + 144, :].astype(BF)
    index = index_ref[...]
    order = order_ref[...]
    pieces = []
    for part in (index & 127, index >> 7):
        moved = dot_nt(dot_nn(order, part.astype(F32).astype(BF)).astype(BF), order)
        pieces.append((moved[:, 0:128].astype(I32), pack_tail(moved[:, 128:144].astype(BF)).astype(I32)))
    for rows, low, high in ((slice(0, 144), pieces[0][0], pieces[1][0]), (slice(144, 168), pieces[0][1], pieces[1][1])):
        lo_ref[rows, :] = low + (high & 1) * 128
        hi_ref[rows, :] = high >> 1
    table[...] = jnp.zeros((160, 256), F32)
    for r in range(12):
        line = bias_ref[r % 3, r // 3 : r // 3 + 1, :]
        line = line - jnp.max(line, axis=1, keepdims=True)
        for c in range(13):
            wide = min(256, 3312 - c * 256)
            row = c * 8 + r if r < 8 else 104 + (c // 2) * 8 + (c % 2) * 4 + r - 8
            table[row : row + 1, 0:wide] = line[:, c * 256 : c * 256 + wide]
    upper = table[...].astype(BF)
    terms_ref[:, 0:256] = upper
    terms_ref[:, 256:512] = (table[...] - upper.astype(F32)).astype(BF)
    code = (ids_ref[...] * 2 + (valid_ref[...] > 0).astype(I32)).astype(F32).reshape(48, 12).astype(BF)
    row = lax.broadcasted_iota(I32, (24, 48), 0)
    column = lax.broadcasted_iota(I32, (24, 48), 1)
    lines = []
    for level in range(2):
        pick = ((row >> 2) * 8 + (row & 3) * 2 + level) == column
        picked = dot_nn(pick.astype(F32).astype(BF), code)
        lines += [picked[lat * 4 : lat * 4 + 4] for lat in range(6)]
    lines = jnp.concatenate(lines, axis=1)
    code_ref[...] = dot_nt(lines.astype(BF), order)
    look_up(terms_ref[...], lo_ref, hi_ref, stage, 0, 5)


def gather_first(index, bias, ids, valid, x):
    return pl.pallas_call(
        gather_first_kernel,
        out_shape=(
            shape((96 * 16, 128), F32),
            shape((168, 128), I32),
            shape((168, 128), I32),
            shape((160, 512), BF),
            shape((4, 144), F32),
        )
        + tuple(shape((144, 192), BF) for _ in range(4)),
        scratch_shapes=[pltpu.VMEM((160, 256), F32), pltpu.VMEM((576, 192), F32)],
        compiler_params=VM,
        cost_estimate=cost(0.5),
        name="gather_first",
    )(index, jnp.asarray(window_order(), BF), bias, ids, valid, x)


def gather_second_kernel(first_stage, lo_ref, hi_ref, terms_ref, a0, a1, a2, a3, main_ref, tail_ref, stage):
    look_up(terms_ref[...], lo_ref, hi_ref, stage, 90, 4)
    for r in range(12):
        main_ref[r, 0:90, :] = first_stage[pl.ds(r, 90, stride=16), :]
        main_ref[r, 90:144, :] = stage[pl.ds(r, 54, stride=16), :]
        packed = stage[pl.ds(54 * 16 + r, 18, stride=16), :]
        for s in range(8):
            tail_ref[r, pl.ds(s, 18, stride=8), :] = pltpu.roll(packed, 128 - 16 * s, 1) if s else packed


def gather_second(first_stage, lo, hi, terms, after):
    return pl.pallas_call(
        gather_second_kernel,
        out_shape=(shape((12, 144, 128), F32), shape((12, 192, 128), F32)),
        in_specs=[VMEM] * 4 + [ANY] * 4,
        scratch_shapes=[pltpu.VMEM((80 * 16, 128), F32)],
        compiler_params=VM,
        cost_estimate=cost(4),
        name="gather_second",
    )(first_stage, lo, hi, terms, *after)


def forward_kernel(x0, x1, x2, x3, order_ref, gain_ref, qkv_ref, main_ref, tail_ref, code_ref,
                   low_ref, q_ref, k_ref, v_ref, prob_ref, att_ref, scratch):
    to_windows((x0, x1, x2, x3), order_ref[...], scratch)
    normed, _ = layer_stats(scratch[...])
    low = (normed * gain_ref[...]).astype(BF)
    low_ref[...] = low
    for j, out in enumerate((q_ref, k_ref, v_ref)):
        out[...] = dot_nn(low, qkv_ref[j]).astype(BF)
    eye = lax.broadcasted_iota(I32, (144, 144), 0) == lax.broadcasted_iota(I32, (144, 144), 1)

    def window(w, _):
        rows = pl.ds(pl.multiple_of(w * 144, 16), 144)
        code = code_ref[pl.ds(w, 1), :].astype(I32)
        label = code >> 1
        column = jnp.sum(jnp.where(eye, label, 0), axis=1, keepdims=True)
        allowed = eye | ((column == label) & ((code & 1) > 0))
        query, key, value = q_ref[rows, :], k_ref[rows, :], v_ref[rows, :]
        heads = []
        for h in range(3):
            cols = slice(h * HD, h * HD + HD)
            bias = jnp.concatenate([main_ref[w * 3 + h], tail_ref[w * 3 + h, 0:144, 0:16]], axis=1)
            scores = dot_nt(query[:, cols], key[:, cols]) * (HD ** -0.5) + bias
            scores = jnp.where(allowed, scores, EXCLUDED)
            expo = jnp.exp(scores - jnp.max(scores, axis=-1, keepdims=True))
            prob = expo * (1.0 / jnp.sum(expo, axis=-1, keepdims=True))
            prob_ref[w * 3 + h] = prob
            heads.append(dot_nn(prob.astype(BF), value[:, cols]))
        att_ref[rows, :] = jnp.concatenate(heads, axis=1).astype(BF)
        return 0

    lax.fori_loop(0, 4, window, 0, unroll=True)


def forward(x, gain, qkv, main, tail, code):
    return pl.pallas_call(
        forward_kernel,
        out_shape=(
            shape((576, 192), BF),
            shape((576, 96), BF),
            shape((576, 96), BF),
            shape((576, 96), BF),
            shape((12, 144, 144), F32),
            shape((576, 96), BF),
        ),
        scratch_shapes=[pltpu.VMEM((576, 192), F32)],
        compiler_params=VM,
        cost_estimate=cost(5),
        name="forward",
    )(*x, level_order(), gain, qkv, main, tail, code)


def backward_kernel(g0, g1, g2, g3, order_ref, proj_ref, qkv_ref, q_ref, k_ref, v_ref, prob_ref,
                    part_ref, score_ref, end_ref, gcols, grad_ref, scratch, gatt):
    to_windows((g0, g1, g2, g3), order_ref[...], scratch)
    grad = scratch[...].astype(BF)
    grad_ref[...] = grad
    gatt[...] = dot_nt(grad, proj_ref[...]).astype(BF)

    def window(w, _):
        rows = pl.ds(pl.multiple_of(w * 144, 16), 144)
        query, key, value, above = q_ref[rows, :], k_ref[rows, :], v_ref[rows, :], gatt[rows, :]
        queries, keys, values = [], [], []
        for h in range(3):
            cols = slice(h * HD, h * HD + HD)
            prob = prob_ref[w * 3 + h]
            values.append(dot_tn(above[:, cols], prob.astype(BF)))
            grad_prob = dot_nt(above[:, cols], value[:, cols])
            score = prob * (grad_prob - jnp.sum(grad_prob * prob, axis=-1, keepdims=True))
            score_ref[w * 3 + h] = score[:, 0:128]
            end_ref[w * 3 + h, 0:144, 0:16] = score[:, 128:144]
            low_score = (score * (HD ** -0.5)).astype(BF)
            queries.append(dot_nn(low_score, key[:, cols]))
            keys.append(dot_tn(query[:, cols], low_score))
        gcols[0, rows, :] = jnp.concatenate(queries, axis=1).astype(BF)
        gcols[1, rows, :] = jnp.concatenate(keys, axis=0).T.astype(BF)
        gcols[2, rows, :] = jnp.concatenate(values, axis=0).T.astype(BF)
        return 0

    lax.fori_loop(0, 4, window, 0, unroll=True)
    total = None
    for j in range(3):
        term = dot_nt(gcols[j], qkv_ref[j])
        total = term if total is None else total + term
    scratch[...] = total
    for s in range(4):
        pieces = [scratch[w * 144 + s * 36 : w * 144 + s * 36 + 36, :] for w in range(4)]
        piece = jnp.concatenate(pieces, axis=0).astype(BF)
        part_ref[s * 144 : s * 144 + 144, :] = dot_tn(order_ref[...], piece).astype(BF)


def backward(g, proj, qkv, q, k, v, prob):
    return pl.pallas_call(
        backward_kernel,
        out_shape=(
            shape((576, 192), BF),
            shape((12, 144, 128), F32),
            shape((12, 192, 128), F32),
            shape((3, 576, 96), BF),
            shape((576, 192), BF),
        ),
        scratch_shapes=[pltpu.VMEM((576, 192), F32), pltpu.VMEM((576, 96), BF)],
        compiler_params=VM,
        cost_estimate=cost(7),
        name="backward",
    )(*g, level_order(), proj, qkv, q, k, v, prob)


def scatter_kernel(score_ref, end_ref, lo_ref, hi_ref, after_ref, out_ref, tails):
    total = jnp.zeros((256, 192), F32)
    place = lax.broadcasted_iota(I32, (16, 128), 0)
    group = lax.broadcasted_iota(I32, (18, 128), 1) >> 4
    for r in range(12):
        packed = end_ref[r, pl.ds(0, 18, stride=8), :]
        for j in range(1, 8):
            moved_on = pltpu.roll(end_ref[r, pl.ds(j, 18, stride=8), :], 16 * j, 1)
            packed = jnp.where(group == j, moved_on, packed)
        tails[r, 0:18, :] = packed
    for i in range(9):
        left, right = [], []
        for j in range(18):
            row = slice(i * 18 + j, i * 18 + j + 1)
            here = place == hi_ref[row, :]
            right.append(one_hot(lo_ref[row, :]))
            lines = [score_ref[r, row, :] if i < 8 else tails[r, j : j + 1, :] for r in range(12)]
            left.append(jnp.concatenate([jnp.where(here, line, 0.0).astype(BF) for line in lines], axis=0))
        total = total + dot_nt(jnp.concatenate(right, axis=1), jnp.concatenate(left, axis=1))
    out_ref[...] = total.T


def scatter(score, end, lo, hi, after):
    return pl.pallas_call(
        scatter_kernel,
        out_shape=shape((192, 256), F32),
        in_specs=[VMEM] * 4 + [ANY],
        scratch_shapes=[pltpu.VMEM((12, 24, 128), F32)],
        compiler_params=VM,
        cost_estimate=cost(4),
        name="scatter",
    )(score, end, lo, hi, after)


def weigh_kernel(low_ref, gcols, att_ref, grad_ref, first_ref, keep_ref, send_ref, grads_ref):
    gproj = dot_tn(att_ref[...], grad_ref[...]).astype(BF)
    grads_ref[0:96, :] = gproj[:, 0:128]
    grads_ref[96:144, :] = jnp.concatenate([gproj[0:48, 128:192], gproj[48:96, 128:192]], axis=1)
    low = low_ref[...]
    a, b, c = [dot_tn(low, gcols[j]).astype(BF) for j in range(3)]
    grads_ref[144:336, :] = jnp.concatenate([a, c[:, 0:32]], axis=1)
    grads_ref[336:528, :] = jnp.concatenate([b, c[:, 32:64]], axis=1)
    grads_ref[528:576, :] = jnp.concatenate([c[i * 48 : i * 48 + 48, 64:96] for i in range(4)], axis=1)
    core = lax.rem(lax.axis_index("lat"), 2)
    keep_ref[...] = grads_ref[pl.ds(pl.multiple_of(core * 288, 16), 288), :]
    send_ref[0:576, :] = first_ref[...]
    send_ref[576:864, :] = grads_ref[pl.ds(pl.multiple_of((1 - core) * 288, 16), 288), :]


def weigh(low, gcols, att, grad, first):
    return pl.pallas_call(
        weigh_kernel,
        out_shape=(shape((288, 128), BF), shape((864, 128), BF)),
        scratch_shapes=[pltpu.VMEM((576, 128), BF)],
        compiler_params=VM,
        cost_estimate=cost(0.5),
        name="weigh",
    )(low, gcols, att, grad, first)


def gain_rows(line):
    none = jnp.zeros((1, 64), F32)
    return [line[:, 0:128], jnp.concatenate([line[:, 128:192], none], axis=1)]


def pack_kernel(first_ref, second_ref, other_ref, table_ref, gain_ref, out_ref):
    out_ref[0:576, :] = both(first_ref[...], other_ref[0:576, :])
    out_ref[576:864, :] = both(second_ref[...], other_ref[576:864, :])
    rows = []
    for r in range(12):
        pair = table_ref[r * 16 : r * 16 + 13, :]
        rows += [pair[:, 0:128], pair[:, 128:256]]
    rows += gain_rows(gain_ref[...]) + [jnp.zeros((102, 128), F32)]
    out_ref[864:1280, :] = jnp.concatenate(rows, axis=0).astype(BF)


def pack(first, second, other, table, gain):
    return pl.pallas_call(
        pack_kernel, out_shape=shape((1280, 128), BF), compiler_params=VM, cost_estimate=cost(1), name="pack"
    )(first, second, other, table, gain)


def meet_kernel(own_ref, other_ref, x0, x1, x2, x3, g0, g1, g2, g3, gain_out):
    gain = jnp.zeros((1, 192), F32)
    for s, (x, g) in enumerate(zip((x0, x1, x2, x3), (g0, g1, g2, g3))):
        rows = slice(s * 144, s * 144 + 144)
        grad = own_ref[rows, :].astype(F32) + other_ref[rows, :].astype(F32)
        normed, _ = layer_stats(x[...].astype(F32))
        gain = gain + jnp.sum(grad * normed, axis=0, keepdims=True)
        g[...] = fold(grad).astype(BF)
    gain_out[...] = jnp.concatenate(gain_rows(gain) + [jnp.zeros((6, 128), F32)], axis=0)


def meet(own, other, x):
    return pl.pallas_call(
        meet_kernel,
        out_shape=tuple(shape((216, 128), BF) for _ in range(4)) + (shape((8, 128), F32),),
        compiler_params=VM,
        cost_estimate=cost(60),
        name="meet",
    )(own, other, *x)


def finish_kernel(x0, x1, x2, x3, m0, m1, m2, m3, g0, g1, g2, g3, gain_ref, out_ref):
    for q, (x, m, g) in enumerate(zip((x0, x1, x2, x3), (m0, m1, m2, m3), (g0, g1, g2, g3))):
        normed, inverse = layer_stats(x[...].astype(F32))
        rows = m[...].astype(F32) + norm_backward(unfold(g[...].astype(F32)), gain_ref[...], normed, inverse)
        for lat in range(3):
            piece = rows[lat * 48 : lat * 48 + 48].reshape(6, 8, 192)
            out_ref[(q // 2) * 3 + lat, (q % 2) * 6 : (q % 2) * 6 + 6] = piece.astype(BF)


def finish(x, m, g, gain):
    return pl.pallas_call(
        finish_kernel,
        out_shape=shape((6, 12, 8, 192), BF),
        compiler_params=VM,
        cost_estimate=cost(1),
        name="finish",
    )(*x, *m, *g, gain)


def add_kernel(got_ref, gain_ref, b0, b1, b2, out_ref):
    total = got_ref[0].astype(F32)
    for i in range(1, 32):
        total = total + got_ref[i].astype(F32)
    out_ref[...] = jnp.concatenate([total, gain_ref[...]], axis=0).astype(BF)


def add(got, gain, after):
    return pl.pallas_call(
        add_kernel,
        out_shape=shape((48, 128), BF),
        in_specs=[VMEM] * 2 + [ANY] * 3,
        compiler_params=VM,
        cost_estimate=cost(1),
        name="add",
    )(got, gain, *after)


def spread_kernel(own_ref, other_ref, out_ref):
    own = own_ref[...].astype(F32)
    place = lax.broadcasted_iota(I32, (48, 128), 0)
    row = lax.axis_index("lon") * 40 + place
    table = (row >= 864) & (row < 1176) & (place < 40)
    total = own + jnp.where(table, 0.0, other_ref[...].astype(F32))
    out_ref[...] = jnp.broadcast_to(total.astype(BF)[None], (32, 48, 128))


def spread(own, other):
    return pl.pallas_call(
        spread_kernel, out_shape=shape((32, 48, 128), BF), compiler_params=VM, cost_estimate=cost(1), name="spread"
    )(own, other)


def unpack_kernel(weight_scale, table_scale, own_ref, other_ref,
                  qkv_ref, proj_ref, upg_ref, down_ref, one_ref, two_ref, table_ref):
    swap = lax.rem(lax.axis_index("lat"), 2) == 1
    fields = []
    gain = jnp.zeros((8, 128), F32)
    for ref in (own_ref, other_ref):
        pieces = [ref[c].astype(F32) for c in range(32)]
        fields.append(jnp.concatenate([piece[0:40] for piece in pieces], axis=0))
        for piece in pieces:
            gain = gain + piece[40:48]
    own, other = fields[0][0:864] * weight_scale, fields[1][0:864] * weight_scale
    lower, upper = jnp.where(swap, other, own), jnp.where(swap, own, other)
    for j in range(3):
        upg_ref[:, j * 128 : j * 128 + 128] = lower[j * 192 : j * 192 + 192]
        down_ref[:, j * 128 : j * 128 + 128] = upper[j * 192 : j * 192 + 192]
    second = jnp.concatenate([lower[576:864], upper[576:864]], axis=0)
    proj_ref[:, 0:128] = second[0:96]
    proj_ref[0:48, 128:192] = second[96:144, 0:64]
    proj_ref[48:96, 128:192] = second[96:144, 64:128]
    qkv_ref[0] = second[144:336, 0:96]
    qkv_ref[1] = second[336:528, 0:96]
    qkv_ref[2, :, 0:32] = second[144:336, 96:128]
    qkv_ref[2, :, 32:64] = second[336:528, 96:128]
    for i in range(4):
        qkv_ref[2, i * 48 : i * 48 + 48, 64:96] = second[528:576, i * 32 : i * 32 + 32]
    table = fields[0][864:1176]
    for r in range(12):
        for half in range(2):
            piece = table[r * 26 + half * 13 : r * 26 + half * 13 + 13] * table_scale
            for a in range(13):
                start = a * 256 + half * 128
                wide = min(128, 3312 - start)
                table_ref[r % 3, r // 3 : r // 3 + 1, start : start + wide] = piece[a : a + 1, 0:wide]
    for rows, out in ((gain, one_ref), (fields[0][1176:1184] + fields[1][1176:1184], two_ref)):
        line = rows[0:1]
        later = jnp.concatenate([line[:, 96:128], rows[1:2, 0:64]], axis=1)
        out[...] = jnp.where(lax.axis_index("tp") == 0, line[:, 0:96], later) * weight_scale


def unpack(weight_scale, table_scale, got, other):
    return pl.pallas_call(
        functools.partial(unpack_kernel, weight_scale, table_scale),
        out_shape=(
            shape((3, 192, 96), F32),
            shape((96, 192), F32),
            shape((192, 384), F32),
            shape((192, 384), F32),
            shape((1, 96), F32),
            shape((1, 96), F32),
            shape((3, 4, 3312), F32),
        ),
        compiler_params=VM,
        name="unpack",
    )(got, other)


def moved(value, band, sector, half):
    sizes = [lax.axis_size(name) for name in ("lat", "lon", "tp")]
    pairs = []
    for a in range(sizes[0]):
        for b in range(sizes[1]):
            for c in range(sizes[2]):
                source = ((a + band) % sizes[0], (b + sector) % sizes[1], (c + half) % sizes[2])
                pairs.append(tuple((x * sizes[1] + y) * sizes[2] + z for x, y, z in (source, (a, b, c))))
    return lax.ppermute(value, ("lat", "lon", "tp"), pairs)


def shifted_parts(quarters):
    return (
        quarters[3],
        moved(quarters[2], 0, 1, 0),
        moved(quarters[1], 1, 0, 0),
        moved(quarters[0], 1, 1, 0),
    )


def other_core(value):
    return lax.ppermute(value, "lat", [(a, a ^ 1) for a in range(lax.axis_size("lat"))])


def local(
    inputs,
    residual_mid,
    grad_out,
    mask_ids,
    key_valid,
    bias_index,
    pos_bias,
    norm1_gain,
    qkv_weight,
    proj_weight,
    norm2_gain,
    fc1_weight,
    fc2_weight,
):
    levels, lat_cells, lon_cells, channels = inputs.shape
    cell_count = levels * lat_cells * lon_cells
    weight_scale = (cell_count * lax.axis_size("lat") * lax.axis_size("lon")) ** (-0.5)
    table_scale = (lon_cells * lax.axis_size("lon") // 12) ** (-0.5)
    gain1, gain2 = norm1_gain.reshape(1, -1), norm2_gain.reshape(1, -1)

    def turned(field):
        return field.transpose(1, 2, 0, 3)

    x_in, mid_in, up_in = turned(inputs), turned(residual_mid), turned(grad_out)
    part2, first, first_send = head(mid_in, up_in, gain2, fc1_weight, fc2_weight.T)
    other2 = moved(part2, 0, 0, 1)
    stage, lo, hi, terms, code, *x = gather_first(
        bias_index, pos_bias[0].transpose(1, 0, 2), mask_ids.transpose(1, 0, 2), key_valid.transpose(1, 0, 2), x_in
    )
    xw = shifted_parts(x)
    *gm, gain_two = middle(mid_in, up_in, part2, other2, gain2, lo)
    gw = shifted_parts(gm)
    main, tail = gather_second(stage, lo, hi, terms, (gain_two, *xw[1:]))
    low, q, k, v, prob, att = forward(xw, gain1, qkv_weight, main, tail, code)
    part1, score, end, gcols, grad = backward(gw, proj_weight, qkv_weight, q, k, v, prob)
    other1 = moved(part1, 0, 0, 1)
    second, send = weigh(low, gcols, att, grad, first_send)
    table = scatter(score, end, lo, hi, second)
    sums = pack(first, second, other_core(send), table, gain_two)
    *g, gain_one = meet(part1, other1, xw)
    back = (moved(g[3], -1, -1, 0), moved(g[2], -1, 0, 0), moved(g[1], 0, -1, 0), g[0])
    own = add(lax.all_to_all(sums.reshape(32, 40, 128), "lon", 0, 0), gain_one, back[:3])
    totals = spread(own, moved(own, 2, 0, 0))
    result = finish(x, gm, back, gain1)
    got = lax.all_to_all(totals, "lon", 0, 0)
    qkv_out, proj_out, up_out, down_out, one, two, table_out = unpack(
        weight_scale, table_scale, got, other_core(got)
    )
    return (
        result.transpose(2, 0, 1, 3),
        qkv_out,
        proj_out,
        up_out,
        down_out.T,
        one.reshape(channels // lax.axis_size("tp")),
        two.reshape(channels // lax.axis_size("tp")),
        table_out.transpose(1, 0, 2)[None],
    )


def solution(mesh):
    return jax.shard_map(
        local,
        mesh=mesh,
        in_specs=(
            P(None, "lat", "lon", None),
            P(None, "lat", "lon", None),
            P(None, "lat", "lon", None),
            P(None, "lat", "lon"),
            P(None, "lat", "lon"),
            P(),
            P("lat", None, "tp", None),
            P(),
            P(None, None, "tp"),
            P("tp", None),
            P(),
            P(None, "tp"),
            P("tp", None),
        ),
        out_specs=(
            P(None, "lat", "lon", None),
            P(None, None, "tp"),
            P("tp", None),
            P(None, "tp"),
            P("tp", None),
            P("tp"),
            P("tp"),
            P("lat", None, "tp", None),
        ),
        check_vma=False,
    )
```
